32 devices in a mesh: section: 2 (over core), dp: 8 (over z, y), head: 2 (over x).
Axes of the slice: x: 2, y: 2, z: 4, core: 2. Of those that a mesh axis runs over, the one named last changes fastest.
Arguments:
- tokens: bfloat16 [2, 2048, 1152], P(None, 'dp'), may hold values from -6 to 6
- kept_mask: int32 [2, 8, 256], P(None, 'dp'), may hold values 0 or 1
- timesteps: int32 [2, 8], P(None, 'dp'), may hold values from 0 to 999
- labels: int32 [2, 8], P(None, 'dp'), may hold values from 0 to 999
- w_qkv: bfloat16 [2, 1152, 3, 1152], P('section', 'dp', None, 'head'), may hold values from -0.1875 to 0.1875
- b_qv: bfloat16 [2, 2, 1152], P('section', None, 'head'), may hold values from -2 to 2
- w_out: bfloat16 [2, 1152, 1152], P('section', 'head', 'dp'), may hold values from -0.5 to 0.5
- b_out: bfloat16 [2, 1152], P('section'), may hold values from -2 to 2
- w_up: bfloat16 [2, 1152, 4608], P('section', 'dp', 'head'), may hold values from -0.1875 to 0.1875
- b_up: bfloat16 [2, 4608], P('section', 'head'), may hold values from -2 to 2
- w_down: bfloat16 [2, 4608, 1152], P('section', 'head', 'dp'), may hold values from -0.1875 to 0.1875
- b_down: bfloat16 [2, 1152], P('section'), may hold values from -2 to 2
- w_ada: bfloat16 [2, 1152, 6, 1152], P('section', 'dp', None, 'head'), may hold values from -0.1875 to 0.1875
- b_ada: bfloat16 [2, 6, 1152], P('section', None, 'head'), may hold values from -3 to 3
- rel_table: bfloat16 [2, 16, 511], P('section', 'head'), may hold values from -5 to 5
- mask_token: bfloat16 [1152], replicated, may hold values from -5 to 5
- class_table: bfloat16 [1000, 1152], replicated, may hold values from -5 to 5
- out_grad: bfloat16 [2, 2048, 1152], P(None, 'dp'), may hold values from -6 to 6
Outputs:
- block_outputs: float32 [2, 2, 2048, 1152], P('section', None, 'dp')
- input_grads: float32 [2, 2, 2048, 1152], P('section', None, 'dp')
- g_w_qkv: float32 [2, 1152, 3, 1152], P('section', 'dp', None, 'head')
- g_b_qv: float32 [2, 2, 1152], P('section', None, 'head')
- g_w_out: float32 [2, 1152, 1152], P('section', 'head', 'dp')
- g_b_out: float32 [2, 1152], P('section', 'head')
- g_w_up: float32 [2, 1152, 4608], P('section', 'dp', 'head')
- g_b_up: float32 [2, 4608], P('section', 'head')
- g_w_down: float32 [2, 4608, 1152], P('section', 'head', 'dp')
- g_b_down: float32 [2, 1152], P('section', 'head')
- g_w_ada: float32 [2, 1152, 6, 1152], P('section', 'dp', None, 'head')
- g_b_ada: float32 [2, 6, 1152], P('section', None, 'head')
- g_rel_table: float32 [2, 16, 511], P('section', 'head')
- g_mask_token: float32 [1152], P('head')
- g_class_table: float32 [1000, 1152], P(None, 'head')
The draws below stay inside these ranges and needn't reach their ends.
All inputs are finite; a program needn't handle non-finite values. No bound on the sum of `kept_mask` on one device may be relied on, other than what follows from the above.
Results may differ from the reference program's by a relative error of at most 0.03.
Values may be sent and summed in bfloat16 or wider, within the bound.
A program may use at most 384 MiB of HBM per device.

```python
import math
import jax
import jax.numpy as jnp
from jax import lax

D = 1152
HEADS = 16
FF = 4608
NCLS = 1000
L = 256
MICRO = 2
IMAGES = 1
ROWS = 256
TOKENS = 2048
IMAGES_ALL = 8
N_SECTION = 2
N_DP = 8


def set_ends(array, key, least, high):
    longest = array.shape.index(max(array.shape))
    spots = []
    for shift in (0, 1):
        where = [jax.random.randint(jax.random.fold_in(key, axis), (), 0, length) for axis, length in enumerate(array.shape)]
        where[longest] = (where[longest] + shift) % array.shape[longest]
        spots.append(tuple(where))
    return array.at[spots[0]].set(least).at[spots[1]].set(high)


def level_of(own_key, shape, pieces, low, high):
    def one(dim, blocks):
        heights = jax.random.uniform(jax.random.fold_in(jax.random.fold_in(own_key, 6), dim), (blocks,), jnp.float32, low / len(pieces), high / len(pieces))
        return jnp.repeat(jnp.exp(heights), shape[dim] // blocks).reshape((-1,) + (1,) * (len(shape) - dim - 1))

    loudness = one(*pieces[0])
    for cut in pieces[1:]:
        loudness = loudness * one(*cut)
    return loudness


def scatter_about(key, shape, spread, reach, cuts=(), kind=jnp.bfloat16):
    values = spread * jax.random.normal(key, shape, jnp.float32)
    if cuts:
        values = values * level_of(key, shape, cuts, -0.22, 0.18)
    return jnp.clip(values, -reach, reach).astype(kind)


def setup_inputs(seed: int = 0) -> dict:
    arg_keys = jax.random.split(jax.random.key(seed), 19)
    tokens = scatter_about(arg_keys[0], (MICRO, TOKENS, D), 1.0, 6.0, ((1, 8),))
    kept_mask = set_ends((jax.random.randint(arg_keys[1], (MICRO, IMAGES_ALL, L), 0, 10) < 7).astype(jnp.int32), jax.random.fold_in(arg_keys[1], 1), 0, 1)
    timesteps = set_ends(jax.random.randint(arg_keys[2], (MICRO, IMAGES_ALL), 0, 1000), jax.random.fold_in(arg_keys[2], 1), 0, 999).astype(jnp.int32)
    labels = set_ends(jax.random.randint(arg_keys[3], (MICRO, IMAGES_ALL), 0, NCLS), jax.random.fold_in(arg_keys[3], 1), 0, NCLS - 1).astype(jnp.int32)
    w_qkv = scatter_about(arg_keys[4], (N_SECTION, D, 3, D), D ** -0.5, 0.1875, ((0, 2), (1, 8), (3, 2)))
    b_qv = scatter_about(arg_keys[5], (N_SECTION, 2, D), 0.3, 2.0, ((0, 2), (2, 2)))
    w_out = scatter_about(arg_keys[6], (N_SECTION, D, D), (D // 8) ** -0.5, 0.5, ((0, 2), (1, 2), (2, 8)))
    b_out = scatter_about(arg_keys[7], (N_SECTION, D), 0.3, 2.0, ((0, 2),))
    w_up = scatter_about(arg_keys[8], (N_SECTION, D, FF), D ** -0.5, 0.1875, ((0, 2), (1, 8), (2, 2)))
    b_up = scatter_about(arg_keys[9], (N_SECTION, FF), 0.3, 2.0, ((0, 2), (1, 2)))
    w_down = scatter_about(arg_keys[10], (N_SECTION, FF, D), (FF // 4) ** -0.5, 0.1875, ((0, 2), (1, 2), (2, 8)))
    b_down = scatter_about(arg_keys[11], (N_SECTION, D), 0.3, 2.0, ((0, 2),))
    w_ada = scatter_about(arg_keys[12], (N_SECTION, D, 6, D), D ** -0.5, 0.1875, ((0, 2), (1, 8), (3, 2)))
    b_ada = scatter_about(arg_keys[13], (N_SECTION, 6, D), 0.5, 3.0, ((0, 2), (2, 2)))
    rel_table = scatter_about(arg_keys[14], (N_SECTION, HEADS, 2 * L - 1), 1.0, 5.0, ((0, 2), (1, 2)))
    mask_token = scatter_about(arg_keys[15], (D,), 1.0, 5.0)
    class_table = scatter_about(arg_keys[16], (NCLS, D), 1.0, 5.0)
    out_grad = scatter_about(arg_keys[17], (MICRO, TOKENS, D), 1.0, 6.0, ((1, 8),))
    return dict(tokens=tokens, kept_mask=kept_mask, timesteps=timesteps, labels=labels, w_qkv=w_qkv, b_qv=b_qv, w_out=w_out, b_out=b_out, w_up=w_up, b_up=b_up, w_down=w_down, b_down=b_down, w_ada=w_ada, b_ada=b_ada, rel_table=rel_table, mask_token=mask_token, class_table=class_table, out_grad=out_grad)


@jax.custom_vjp
def low(v):
    return lax.optimization_barrier(v.astype(jnp.bfloat16)).astype(jnp.float32)

@jax.custom_vjp
def low_back(v):
    return v

def low_keep(v):
    return (low(v), None)

def low_pass(kept, grad):
    return (grad,)

def back_keep(v):
    return (v, None)

def back_low(kept, grad):
    return (low(grad),)
low.defvjp(low_keep, low_pass)
low_back.defvjp(back_keep, back_low)
PRECISE = lax.Precision.HIGHEST
EPSILON = 1e-06
NEGATIVE = -1e+30

def round_both(values_in):
    return low(low_back(values_in))

def time_features(step_ids, model_width):
    half_width = model_width // 2
    frequency = jnp.exp(-math.log(10000.0) * jnp.arange(half_width).astype(jnp.float32) / half_width)
    angles = step_ids.astype(jnp.float32)[..., None] * frequency
    return jnp.concatenate([jnp.cos(angles), jnp.sin(angles)], axis=-1)

def layout(mask_group, image_count, length):
    kept_flags = mask_group.reshape(-1).astype(jnp.int32)
    row_count = kept_flags.shape[0]
    slot_ids = jnp.arange(row_count, dtype=jnp.int32)
    source = jnp.where(kept_flags == 1, jnp.cumsum(kept_flags).astype(jnp.int32) - 1, row_count).astype(jnp.int32)
    image_of = (slot_ids // length).astype(jnp.int32)
    positions = (slot_ids % length).astype(jnp.int32)
    packed_pos = jnp.zeros((row_count,), jnp.int32).at[source].set(positions, mode='drop')
    packed_seg = jnp.full((row_count,), image_count, jnp.int32).at[source].set(image_of, mode='drop')
    return (kept_flags, source, image_of, positions, packed_pos, packed_seg)

def normalize(values_in):
    centered = values_in - lax.optimization_barrier(jnp.mean(values_in, axis=-1, keepdims=True))
    return centered * lax.rsqrt(lax.optimization_barrier(jnp.mean(centered * centered, axis=-1, keepdims=True)) + EPSILON)

def block(state_in, segment, positions, image_rows, cond_low, params, length):
    w_qkv, b_qv, w_out, b_out, w_up, b_up, w_down, b_down, w_ada, b_ada, rel_table = params
    row_count, model_width = state_in.shape
    head_count = rel_table.shape[0]
    head_dim = model_width // head_count
    score_scale = 1.0 / math.sqrt(head_dim)
    mod_table = jnp.einsum('id,dke->ike', cond_low, w_ada, precision=PRECISE) + b_ada
    picker = (image_rows[:, None] == jnp.arange(mod_table.shape[0])[None, :]).astype(jnp.float32)
    per_row = jnp.einsum('ri,ike->rke', picker, mod_table, precision=PRECISE)
    normed = low(normalize(state_in) * (1.0 + per_row[:, 1]) + per_row[:, 0])
    joined = jnp.einsum('rd,dke->rke', normed, w_qkv, precision=PRECISE)
    shape_heads = (row_count, head_count, head_dim)
    queries = round_both(joined[:, 0] + b_qv[0]).reshape(shape_heads)
    keys_all = round_both(joined[:, 1]).reshape(shape_heads)
    values_all = round_both(joined[:, 2] + b_qv[1]).reshape(shape_heads)
    offsets = positions[:, None] - positions[None, :] + length - 1
    logits = jnp.einsum('qhd,khd->hqk', queries, keys_all, precision=PRECISE) * score_scale + rel_table[:, offsets]
    logits = jnp.where((segment[:, None] == segment[None, :])[None], low_back(logits), NEGATIVE)
    att_probs = low(jax.nn.softmax(logits, axis=-1))
    att_mixed = jnp.einsum('hqk,khd->qhd', att_probs, values_all, precision=PRECISE)
    att_mixed = round_both(att_mixed.reshape(row_count, model_width))
    branch = low_back(jnp.dot(att_mixed, w_out, precision=PRECISE) + b_out)
    middle = state_in + per_row[:, 2] * branch
    normed_two = low(normalize(middle) * (1.0 + per_row[:, 4]) + per_row[:, 3])
    hidden_pre = low_back(jnp.dot(normed_two, w_up, precision=PRECISE) + b_up)
    hidden = low(jax.nn.gelu(hidden_pre, approximate=True))
    result = low_back(jnp.dot(hidden, w_down, precision=PRECISE) + b_down)
    return middle + per_row[:, 5] * result

def reference(tokens, kept_mask, timesteps, labels, w_qkv, b_qv, w_out, b_out, w_up, b_up, w_down, b_down, w_ada, b_ada, rel_table, mask_token, class_table, out_grad):
    micro_count, token_count, model_width = tokens.shape
    group_count = micro_count * N_DP
    stacked = tuple((item.astype(jnp.float32) for item in (w_qkv, b_qv, w_out, b_out, w_up, b_up, w_down, b_down, w_ada, b_ada, rel_table)))
    token_groups = tokens.astype(jnp.float32).reshape(group_count, ROWS, model_width)
    mask_groups = kept_mask.reshape(group_count, IMAGES, L)
    step_groups = timesteps.reshape(group_count, IMAGES)
    label_groups = labels.reshape(group_count, IMAGES)
    zero_rows = jnp.zeros_like(token_groups)

    def forward(params, token_in, mask_in, table_in, zero_in):
        first_params = tuple((item[0] for item in params))
        second_params = tuple((item[1] for item in params))

        def one_group(group_items):
            token_rows, mask_group, step_row, label_row, zero_rows_in = group_items
            kept_flags, source, image_of, positions, packed_pos, packed_seg = layout(mask_group, IMAGES, L)
            label_pick = (label_row[:, None] == jnp.arange(NCLS)[None, :]).astype(jnp.float32)
            condition = jnp.dot(label_pick, table_in, precision=PRECISE) + time_features(step_row, model_width)
            cond_low = jax.nn.silu(condition)
            encoded = block(token_rows, packed_seg, packed_pos, jnp.minimum(packed_seg, IMAGES - 1), cond_low, first_params, L)
            sent_rows = round_both(encoded)
            picked = jnp.take(sent_rows, jnp.minimum(source, ROWS - 1), axis=0)
            placed = jnp.where(kept_flags[:, None] == 1, picked, mask_in[None, :]) + zero_rows_in
            decoded = block(placed, image_of, positions, image_of, cond_low, second_params, L)
            return (encoded, decoded)
        return lax.map(jax.checkpoint(one_group), (token_in, mask_groups, step_groups, label_groups, zero_in))
    primal, pullback = jax.vjp(forward, stacked, token_groups, mask_token.astype(jnp.float32), class_table.astype(jnp.float32), zero_rows)
    cot_decoded = out_grad.astype(jnp.float32).reshape(group_count, ROWS, model_width)
    param_grads, token_grad, mask_grad, table_grad, placed_grad = pullback((jnp.zeros_like(primal[0]), cot_decoded))
    shape_back = (micro_count, token_count, model_width)
    outputs = jnp.stack([primal[0].reshape(shape_back), primal[1].reshape(shape_back)])
    inputs_grad = jnp.stack([token_grad.reshape(shape_back), placed_grad.reshape(shape_back)])
    return (outputs, inputs_grad, param_grads[0], param_grads[1], param_grads[2], param_grads[3], param_grads[4], param_grads[5], param_grads[6], param_grads[7], param_grads[8], param_grads[9], param_grads[10], mask_grad, table_grad)
```

```python
import math

import jax
import jax.numpy as jnp
from jax import lax
from jax.experimental import pallas as pl
from jax.experimental.pallas import tpu as pltpu
from jax.sharding import PartitionSpec as P

PRECISE = lax.Precision.HIGHEST
EPSILON = 1e-06
NEGATIVE = -1e30
MESH = pl.DeviceIdType.MESH
BF = jnp.bfloat16
F32 = jnp.float32


def time_features(step_ids, model_width):
    half_width = model_width // 2
    frequency = jnp.exp(-math.log(10000.0) * jnp.arange(half_width).astype(F32) / half_width)
    angles = step_ids.astype(F32)[..., None] * frequency
    return jnp.concatenate([jnp.cos(angles), jnp.sin(angles)], axis=-1)


def swap(value, axis):
    return lax.ppermute(value, axis, [(0, 1), (1, 0)])


def pick(index, first, second):
    return jnp.where(index == 0, first, second)


def gather_kernel(chain, x_ref, w_ref, ssem, rsem, lsem):
    pieces = x_ref.shape[0]
    core = lax.axis_index("section")
    dp = lax.axis_index("dp")
    head = lax.axis_index("head")
    z = dp // 2
    y = dp % 2
    mate = z + 1 - 2 * (z % 2)

    def device(c, zz, yy):
        return (c, zz * 2 + yy, head)

    barrier = pltpu.get_barrier_semaphore()

    @pl.when(z < chain - 1)
    def _():
        pl.semaphore_signal(barrier, inc=1, device_id=device(core, z + 1, y), device_id_type=MESH)

    @pl.when(z > 0)
    def _():
        pl.semaphore_signal(barrier, inc=1, device_id=device(core, z - 1, y), device_id_type=MESH)

    pl.semaphore_signal(barrier, inc=1, device_id=device(core, z, 1 - y), device_id_type=MESH)
    pl.semaphore_signal(barrier, inc=1, device_id=device(1 - core, z, y), device_id_type=MESH)

    @pl.when((z > 0) & (z < chain - 1))
    def _():
        pl.semaphore_wait(barrier, 4)

    @pl.when((z == 0) | (z == chain - 1))
    def _():
        pl.semaphore_wait(barrier, 3)

    def block(p, zz, yy):
        return w_ref.at[p, core, zz * 2 + yy]

    def remote(src, dst, p, kind, target):
        return pltpu.make_async_remote_copy(
            src_ref=src,
            dst_ref=dst,
            send_sem=ssem.at[p, kind],
            recv_sem=rsem.at[p, kind],
            device_id=target,
            device_id_type=MESH,
        )

    def up(p, k):
        b = block(p, z - (k - 1), y)
        return remote(x_ref.at[p] if k == 1 else b, b, p, k - 1, device(core, z + 1, y))

    def up_in(p, k):
        b = block(p, z - k, y)
        return remote(b, b, p, k - 1, device(core, z - 1, y))

    def down(p, k):
        b = block(p, z + (k - 1), y)
        return remote(
            x_ref.at[p] if k == 1 else b, b, p, chain + k - 1, device(core, z - 1, y)
        )

    def down_in(p, k):
        b = block(p, z + k, y)
        return remote(b, b, p, chain + k - 1, device(core, z + 1, y))

    def across(p, zz, own=False):
        b = block(p, zz, y)
        return remote(x_ref.at[p] if own else b, b, p, 2 * chain + zz, device(core, z, 1 - y))

    def across_in(p, zz):
        b = block(p, zz, 1 - y)
        return remote(b, b, p, 2 * chain + zz, device(core, z, 1 - y))

    def mate_out(p):
        b = block(p, z, 1 - y)
        return remote(b, b, p, 3 * chain, device(core, mate, y))

    def mate_in(p):
        b = block(p, mate, 1 - y)
        return remote(b, b, p, 3 * chain, device(core, mate, y))

    def other_out(p):
        return remote(
            w_ref.at[p, core], w_ref.at[p, core], p, 3 * chain + 1, device(1 - core, z, y)
        )

    def other_in(p):
        return remote(
            w_ref.at[p, 1 - core], w_ref.at[p, 1 - core], p, 3 * chain + 1, device(1 - core, z, y)
        )

    def local(p):
        return pltpu.make_async_copy(x_ref.at[p], block(p, z, y), lsem.at[p])

    def by_mate(p):
        return p % 2 == 1

    def start(p):
        local(p).start()
        across(p, z, True).start()

        @pl.when(z < chain - 1)
        def _():
            up(p, 1).start()

        @pl.when(z > 0)
        def _():
            down(p, 1).start()

    def step(p, k):
        @pl.when(z >= k)
        def _():
            up_in(p, k).wait_recv()

            @pl.when(z < chain - 1)
            def _():
                up(p, k + 1).start()

            if k == 1 and by_mate(p):

                @pl.when(z % 2 == 0)
                def _():
                    across(p, z - k).start()

            else:
                across(p, z - k).start()

        @pl.when(z + k < chain)
        def _():
            down_in(p, k).wait_recv()

            @pl.when(z > 0)
            def _():
                down(p, k + 1).start()

            if k == 1 and by_mate(p):

                @pl.when(z % 2 == 1)
                def _():
                    across(p, z + k).start()

            else:
                across(p, z + k).start()

    def finish(p):
        local(p).wait()
        for j in range(chain):
            if by_mate(p):

                @pl.when((j != z) & (j != mate))
                def _():
                    across_in(p, j).wait_recv()

            else:
                across_in(p, j).wait_recv()
        if by_mate(p):
            mate_in(p).wait_recv()
        other_out(p).start()

    def drain(p):
        for j in range(chain):
            if by_mate(p):

                @pl.when(j != mate)
                def _():
                    across(p, j).wait_send()

            else:
                across(p, j).wait_send()
        if by_mate(p):
            mate_out(p).wait_send()
        for k in range(1, chain):

            @pl.when((z < chain - 1) & (z >= k - 1))
            def _():
                up(p, k).wait_send()

            @pl.when((z > 0) & (z + k - 1 < chain))
            def _():
                down(p, k).wait_send()

        other_out(p).wait_send()
        other_in(p).wait_recv()

    ahead = min(2, pieces)
    for p in range(ahead):
        start(p)
    for p in range(pieces):
        step(p, 1)
        if by_mate(p):
            across_in(p, z).wait_recv()
            mate_out(p).start()
        if p + ahead < pieces:
            start(p + ahead)
        for k in range(2, chain):
            step(p, k)
        if p > 0:
            finish(p - 1)
    finish(pieces - 1)
    for p in range(pieces):
        drain(p)


def gather_pieces(x, dp_count):
    pieces, rows, cols = x.shape
    chain = dp_count // 2
    kinds = 3 * chain + 2

    def body(*refs):
        gather_kernel(chain, *refs)

    return pl.pallas_call(
        body,
        out_shape=jax.ShapeDtypeStruct((pieces, 2, dp_count, rows, cols), x.dtype),
        in_specs=[pl.BlockSpec(memory_space=pl.ANY)],
        out_specs=pl.BlockSpec(memory_space=pl.ANY),
        scratch_shapes=[
            pltpu.SemaphoreType.DMA((pieces, kinds)),
            pltpu.SemaphoreType.DMA((pieces, kinds)),
            pltpu.SemaphoreType.DMA((pieces,)),
        ],
        compiler_params=pltpu.CompilerParams(collective_id=0, has_side_effects=True),
        name="gather_weights",
    )(x)


def normalize(values_in):
    centered = values_in - jnp.mean(values_in, axis=-1, keepdims=True)
    inverse = lax.rsqrt(jnp.mean(centered * centered, axis=-1, keepdims=True) + EPSILON)
    return (centered * inverse, inverse)


def norm_back(grad_hat, normed, inverse):
    return inverse * (
        grad_hat
        - jnp.mean(grad_hat, axis=-1, keepdims=True)
        - normed * jnp.mean(grad_hat * normed, axis=-1, keepdims=True)
    )


GELU_SCALE = math.sqrt(2.0 / math.pi)


def gelu_both(v):
    inner = GELU_SCALE * (v + 0.044715 * v * v * v)
    t = jnp.tanh(inner)
    slope = 0.5 * (1.0 + t) + 0.5 * v * (1.0 - t * t) * GELU_SCALE * (1.0 + 3 * 0.044715 * v * v)
    return 0.5 * v * (1.0 + t), slope


def nn(a, b):
    return lax.dot_general(a, b, (((1,), (0,)), ((), ())), preferred_element_type=F32)


def nt(a, b):
    return lax.dot_general(a, b, (((1,), (1,)), ((), ())), preferred_element_type=F32)


def tn(a, b):
    return lax.dot_general(a, b, (((0,), (0,)), ((), ())), preferred_element_type=F32)


def head_sum(partial_sum):
    own = partial_sum.astype(BF)
    return own.astype(F32) + swap(own, "head").astype(F32)


def forward(x, mod, wa, wu, wd, b_qv, b_out, b_up, b_down, bias, heads, head_dim):
    hw = heads // 2 * head_dim
    scale = 1.0 / math.sqrt(head_dim)
    hat1, inv1 = normalize(x)
    n1 = (hat1 * (1.0 + mod[1]) + mod[0]).astype(BF)
    branch = 0.0
    q, k, v, o, p = [], [], [], [], []
    for half in range(2):
        r = nn(n1, wa[half][:, hw:])
        bq = b_qv[0, half * hw : (half + 1) * hw]
        bv = b_qv[1, half * hw : (half + 1) * hw]
        q.append((r[:, :hw] + bq).astype(BF))
        k.append(r[:, hw : 2 * hw].astype(BF))
        v.append((r[:, 2 * hw :] + bv).astype(BF))
        outs = []
        for i in range(heads // 2):
            at = slice(i * head_dim, (i + 1) * head_dim)
            z = nt(q[half][:, at], k[half][:, at]) * scale + bias[half * heads // 2 + i]
            e = jnp.exp(z - jnp.max(z, axis=-1, keepdims=True))
            probs = (e / jnp.sum(e, axis=-1, keepdims=True)).astype(BF)
            p.append(probs)
            outs.append(nn(probs, v[half][:, at]).astype(BF))
        o.append(jnp.concatenate(outs, axis=1))
        branch = branch + nt(o[half], wa[half][:, :hw])
    branch = head_sum(branch) + b_out
    xm = x + mod[2] * branch
    hat2, inv2 = normalize(xm)
    n2 = (hat2 * (1.0 + mod[4]) + mod[3]).astype(BF)
    y = 0.0
    hidden, slope = [], []
    for half in range(2):
        hp = nn(n2, wu[half]) + b_up[half * wu.shape[2] : (half + 1) * wu.shape[2]]
        value, sl = gelu_both(hp)
        hidden.append(value.astype(BF))
        slope.append(sl)
        y = y + nt(hidden[half], wd[half])
    y = head_sum(y) + b_down
    out = xm + mod[5] * y
    return out, (hat1, inv1, n1, q, k, v, p, o, branch, hat2, inv2, n2, hidden, slope, y)


def both(value):
    c = lax.axis_index("section")
    got = swap(value, "section")
    return pick(c, value, got), pick(c, got, value)


def mine(c, pair):
    return pick(c, pair[0], pair[1])


def paired(lhs, rhs_halves):
    c = lax.axis_index("section")
    lhs_all = jnp.concatenate([lhs, swap(lhs, "section")], axis=0)
    got = swap(mine(1 - c, rhs_halves), "section")
    rhs_all = jnp.concatenate([mine(c, rhs_halves), got], axis=0)
    return tn(lhs_all, rhs_all).astype(BF)


def backward(d, mod, wa, wu, wd, kept, heads, head_dim):
    hat1, inv1, n1, q, k, v, p, o, branch, hat2, inv2, n2, hidden, slope, y = kept
    hw = heads // 2 * head_dim
    scale = 1.0 / math.sqrt(head_dim)
    dy = (d * mod[5]).astype(BF)
    g_gate2 = jnp.sum(d * y, axis=0)
    g_b_down = jnp.sum(dy.astype(F32), axis=0)
    dpre = [(nn(dy, wd[half]) * slope[half]).astype(BF) for half in range(2)]
    g_b_up = jnp.concatenate([jnp.sum(v_.astype(F32), axis=0) for v_ in dpre])
    dn2 = head_sum(nt(dpre[0], wu[0]) + nt(dpre[1], wu[1]))
    g_d = paired(dy, hidden)
    g_u = paired(n2, dpre)
    dxm = d + norm_back(dn2 * (1.0 + mod[4]), hat2, inv2)
    g_shift2 = jnp.sum(dn2, axis=0)
    g_scale2 = jnp.sum(dn2 * hat2, axis=0)
    g_gate1 = jnp.sum(dxm * branch, axis=0)
    dattn = (dxm * mod[2]).astype(BF)
    g_b_out = jnp.sum(dattn.astype(F32), axis=0)
    dn1 = 0.0
    dqkv, dz_all = [], []
    for half in range(2):
        do = nn(dattn, wa[half][:, :hw]).astype(BF)
        dq, dk, dv = [], [], []
        for i in range(heads // 2):
            at = slice(i * head_dim, (i + 1) * head_dim)
            probs = p[half * heads // 2 + i]
            dv.append(tn(probs, do[:, at]).astype(BF))
            ds = nt(do[:, at], v[half][:, at])
            pf = probs.astype(F32)
            dz = (pf * (ds - jnp.sum(pf * ds, axis=-1, keepdims=True))).astype(BF)
            dz_all.append(dz)
            dq.append((nn(dz, k[half][:, at]) * scale).astype(BF))
            dk.append((tn(dz, q[half][:, at]) * scale).astype(BF))
        dqkv.append(jnp.concatenate(dq + dk + dv, axis=1))
        dn1 = dn1 + nt(dqkv[half], wa[half][:, hw:])
    dn1 = head_sum(dn1)
    g_a = jnp.concatenate([paired(dattn, o), paired(n1, dqkv)], axis=1)
    sums = [jnp.sum(v_.astype(F32), axis=0) for v_ in dqkv]
    g_b_qv = jnp.concatenate([sums[0][:hw], sums[1][:hw], sums[0][2 * hw :], sums[1][2 * hw :]])
    dx = dxm + norm_back(dn1 * (1.0 + mod[1]), hat1, inv1)
    dmod = jnp.stack(
        [jnp.sum(dn1, axis=0), jnp.sum(dn1 * hat1, axis=0), g_gate1, g_shift2, g_scale2, g_gate2]
    )
    return dx, (g_a, g_u, g_d), (g_b_qv, g_b_out, g_b_up, g_b_down), dmod, dz_all


def toeplitz(rel, length):
    span = jnp.arange(length, dtype=jnp.int32)
    return jnp.take(rel, span[:, None] - span[None, :] + length - 1, axis=1)


def diagonals(square, length):
    heads = square.shape[0]
    padded = jnp.pad(square[:, :, ::-1], ((0, 0), (0, 0), (0, length)))
    flat = padded.reshape(heads, 2 * length * length)[:, : length * (2 * length - 1)]
    return jnp.sum(flat.reshape(heads, length, 2 * length - 1), axis=1)


def per_device(
    tokens,
    kept_mask,
    timesteps,
    labels,
    w_qkv,
    b_qv,
    w_out,
    b_out,
    w_up,
    b_up,
    w_down,
    b_down,
    w_ada,
    b_ada,
    rel_table,
    mask_token,
    class_table,
    out_grad,
):
    micro, rows, width = tokens.shape
    length = kept_mask.shape[2]
    classes = class_table.shape[0]
    heads = rel_table.shape[1]
    lw = w_qkv.shape[3]
    head_dim = lw // heads
    hw = lw // 2
    ff = w_up.shape[2]
    fw = ff // 2
    dp_count = lax.axis_size("dp")
    c = lax.axis_index("section")
    dp = lax.axis_index("dp")
    h = lax.axis_index("head")

    qkv = jnp.transpose(w_qkv[0], (1, 0, 2))
    out_t = w_out[0].T
    down_t = w_down[0].T
    pack = []
    for half in range(2):
        at = slice(half * hw, (half + 1) * hw)
        fat = slice(half * fw, (half + 1) * fw)
        a = jnp.concatenate([out_t[:, at], qkv[0][:, at], qkv[1][:, at], qkv[2][:, at]], axis=1)
        pack.append(jnp.stack([a, w_up[0][:, fat], down_t[:, fat]]))
    keep = mine(c, pack)
    got = swap(mine(1 - c, pack), "section")
    own = jnp.concatenate([pick(c, keep, got), pick(c, got, keep)])
    full = gather_pieces(own, dp_count)
    full = full.reshape(2, 3, 2, width, own.shape[2])

    ids = lax.all_gather(jnp.stack([labels[:, 0], timesteps[:, 0]]), "dp")
    labels_all = ids[:, 0].reshape(-1)
    steps_all = ids[:, 1].reshape(-1)
    label_pick = (labels_all[:, None] == jnp.arange(classes)[None, :]).astype(BF)
    cond = nn(label_pick, class_table) + time_features(steps_all, width)
    cond_low = jax.nn.silu(cond)
    fr = width // dp_count
    cond_part = lax.dynamic_slice_in_dim(cond_low, dp * fr, fr, 1)
    ada = w_ada[0].astype(F32).reshape(fr, 6 * lw)
    part = jnp.dot(cond_part, ada, precision=PRECISE).reshape(dp_count, micro, 6, lw)
    summed = jnp.sum(lax.all_to_all(part, "dp", 0, 0, tiled=True), axis=0) + b_ada[0].astype(F32)
    mod_own = mine(c, summed)
    mod_got = swap(mine(1 - c, summed), "section")
    mod_half = jnp.stack([pick(c, mod_own, mod_got), pick(c, mod_got, mod_own)])
    mod_other = swap(mod_half, "head")
    mod = jnp.concatenate(
        [pick(h, mod_half, mod_other), pick(h, mod_other, mod_half)], axis=2
    )

    def shared(value):
        return both(value[0].astype(BF))

    b_qv2, b_out2, b_up2, b_down2, rel2 = [
        [v.astype(F32) for v in shared(t)] for t in (b_qv, b_out, b_up, b_down, rel_table)
    ]

    kept = kept_mask[c, 0]
    source = jnp.cumsum(kept) - 1
    count = jnp.sum(kept)
    span = jnp.arange(length, dtype=jnp.int32)
    place = ((kept[:, None] == 1) & (source[:, None] == span[None, :])).astype(BF)
    pad = span >= count
    pos = place.T + (pad[:, None] & (span[None, :] == 0)).astype(BF)
    same = pad[:, None] == pad[None, :]
    t0 = toeplitz(rel2[0], length).astype(BF)
    left = jnp.einsum("ri,hij->hrj", pos, t0, preferred_element_type=F32).astype(BF)
    bias0 = jnp.einsum("hrj,sj->hrs", left, pos, preferred_element_type=F32)
    bias0 = jnp.where(same[None], bias0, NEGATIVE)
    bias1 = toeplitz(rel2[1], length)

    def weights(s):
        return full[s, 0], full[s, 1], full[s, 2]

    x0 = tokens[c].astype(F32)
    e, saved0 = forward(
        x0, mod[0], *weights(0), b_qv2[0], b_out2[0], b_up2[0], b_down2[0], bias0, heads, head_dim
    )
    placed = nn(place, e.astype(BF)) + (1 - kept)[:, None] * mask_token.astype(F32)[None, :]
    out1, saved1 = forward(
        placed, mod[1], *weights(1), b_qv2[1], b_out2[1], b_up2[1], b_down2[1], bias1, heads, head_dim
    )
    d = out_grad[c].astype(F32)
    da, big1, small1, dmod1, dz1 = backward(d, mod[1], *weights(1), saved1, heads, head_dim)
    mask_sum = jnp.sum(da * (1 - kept)[:, None].astype(F32), axis=0)
    de = tn(place, da.astype(BF))
    dtok, big0, small0, dmod0, dz0 = backward(de, mod[0], *weights(0), saved0, heads, head_dim)
    rel1 = diagonals(jnp.stack(dz1).astype(F32), length)
    sq = jnp.einsum("ri,hrs->his", pos, jnp.stack(dz0), preferred_element_type=F32)
    sq = jnp.einsum("his,sj->hij", sq, pos.astype(F32), precision=PRECISE)
    rel0 = diagonals(sq, length)

    red = []
    for s, big in ((1, big1), (0, big0)):
        red.append([lax.psum_scatter(t, "dp", scatter_dimension=0, tiled=True) for t in big])
    red = jnp.stack([jnp.stack(red[1]), jnp.stack(red[0])]).astype(F32)
    g_own = mine(c, red)
    g_got = swap(mine(1 - c, red), "section")
    g0, g1 = pick(c, g_own, g_got), pick(c, g_got, g_own)
    g_qkv = jnp.stack(
        [
            jnp.concatenate([g0[0][:, i * hw : (i + 1) * hw], g1[0][:, i * hw : (i + 1) * hw]], axis=1)
            for i in (1, 2, 3)
        ],
        axis=1,
    )
    g_out = jnp.concatenate([g0[0][:, :hw], g1[0][:, :hw]], axis=1).T
    g_up = jnp.concatenate([g0[1], g1[1]], axis=1)
    g_down = jnp.concatenate([g0[2], g1[2]], axis=1).T

    half_w = width // 2

    def half(v):
        return lax.dynamic_slice_in_dim(v, h * half_w, half_w, v.ndim - 1)

    vecs = []
    for small, rel in ((small0, rel0), (small1, rel1)):
        vecs.append(
            jnp.concatenate([small[0], half(small[1]), small[2], half(small[3]), rel.reshape(-1)])
        )
    mask_half = half(mask_sum)
    sent = jnp.concatenate([mine(1 - c, vecs), mask_half])
    total = jnp.concatenate([mine(c, vecs), mask_half]) + swap(sent, "section")
    total = lax.psum(total, "dp")
    cuts = [2 * lw, half_w, ff, half_w, heads * (2 * length - 1), half_w]
    parts = []
    at = 0
    for n in cuts:
        parts.append(total[at : at + n])
        at += n
    g_b_qv = parts[0].reshape(2, lw)
    g_rel = parts[4].reshape(heads, 2 * length - 1)

    dm = [half(dmod0), half(dmod1)]
    dm_own = mine(c, dm)
    dm_got = swap(mine(1 - c, dm), "section")
    dm_pair = jnp.stack([pick(c, dm_own, dm_got), pick(c, dm_got, dm_own)])
    dm_all = lax.all_gather(dm_pair, "dp").reshape(dp_count * micro, 6 * lw)
    g_ada = jnp.einsum("id,ie->de", cond_part, dm_all, precision=PRECISE).reshape(fr, 6, lw)
    g_b_ada = jnp.sum(dm_all, axis=0).reshape(6, lw)
    dcl = jnp.einsum("ie,de->id", dm_all, ada, precision=PRECISE)
    dcl = lax.psum(dcl, ("section", "head"))
    dcl = lax.all_gather(dcl, "dp", axis=1, tiled=True)
    sig = jax.nn.sigmoid(cond)
    dcond = half(dcl * (sig * (1.0 + cond * (1.0 - sig))))
    g_class = jnp.einsum("ic,id->cd", label_pick.astype(F32), dcond, precision=PRECISE)

    def settle(first, second):
        got = swap(pick(c, second, first), "section")
        own_part = pick(c, first, second)
        return jnp.stack([pick(c, own_part, got), pick(c, got, own_part)])[None]

    return (
        settle(e, out1),
        settle(dtok, da),
        g_qkv[None],
        g_b_qv[None],
        g_out[None],
        parts[1][None],
        g_up[None],
        parts[2][None],
        g_down[None],
        parts[3][None],
        g_ada[None],
        g_b_ada[None],
        g_rel[None],
        parts[5],
        g_class,
    )


def solution(mesh):
    placed = (
        P(None, "dp", None),
        P(None, "dp", None),
        P(None, "dp"),
        P(None, "dp"),
        P("section", "dp", None, "head"),
        P("section", None, "head"),
        P("section", "head", "dp"),
        P("section", None),
        P("section", "dp", "head"),
        P("section", "head"),
        P("section", "head", "dp"),
        P("section", None),
        P("section", "dp", None, "head"),
        P("section", None, "head"),
        P("section", "head", None),
        P(),
        P(),
        P(None, "dp", None),
    )
    return jax.shard_map(
        per_device,
        mesh=mesh,
        in_specs=placed,
        out_specs=(
            P("section", None, "dp", None),
            P("section", None, "dp", None),
            P("section", "dp", None, "head"),
            P("section", None, "head"),
            P("section", "head", "dp"),
            P("section", "head"),
            P("section", "dp", "head"),
            P("section", "head"),
            P("section", "head", "dp"),
            P("section", "head"),
            P("section", "dp", None, "head"),
            P("section", None, "head"),
            P("section", "head", None),
            P("head"),
            P(None, "head"),
        ),
        check_vma=False,
    )
```

```python
import math

import jax
import jax.numpy as jnp
from jax import lax
from jax.experimental import pallas as pl
from jax.experimental.pallas import tpu as pltpu
from jax.sharding import PartitionSpec as P

PRECISE = lax.Precision.HIGHEST
EPSILON = 1e-06
NEGATIVE = -1e30
MESH = pl.DeviceIdType.MESH
BF = jnp.bfloat16
VMEM_BYTES = 62 * 1024 * 1024
F32 = jnp.float32


def time_features(step_ids, model_width):
    half_width = model_width // 2
    frequency = jnp.exp(-math.log(10000.0) * jnp.arange(half_width).astype(F32) / half_width)
    angles = step_ids.astype(F32)[..., None] * frequency
    return jnp.concatenate([jnp.cos(angles), jnp.sin(angles)], axis=-1)


def swap(value, axis):
    return lax.ppermute(value, axis, [(0, 1), (1, 0)])


def pick(index, first, second):
    return jnp.where(index == 0, first, second)


def mine(c, pair):
    return pick(c, pair[0], pair[1])


def both(value):
    c = lax.axis_index("section")
    got = swap(value, "section")
    return pick(c, value, got), pick(c, got, value)


HEAD_LANES = 384


def nn(a, b):
    return lax.dot_general(a, b, (((1,), (0,)), ((), ())), preferred_element_type=F32)


def nt(a, b):
    return lax.dot_general(a, b, (((1,), (1,)), ((), ())), preferred_element_type=F32)


def tn(a, b):
    return lax.dot_general(a, b, (((0,), (0,)), ((), ())), preferred_element_type=F32)


def flat(value):
    return value.reshape(value.shape[0] * value.shape[1], value.shape[2])


GELU_SCALE = math.sqrt(2.0 / math.pi)


def gelu_both(v):
    t = jnp.tanh(GELU_SCALE * (v + 0.044715 * v * v * v))
    slope = 0.5 * (1.0 + t) + (0.5 * GELU_SCALE) * v * (1.0 - t * t) * (1.0 + 0.134145 * v * v)
    return 0.5 * v * (1.0 + t), slope


class Place:
    def __init__(self, chain):
        self.chain = chain
        self.core = lax.axis_index("section")
        self.dp = lax.axis_index("dp")
        self.head = lax.axis_index("head")
        self.z = self.dp // 2
        self.y = self.dp % 2
        self.mate_z = self.z + 1 - 2 * (self.z % 2)
        self.above = (self.core, self.dp + 2, self.head)
        self.below = (self.core, self.dp - 2, self.head)
        self.across = (self.core, self.z * 2 + 1 - self.y, self.head)
        self.mate = (self.core, self.mate_z * 2 + self.y, self.head)
        self.other = (1 - self.core, self.dp, self.head)
        self.beside = (self.core, self.dp, 1 - self.head)

    def greet(self, whole):
        barrier = pltpu.get_barrier_semaphore()

        def tell(device):
            pl.semaphore_signal(barrier, inc=1, device_id=device, device_id_type=MESH)

        tell(self.other)
        tell(self.beside)
        if not whole:
            pl.semaphore_wait(barrier, 2)
            return
        tell(self.across)

        @pl.when(self.z < self.chain - 1)
        def _():
            tell(self.above)

        @pl.when(self.z > 0)
        def _():
            tell(self.below)

        @pl.when((self.z > 0) & (self.z < self.chain - 1))
        def _():
            pl.semaphore_wait(barrier, 5)

        @pl.when((self.z == 0) | (self.z == self.chain - 1))
        def _():
            pl.semaphore_wait(barrier, 4)


def remote(src, dst, ssem, rsem, device):
    return pltpu.make_async_remote_copy(
        src_ref=src, dst_ref=dst, send_sem=ssem, recv_sem=rsem, device_id=device, device_id_type=MESH
    )


class Numbered:
    def __init__(self, ref):
        self.ref = ref
        self.count = 0

    def next(self):
        self.count += 1
        assert self.count <= self.ref.shape[0]
        return self.ref.at[self.count - 1]


class Gather:
    def __init__(self, at, own, w, ssem, rsem, lsem):
        self.at, self.own, self.w = at, own, w
        self.ssem, self.rsem, self.lsem = ssem, rsem, lsem
        self.pieces = own.shape[0]

    def block(self, p, zz, yy):
        return self.w.at[p, self.at.core, zz * 2 + yy]

    def copy(self, src, dst, p, kind, device):
        return remote(src, dst, self.ssem.at[p, kind], self.rsem.at[p, kind], device)

    def up(self, p, k):
        b = self.block(p, self.at.z - (k - 1), self.at.y)
        return self.copy(self.own.at[p] if k == 1 else b, b, p, k - 1, self.at.above)

    def up_in(self, p, k):
        b = self.block(p, self.at.z - k, self.at.y)
        return self.copy(b, b, p, k - 1, self.at.below)

    def down(self, p, k):
        b = self.block(p, self.at.z + (k - 1), self.at.y)
        return self.copy(
            self.own.at[p] if k == 1 else b, b, p, self.at.chain + k - 1, self.at.below
        )

    def down_in(self, p, k):
        b = self.block(p, self.at.z + k, self.at.y)
        return self.copy(b, b, p, self.at.chain + k - 1, self.at.above)

    def cross(self, p, zz, own=False):
        b = self.block(p, zz, self.at.y)
        return self.copy(self.own.at[p] if own else b, b, p, 2 * self.at.chain + zz, self.at.across)

    def cross_in(self, p, zz):
        b = self.block(p, zz, 1 - self.at.y)
        return self.copy(b, b, p, 2 * self.at.chain + zz, self.at.across)

    def mate_out(self, p):
        b = self.block(p, self.at.z, 1 - self.at.y)
        return self.copy(b, b, p, 3 * self.at.chain, self.at.mate)

    def mate_in(self, p):
        b = self.block(p, self.at.mate_z, 1 - self.at.y)
        return self.copy(b, b, p, 3 * self.at.chain, self.at.mate)

    def other_out(self, p):
        b = self.w.at[p, self.at.core]
        return self.copy(b, b, p, 3 * self.at.chain + 1, self.at.other)

    def other_in(self, p):
        b = self.w.at[p, 1 - self.at.core]
        return self.copy(b, b, p, 3 * self.at.chain + 1, self.at.other)

    def local(self, p):
        return pltpu.make_async_copy(
            self.own.at[p], self.block(p, self.at.z, self.at.y), self.lsem.at[p]
        )

    def start(self, p):
        self.local(p).start()
        self.cross(p, self.at.z, True).start()

        @pl.when(self.at.z < self.at.chain - 1)
        def _():
            self.up(p, 1).start()

        @pl.when(self.at.z > 0)
        def _():
            self.down(p, 1).start()

    def step(self, p, k):
        z, chain = self.at.z, self.at.chain
        odd = p % 2 == 1

        @pl.when(z >= k)
        def _():
            self.up_in(p, k).wait_recv()

            @pl.when(z < chain - 1)
            def _():
                self.up(p, k + 1).start()

            if k == 1 and odd:

                @pl.when(z % 2 == 0)
                def _():
                    self.cross(p, z - k).start()

            else:
                self.cross(p, z - k).start()

        @pl.when(z + k < chain)
        def _():
            self.down_in(p, k).wait_recv()

            @pl.when(z > 0)
            def _():
                self.down(p, k + 1).start()

            if k == 1 and odd:

                @pl.when(z % 2 == 1)
                def _():
                    self.cross(p, z + k).start()

            else:
                self.cross(p, z + k).start()

        if k == 1 and odd:
            self.cross_in(p, z).wait_recv()
            self.mate_out(p).start()

    def finish(self, p):
        z = self.at.z
        self.local(p).wait()
        for j in range(self.at.chain):
            if p % 2 == 1:

                @pl.when((j != z) & (j != self.at.mate_z))
                def _():
                    self.cross_in(p, j).wait_recv()

            else:
                self.cross_in(p, j).wait_recv()
        if p % 2 == 1:
            self.mate_in(p).wait_recv()
        self.other_out(p).start()

    def drain(self, p):
        z, chain = self.at.z, self.at.chain
        for j in range(chain):
            if p % 2 == 1:

                @pl.when(j != self.at.mate_z)
                def _():
                    self.cross(p, j).wait_send()

            else:
                self.cross(p, j).wait_send()
        if p % 2 == 1:
            self.mate_out(p).wait_send()
        for k in range(1, chain):

            @pl.when((z < chain - 1) & (z >= k - 1))
            def _():
                self.up(p, k).wait_send()

            @pl.when((z > 0) & (z + k - 1 < chain))
            def _():
                self.down(p, k).wait_send()

        self.other_out(p).wait_send()


TILE = 32


def by_rows(rows, body, carry, tile=TILE):
    def step(i, c):
        return body(pl.ds(pl.multiple_of(i * tile, tile), tile), c)

    return lax.fori_loop(0, rows // tile, step, carry)


def column_sum(value):
    rows, width = value.shape
    return jnp.sum(value.reshape(rows // 8, 8, width), axis=0)


def layer_norm(v):
    cen = v - jnp.mean(v, axis=-1, keepdims=True)
    inv = lax.rsqrt(jnp.mean(cen * cen, axis=-1, keepdims=True) + EPSILON)
    return cen * inv, inv


def layer_norm_back(w, hat, inv):
    return inv * (
        w - jnp.mean(w, axis=-1, keepdims=True) - hat * jnp.mean(w * hat, axis=-1, keepdims=True)
    )


def head_mask(i, head_dim):
    lane = lax.broadcasted_iota(jnp.int32, (1, HEAD_LANES), 1)
    return ((lane >= i * head_dim) & (lane < (i + 1) * head_dim)).astype(F32)


def forward_kernel(cfg, *refs):
    fused, chain, heads, head_dim = cfg
    refs = list(refs)
    own = refs.pop(0)
    tok, mod, bqv, bout, bup, bdown, rel, pos, seg, place, drop, mtok = refs[:12]
    refs = refs[12:]
    w = refs.pop(0) if fused else own
    s_hat1, s_inv, s_n1, s_qkv, s_p, s_o, s_branch, s_hat2, s_n2, s_hid, s_slope, s_y, outs = refs[:13]
    refs = refs[13:]
    (
        wa, wu, wd, res, hat, inv, n, r, qkv, prob, o, branch, hid, slope, y_keep,
        xs, xr, toep, gs, gr, gl, ssem, rsem, lsem,
    ) = refs
    at = Place(chain)
    rows, width = res.shape
    half_heads = heads // 2
    scale = 1.0 / math.sqrt(head_dim)
    sends, recvs, locals_ = Numbered(ssem), Numbered(rsem), Numbered(lsem)
    at.greet(fused)
    gather = Gather(at, own, w, gs, gr, gl) if fused else None
    waiting = {}

    def keep(name, src, dst):
        copy = pltpu.make_async_copy(src, dst, locals_.next())
        copy.start()
        waiting.setdefault(name, []).append(copy.wait)

    def give(name, src, dst):
        copy = remote(src, dst, sends.next(), recvs.next(), at.other)
        copy.start()
        waiting.setdefault(name, []).append(copy.wait_send)
        waiting.setdefault("end", []).append(copy.wait_recv)

    def settle(name):
        for wait in waiting.pop(name, []):
            wait()

    def pump(*what):
        if not fused:
            return
        for name, p, *k in what:
            if p < gather.pieces:
                getattr(gather, name)(p, *k)

    def load(p, slot):
        if fused:
            gather.other_in(p).wait_recv()
        copy = pltpu.make_async_copy(w.at[p], slot, locals_.next())
        copy.start()
        copy.wait()

    def send_across(i):
        copy = remote(xs.at[i], xr.at[i], sends.next(), recvs.next(), at.beside)
        copy.start()
        waiting.setdefault("end", []).append(copy.wait_send)
        return copy

    def total(i, ds):
        return xs[i, ds, :].astype(F32) + xr[i, ds, :].astype(F32)

    def norm_one(s):
        settle("hat1")
        settle("n1")
        settle("inv")

        def body(ds, c):
            v, iv = layer_norm(res[ds, :])
            hat[0, ds, :] = v.astype(BF)
            inv[0, ds, :] = jnp.broadcast_to(iv, (TILE, 128))
            n[0, ds, :] = (v * (1.0 + mod[s, 1:2, :]) + mod[s, 0:1, :]).astype(BF)
            return c

        by_rows(rows, body, 0)
        keep("hat1", hat.at[0], s_hat1.at[s])
        keep("n1", n.at[0], s_n1.at[s, 0])
        give("n1", n.at[0], s_n1.at[s, 1])

    def project(s):
        settle("qkv")
        for half in range(2):
            for j in range(3):
                cols = slice(j * 384, (j + 1) * 384)
                r[:, cols] = nn(n[0], flat(wa[half, :, :, cols]))

            def body(ds, c):
                v = r[ds, :]
                for kind, shift in ((0, 864), (1, 576), (2, 288)):
                    part = pltpu.roll(v, shift, 1)[:, :HEAD_LANES]
                    row = s * 8 + half * 4 + kind
                    qkv[kind, half, ds, :] = (part + bqv[row : row + 1, :]).astype(BF)
                return c

            by_rows(rows, body, 0)
        keep("qkv", qkv, s_qkv.at[s])

    def attend(s, half):
        if half == 0:
            settle("p")
            settle("o")
        o[half] = jnp.zeros_like(o[half])

        def one(i, c):
            index = half * half_heads + i
            mask = head_mask(i, head_dim).astype(BF)
            line = rel[pl.ds(s * heads + index, 1), :]
            skew = pltpu.roll(jnp.broadcast_to(line, (rows, 2 * rows)), 0, 1, stride=1, stride_axis=0)
            bias = skew[:, :rows]
            if s == 0:
                toep[...] = bias.astype(BF)
                left = nn(pos[...], toep[...]).astype(BF)
                bias = nt(left, pos[...]) + seg[...]
            z = nt(qkv[0, half] * mask, qkv[1, half]) * scale + bias
            e = jnp.exp(z - jnp.max(z, axis=-1, keepdims=True))
            p = (e / jnp.sum(e, axis=-1, keepdims=True)).astype(BF)
            prob[index] = p
            o[half] = o[half] + nn(p, qkv[2, half]).astype(BF) * mask
            return c

        lax.fori_loop(0, half_heads, one, 0)
        if half == 1:
            keep("p", prob, s_p.at[s])
            keep("o", o.at[at.core], s_o.at[s, 0])
            give("o", o.at[1 - at.core], s_o.at[s, 1])

    def project_out(i):
        xs[i] = (
            nt(o[0], flat(wa[0, :, :, :HEAD_LANES])) + nt(o[1], flat(wa[1, :, :, :HEAD_LANES]))
        ).astype(BF)
        return send_across(i)

    def norm_two(s, i, copy):
        copy.wait_recv()
        settle("branch")
        settle("hat2")
        settle("n2")

        def body(ds, c):
            b = total(i, ds) + bout[s : s + 1, :]
            branch[ds, :] = b.astype(BF)
            xm = res[ds, :] + mod[s, 2:3, :] * b
            res[ds, :] = xm
            v, iv = layer_norm(xm)
            hat[1, ds, :] = v.astype(BF)
            inv[1, ds, :] = jnp.broadcast_to(iv, (TILE, 128))
            n[1, ds, :] = (v * (1.0 + mod[s, 4:5, :]) + mod[s, 3:4, :]).astype(BF)
            return c

        by_rows(rows, body, 0)
        keep("branch", branch, s_branch.at[s])
        keep("inv", inv, s_inv.at[s])
        keep("hat2", hat.at[1], s_hat2.at[s])
        keep("n2", n.at[1], s_n2.at[s, 0])
        give("n2", n.at[1], s_n2.at[s, 1])

    def hidden(s, half):
        if half == 0:
            settle("hid")
            settle("slope")
        for j in range(3):
            cols = slice(j * 384, (j + 1) * 384)
            r[:, cols] = nn(n[1], flat(wu[half, :, :, cols])) + bup[s, half : half + 1, cols]

        def body(ds, c):
            value, sl = gelu_both(r[ds, :])
            hid[half, ds, :] = value.astype(BF)
            slope[half, ds, :] = sl.astype(BF)
            return c

        by_rows(rows, body, 0)
        if half == 1:
            keep("slope", slope, s_slope.at[s])
            keep("hid", hid.at[at.core], s_hid.at[s, 0])
            give("hid", hid.at[1 - at.core], s_hid.at[s, 1])

    def project_down(i):
        xs[i] = (nt(hid[0], flat(wd[0])) + nt(hid[1], flat(wd[1]))).astype(BF)
        return send_across(i)

    def end_block(s, i, copy):
        copy.wait_recv()
        settle("y")
        settle("out")

        def body(ds, c):
            v = total(i, ds) + bdown[s : s + 1, :]
            y_keep[ds, :] = v.astype(BF)
            res[ds, :] = res[ds, :] + mod[s, 5:6, :] * v
            return c

        by_rows(rows, body, 0)
        keep("y", y_keep, s_y.at[s])
        keep("out", res, outs.at[s])

    def spread():
        r[...] = nn(place[...], res[...].astype(BF))
        settle("out")

        def body(ds, c):
            res[ds, :] = r[ds, :] + drop[ds, 0:1] * mtok[...]
            return c

        by_rows(rows, body, 0)

    if fused:
        gather.start(0)
        gather.start(1)

    def start_residual(ds, c):
        res[ds, :] = tok[ds, :].astype(F32)
        return c

    by_rows(rows, start_residual, 0)
    norm_one(0)
    pump(("step", 0, 1), ("start", 2), ("step", 0, 2), ("step", 0, 3))
    for s in range(2):
        p = 3 * s
        pump(("step", p + 1, 1), ("start", p + 3), ("finish", p), ("step", p + 1, 2))
        load(p, wa)
        project(s)
        pump(("step", p + 1, 3))
        attend(s, 0)
        pump(("step", p + 2, 1), ("start", p + 4), ("finish", p + 1))
        attend(s, 1)
        copy = project_out(2 * s)
        pump(("step", p + 2, 2))
        norm_two(s, 2 * s, copy)
        pump(("step", p + 2, 3))
        load(p + 1, wu)
        hidden(s, 0)
        pump(("step", p + 3, 1), ("start", p + 5))
        pump(("finish", p + 2))
        hidden(s, 1)
        pump(("step", p + 3, 2))
        load(p + 2, wd)
        copy = project_down(2 * s + 1)
        pump(("step", p + 3, 3))
        end_block(s, 2 * s + 1, copy)
        if s == 0:
            spread()
            norm_one(1)
    if fused:
        for p in range(gather.pieces):
            gather.drain(p)
    for name in list(waiting):
        settle(name)


def forward_call(cfg, own, small, dp_count):
    fused, chain, heads, head_dim = cfg
    rows, width = small[0].shape
    pieces = own.shape[0]
    shard = own.shape[-2]
    groups = width // shard
    bf, f = lambda *s: jax.ShapeDtypeStruct(s, BF), lambda *s: jax.ShapeDtypeStruct(s, F32)
    out_shape = [
        bf(2, rows, width),
        f(2, 2, rows, 128),
        bf(2, 2, rows, width),
        bf(2, 3, 2, rows, HEAD_LANES),
        bf(2, heads, rows, rows),
        bf(2, 2, rows, HEAD_LANES),
        bf(2, rows, width),
        bf(2, rows, width),
        bf(2, 2, rows, width),
        bf(2, 2, rows, width),
        bf(2, 2, rows, width),
        bf(2, rows, width),
        f(2, rows, width),
    ]
    if fused:
        out_shape = [bf(pieces, 2, groups, shard, width)] + out_shape
    kinds = 3 * chain + 2
    slot = pltpu.VMEM((2, groups, shard, width), BF)
    scratch = [
        slot,
        slot,
        slot,
        pltpu.VMEM((rows, width), F32),
        pltpu.VMEM((2, rows, width), BF),
        pltpu.VMEM((2, rows, 128), F32),
        pltpu.VMEM((2, rows, width), BF),
        pltpu.VMEM((rows, width), F32),
        pltpu.VMEM((3, 2, rows, HEAD_LANES), BF),
        pltpu.VMEM((heads, rows, rows), BF),
        pltpu.VMEM((2, rows, HEAD_LANES), BF),
        pltpu.VMEM((rows, width), BF),
        pltpu.VMEM((2, rows, width), BF),
        pltpu.VMEM((2, rows, width), BF),
        pltpu.VMEM((rows, width), BF),
        pltpu.VMEM((4, rows, width), BF),
        pltpu.VMEM((4, rows, width), BF),
        pltpu.VMEM((rows, rows), BF),
        pltpu.SemaphoreType.DMA((pieces, kinds)),
        pltpu.SemaphoreType.DMA((pieces, kinds)),
        pltpu.SemaphoreType.DMA((pieces,)),
        pltpu.SemaphoreType.DMA((16,)),
        pltpu.SemaphoreType.DMA((16,)),
        pltpu.SemaphoreType.DMA((40,)),
    ]

    def body(*refs):
        forward_kernel(cfg, *refs)

    vm = pl.BlockSpec(memory_space=pltpu.VMEM)
    hbm = pl.BlockSpec(memory_space=pl.ANY)
    result = pl.pallas_call(
        body,
        out_shape=out_shape,
        in_specs=[hbm] + [vm] * len(small),
        out_specs=[hbm] * len(out_shape),
        scratch_shapes=scratch,
        compiler_params=pltpu.CompilerParams(
            collective_id=0, has_side_effects=True, vmem_limit_bytes=VMEM_BYTES
        ),
        name="forward_blocks",
    )(own, *small)
    return (result if fused else [own] + list(result))


class Scatter:
    def __init__(self, at, order, g, yr, zr, mr, red, out, ssem, rsem, osem, isem, lsem, credit):
        self.at, self.order = at, order
        self.g, self.yr, self.zr, self.mr, self.red, self.out = g, yr, zr, mr, red, out
        self.ssem, self.rsem, self.osem, self.isem, self.lsem = ssem, rsem, osem, isem, lsem
        self.credit = credit
        chain = at.chain
        need = lambda z, t: chain if t == z else (chain - t + z if t > z else chain - z + t)
        self.table = [sorted(range(chain), key=lambda t: (need(z, t), t)) for z in range(chain)]

    def slots(self, r):
        return r % self.g.shape[0], r % self.yr.shape[0]

    def target(self, i):
        return sum(jnp.where(self.at.z == z, self.table[z][i], 0) for z in range(self.at.chain))

    def own(self, r, t):
        return self.g.at[self.slots(r)[0], t * 2 + self.at.y]

    def theirs(self, r, t):
        return self.g.at[self.slots(r)[0], t * 2 + 1 - self.at.y]

    def copy(self, src, dst, r, kind, device):
        return remote(src, dst, self.ssem.at[r, kind], self.rsem.at[r, kind], device)

    def cross(self, r, t):
        return self.copy(
            self.theirs(r, t), self.yr.at[self.slots(r)[1], t], r, t, self.at.across
        )

    def up(self, r, t):
        return self.copy(
            self.own(r, t), self.zr.at[self.slots(r)[1], t], r, self.at.chain + t, self.at.above
        )

    def down(self, r, t, last=None):
        z = self.at.z - 1 if last is None else last
        place = jnp.where(t == z, self.at.chain, t)
        return self.copy(
            self.own(r, t), self.zr.at[self.slots(r)[1], place], r, 2 * self.at.chain + t, self.at.below
        )

    def to_mate(self, r):
        return self.copy(
            self.theirs(r, self.at.mate_z), self.mr.at[self.slots(r)[1]], r, 3 * self.at.chain, self.at.mate
        )

    def add(self, block, got):
        block[...] = (block[...].astype(F32) + got[...].astype(F32)).astype(BF)

    def begin(self, r):
        at, chain = self.at, self.at.chain
        if r >= self.yr.shape[0]:
            pl.semaphore_wait(self.credit.at[0], 1)

            @pl.when(at.z < chain - 1)
            def _():
                pl.semaphore_wait(self.credit.at[1], 1)

            @pl.when(at.z > 0)
            def _():
                pl.semaphore_wait(self.credit.at[2], 1)

        if r % 2 == 1:
            self.to_mate(r).start()
        for i in range(chain - 1):
            t = self.target(i)
            if r % 2 == 1:

                @pl.when(t != at.mate_z)
                def _():
                    self.cross(r, t).start()

            else:
                self.cross(r, t).start()
        if r % 2 == 0:
            self.cross(r, at.z).start()

    def mated(self, r):
        if r % 2 == 1:
            self.to_mate(r).wait_recv()
            self.add(self.theirs(r, self.at.z), self.mr.at[self.slots(r)[1]])
            self.cross(r, self.at.z).start()

    def arrive(self, r, i):
        t = self.target(i)

        def take():
            self.cross(r, t).wait_recv()
            self.add(self.own(r, t), self.yr.at[self.slots(r)[1], t])

        if r % 2 == 1:
            pl.when(t != self.at.mate_z)(take)
        else:
            take()

    def step(self, r, k):
        z, chain = self.at.z, self.at.chain

        @pl.when((z <= k - 1) & (z < chain - 1))
        def _():
            t = chain - k + z
            if k > 1:

                @pl.when(z > 0)
                def _():
                    self.up(r, t).wait_recv()
                    self.add(self.own(r, t), self.zr.at[self.slots(r)[1], t])

            self.up(r, t).start()

        @pl.when((chain - 1 - z <= k - 1) & (z > 0))
        def _():
            t = k - chain + z
            if k > 1:

                @pl.when(z < chain - 1)
                def _():
                    self.down(r, t, last=z).wait_recv()
                    self.add(self.own(r, t), self.zr.at[self.slots(r)[1], t])

            self.down(r, t).start()

    def finish(self, r):
        at, chain = self.at, self.at.chain
        z = at.z
        slot = self.slots(r)[1]
        if r >= self.yr.shape[0]:
            self.hand_over_done(r - self.yr.shape[0])
        red = self.red.at[slot]
        red[...] = self.own(r, z)[...].astype(F32)

        @pl.when(z > 0)
        def _():
            self.up(r, z).wait_recv()
            red[...] = red[...] + self.zr[slot, z].astype(F32)

        @pl.when(z < chain - 1)
        def _():
            self.down(r, z, last=z).wait_recv()
            red[...] = red[...] + self.zr[slot, chain].astype(F32)

        if r + self.yr.shape[0] < len(self.order):
            pl.semaphore_signal(self.credit.at[0], inc=1, device_id=at.across, device_id_type=MESH)

            @pl.when(z > 0)
            def _():
                pl.semaphore_signal(self.credit.at[1], inc=1, device_id=at.below, device_id_type=MESH)

            @pl.when(z < chain - 1)
            def _():
                pl.semaphore_signal(self.credit.at[2], inc=1, device_id=at.above, device_id_type=MESH)

        s, t = self.order[r]

        @pl.when(at.core == s)
        def _():
            self.keep(r).start()

        @pl.when(at.core != s)
        def _():
            self.hand_over(r).start()

    def keep(self, r):
        return pltpu.make_async_copy(
            self.red.at[self.slots(r)[1]], self.out.at[self.order[r][1], self.at.core], self.lsem.at[r]
        )

    def hand_over(self, r):
        return remote(
            self.red.at[self.slots(r)[1]],
            self.out.at[self.order[r][1], self.at.core],
            self.osem.at[r],
            self.isem.at[r],
            self.at.other,
        )

    def hand_over_done(self, r):
        s, t = self.order[r]

        @pl.when(self.at.core == s)
        def _():
            self.keep(r).wait()

        @pl.when(self.at.core != s)
        def _():
            self.hand_over(r).wait_send()

    def drain(self, r):
        z, chain = self.at.z, self.at.chain
        if r % 2 == 1:
            self.to_mate(r).wait_send()
        for t in range(chain):
            if r % 2 == 1:

                @pl.when(t != self.at.mate_z)
                def _():
                    self.cross(r, t).wait_send()

            else:
                self.cross(r, t).wait_send()

            @pl.when(t > z)
            def _():
                self.up(r, t).wait_send()

            @pl.when(t < z)
            def _():
                self.down(r, t).wait_send()

    def end(self):
        for r in range(len(self.order)):
            if r + self.yr.shape[0] >= len(self.order):
                self.hand_over_done(r)
            s, t = self.order[r]

            @pl.when(self.at.core == s)
            def _():
                remote(
                    self.red.at[0],
                    self.out.at[t, 1 - self.at.core],
                    self.osem.at[r],
                    self.isem.at[r],
                    self.at.other,
                ).wait_recv()


ORDER = ((1, 2), (1, 1), (1, 0), (0, 2), (0, 1), (0, 0))


def backward_kernel(cfg, *refs):
    fused, chain, heads, head_dim = cfg
    refs = list(refs)
    w = refs.pop(0)
    i_hat1, i_inv, i_n1, i_qkv, i_p, i_o, i_branch, i_hat2, i_n2, i_hid, i_slope, i_y = refs[:12]
    refs = refs[12:]
    dout, mod, flips, pos, place, drop = refs[:6]
    refs = refs[6:]
    red_out, o_dx, stats, rel_out = refs[:4]
    refs = refs[4:]
    (
        wslot, hat1, inv, n1, qkv, prob, o, branch, hat2, n2, hid, slope, y_keep,
        d, r, dy, dpre, dattn, dqkv, do, acc, xs, xr, g, yr, zr, mr, red,
        gs, gr, go, gi, gl, credit, ssem, rsem, lsem,
    ) = refs
    at = Place(chain)
    rows, width = d.shape
    half_heads = heads // 2
    scale = 1.0 / math.sqrt(head_dim)
    sends, recvs, locals_ = Numbered(ssem), Numbered(rsem), Numbered(lsem)
    at.greet(fused)
    scatter = (
        Scatter(at, ORDER, g, yr, zr, mr, red, red_out, gs, gr, go, gi, gl, credit) if fused else None
    )
    slots = g.shape[0]
    waiting = {}

    def fetch(name, src, dst):
        copy = pltpu.make_async_copy(src, dst, locals_.next())
        copy.start()
        waiting.setdefault(name, []).append(copy.wait)

    def settle(name):
        for wait in waiting.pop(name, []):
            wait()

    def give(name, src, dst):
        copy = remote(src, dst, sends.next(), recvs.next(), at.other)
        copy.start()
        waiting.setdefault(name + " in", []).append(copy.wait_recv)
        waiting.setdefault(name + " out", []).append(copy.wait_send)

    def pump(*what):
        if not fused:
            return
        for name, r_, *k in what:
            if 0 <= r_ < len(ORDER):
                getattr(scatter, name)(r_, *k)

    def pump_rest(r_, start):
        for i in range(start, chain):
            pump(("arrive", r_, i))
            if i < chain - 1:
                pump(("step", r_, i + 1))
        pump(("finish", r_))

    def send_across(i):
        if i > 1:
            settle("x out %d" % (i - 2))
        copy = remote(xs.at[i % 2], xr.at[i], sends.next(), recvs.next(), at.beside)
        copy.start()
        waiting.setdefault("x in %d" % i, []).append(copy.wait_recv)
        waiting.setdefault("x out %d" % i, []).append(copy.wait_send)

    def total(i, ds):
        return xs[i % 2, ds, :].astype(F32) + xr[i, ds, :].astype(F32)

    def stat(s, row, value):
        stats[s, row : row + 1, :] = jnp.sum(value, axis=0, keepdims=True)

    zero8 = lambda: jnp.zeros((8, width), F32)
    spot = lambda half: jnp.where(half == at.core, 0, 2)

    def loads(s):
        fetch("y", i_y.at[s], y_keep)
        fetch("slope", i_slope.at[s], slope)
        fetch("hid", i_hid.at[s], hid)
        fetch("n2", i_n2.at[s], n2)
        fetch("hat2", i_hat2.at[s], hat2)
        fetch("inv", i_inv.at[s], inv)
        fetch("branch", i_branch.at[s], branch)
        fetch("p", i_p.at[s], prob)
        fetch("qkv", i_qkv.at[s], qkv)
        fetch("o", i_o.at[s], o)
        fetch("n1", i_n1.at[s], n1)
        fetch("hat1", i_hat1.at[s], hat1)

    def product(r_, parts):
        slot = r_ % slots
        if r_ >= slots:
            if fused:
                scatter.drain(r_ - slots)
            else:
                settle("g%d" % (r_ - slots))
        for j in range(width // 384):
            cols = slice(j * 384, (j + 1) * 384)
            value = 0.0
            for lhs, rhs in parts(j):
                value = value + tn(lhs, rhs)
            g[slot, :, :, cols] = value.astype(BF).reshape(g.shape[1], g.shape[2], 384)
        if not fused:
            s, t = ORDER[r_]
            fetch("g%d" % r_, g.at[slot], red_out.at[s * 3 + t])

    def cols_of(ref, j):
        return flat(ref[0:2, :, j * 384 : (j + 1) * 384])

    def block_back(s):
        base = 0 if s == 1 else 3
        xi = 0 if s == 1 else 2
        first, second, third = (0, 1, 0) if s == 1 else (1, 0, 1)
        settle("y")
        settle("dy out")

        def one(ds, c):
            a, b = c
            dv = d[ds, :]
            v = (dv * mod[s, 5:6, :]).astype(BF)
            dy[0, ds, :] = v
            return (
                a + column_sum(dv * y_keep[ds, :].astype(F32)),
                b + column_sum(v.astype(F32)),
            )

        a, b = by_rows(rows, one, (zero8(), zero8()))
        stat(s, 5, a)
        stat(s, 6, b)
        give("dy", dy.at[0], dy.at[1])
        settle("w%d" % first)
        settle("slope")
        settle("dpre out")
        for half in range(2):
            for j in range(3):
                cols = slice(j * 384, (j + 1) * 384)
                v = (nn(dy[0], flat(wslot[first, half, :, :, cols])) * slope[half, :, cols].astype(F32)).astype(BF)
                dpre[spot(half), :, cols] = v
                stats[s, 8 + half : 9 + half, cols] = jnp.sum(v.astype(F32), axis=0, keepdims=True)
        give("dpre", dpre.at[2], dpre.at[1])
        fetch("w%d" % first, w.at[3 * s], wslot.at[first])
        settle("w%d" % second)
        if xi > 1:
            settle("x out %d" % (xi - 2))
        xs[xi % 2] = (
            nt(dpre[spot(0)], flat(wslot[second, 0])) + nt(dpre[spot(1)], flat(wslot[second, 1]))
        ).astype(BF)
        send_across(xi)
        if s == 1:
            fetch("w%d" % second, w.at[2], wslot.at[second])
        settle("dy in")
        settle("hid")
        product(base, lambda j: [(flat(dy[...]), cols_of(hid, j))])
        pump(("begin", base))
        if s == 0:
            pump_rest(2, 0)
        settle("dpre in")
        settle("n2")
        product(base + 1, lambda j: [(flat(n2[...]), cols_of(dpre, j))])
        pump(("begin", base + 1))
        settle("x in %d" % xi)
        settle("hat2")
        settle("inv")
        settle("branch")
        settle("dattn out")

        def two(ds, c):
            c0, c1, c2, c3 = c
            dn = total(xi, ds)
            hv = hat2[ds, :].astype(F32)
            dxm = d[ds, :] + layer_norm_back(dn * (1.0 + mod[s, 4:5, :]), hv, inv[1, ds, 0:1])
            d[ds, :] = dxm
            da = (dxm * mod[s, 2:3, :]).astype(BF)
            dattn[0, ds, :] = da
            return (
                c0 + column_sum(dn),
                c1 + column_sum(dn * hv),
                c2 + column_sum(dxm * branch[ds, :].astype(F32)),
                c3 + column_sum(da.astype(F32)),
            )

        c0, c1, c2, c3 = by_rows(rows, two, (zero8(),) * 4)
        stat(s, 3, c0)
        stat(s, 4, c1)
        stat(s, 2, c2)
        stat(s, 7, c3)
        give("dattn", dattn.at[0], dattn.at[1])
        settle("w%d" % third)
        settle("p")
        settle("qkv")
        settle("dqkv out")
        for half in range(2):
            if half == 0:
                pump(("mated", base))
            pump(("arrive", base, half))
            if half < chain - 1:
                pump(("step", base, half + 1))
            do[half] = nn(dattn[0], flat(wslot[third, half, :, :, :HEAD_LANES])).astype(BF)
            acc[...] = jnp.zeros_like(acc)

            def head(i, c):
                index = half * half_heads + i
                mask = head_mask(i, head_dim)
                low_mask = mask.astype(BF)
                p = prob[index]
                dom = do[half] * low_mask
                acc[2] = acc[2] + tn(p, dom)
                ds = nt(dom, qkv[2, half])
                pf = p.astype(F32)
                dz = (pf * (ds - jnp.sum(pf * ds, axis=-1, keepdims=True))).astype(BF)
                acc[0] = acc[0] + nn(dz, qkv[1, half]) * mask
                acc[1] = acc[1] + tn(dz, qkv[0, half]) * mask
                square = tn(flips[s], dz)
                if s == 0:
                    high = square.astype(BF)
                    low = (square - high.astype(F32)).astype(BF)
                    square = nn(high, pos[...]) + nn(low, pos[...])
                wide = jnp.concatenate([square, jnp.zeros_like(square)], axis=1)
                skew = pltpu.roll(wide, 0, 1, stride=1, stride_axis=0)
                rel_out[pl.ds(s * heads + index, 1), :] = jnp.sum(skew, axis=0, keepdims=True)
                return c

            lax.fori_loop(0, half_heads, head, 0)
            where = spot(half)

            def gather_rows(ds, c):
                blank = jnp.zeros((TILE, HEAD_LANES), F32)
                v = 0.0
                for kind, shift, factor in ((0, 288, scale), (1, 576, scale), (2, 864, 1.0)):
                    part = jnp.concatenate([acc[kind, ds, :] * factor, blank, blank], axis=1)
                    v = v + pltpu.roll(part, shift, 1)
                v = v.astype(BF)
                dqkv[where, ds, :] = v
                return c + column_sum(v.astype(F32))

            stat(s, 10 + half, by_rows(rows, gather_rows, zero8()))
        give("dqkv", dqkv.at[2], dqkv.at[1])
        xs_free = xi + 1
        if xs_free > 1:
            settle("x out %d" % (xs_free - 2))
        xs[xs_free % 2] = (
            nt(dqkv[spot(0)], flat(wslot[third, 0])) + nt(dqkv[spot(1)], flat(wslot[third, 1]))
        ).astype(BF)
        send_across(xs_free)
        if s == 1:
            fetch("w%d" % third, w.at[1], wslot.at[third])
        settle("dqkv in")
        settle("dattn in")
        settle("n1")
        settle("o")
        product(
            base + 2,
            lambda j: [(flat(n1[...]), cols_of(dqkv, j))]
            + ([(flat(dattn[...]), flat(o[...]))] if j == 0 else []),
        )
        pump(("begin", base + 2))
        settle("x in %d" % xs_free)
        settle("hat1")

        def three(ds, c):
            c0, c1, c2 = c
            dn = total(xs_free, ds)
            hv = hat1[ds, :].astype(F32)
            dx = d[ds, :] + layer_norm_back(dn * (1.0 + mod[s, 1:2, :]), hv, inv[0, ds, 0:1])
            d[ds, :] = dx
            return (c0 + column_sum(dn), c1 + column_sum(dn * hv), c2 + column_sum(dx * drop[ds, 0:1]))

        c0, c1, c2 = by_rows(rows, three, (zero8(),) * 3)
        stat(s, 0, c0)
        stat(s, 1, c1)
        stat(s, 12, c2)
        fetch("dx", d, o_dx.at[s])
        pump_rest(base, 2)

    loads(1)
    fetch("w0", w.at[5], wslot.at[0])
    fetch("w1", w.at[4], wslot.at[1])

    def start_rows(ds, c):
        d[ds, :] = dout[ds, :].astype(F32)
        return c

    by_rows(rows, start_rows, 0)
    block_back(1)
    loads(0)
    r[...] = tn(place[...], d[...].astype(BF))
    settle("dx")

    def move(ds, c):
        d[ds, :] = r[ds, :]
        return c

    by_rows(rows, move, 0)
    pump(("mated", 1))
    pump_rest(1, 0)
    block_back(0)
    for r_ in (4, 5):
        pump(("mated", r_))
        pump_rest(r_, 0)
    if fused:
        for r_ in range(len(ORDER) - slots, len(ORDER)):
            scatter.drain(r_)
        scatter.end()
    for name in list(waiting):
        settle(name)


def backward_call(cfg, w, saved, small):
    fused, chain, heads, head_dim = cfg
    rows, width = small[0].shape
    pieces, _, groups, shard, _ = w.shape
    bf, f = lambda *s: pltpu.VMEM(s, BF), lambda *s: pltpu.VMEM(s, F32)
    dma = lambda *s: pltpu.SemaphoreType.DMA(s)
    out_shape = [
        jax.ShapeDtypeStruct((3, 2, shard, width), F32)
        if fused
        else jax.ShapeDtypeStruct((pieces, groups, shard, width), BF),
        jax.ShapeDtypeStruct((2, rows, width), F32),
        jax.ShapeDtypeStruct((2, 16, width), F32),
        jax.ShapeDtypeStruct((2 * heads, 2 * rows), F32),
    ]
    some = 3 if fused else 1
    links = chain if fused else 1
    block = shard if fused else 16
    scratch = [
        bf(2, 2, groups, shard, width),
        bf(rows, width),
        f(2, rows, 128),
        bf(2, rows, width),
        bf(3, 2, rows, HEAD_LANES),
        bf(heads, rows, rows),
        bf(2, rows, HEAD_LANES),
        bf(rows, width),
        bf(rows, width),
        bf(2, rows, width),
        bf(2, rows, width),
        bf(2, rows, width),
        bf(rows, width),
        f(rows, width),
        f(rows, width),
        bf(2, rows, width),
        bf(3, rows, width),
        bf(2, rows, width),
        bf(3, rows, width),
        bf(2, rows, HEAD_LANES),
        f(3, rows, HEAD_LANES),
        bf(2, rows, width),
        bf(4, rows, width),
        bf(4, groups, shard, width),
        bf(some, links, block, width),
        bf(some, links + 1, block, width),
        bf(some, block, width),
        f(some, block, width),
        dma(6, 3 * links + 1),
        dma(6, 3 * links + 1),
        dma(6),
        dma(6),
        dma(6),
        pltpu.SemaphoreType.REGULAR((3,)),
        dma(16),
        dma(16),
        dma(48),
    ]

    def body(*refs):
        backward_kernel(cfg, *refs)

    vm = pl.BlockSpec(memory_space=pltpu.VMEM)
    hbm = pl.BlockSpec(memory_space=pl.ANY)
    return pl.pallas_call(
        body,
        out_shape=out_shape,
        in_specs=[hbm] * (1 + len(saved)) + [vm] * len(small),
        out_specs=[hbm, hbm, vm, vm],
        scratch_shapes=scratch,
        compiler_params=pltpu.CompilerParams(
            collective_id=1, has_side_effects=True, vmem_limit_bytes=VMEM_BYTES
        ),
        name="backward_blocks",
    )(w, *saved, *small)


def per_device(
    tokens,
    kept_mask,
    timesteps,
    labels,
    w_qkv,
    b_qv,
    w_out,
    b_out,
    w_up,
    b_up,
    w_down,
    b_down,
    w_ada,
    b_ada,
    rel_table,
    mask_token,
    class_table,
    out_grad,
):
    micro, rows, width = tokens.shape
    length = kept_mask.shape[2]
    classes = class_table.shape[0]
    heads = rel_table.shape[1]
    lw = w_qkv.shape[3]
    head_dim = lw // heads
    hw = lw // 2
    ff = w_up.shape[2]
    fw = ff // 2
    dp_count = lax.axis_size("dp")
    c = lax.axis_index("section")
    dp = lax.axis_index("dp")
    h = lax.axis_index("head")

    qkv = jnp.transpose(w_qkv[0], (1, 0, 2))
    out_t = w_out[0].T
    down_t = w_down[0].T
    pack = []
    for half in range(2):
        at = slice(half * hw, (half + 1) * hw)
        fat = slice(half * fw, (half + 1) * fw)
        a = jnp.concatenate([out_t[:, at], qkv[0][:, at], qkv[1][:, at], qkv[2][:, at]], axis=1)
        pack.append(jnp.stack([a, w_up[0][:, fat], down_t[:, fat]]))
    keep = mine(c, pack)
    got = swap(mine(1 - c, pack), "section")
    own = jnp.concatenate([pick(c, keep, got), pick(c, got, keep)])
    ids = lax.all_gather(jnp.stack([labels[:, 0], timesteps[:, 0]]), "dp")
    labels_all = ids[:, 0].reshape(-1)
    steps_all = ids[:, 1].reshape(-1)
    label_pick = (labels_all[:, None] == jnp.arange(classes)[None, :]).astype(BF)
    cond = nn(label_pick, class_table) + time_features(steps_all, width)
    cond_low = jax.nn.silu(cond)
    fr = width // dp_count
    cond_part = lax.dynamic_slice_in_dim(cond_low, dp * fr, fr, 1)
    ada = w_ada[0].astype(F32).reshape(fr, 6 * lw)
    part = jnp.dot(cond_part, ada, precision=PRECISE).reshape(dp_count, micro, 6, lw)
    summed = jnp.sum(lax.all_to_all(part, "dp", 0, 0, tiled=True), axis=0) + b_ada[0].astype(F32)
    mod_own = mine(c, summed)
    mod_got = swap(mine(1 - c, summed), "section")
    mod_half = jnp.stack([pick(c, mod_own, mod_got), pick(c, mod_got, mod_own)])
    mod_other = swap(mod_half, "head")
    mod = jnp.concatenate(
        [pick(h, mod_half, mod_other), pick(h, mod_other, mod_half)], axis=2
    )

    def shared(value):
        return both(value[0].astype(BF))

    b_qv2, b_out2, b_up2, b_down2, rel2 = [
        [v.astype(F32) for v in shared(t)] for t in (b_qv, b_out, b_up, b_down, rel_table)
    ]


    kept = kept_mask[c, 0]
    source = jnp.cumsum(kept) - 1
    count = jnp.sum(kept)
    span = jnp.arange(length, dtype=jnp.int32)
    place = ((kept[:, None] == 1) & (source[:, None] == span[None, :])).astype(BF)
    pad = span >= count
    pos = place.T + (pad[:, None] & (span[None, :] == 0)).astype(BF)
    seg = jnp.where(pad[:, None] == pad[None, :], 0.0, NEGATIVE)
    mirror = (span[:, None] + span[None, :] == length - 1).astype(BF)
    flips = jnp.stack([pos[:, ::-1], mirror])
    drop = jnp.broadcast_to((1 - kept)[:, None].astype(F32), (rows, 128))

    lanes = HEAD_LANES - hw
    rel_rows = jnp.stack(rel2)
    blank = jnp.zeros((2, heads, 1), F32)
    rel_rows = jnp.concatenate(
        [rel_rows[:, :, length - 1 :: -1], blank, rel_rows[:, :, : length - 1 : -1]], axis=2
    ).reshape(2 * heads, 2 * length)
    bqv = jnp.stack(b_qv2).reshape(2, 2, 2, hw)
    none = jnp.zeros((2, 2, hw), F32)
    bqv = jnp.stack([bqv[:, 0], none, bqv[:, 1], none], axis=2)
    bqv = jnp.pad(bqv, ((0, 0), (0, 0), (0, 0), (0, lanes))).reshape(16, HEAD_LANES)
    mod = jnp.pad(mod, ((0, 0), (0, 2), (0, 0)))
    fused = (width // dp_count) % 16 == 0
    cfg = (fused, dp_count // 2, heads, head_dim)
    if fused:
        source_w = own
    else:
        half_w_ = lax.all_gather(own, "dp", axis=1, tiled=True)
        other_w = swap(half_w_, "section")
        source_w = jnp.stack([pick(c, half_w_, other_w), pick(c, other_w, half_w_)], axis=1)
        source_w = source_w.reshape(6, 2, 8, width // 8, own.shape[2])
    small_in = (
        tokens[c],
        mod,
        bqv,
        jnp.stack(b_out2),
        jnp.stack(b_up2).reshape(2, 2, fw),
        jnp.stack(b_down2),
        rel_rows,
        pos,
        seg,
        place,
        drop,
        mask_token.astype(F32)[None, :],
    )
    full, *saved, outs = forward_call(cfg, source_w, small_in, dp_count)
    small_back = (out_grad[c], mod, flips, pos, place, drop)
    red, dx, stats, rel_out = backward_call(cfg, full, saved, small_back)
    rel_out = rel_out.reshape(2, heads, 2 * length)[:, :, 2 * length - 2 :: -1]

    if fused:
        g0, g1 = red[:, 0], red[:, 1]
    else:
        red = lax.psum_scatter(
            red.reshape(6, width, own.shape[2]), "dp", scatter_dimension=1, tiled=True
        ).astype(F32)
        red = red.reshape(2, 3, fr, own.shape[2])
        g_own = mine(c, red)
        g_got = swap(mine(1 - c, red), "section")
        g0, g1 = pick(c, g_own, g_got), pick(c, g_got, g_own)
    g_qkv = jnp.stack(
        [
            jnp.concatenate([g0[0][:, i * hw : (i + 1) * hw], g1[0][:, i * hw : (i + 1) * hw]], axis=1)
            for i in (1, 2, 3)
        ],
        axis=1,
    )
    g_out = jnp.concatenate([g0[0][:, :hw], g1[0][:, :hw]], axis=1).T
    g_up = jnp.concatenate([g0[1], g1[1]], axis=1)
    g_down = jnp.concatenate([g0[2], g1[2]], axis=1).T
    dmod0, dmod1 = stats[0, :6], stats[1, :6]
    mask_sum = stats[1, 12]

    def small_of(s):
        qv = [stats[s, 10 + half, at * hw : (at + 1) * hw] for at in (1, 3) for half in range(2)]
        return (jnp.concatenate(qv), stats[s, 7], stats[s, 8:10].reshape(-1), stats[s, 6])

    small0, small1 = small_of(0), small_of(1)
    rel0, rel1 = rel_out[0], rel_out[1]

    half_w = width // 2

    def half(v):
        return lax.dynamic_slice_in_dim(v, h * half_w, half_w, v.ndim - 1)

    vecs = []
    for small, rel in ((small0, rel0), (small1, rel1)):
        vecs.append(
            jnp.concatenate([small[0], half(small[1]), small[2], half(small[3]), rel.reshape(-1)])
        )
    mask_half = half(mask_sum)
    sent = jnp.concatenate([mine(1 - c, vecs), mask_half])
    total = jnp.concatenate([mine(c, vecs), mask_half]) + swap(sent, "section")
    total = lax.psum(total, "dp")
    cuts = [2 * lw, half_w, ff, half_w, heads * (2 * length - 1), half_w]
    parts = []
    at = 0
    for n in cuts:
        parts.append(total[at : at + n])
        at += n
    g_b_qv = parts[0].reshape(2, lw)
    g_rel = parts[4].reshape(heads, 2 * length - 1)

    dm = [half(dmod0), half(dmod1)]
    dm_own = mine(c, dm)
    dm_got = swap(mine(1 - c, dm), "section")
    dm_pair = jnp.stack([pick(c, dm_own, dm_got), pick(c, dm_got, dm_own)])
    dm_all = lax.all_gather(dm_pair, "dp").reshape(dp_count * micro, 6 * lw)
    g_ada = jnp.einsum("id,ie->de", cond_part, dm_all, precision=PRECISE).reshape(fr, 6, lw)
    g_b_ada = jnp.sum(dm_all, axis=0).reshape(6, lw)
    dcl = jnp.einsum("ie,de->id", dm_all, ada, precision=PRECISE)
    dcl = lax.psum(dcl, ("section", "head"))
    dcl = lax.all_gather(dcl, "dp", axis=1, tiled=True)
    sig = jax.nn.sigmoid(cond)
    dcond = half(dcl * (sig * (1.0 + cond * (1.0 - sig))))
    g_class = jnp.einsum("ic,id->cd", label_pick.astype(F32), dcond, precision=PRECISE)

    def settle(first, second):
        got = swap(pick(c, second, first), "section")
        own_part = pick(c, first, second)
        return jnp.stack([pick(c, own_part, got), pick(c, got, own_part)])[None]

    return (
        settle(outs[0], outs[1]),
        settle(dx[0], dx[1]),
        g_qkv[None],
        g_b_qv[None],
        g_out[None],
        parts[1][None],
        g_up[None],
        parts[2][None],
        g_down[None],
        parts[3][None],
        g_ada[None],
        g_b_ada[None],
        g_rel[None],
        parts[5],
        g_class,
    )


def solution(mesh):
    placed = (
        P(None, "dp", None),
        P(None, "dp", None),
        P(None, "dp"),
        P(None, "dp"),
        P("section", "dp", None, "head"),
        P("section", None, "head"),
        P("section", "head", "dp"),
        P("section", None),
        P("section", "dp", "head"),
        P("section", "head"),
        P("section", "head", "dp"),
        P("section", None),
        P("section", "dp", None, "head"),
        P("section", None, "head"),
        P("section", "head", None),
        P(),
        P(),
        P(None, "dp", None),
    )
    return jax.shard_map(
        per_device,
        mesh=mesh,
        in_specs=placed,
        out_specs=(
            P("section", None, "dp", None),
            P("section", None, "dp", None),
            P("section", "dp", None, "head"),
            P("section", None, "head"),
            P("section", "head", "dp"),
            P("section", "head"),
            P("section", "dp", "head"),
            P("section", "head"),
            P("section", "head", "dp"),
            P("section", "head"),
            P("section", "dp", None, "head"),
            P("section", None, "head"),
            P("section", "head", None),
            P("head"),
            P(None, "head"),
        ),
        check_vma=False,
    )
```

```python
import math

import jax
import jax.numpy as jnp
from jax import lax
from jax.experimental import pallas as pl
from jax.experimental.pallas import tpu as pltpu
from jax.sharding import PartitionSpec as P

PRECISE = lax.Precision.HIGHEST
EPSILON = 1e-06
NEGATIVE = -1e30
MESH = pl.DeviceIdType.MESH
BF = jnp.bfloat16
VMEM_BYTES = 62 * 1024 * 1024
F32 = jnp.float32


def time_features(step_ids, model_width):
    half_width = model_width // 2
    frequency = jnp.exp(-math.log(10000.0) * jnp.arange(half_width).astype(F32) / half_width)
    angles = step_ids.astype(F32)[..., None] * frequency
    return jnp.concatenate([jnp.cos(angles), jnp.sin(angles)], axis=-1)


def swap(value, axis):
    return lax.ppermute(value, axis, [(0, 1), (1, 0)])


def pick(index, first, second):
    return jnp.where(index == 0, first, second)


def mine(c, pair):
    return pick(c, pair[0], pair[1])


def both(value):
    c = lax.axis_index("section")
    got = swap(value, "section")
    return pick(c, value, got), pick(c, got, value)


HEAD_LANES = 384
ADA_LANES = 640


def nn(a, b):
    return lax.dot_general(a, b, (((1,), (0,)), ((), ())), preferred_element_type=F32)


def nt(a, b):
    return lax.dot_general(a, b, (((1,), (1,)), ((), ())), preferred_element_type=F32)


def tn(a, b):
    return lax.dot_general(a, b, (((0,), (0,)), ((), ())), preferred_element_type=F32)


def flat(value):
    return value.reshape(value.shape[0] * value.shape[1], value.shape[2])


GELU_SCALE = math.sqrt(2.0 / math.pi)


def gelu_both(v):
    t = jnp.tanh(GELU_SCALE * (v + 0.044715 * v * v * v))
    slope = 0.5 * (1.0 + t) + (0.5 * GELU_SCALE) * v * (1.0 - t * t) * (1.0 + 0.134145 * v * v)
    return 0.5 * v * (1.0 + t), slope


class Place:
    def __init__(self, chain):
        self.chain = chain
        self.core = lax.axis_index("section")
        self.dp = lax.axis_index("dp")
        self.head = lax.axis_index("head")
        self.z = self.dp // 2
        self.y = self.dp % 2
        self.mate_z = self.z + 1 - 2 * (self.z % 2)
        self.above = (self.core, self.dp + 2, self.head)
        self.below = (self.core, self.dp - 2, self.head)
        self.across = (self.core, self.z * 2 + 1 - self.y, self.head)
        self.mate = (self.core, self.mate_z * 2 + self.y, self.head)
        self.other = (1 - self.core, self.dp, self.head)
        self.beside = (self.core, self.dp, 1 - self.head)

        self.beyond = (1 - self.core, self.dp, 1 - self.head)
        self.count = 2 * chain

    def peer(self, k):
        return lax.rem(self.dp + k, self.count)

    def source(self, k):
        return lax.rem(self.dp + self.count - k, self.count)

    def flip(self, b):
        bit = lax.rem(self.dp // (1 << b), 2)
        return self.dp + (1 << b) * (1 - 2 * bit)

    def in_dp(self, dp):
        return (self.core, dp, self.head)

    def greet(self):
        barrier = pltpu.get_barrier_semaphore()
        others = [self.other, self.beside, self.beyond]
        others += [self.in_dp(self.peer(k)) for k in range(1, self.count)]
        for device in others:
            pl.semaphore_signal(barrier, inc=1, device_id=device, device_id_type=MESH)
        pl.semaphore_wait(barrier, len(others))


def remote(src, dst, ssem, rsem, device):
    return pltpu.make_async_remote_copy(
        src_ref=src, dst_ref=dst, send_sem=ssem, recv_sem=rsem, device_id=device, device_id_type=MESH
    )


class Numbered:
    def __init__(self, ref):
        self.ref = ref
        self.count = 0

    def next(self):
        self.count += 1
        assert self.count <= self.ref.shape[0]
        return self.ref.at[self.count - 1]


class Links:
    def __init__(self, at, ssem, rsem):
        self.at, self.sends, self.recvs = at, Numbered(ssem), Numbered(rsem)
        self.waiting = []

    def copy(self, src, dst, device):
        copy = remote(src, dst, self.sends.next(), self.recvs.next(), device)
        copy.start()
        self.waiting.append(copy.wait_send)
        return copy

    def to_all(self, src_of, dst):
        copies = []
        for k in range(1, self.at.count):
            peer = self.at.peer(k)
            copies.append(self.copy(src_of(peer), dst, self.at.in_dp(peer)))
        return copies

    def around(self, ref):
        mine_ = ref.at[self.at.core, self.at.head]
        return [
            self.copy(mine_, mine_, device)
            for device in (self.at.other, self.at.beside, self.at.beyond)
        ]


class Gather:
    def __init__(self, at, pack, w, ssem, rsem, lsem):
        self.at, self.pack, self.w = at, pack, w
        self.ssem, self.rsem, self.lsem = ssem, rsem, lsem
        self.pieces = w.shape[0]

    def local(self, t):
        core = self.at.core
        return pltpu.make_async_copy(
            self.pack.at[core, t], self.w.at[3 * core + t, core, self.at.dp], self.lsem.at[t]
        )

    def share(self, t):
        core = self.at.core
        return remote(
            self.pack.at[1 - core, t],
            self.w.at[3 * core + t, 1 - core, self.at.dp],
            self.ssem.at[t, 3 * self.at.chain + 2],
            self.rsem.at[t, 3 * self.at.chain + 2],
            self.at.other,
        )

    def shared(self, t):
        core = self.at.core
        block = self.w.at[3 * (1 - core) + t, core, self.at.dp]
        return remote(
            self.pack.at[1 - core, t],
            block,
            self.ssem.at[t, 3 * self.at.chain + 2],
            self.rsem.at[t, 3 * self.at.chain + 2],
            self.at.other,
        )

    def split(self):
        for t in range(3):
            self.local(t).start()
            self.share(t).start()

    def block(self, p, zz, yy):
        return self.w.at[p, self.at.core, zz * 2 + yy]

    def copy(self, src, dst, p, kind, device):
        return remote(src, dst, self.ssem.at[p, kind], self.rsem.at[p, kind], device)

    def up(self, p, k):
        b = self.block(p, self.at.z - (k - 1), self.at.y)
        return self.copy(b, b, p, k - 1, self.at.above)

    def up_in(self, p, k):
        b = self.block(p, self.at.z - k, self.at.y)
        return self.copy(b, b, p, k - 1, self.at.below)

    def down(self, p, k):
        b = self.block(p, self.at.z + (k - 1), self.at.y)
        return self.copy(b, b, p, self.at.chain + k - 1, self.at.below)

    def down_in(self, p, k):
        b = self.block(p, self.at.z + k, self.at.y)
        return self.copy(b, b, p, self.at.chain + k - 1, self.at.above)

    def cross(self, p, zz):
        b = self.block(p, zz, self.at.y)
        return self.copy(b, b, p, 2 * self.at.chain + zz, self.at.across)

    def cross_in(self, p, zz):
        b = self.block(p, zz, 1 - self.at.y)
        return self.copy(b, b, p, 2 * self.at.chain + zz, self.at.across)

    def mate_out(self, p):
        b = self.block(p, self.at.z, 1 - self.at.y)
        return self.copy(b, b, p, 3 * self.at.chain, self.at.mate)

    def mate_in(self, p):
        b = self.block(p, self.at.mate_z, 1 - self.at.y)
        return self.copy(b, b, p, 3 * self.at.chain, self.at.mate)

    def other_out(self, p):
        b = self.w.at[p, self.at.core]
        return self.copy(b, b, p, 3 * self.at.chain + 1, self.at.other)

    def other_in(self, p):
        b = self.w.at[p, 1 - self.at.core]
        return self.copy(b, b, p, 3 * self.at.chain + 1, self.at.other)

    def start(self, p):
        s, t = divmod(p, 3)

        @pl.when(self.at.core == s)
        def _():
            self.local(t).wait()

        @pl.when(self.at.core != s)
        def _():
            self.shared(t).wait_recv()

        self.cross(p, self.at.z).start()

        @pl.when(self.at.z < self.at.chain - 1)
        def _():
            self.up(p, 1).start()

        @pl.when(self.at.z > 0)
        def _():
            self.down(p, 1).start()

    def step(self, p, k):
        z, chain = self.at.z, self.at.chain
        odd = p % 2 == 1

        @pl.when(z >= k)
        def _():
            self.up_in(p, k).wait_recv()

            @pl.when(z < chain - 1)
            def _():
                self.up(p, k + 1).start()

            if k == 1 and odd:

                @pl.when(z % 2 == 0)
                def _():
                    self.cross(p, z - k).start()

            else:
                self.cross(p, z - k).start()

        @pl.when(z + k < chain)
        def _():
            self.down_in(p, k).wait_recv()

            @pl.when(z > 0)
            def _():
                self.down(p, k + 1).start()

            if k == 1 and odd:

                @pl.when(z % 2 == 1)
                def _():
                    self.cross(p, z + k).start()

            else:
                self.cross(p, z + k).start()

        if k == 1 and odd:
            self.cross_in(p, z).wait_recv()
            self.mate_out(p).start()

    def finish(self, p):
        z = self.at.z
        for j in range(self.at.chain):
            if p % 2 == 1:

                @pl.when((j != z) & (j != self.at.mate_z))
                def _():
                    self.cross_in(p, j).wait_recv()

            else:
                self.cross_in(p, j).wait_recv()
        if p % 2 == 1:
            self.mate_in(p).wait_recv()
        self.other_out(p).start()

    def drain(self, p):
        z, chain = self.at.z, self.at.chain
        for j in range(chain):
            if p % 2 == 1:

                @pl.when(j != self.at.mate_z)
                def _():
                    self.cross(p, j).wait_send()

            else:
                self.cross(p, j).wait_send()
        if p % 2 == 1:
            self.mate_out(p).wait_send()
        for k in range(1, chain):

            @pl.when((z < chain - 1) & (z >= k - 1))
            def _():
                self.up(p, k).wait_send()

            @pl.when((z > 0) & (z + k - 1 < chain))
            def _():
                self.down(p, k).wait_send()

        self.other_out(p).wait_send()
        if p < 3:
            self.share(p).wait_send()


TILE = 32


def silu(v):
    return v / (1.0 + jnp.exp(-v))


def thirds(v):
    a = v.astype(BF)
    rest = v - a.astype(F32)
    b = rest.astype(BF)
    return a, b, (rest - b.astype(F32)).astype(BF)


def by_rows(rows, body, carry, tile=TILE):
    def step(i, c):
        return body(pl.ds(pl.multiple_of(i * tile, tile), tile), c)

    return lax.fori_loop(0, rows // tile, step, carry)


def column_sum(value):
    rows, width = value.shape
    return jnp.sum(value.reshape(rows // 8, 8, width), axis=0)


def layer_norm(v):
    cen = v - jnp.mean(v, axis=-1, keepdims=True)
    inv = lax.rsqrt(jnp.mean(cen * cen, axis=-1, keepdims=True) + EPSILON)
    return cen * inv, inv


def layer_norm_back(w, hat, inv):
    return inv * (
        w - jnp.mean(w, axis=-1, keepdims=True) - hat * jnp.mean(w * hat, axis=-1, keepdims=True)
    )


def head_mask(i, head_dim):
    lane = lax.broadcasted_iota(jnp.int32, (1, HEAD_LANES), 1)
    return ((lane >= i * head_dim) & (lane < (i + 1) * head_dim)).astype(F32)


def forward_kernel(cfg, *refs):
    fused, chain, heads, head_dim = cfg
    refs = list(refs)
    pack = refs.pop(0)
    tok, cond, wada, bada, small_own, pos, seg, place, drop, mtok = refs[:10]
    refs = refs[10:]
    w = refs.pop(0) if fused else pack
    (
        s_hat1, s_inv, s_n1, s_qkv, s_p, s_o, s_branch, s_hat2, s_n2, s_hid, s_slope, s_y,
        s_full, s_xm, o_mod, o_cl, o_small, outs,
    ) = refs[:18]
    refs = refs[18:]
    (
        wa, wu, wd, res, hat, inv, n, r, qkv, prob, o, branch, hid, slope, y_keep,
        xs, xr, toep, small, cl, part, got, pair, mod, gs, gr, gl, ssem, rsem, lsem, ms, mr,
    ) = refs
    at = Place(chain)
    rows, width = res.shape
    lw = heads * head_dim
    shard = width // at.count
    half_heads = heads // 2
    scale = 1.0 / math.sqrt(head_dim)
    sends, recvs, locals_ = Numbered(ssem), Numbered(rsem), Numbered(lsem)
    at.greet()
    gather = Gather(at, pack, w, gs, gr, gl) if fused else None
    links = Links(at, ms, mr)
    waiting = {}

    def keep(name, src, dst):
        copy = pltpu.make_async_copy(src, dst, locals_.next())
        copy.start()
        waiting.setdefault(name, []).append(copy.wait)

    def give(name, src, dst):
        copy = remote(src, dst, sends.next(), recvs.next(), at.other)
        copy.start()
        waiting.setdefault(name, []).append(copy.wait_send)
        waiting.setdefault("end", []).append(copy.wait_recv)

    def settle(name):
        for wait in waiting.pop(name, []):
            wait()

    def pump(*what):
        if not fused:
            return
        for name, p, *k in what:
            if p < gather.pieces:
                getattr(gather, name)(p, *k)

    def load(p, slot):
        if fused:
            gather.other_in(p).wait_recv()
        keep("load%d" % p, w.at[p], slot)

    def send_cond():
        cl[pl.ds(at.dp, 1)] = cond[pl.ds(at.dp, 1)]
        return links.to_all(lambda peer: cond.at[peer], cl.at[at.dp])

    def modulation_terms(copies):
        for copy in copies:
            copy.wait_recv()
        part[...] = jnp.zeros_like(part)
        parts = thirds(silu(flat(cl[...])[:, :shard]))
        for k in range(6):
            cols = wada[:, k * ADA_LANES : (k + 1) * ADA_LANES]
            value = nn(parts[0], cols) + (nn(parts[1], cols) + nn(parts[2], cols))
            value = value.reshape(at.count, 8, ADA_LANES)
            for m in range(2):
                part[:, m * 8 + k, :] = value[:, m, :]
        got[pl.ds(at.dp, 1)] = part[pl.ds(at.dp, 1)]
        return links.to_all(lambda peer: part.at[peer], got.at[at.dp])

    def modulation_sum(copies):
        for copy in copies:
            copy.wait_recv()
        value = got[0]
        for j in range(1, at.count):
            value = value + got[j]
        pair[at.core, at.head] = value + jnp.concatenate([bada[...], bada[...]], axis=0)
        return links.around(pair)

    def modulation(copies):
        for copy in copies:
            copy.wait_recv()
        lane = lax.broadcasted_iota(jnp.int32, (8, ADA_LANES), 1)
        blank = jnp.zeros((8, width - ADA_LANES), F32)
        mine_ = pl.ds(pl.multiple_of(at.core * 8, 8), 8)
        for s in range(2):
            a, b = [
                jnp.concatenate([jnp.where(lane < lw, pair[s, h, mine_, :], 0.0), blank], axis=1)
                for h in range(2)
            ]
            mod[s] = a + pltpu.roll(b, lw, 1)
        keep("mod", mod, o_mod)
        keep("cl", cl, o_cl)

    def share_small():
        small[pl.ds(at.core, 1)] = small_own[...][None]
        return links.copy(small_own, small.at[at.core], at.other)

    def bqv_row(s, half, kind):
        return small[s, half * 4 + kind : half * 4 + kind + 1, :HEAD_LANES]

    def bup_row(s, half, cols):
        return small[s, 10 + half : 11 + half, cols]

    def send_across(i):
        copy = remote(xs.at[i], xr.at[i], sends.next(), recvs.next(), at.beside)
        copy.start()
        waiting.setdefault("end", []).append(copy.wait_send)
        return copy

    def total(i, ds):
        return xs[i, ds, :].astype(F32) + xr[i, ds, :].astype(F32)

    def norm_one(s):
        settle("hat1")
        settle("n1")
        settle("inv")

        def body(ds, c):
            v, iv = layer_norm(res[ds, :])
            hat[0, ds, :] = v.astype(BF)
            inv[0, ds, :] = jnp.broadcast_to(iv, (TILE, 128))
            n[0, ds, :] = (v * (1.0 + mod[s, 1:2, :]) + mod[s, 0:1, :]).astype(BF)
            return c

        by_rows(rows, body, 0)
        keep("hat1", hat.at[0], s_hat1.at[s])
        keep("n1", n.at[0], s_n1.at[s, 0])
        give("n1", n.at[0], s_n1.at[s, 1])

    def project(s):
        settle("qkv")
        for half in range(2):
            for j in range(3):
                cols = slice(j * 384, (j + 1) * 384)
                r[:, cols] = nn(n[0], flat(wa[half, :, :, cols]))

            def body(ds, c):
                v = r[ds, :]
                for kind, shift in ((0, 864), (1, 576), (2, 288)):
                    piece = pltpu.roll(v, shift, 1)[:, :HEAD_LANES]
                    qkv[kind, half, ds, :] = (piece + bqv_row(s, half, kind)).astype(BF)
                return c

            by_rows(rows, body, 0)
        keep("qkv", qkv, s_qkv.at[s])

    def attend(s, half):
        if half == 0:
            settle("p")
            settle("o")
        o[half] = jnp.zeros_like(o[half])

        def one(i, c):
            index = half * half_heads + i
            mask = head_mask(i, head_dim).astype(BF)
            line = small[s, pl.ds(16 + index, 1), : 2 * rows]
            skew = pltpu.roll(jnp.broadcast_to(line, (rows, 2 * rows)), 0, 1, stride=1, stride_axis=0)
            bias = skew[:, :rows]
            if s == 0:
                toep[...] = bias.astype(BF)
                left = nn(pos[...], toep[...]).astype(BF)
                bias = nt(left, pos[...]) + seg[...]
            z = nt(qkv[0, half] * mask, qkv[1, half]) * scale + bias
            e = jnp.exp(z - jnp.max(z, axis=-1, keepdims=True))
            p = (e / jnp.sum(e, axis=-1, keepdims=True)).astype(BF)
            prob[index] = p
            o[half] = o[half] + nn(p, qkv[2, half]).astype(BF) * mask
            return c

        lax.fori_loop(0, half_heads, one, 0)
        if half == 1:
            keep("p", prob, s_p.at[s])
            keep("o", o.at[at.core], s_o.at[s, 0])
            give("o", o.at[1 - at.core], s_o.at[s, 1])

    def project_out(i):
        xs[i] = (
            nt(o[0], flat(wa[0, :, :, :HEAD_LANES])) + nt(o[1], flat(wa[1, :, :, :HEAD_LANES]))
        ).astype(BF)
        return send_across(i)

    def norm_two(s, i, copy):
        copy.wait_recv()
        settle("branch")
        settle("hat2")
        settle("n2")

        def body(ds, c):
            b = total(i, ds) + small[s, 8:9, :]
            branch[ds, :] = b.astype(BF)
            xm = res[ds, :] + mod[s, 2:3, :] * b
            res[ds, :] = xm
            v, iv = layer_norm(xm)
            hat[1, ds, :] = v.astype(BF)
            inv[1, ds, :] = jnp.broadcast_to(iv, (TILE, 128))
            n[1, ds, :] = (v * (1.0 + mod[s, 4:5, :]) + mod[s, 3:4, :]).astype(BF)
            return c

        by_rows(rows, body, 0)
        keep("branch", branch, s_branch.at[s])
        keep("inv", inv, s_inv.at[s])
        keep("hat2", hat.at[1], s_hat2.at[s])
        if s == 1:
            keep("out", res, s_xm)
        keep("n2", n.at[1], s_n2.at[s, 0])
        give("n2", n.at[1], s_n2.at[s, 1])

    def hidden(s, half):
        if half == 0:
            settle("hid")
            settle("slope")
        for j in range(3):
            cols = slice(j * 384, (j + 1) * 384)
            r[:, cols] = nn(n[1], flat(wu[half, :, :, cols])) + bup_row(s, half, cols)

        def body(ds, c):
            value, sl = gelu_both(r[ds, :])
            hid[half, ds, :] = value.astype(BF)
            slope[half, ds, :] = sl.astype(BF)
            return c

        by_rows(rows, body, 0)
        if half == 1:
            keep("slope", slope, s_slope.at[s])
            keep("hid", hid.at[at.core], s_hid.at[s, 0])
            give("hid", hid.at[1 - at.core], s_hid.at[s, 1])
            if s == 1:
                keep("hid", hid, s_full)

    def project_down(i):
        xs[i] = (nt(hid[0], flat(wd[0])) + nt(hid[1], flat(wd[1]))).astype(BF)
        return send_across(i)

    def end_block(s, i, copy):
        copy.wait_recv()
        settle("y")
        settle("out")

        def body(ds, c):
            v = total(i, ds) + small[s, 9:10, :]
            y_keep[ds, :] = v.astype(BF)
            res[ds, :] = res[ds, :] + mod[s, 5:6, :] * v
            return c

        by_rows(rows, body, 0)
        keep("y", y_keep, s_y)
        here = pltpu.make_async_copy(res, outs.at[at.core], locals_.next())
        there = remote(res, outs.at[at.core], sends.next(), recvs.next(), at.other)

        @pl.when(at.core == 0)
        def _():
            here.start()

        @pl.when(at.core == 1)
        def _():
            there.start()

        def sent():
            @pl.when(at.core == 0)
            def _():
                here.wait()

            @pl.when(at.core == 1)
            def _():
                there.wait_send()

        def arrived():
            @pl.when(at.core == 0)
            def _():
                remote(res, outs.at[1], there_s, there_r, at.other).wait_recv()

        there_s, there_r = sends.ref.at[sends.count - 1], recvs.ref.at[recvs.count - 1]
        waiting.setdefault("out", []).append(sent)
        waiting.setdefault("end", []).append(arrived)

    def spread():
        r[...] = nn(place[...], res[...].astype(BF))
        settle("out")

        def body(ds, c):
            res[ds, :] = r[ds, :] + drop[ds, 0:1] * mtok[...]
            return c

        by_rows(rows, body, 0)

    copies = send_cond()
    small_copy = share_small()
    if fused:
        gather.split()
        gather.start(0)
        gather.start(1)

    def start_residual(ds, c):
        res[ds, :] = tok[ds, :].astype(F32)
        return c

    by_rows(rows, start_residual, 0)
    copies = modulation_terms(copies)
    pump(("step", 0, 1), ("start", 2))
    copies = modulation_sum(copies)
    pump(("step", 0, 2))
    modulation(copies)
    norm_one(0)
    small_copy.wait_recv()
    keep("small", small, o_small)
    pump(("step", 0, 3))
    for s in range(2):
        p = 3 * s
        pump(("step", p + 1, 1), ("start", p + 3), ("finish", p))
        if s == 1:
            end_block(0, 1, copy)
            spread()
            norm_one(1)
        pump(("step", p + 1, 2))
        load(p, wa)
        settle("load%d" % p)
        project(s)
        pump(("step", p + 1, 3))
        attend(s, 0)
        pump(("step", p + 2, 1), ("start", p + 4), ("finish", p + 1))
        attend(s, 1)
        copy = project_out(2 * s)
        load(p + 1, wu)
        pump(("step", p + 2, 2), ("step", p + 2, 3))
        norm_two(s, 2 * s, copy)
        if s == 0:
            pump(("step", p + 3, 1), ("start", p + 5), ("finish", p + 2))
        settle("load%d" % (p + 1))
        hidden(s, 0)
        if s == 0:
            load(p + 2, wd)
            pump(("step", p + 3, 2))
        hidden(s, 1)
        if s == 0:
            settle("load%d" % (p + 2))
            copy = project_down(2 * s + 1)
            pump(("step", p + 3, 3))
    if fused:
        gather.finish(5)
        gather.other_in(5).wait_recv()
        for p in range(gather.pieces):
            gather.drain(p)
    for wait in links.waiting:
        wait()
    for name in list(waiting):
        settle(name)


def forward_call(cfg, own, small, dp_count):
    fused, chain, heads, head_dim = cfg
    rows, width = small[0].shape
    pieces = 6
    shard = own.shape[-2]
    groups = width // shard
    cond_lanes = small[1].shape[2]
    bf, f = lambda *s: jax.ShapeDtypeStruct(s, BF), lambda *s: jax.ShapeDtypeStruct(s, F32)
    out_shape = [
        bf(2, rows, width),
        f(2, 2, rows, 128),
        bf(2, 2, rows, width),
        bf(2, 3, 2, rows, HEAD_LANES),
        bf(2, heads, rows, rows),
        bf(2, 2, rows, HEAD_LANES),
        bf(2, rows, width),
        bf(2, rows, width),
        bf(2, 2, rows, width),
        bf(2, 2, rows, width),
        bf(2, 2, rows, width),
        bf(rows, width),
        bf(2, rows, width),
        f(rows, width),
        f(2, 8, width),
        f(dp_count, 8, cond_lanes),
        f(2, 24, width),
        f(2, rows, width),
    ]
    if fused:
        out_shape = [bf(pieces, 2, groups, shard, width)] + out_shape
    kinds = 3 * chain + 3
    many = 2 * (dp_count - 1) + 8
    slot = pltpu.VMEM((2, groups, shard, width), BF)
    scratch = [
        slot,
        slot,
        slot,
        pltpu.VMEM((rows, width), F32),
        pltpu.VMEM((2, rows, width), BF),
        pltpu.VMEM((2, rows, 128), F32),
        pltpu.VMEM((2, rows, width), BF),
        pltpu.VMEM((rows, width), F32),
        pltpu.VMEM((3, 2, rows, HEAD_LANES), BF),
        pltpu.VMEM((heads, rows, rows), BF),
        pltpu.VMEM((2, rows, HEAD_LANES), BF),
        pltpu.VMEM((rows, width), BF),
        pltpu.VMEM((2, rows, width), BF),
        pltpu.VMEM((2, rows, width), BF),
        pltpu.VMEM((rows, width), BF),
        pltpu.VMEM((4, rows, width), BF),
        pltpu.VMEM((4, rows, width), BF),
        pltpu.VMEM((rows, rows), BF),
        pltpu.VMEM((2, 24, width), F32),
        pltpu.VMEM((dp_count, 8, cond_lanes), F32),
        pltpu.VMEM((dp_count, 16, ADA_LANES), F32),
        pltpu.VMEM((dp_count, 16, ADA_LANES), F32),
        pltpu.VMEM((2, 2, 16, ADA_LANES), F32),
        pltpu.VMEM((2, 8, width), F32),
        pltpu.SemaphoreType.DMA((pieces, kinds)),
        pltpu.SemaphoreType.DMA((pieces, kinds)),
        pltpu.SemaphoreType.DMA((3,)),
        pltpu.SemaphoreType.DMA((16,)),
        pltpu.SemaphoreType.DMA((16,)),
        pltpu.SemaphoreType.DMA((48,)),
        pltpu.SemaphoreType.DMA((many,)),
        pltpu.SemaphoreType.DMA((many,)),
    ]

    def body(*refs):
        forward_kernel(cfg, *refs)

    vm = pl.BlockSpec(memory_space=pltpu.VMEM)
    hbm = pl.BlockSpec(memory_space=pl.ANY)
    result = pl.pallas_call(
        body,
        out_shape=out_shape,
        in_specs=[hbm] + [vm] * len(small),
        out_specs=[hbm] * len(out_shape),
        scratch_shapes=scratch,
        compiler_params=pltpu.CompilerParams(
            collective_id=0, has_side_effects=True, vmem_limit_bytes=VMEM_BYTES
        ),
        name="forward_blocks",
    )(own, *small)
    return result if fused else [own] + list(result)


class Scatter:
    def __init__(self, at, order, g, yr, zr, mr, red, out, ssem, rsem, osem, isem, lsem, credit):
        self.at, self.order = at, order
        self.g, self.yr, self.zr, self.mr, self.red, self.out = g, yr, zr, mr, red, out
        self.ssem, self.rsem, self.osem, self.isem, self.lsem = ssem, rsem, osem, isem, lsem
        self.credit = credit
        chain = at.chain
        need = lambda z, t: chain if t == z else (chain - t + z if t > z else chain - z + t)
        self.table = [sorted(range(chain), key=lambda t: (need(z, t), t)) for z in range(chain)]

    def slots(self, r):
        return r % self.g.shape[0], r % self.yr.shape[0]

    def target(self, i):
        return sum(jnp.where(self.at.z == z, self.table[z][i], 0) for z in range(self.at.chain))

    def own(self, r, t):
        return self.g.at[self.slots(r)[0], t * 2 + self.at.y]

    def theirs(self, r, t):
        return self.g.at[self.slots(r)[0], t * 2 + 1 - self.at.y]

    def copy(self, src, dst, r, kind, device):
        return remote(src, dst, self.ssem.at[r, kind], self.rsem.at[r, kind], device)

    def cross(self, r, t):
        return self.copy(
            self.theirs(r, t), self.yr.at[self.slots(r)[1], t], r, t, self.at.across
        )

    def up(self, r, t):
        return self.copy(
            self.own(r, t), self.zr.at[self.slots(r)[1], t], r, self.at.chain + t, self.at.above
        )

    def down(self, r, t, last=None):
        z = self.at.z - 1 if last is None else last
        place = jnp.where(t == z, self.at.chain, t)
        return self.copy(
            self.own(r, t), self.zr.at[self.slots(r)[1], place], r, 2 * self.at.chain + t, self.at.below
        )

    def to_mate(self, r):
        return self.copy(
            self.theirs(r, self.at.mate_z), self.mr.at[self.slots(r)[1]], r, 3 * self.at.chain, self.at.mate
        )

    def add(self, block, got):
        block[...] = (block[...].astype(F32) + got[...].astype(F32)).astype(BF)

    def begin(self, r):
        at, chain = self.at, self.at.chain
        if r >= self.yr.shape[0]:
            pl.semaphore_wait(self.credit.at[0], 1)

            @pl.when(at.z < chain - 1)
            def _():
                pl.semaphore_wait(self.credit.at[1], 1)

            @pl.when(at.z > 0)
            def _():
                pl.semaphore_wait(self.credit.at[2], 1)

        if r % 2 == 1:
            self.to_mate(r).start()
        for i in range(chain - 1):
            t = self.target(i)
            if r % 2 == 1:

                @pl.when(t != at.mate_z)
                def _():
                    self.cross(r, t).start()

            else:
                self.cross(r, t).start()
        if r % 2 == 0:
            self.cross(r, at.z).start()

    def mated(self, r):
        if r % 2 == 1:
            self.to_mate(r).wait_recv()
            self.add(self.theirs(r, self.at.z), self.mr.at[self.slots(r)[1]])
            self.cross(r, self.at.z).start()

    def arrive(self, r, i):
        t = self.target(i)

        def take():
            self.cross(r, t).wait_recv()
            self.add(self.own(r, t), self.yr.at[self.slots(r)[1], t])

        if r % 2 == 1:
            pl.when(t != self.at.mate_z)(take)
        else:
            take()

    def step(self, r, k):
        z, chain = self.at.z, self.at.chain

        @pl.when((z <= k - 1) & (z < chain - 1))
        def _():
            t = chain - k + z
            if k > 1:

                @pl.when(z > 0)
                def _():
                    self.up(r, t).wait_recv()
                    self.add(self.own(r, t), self.zr.at[self.slots(r)[1], t])

            self.up(r, t).start()

        @pl.when((chain - 1 - z <= k - 1) & (z > 0))
        def _():
            t = k - chain + z
            if k > 1:

                @pl.when(z < chain - 1)
                def _():
                    self.down(r, t, last=z).wait_recv()
                    self.add(self.own(r, t), self.zr.at[self.slots(r)[1], t])

            self.down(r, t).start()

    def finish(self, r):
        at, chain = self.at, self.at.chain
        z = at.z
        slot = self.slots(r)[1]
        held = self.red.shape[0]
        if r >= held:
            self.hand_over_done(r - held)
        red = self.red.at[r % held]
        red[...] = self.own(r, z)[...].astype(F32)

        @pl.when(z > 0)
        def _():
            self.up(r, z).wait_recv()
            red[...] = red[...] + self.zr[slot, z].astype(F32)

        @pl.when(z < chain - 1)
        def _():
            self.down(r, z, last=z).wait_recv()
            red[...] = red[...] + self.zr[slot, chain].astype(F32)

        if r + self.yr.shape[0] < len(self.order):
            pl.semaphore_signal(self.credit.at[0], inc=1, device_id=at.across, device_id_type=MESH)

            @pl.when(z > 0)
            def _():
                pl.semaphore_signal(self.credit.at[1], inc=1, device_id=at.below, device_id_type=MESH)

            @pl.when(z < chain - 1)
            def _():
                pl.semaphore_signal(self.credit.at[2], inc=1, device_id=at.above, device_id_type=MESH)

        s, t = self.order[r]

        @pl.when(at.core == s)
        def _():
            self.keep(r).start()

        @pl.when(at.core != s)
        def _():
            self.hand_over(r).start()

    def keep(self, r):
        return pltpu.make_async_copy(
            self.red.at[r % self.red.shape[0]], self.out.at[self.order[r][1], self.at.core], self.lsem.at[r]
        )

    def hand_over(self, r):
        return remote(
            self.red.at[r % self.red.shape[0]],
            self.out.at[self.order[r][1], self.at.core],
            self.osem.at[r],
            self.isem.at[r],
            self.at.other,
        )

    def hand_over_done(self, r):
        s, t = self.order[r]

        @pl.when(self.at.core == s)
        def _():
            self.keep(r).wait()

        @pl.when(self.at.core != s)
        def _():
            self.hand_over(r).wait_send()

    def drain(self, r):
        z, chain = self.at.z, self.at.chain
        if r % 2 == 1:
            self.to_mate(r).wait_send()
        for t in range(chain):
            if r % 2 == 1:

                @pl.when(t != self.at.mate_z)
                def _():
                    self.cross(r, t).wait_send()

            else:
                self.cross(r, t).wait_send()

            @pl.when(t > z)
            def _():
                self.up(r, t).wait_send()

            @pl.when(t < z)
            def _():
                self.down(r, t).wait_send()

    def end(self):
        for r in range(len(self.order)):
            if r + self.red.shape[0] >= len(self.order):
                self.hand_over_done(r)
            s, t = self.order[r]

            @pl.when(self.at.core == s)
            def _():
                remote(
                    self.red.at[0],
                    self.out.at[t, 1 - self.at.core],
                    self.osem.at[r],
                    self.isem.at[r],
                    self.at.other,
                ).wait_recv()


ORDER = ((1, 2), (1, 1), (1, 0), (0, 2), (0, 1), (0, 0))


def backward_kernel(cfg, *refs):
    fused, chain, heads, head_dim = cfg
    refs = list(refs)
    w = refs.pop(0)
    (
        i_hat1, i_inv, i_n1, i_qkv, i_p, i_o, i_branch, i_hat2, i_n2, i_hid, i_slope, i_y, i_full, i_xm,
    ) = refs[:14]
    refs = refs[14:]
    dout, mod, small, cl, wada, flips, pos, place, drop = refs[:9]
    refs = refs[9:]
    red_out, o_dx, o_out, o_sums, o_dm, o_dc = refs[:6]
    refs = refs[6:]
    (
        wslot, hat1, inv, qkv, prob, o, branch, hat2, n2, hid, slope,
        d, r, dy, dpre, dattn, dqkv, do, xs, xr, g, yr, zr, mr, red,
        stats, got, sums, rounds, dm, dc, dg, gs, gr, go, gi, gl, credit, ssem, rsem, lsem, ms, mrs,
    ) = refs
    at = Place(chain)
    rows, width = d.shape
    lw = heads * head_dim
    shard = width // at.count
    half_heads = heads // 2
    scale = 1.0 / math.sqrt(head_dim)
    sends, recvs, locals_ = Numbered(ssem), Numbered(rsem), Numbered(lsem)
    at.greet()
    links = Links(at, ms, mrs)
    stats[...] = jnp.zeros_like(stats)
    scatter = (
        Scatter(at, ORDER, g, yr, zr, mr, red, red_out, gs, gr, go, gi, gl, credit) if fused else None
    )
    slots = g.shape[0]
    waiting = {}

    def fetch(name, src, dst):
        copy = pltpu.make_async_copy(src, dst, locals_.next())
        copy.start()
        waiting.setdefault(name, []).append(copy.wait)

    def settle(name):
        for wait in waiting.pop(name, []):
            wait()

    def give(name, src, dst):
        copy = remote(src, dst, sends.next(), recvs.next(), at.other)
        copy.start()
        waiting.setdefault(name + " in", []).append(copy.wait_recv)
        waiting.setdefault(name + " out", []).append(copy.wait_send)

    def pump(*what):
        if not fused:
            return
        for name, r_, *k in what:
            if 0 <= r_ < len(ORDER):
                getattr(scatter, name)(r_, *k)

    def pump_rest(r_, start):
        for i in range(start, chain):
            pump(("arrive", r_, i))
            if i < chain - 1:
                pump(("step", r_, i + 1))
        pump(("finish", r_))

    def send_across(i):
        if i > 1:
            settle("x out %d" % (i - 2))
        copy = remote(xs.at[i % 2], xr.at[i % 2], sends.next(), recvs.next(), at.beside)
        copy.start()
        waiting.setdefault("x in %d" % i, []).append(copy.wait_recv)
        waiting.setdefault("x out %d" % i, []).append(copy.wait_send)

    def total(i, ds):
        return xs[i % 2, ds, :].astype(F32) + xr[i % 2, ds, :].astype(F32)

    def stat(s, row, value):
        stats[s, row : row + 1, :] = jnp.sum(value, axis=0, keepdims=True)

    zero8 = lambda: jnp.zeros((8, width), F32)
    spans = [slice(k * HEAD_LANES, (k + 1) * HEAD_LANES) for k in range(3)]
    spot = lambda half: jnp.where(half == at.core, 0, 2)

    def loads(s):
        fetch("slope", i_slope.at[s], slope)
        if s == 0:
            fetch("y", i_y, xs.at[2])
        else:
            fetch("full", i_full, dqkv.at[0:2])
        fetch("hid", i_hid.at[s], hid)
        fetch("n2", i_n2.at[s], n2)
        fetch("hat2", i_hat2.at[s], hat2)
        fetch("inv", i_inv.at[s], inv)
        fetch("branch", i_branch.at[s], branch)
        fetch("p", i_p.at[s], prob)
        fetch("qkv", i_qkv.at[s], qkv)
        fetch("o", i_o.at[s], o)
        fetch("hat1", i_hat1.at[s], hat1)

    def product(r_, parts):
        slot = r_ % slots
        if r_ >= slots:
            if fused:
                scatter.drain(r_ - slots)
            else:
                settle("g%d" % (r_ - slots))
        for j in range(width // 384):
            cols = slice(j * 384, (j + 1) * 384)
            value = 0.0
            for lhs, rhs in parts(j):
                value = value + tn(lhs, rhs)
            g[slot, :, :, cols] = value.astype(BF).reshape(g.shape[1], g.shape[2], 384)
        if not fused:
            s, t = ORDER[r_]
            fetch("g%d" % r_, g.at[slot], red_out.at[s * 3 + t])

    def cols_of(ref, j):
        return flat(ref[0:2, :, j * 384 : (j + 1) * 384])

    def block_back(s):
        base = 0 if s == 1 else 3
        xi = 0 if s == 1 else 2
        first, second, third = (0, 1, 0) if s == 1 else (1, 0, 1)
        settle("y")
        settle("dy out")

        def one(ds, c):
            a, b = c
            dv = d[ds, :]
            v = (dv * mod[s, 5:6, :]).astype(BF)
            dy[0, ds, :] = v
            if s == 0:
                a = a + column_sum(dv * xs[2, ds, :].astype(F32))
            return (a, b + column_sum(v.astype(F32)))

        a, b = by_rows(rows, one, (zero8(), zero8()))
        if s == 0:
            stat(s, 5, a)
        stat(s, 6, b)
        give("dy", dy.at[0], dy.at[1])
        settle("w%d" % first)
        settle("slope")
        settle("dpre out")
        if s == 1:
            settle("full")
            project_down()
        for half in range(2):
            for j in range(3):
                cols = slice(j * 384, (j + 1) * 384)
                v = (nn(dy[0], flat(wslot[first, half, :, :, cols])) * slope[half, :, cols].astype(F32)).astype(BF)
                dpre[spot(half), :, cols] = v
                stats[s, 8 + half : 9 + half, cols] = jnp.sum(v.astype(F32), axis=0, keepdims=True)
        give("dpre", dpre.at[2], dpre.at[1])
        fetch("w%d" % first, w.at[3 * s], wslot.at[first])
        settle("dy in")
        settle("hid")
        product(base, lambda j: [(flat(dy[...]), cols_of(hid, j))])
        fetch("n1", i_n1.at[s], hid)
        pump(("begin", base))
        settle("w%d" % second)
        if xi > 1:
            settle("x out %d" % (xi - 2))
        xs[xi % 2] = (
            nt(dpre[spot(0)], flat(wslot[second, 0])) + nt(dpre[spot(1)], flat(wslot[second, 1]))
        ).astype(BF)
        send_across(xi)
        if s == 1:
            fetch("w%d" % second, w.at[2], wslot.at[second])
        if s == 0:
            pump(("arrive", 1, 3), ("finish", 1))
        settle("dpre in")
        settle("n2")
        product(base + 1, lambda j: [(flat(n2[...]), cols_of(dpre, j))])
        pump(("begin", base + 1))
        if s == 1:
            pump(("arrive", 0, 0), ("step", 0, 1), ("arrive", 0, 1), ("step", 0, 2))
        else:
            pump(("arrive", 2, 0), ("step", 2, 1), ("arrive", 2, 1), ("step", 2, 2), ("arrive", 2, 2), ("step", 2, 3))
        settle("x in %d" % xi)
        settle("hat2")
        settle("inv")
        settle("branch")
        settle("dattn out")

        def two(ds, c):
            c0, c1, c2, c3 = c
            dn = total(xi, ds)
            hv = hat2[ds, :].astype(F32)
            dxm = d[ds, :] + layer_norm_back(dn * (1.0 + mod[s, 4:5, :]), hv, inv[1, ds, 0:1])
            d[ds, :] = dxm
            da = (dxm * mod[s, 2:3, :]).astype(BF)
            dattn[0, ds, :] = da
            return (
                c0 + column_sum(dn),
                c1 + column_sum(dn * hv),
                c2 + column_sum(dxm * branch[ds, :].astype(F32)),
                c3 + column_sum(da.astype(F32)),
            )

        c0, c1, c2, c3 = by_rows(rows, two, (zero8(),) * 4)
        stat(s, 3, c0)
        stat(s, 4, c1)
        stat(s, 2, c2)
        stat(s, 7, c3)
        give("dattn", dattn.at[0], dattn.at[1])
        settle("w%d" % third)
        settle("p")
        settle("qkv")
        settle("dqkv out")
        for half in range(2):
            if s == 1 and half == 0:
                pump(("arrive", 0, 2), ("step", 0, 3))
            if s == 1 and half == 1:
                pump(("arrive", 0, 3))
            if s == 0 and half == 0:
                pump(("arrive", 2, 3), ("finish", 2))
            if s == 0 and half == 1:
                pump(("mated", 3), ("arrive", 3, 0), ("step", 3, 1))
            do[half] = nn(dattn[0], flat(wslot[third, half, :, :, :HEAD_LANES])).astype(BF)
            r[...] = jnp.zeros_like(r)

            def head(i, c):
                index = half * half_heads + i
                mask = head_mask(i, head_dim)
                low_mask = mask.astype(BF)
                p = prob[index]
                dom = do[half] * low_mask
                r[:, spans[2]] = r[:, spans[2]] + tn(p, dom)
                ds = nt(dom, qkv[2, half])
                pf = p.astype(F32)
                dz = (pf * (ds - jnp.sum(pf * ds, axis=-1, keepdims=True))).astype(BF)
                r[:, spans[0]] = r[:, spans[0]] + nn(dz, qkv[1, half]) * mask
                r[:, spans[1]] = r[:, spans[1]] + tn(dz, qkv[0, half]) * mask
                square = tn(flips[s], dz)
                if s == 0:
                    high = square.astype(BF)
                    low = (square - high.astype(F32)).astype(BF)
                    square = nn(high, pos[...]) + nn(low, pos[...])
                wide = jnp.concatenate([square, jnp.zeros_like(square)], axis=1)
                skew = pltpu.roll(wide, 0, 1, stride=1, stride_axis=0)
                stats[s, pl.ds(16 + index, 1), : 2 * rows] = jnp.sum(skew, axis=0, keepdims=True)
                return c

            lax.fori_loop(0, half_heads, head, 0)
            where = spot(half)

            def gather_rows(ds, c):
                blank = jnp.zeros((TILE, HEAD_LANES), F32)
                v = 0.0
                for kind, shift, factor in ((0, 288, scale), (1, 576, scale), (2, 864, 1.0)):
                    part = jnp.concatenate([r[ds, spans[kind]] * factor, blank, blank], axis=1)
                    v = v + pltpu.roll(part, shift, 1)
                v = v.astype(BF)
                dqkv[where, ds, :] = v
                return c + column_sum(v.astype(F32))

            stat(s, 10 + half, by_rows(rows, gather_rows, zero8()))
        give("dqkv", dqkv.at[2], dqkv.at[1])
        if s == 1:
            fetch("xm", i_xm, r)
        xs_free = xi + 1
        if xs_free > 1:
            settle("x out %d" % (xs_free - 2))
        xs[xs_free % 2] = (
            nt(dqkv[spot(0)], flat(wslot[third, 0])) + nt(dqkv[spot(1)], flat(wslot[third, 1]))
        ).astype(BF)
        send_across(xs_free)
        if s == 1:
            fetch("w%d" % third, w.at[1], wslot.at[third])
        if s == 1:
            pump(("finish", 0))
        settle("dqkv in")
        settle("dattn in")
        settle("n1")
        settle("o")
        product(
            base + 2,
            lambda j: [(flat(hid[...]), cols_of(dqkv, j))]
            + ([(flat(dattn[...]), flat(o[...]))] if j == 0 else []),
        )
        pump(("begin", base + 2))
        if s == 1:
            pump(("mated", 1), ("arrive", 1, 0), ("step", 1, 1))
            end_forward()
            pump(("arrive", 1, 1), ("step", 1, 2))
        else:
            pump(("arrive", 3, 1), ("step", 3, 2), ("arrive", 3, 2), ("step", 3, 3))
        settle("x in %d" % xs_free)
        settle("hat1")

        def three(ds, c):
            c0, c1, c2 = c
            dn = total(xs_free, ds)
            hv = hat1[ds, :].astype(F32)
            dx = d[ds, :] + layer_norm_back(dn * (1.0 + mod[s, 1:2, :]), hv, inv[0, ds, 0:1])
            d[ds, :] = dx
            return (c0 + column_sum(dn), c1 + column_sum(dn * hv), c2 + column_sum(dx * drop[ds, 0:1]))

        c0, c1, c2 = by_rows(rows, three, (zero8(),) * 3)
        stat(s, 0, c0)
        stat(s, 1, c1)
        stat(s, 12, c2)
        to_section("dx", s, d, o_dx)

    def to_section(name, s, src, out):
        here = pltpu.make_async_copy(src, out.at[at.core], locals_.next())
        ss, rs = sends.next(), recvs.next()

        @pl.when(at.core == s)
        def _():
            here.start()

        @pl.when(at.core != s)
        def _():
            remote(src, out.at[at.core], ss, rs, at.other).start()

        def sent():
            @pl.when(at.core == s)
            def _():
                here.wait()

            @pl.when(at.core != s)
            def _():
                remote(src, out.at[at.core], ss, rs, at.other).wait_send()

        def arrived():
            @pl.when(at.core == s)
            def _():
                remote(src, out.at[1 - at.core], ss, rs, at.other).wait_recv()

        waiting.setdefault(name, []).append(sent)
        waiting.setdefault("end", []).append(arrived)

    def project_down():
        xs[2] = (nt(dqkv[0], flat(wslot[0, 0])) + nt(dqkv[1], flat(wslot[0, 1]))).astype(BF)
        copy = remote(xs.at[2], xr.at[2], sends.next(), recvs.next(), at.beside)
        copy.start()
        waiting.setdefault("y in", []).append(copy.wait_recv)
        waiting.setdefault("y out", []).append(copy.wait_send)

    def end_forward():
        settle("y in")
        settle("y out")
        settle("xm")

        def body(ds, c):
            v = xs[2, ds, :].astype(F32) + xr[2, ds, :].astype(F32) + small[1, 9:10, :]
            r[ds, :] = r[ds, :] + mod[1, 5:6, :] * v
            return c + column_sum(dout[ds, :].astype(F32) * v)

        stat(1, 5, by_rows(rows, body, zero8()))
        to_section("result", 1, r, o_out)

    def sums_begin():
        stats[0, 12:13, :] = stats[1, 12:13, :]
        return links.copy(stats.at[1 - at.core], got, at.other)

    def sums_share(copy):
        copy.wait_recv()
        sums[0] = stats[at.core] + got[...]
        row = lax.broadcasted_iota(jnp.int32, (8, ADA_LANES), 0)
        lane = lax.broadcasted_iota(jnp.int32, (8, ADA_LANES), 1)
        for m, value in ((at.core, stats[at.core, 0:8, :]), (1 - at.core, got[0:8, :])):
            cut = jnp.where(
                at.head == 0, value[:, :ADA_LANES], pltpu.roll(value, width - lw, 1)[:, :ADA_LANES]
            )
            cut = jnp.where((row < 6) & (lane < lw), cut, 0.0)
            dm[at.dp, pl.ds(pl.multiple_of(m * 8, 8), 8), :] = cut
        copies = links.to_all(lambda peer: dm.at[at.dp], dm.at[at.dp])
        return copies, sums_round(0)

    def sums_round(b):
        return links.copy(sums.at[b], rounds.at[b], at.in_dp(at.flip(b)))

    def sums_next(b, copy):
        copy.wait_recv()
        sums[b + 1] = sums[b] + rounds[b]
        if b + 1 < rounds.shape[0]:
            return sums_round(b + 1)
        fetch("sums", sums.at[b + 1], o_sums)
        return None

    def cond_terms(copies):
        for copy in copies:
            copy.wait_recv()
        fetch("dm", dm, o_dm)
        lhs = flat(dm[...])
        high = lhs.astype(BF)
        low = (lhs - high.astype(F32)).astype(BF)
        row = lax.rem(lax.broadcasted_iota(jnp.int32, (lhs.shape[0], 1), 0), 8)
        total_ = jnp.zeros((lhs.shape[0], shard), F32)
        for k in range(6):
            cols = wada[:, k * ADA_LANES : (k + 1) * ADA_LANES]
            total_ = total_ + jnp.where(row == k, nt(high, cols) + nt(low, cols), 0.0)
        total_ = total_.reshape(at.count, 16, shard)
        for m in range(2):
            dc[at.core, at.head, m, :, :shard] = jnp.sum(total_[:, m * 8 : (m + 1) * 8, :], axis=1)
        return links.around(dc)

    def cond_share(copies):
        for copy in copies:
            copy.wait_recv()
        for m in range(2):
            value = (dc[0, 0, m] + dc[0, 1, m]) + (dc[1, 0, m] + dc[1, 1, m])
            v = cl[:, m, :]
            sig = 1.0 / (1.0 + jnp.exp(-v))
            dg[at.dp, m] = value * (sig * (1.0 + v * (1.0 - sig)))
        return links.to_all(lambda peer: dg.at[at.dp], dg.at[at.dp])

    def cond_end(copies):
        for copy in copies:
            copy.wait_recv()
        fetch("dg", dg, o_dc)

    dc[...] = jnp.zeros_like(dc)
    loads(1)
    fetch("w0", w.at[5], wslot.at[0])
    fetch("w1", w.at[4], wslot.at[1])

    def start_rows(ds, c):
        d[ds, :] = dout[ds, :].astype(F32)
        return c

    by_rows(rows, start_rows, 0)
    block_back(1)
    loads(0)
    settle("result")
    r[...] = tn(place[...], d[...].astype(BF))
    settle("dx")
    pump(("arrive", 1, 2), ("step", 1, 3))

    def move(ds, c):
        d[ds, :] = r[ds, :]
        return c

    by_rows(rows, move, 0)
    block_back(0)
    copy = sums_begin()
    pump(("arrive", 3, 3), ("finish", 3))
    copies, copy = sums_share(copy)
    pump(("arrive", 4, 0), ("step", 4, 1))
    copy = sums_next(0, copy)
    copies = cond_terms(copies)
    pump(("arrive", 4, 1), ("step", 4, 2))
    for b in range(1, rounds.shape[0]):
        copy = sums_next(b, copy)
        pump(("arrive", 4, b + 1))
        if b + 2 < chain:
            pump(("step", 4, b + 2))
    copies = cond_share(copies)
    pump(("finish", 4), ("mated", 5), ("arrive", 5, 0), ("step", 5, 1))
    cond_end(copies)
    pump_rest(5, 1)
    if fused:
        for r_ in range(len(ORDER) - slots, len(ORDER)):
            scatter.drain(r_)
        scatter.end()
    for wait in links.waiting:
        wait()
    for name in list(waiting):
        settle(name)


def backward_call(cfg, w, saved, small):
    fused, chain, heads, head_dim = cfg
    rows, width = small[0].shape
    pieces, _, groups, shard, _ = w.shape
    count, _, cond_lanes = small[3].shape
    steps = count.bit_length() - 1
    many = 2 * (count - 1) + 6 + steps
    bf, f = lambda *s: pltpu.VMEM(s, BF), lambda *s: pltpu.VMEM(s, F32)
    dma = lambda *s: pltpu.SemaphoreType.DMA(s)
    out_shape = [
        jax.ShapeDtypeStruct((3, 2, shard, width), F32)
        if fused
        else jax.ShapeDtypeStruct((pieces, groups, shard, width), BF),
        jax.ShapeDtypeStruct((2, rows, width), F32),
        jax.ShapeDtypeStruct((2, rows, width), F32),
        jax.ShapeDtypeStruct((24, width), F32),
        jax.ShapeDtypeStruct((count, 16, ADA_LANES), F32),
        jax.ShapeDtypeStruct((count, 2, count, cond_lanes), F32),
    ]
    some = 3 if fused else 1
    links = chain if fused else 1
    block = shard if fused else 16
    scratch = [
        bf(2, 2, groups, shard, width),
        bf(rows, width),
        f(2, rows, 128),
        bf(3, 2, rows, HEAD_LANES),
        bf(heads, rows, rows),
        bf(2, rows, HEAD_LANES),
        bf(rows, width),
        bf(rows, width),
        bf(2, rows, width),
        bf(2, rows, width),
        bf(2, rows, width),
        f(rows, width),
        f(rows, width),
        bf(2, rows, width),
        bf(3, rows, width),
        bf(2, rows, width),
        bf(3, rows, width),
        bf(2, rows, HEAD_LANES),
        bf(3, rows, width),
        bf(3, rows, width),
        bf(4, groups, shard, width),
        bf(some, links, block, width),
        bf(some, links + 1, block, width),
        bf(some, block, width),
        f(2, block, width),
        f(2, 24, width),
        f(24, width),
        f(steps + 1, 24, width),
        f(steps, 24, width),
        f(count, 16, ADA_LANES),
        f(2, 2, 2, count, cond_lanes),
        f(count, 2, count, cond_lanes),
        dma(6, 3 * links + 1),
        dma(6, 3 * links + 1),
        dma(6),
        dma(6),
        dma(6),
        pltpu.SemaphoreType.REGULAR((3,)),
        dma(16),
        dma(16),
        dma(56),
        dma(many),
        dma(many),
    ]

    def body(*refs):
        backward_kernel(cfg, *refs)

    vm = pl.BlockSpec(memory_space=pltpu.VMEM)
    hbm = pl.BlockSpec(memory_space=pl.ANY)
    return pl.pallas_call(
        body,
        out_shape=out_shape,
        in_specs=[hbm] * (1 + len(saved)) + [vm] * len(small),
        out_specs=[hbm] * len(out_shape),
        scratch_shapes=scratch,
        compiler_params=pltpu.CompilerParams(
            collective_id=1, has_side_effects=True, vmem_limit_bytes=VMEM_BYTES
        ),
        name="backward_blocks",
    )(w, *saved, *small)


def per_device(
    tokens,
    kept_mask,
    timesteps,
    labels,
    w_qkv,
    b_qv,
    w_out,
    b_out,
    w_up,
    b_up,
    w_down,
    b_down,
    w_ada,
    b_ada,
    rel_table,
    mask_token,
    class_table,
    out_grad,
):
    micro, rows, width = tokens.shape
    length = kept_mask.shape[2]
    classes = class_table.shape[0]
    heads = rel_table.shape[1]
    lw = w_qkv.shape[3]
    head_dim = lw // heads
    hw = lw // 2
    ff = w_up.shape[2]
    fw = ff // 2
    dp_count = lax.axis_size("dp")
    c = lax.axis_index("section")
    dp = lax.axis_index("dp")
    h = lax.axis_index("head")

    qkv = jnp.transpose(w_qkv[0], (1, 0, 2))
    out_t = w_out[0].T
    down_t = w_down[0].T
    halves = []
    for half in range(2):
        at = slice(half * hw, (half + 1) * hw)
        fat = slice(half * fw, (half + 1) * fw)
        a = jnp.concatenate([out_t[:, at], qkv[0][:, at], qkv[1][:, at], qkv[2][:, at]], axis=1)
        halves.append(jnp.stack([a, w_up[0][:, fat], down_t[:, fat]]))
    pack = jnp.stack(halves)
    fr = width // dp_count

    label_pick = (labels == jnp.arange(classes)[None, :]).astype(BF)
    cond = nn(label_pick, class_table) + time_features(timesteps[:, 0], width)
    blocks = jnp.transpose(cond.reshape(micro, dp_count, fr), (1, 0, 2))
    tags = jnp.broadcast_to(labels.astype(F32)[None], (dp_count, micro, 1))
    cond_lanes = -(-(fr + 1) // 128) * 128
    blocks = jnp.concatenate([blocks, tags], axis=2)
    blocks = jnp.pad(blocks, ((0, 0), (0, 8 - micro), (0, cond_lanes - fr - 1)))
    ada = jnp.pad(w_ada[0], ((0, 0), (0, 0), (0, ADA_LANES - lw))).reshape(fr, 6 * ADA_LANES)
    b_ada_in = jnp.pad(b_ada[0].astype(F32), ((0, 2), (0, ADA_LANES - lw)))

    def row_block(value):
        return jnp.pad(value.astype(F32), ((0, 0), (0, width - value.shape[1])))

    qv = b_qv[0].reshape(2, 2, hw)
    none = jnp.zeros((2, hw), BF)
    qv_rows = jnp.stack([qv[0], none, qv[1], none], axis=1).reshape(8, hw)
    qv_rows = jnp.pad(qv_rows, ((0, 0), (0, HEAD_LANES - hw)))
    rel = rel_table[0]
    rel = jnp.concatenate(
        [rel[:, length - 1 :: -1], jnp.zeros((heads, 1), BF), rel[:, : length - 1 : -1]], axis=1
    )
    small_own = jnp.concatenate(
        [
            row_block(qv_rows),
            row_block(b_out),
            row_block(b_down),
            row_block(b_up[0].reshape(2, fw)),
            jnp.zeros((4, width), F32),
            row_block(rel),
        ]
    )

    kept = kept_mask[c, 0]
    source = jnp.cumsum(kept) - 1
    count = jnp.sum(kept)
    span = jnp.arange(length, dtype=jnp.int32)
    place = ((kept[:, None] == 1) & (source[:, None] == span[None, :])).astype(BF)
    pad = span >= count
    pos = place.T + (pad[:, None] & (span[None, :] == 0)).astype(BF)
    seg = jnp.where(pad[:, None] == pad[None, :], 0.0, NEGATIVE)
    mirror = (span[:, None] + span[None, :] == length - 1).astype(BF)
    flips = jnp.stack([pos[:, ::-1], mirror])
    drop = jnp.broadcast_to((1 - kept)[:, None].astype(F32), (rows, 128))

    fused = dp_count == 8 and fr % 16 == 0
    cfg = (fused, dp_count // 2, heads, head_dim)
    if fused:
        source_w = pack
    else:
        other_w = swap(mine(1 - c, halves), "section")
        own_w = mine(c, halves)
        own_w = jnp.concatenate([pick(c, own_w, other_w), pick(c, other_w, own_w)])
        half_w_ = lax.all_gather(own_w, "dp", axis=1, tiled=True)
        other_w = swap(half_w_, "section")
        source_w = jnp.stack([pick(c, half_w_, other_w), pick(c, other_w, half_w_)], axis=1)
        source_w = source_w.reshape(6, 2, 8, width // 8, pack.shape[3])
    small_in = (
        tokens[c],
        blocks,
        ada,
        b_ada_in,
        small_own,
        pos,
        seg,
        place,
        drop,
        mask_token.astype(F32)[None, :],
    )
    full, *saved, mod, cond_all, small_all, outs = forward_call(cfg, source_w, small_in, dp_count)
    small_back = (out_grad[c], mod, small_all, cond_all, ada, flips, pos, place, drop)
    red, dx, outs_b, sums, dm, dc = backward_call(cfg, full, saved, small_back)

    if fused:
        g0, g1 = red[:, 0], red[:, 1]
    else:
        red = lax.psum_scatter(
            red.reshape(6, width, pack.shape[3]), "dp", scatter_dimension=1, tiled=True
        ).astype(F32)
        red = red.reshape(2, 3, fr, pack.shape[3])
        g_own = mine(c, red)
        g_got = swap(mine(1 - c, red), "section")
        g0, g1 = pick(c, g_own, g_got), pick(c, g_got, g_own)
    g_qkv = jnp.stack(
        [
            jnp.concatenate([g0[0][:, i * hw : (i + 1) * hw], g1[0][:, i * hw : (i + 1) * hw]], axis=1)
            for i in (1, 2, 3)
        ],
        axis=1,
    )
    g_out = jnp.concatenate([g0[0][:, :hw], g1[0][:, :hw]], axis=1).T
    g_up = jnp.concatenate([g0[1], g1[1]], axis=1)
    g_down = jnp.concatenate([g0[2], g1[2]], axis=1).T

    half_w = width // 2

    def half(v):
        return lax.dynamic_slice_in_dim(v, h * half_w, half_w, v.ndim - 1)

    g_b_qv = jnp.stack(
        [
            jnp.concatenate([sums[10, at * hw : (at + 1) * hw], sums[11, at * hw : (at + 1) * hw]])
            for at in (1, 3)
        ]
    )
    g_b_up = sums[8:10, :fw].reshape(-1)
    g_rel = sums[16 : 16 + heads, 2 * length - 2 :: -1]

    dm = dm.reshape(dp_count, micro, 8, ADA_LANES)[:, :, :6, :lw]
    cond_part = jax.nn.silu(cond_all[:, :micro, :fr])
    g_ada = jnp.einsum("jmf,jmke->fke", cond_part, dm, precision=PRECISE)
    g_b_ada = jnp.sum(dm, axis=(0, 1))
    labels_all = cond_all[:, :micro, fr].astype(jnp.int32).T.reshape(-1)
    dcond = jnp.transpose(dc[..., :fr], (1, 2, 0, 3)).reshape(micro * dp_count, width)
    pick_all = (labels_all[:, None] == jnp.arange(classes)[None, :]).astype(F32)
    g_class = jnp.einsum("ic,id->cd", pick_all, half(dcond), precision=PRECISE)

    return (
        pick(c, outs, outs_b)[None],
        dx[None],
        g_qkv[None],
        g_b_qv[None],
        g_out[None],
        half(sums[7])[None],
        g_up[None],
        g_b_up[None],
        g_down[None],
        half(sums[6])[None],
        g_ada[None],
        g_b_ada[None],
        g_rel[None],
        half(sums[12]),
        g_class,
    )


def solution(mesh):
    placed = (
        P(None, "dp", None),
        P(None, "dp", None),
        P(None, "dp"),
        P(None, "dp"),
        P("section", "dp", None, "head"),
        P("section", None, "head"),
        P("section", "head", "dp"),
        P("section", None),
        P("section", "dp", "head"),
        P("section", "head"),
        P("section", "head", "dp"),
        P("section", None),
        P("section", "dp", None, "head"),
        P("section", None, "head"),
        P("section", "head", None),
        P(),
        P(),
        P(None, "dp", None),
    )
    return jax.shard_map(
        per_device,
        mesh=mesh,
        in_specs=placed,
        out_specs=(
            P("section", None, "dp", None),
            P("section", None, "dp", None),
            P("section", "dp", None, "head"),
            P("section", None, "head"),
            P("section", "head", "dp"),
            P("section", "head"),
            P("section", "dp", "head"),
            P("section", "head"),
            P("section", "head", "dp"),
            P("section", "head"),
            P("section", "dp", None, "head"),
            P("section", None, "head"),
            P("section", "head", None),
            P("head"),
            P(None, "head"),
        ),
        check_vma=False,
    )
```

```python
import math

import jax
import jax.numpy as jnp
from jax import lax
from jax.experimental import pallas as pl
from jax.experimental.pallas import tpu as pltpu
from jax.sharding import PartitionSpec as P

PRECISE = lax.Precision.HIGHEST
EPSILON = 1e-06
NEGATIVE = -1e30
MESH = pl.DeviceIdType.MESH
BF = jnp.bfloat16
VMEM_BYTES = 62 * 1024 * 1024
F32 = jnp.float32


def time_features(step_ids, model_width):
    half_width = model_width // 2
    frequency = jnp.exp(-math.log(10000.0) * jnp.arange(half_width).astype(F32) / half_width)
    angles = step_ids.astype(F32)[..., None] * frequency
    return jnp.concatenate([jnp.cos(angles), jnp.sin(angles)], axis=-1)


def swap(value, axis):
    return lax.ppermute(value, axis, [(0, 1), (1, 0)])


def pick(index, first, second):
    return jnp.where(index == 0, first, second)


def mine(c, pair):
    return pick(c, pair[0], pair[1])


def both(value):
    c = lax.axis_index("section")
    got = swap(value, "section")
    return pick(c, value, got), pick(c, got, value)


HEAD_LANES = 384
ADA_LANES = 640


def nn(a, b):
    return lax.dot_general(a, b, (((1,), (0,)), ((), ())), preferred_element_type=F32)


def nt(a, b):
    return lax.dot_general(a, b, (((1,), (1,)), ((), ())), preferred_element_type=F32)


def tn(a, b):
    return lax.dot_general(a, b, (((0,), (0,)), ((), ())), preferred_element_type=F32)


def flat(value):
    return value.reshape(value.shape[0] * value.shape[1], value.shape[2])


GELU_SCALE = math.sqrt(2.0 / math.pi)


def gelu_both(v):
    t = jnp.tanh(GELU_SCALE * (v + 0.044715 * v * v * v))
    slope = 0.5 * (1.0 + t) + (0.5 * GELU_SCALE) * v * (1.0 - t * t) * (1.0 + 0.134145 * v * v)
    return 0.5 * v * (1.0 + t), slope


class Place:
    def __init__(self, chain):
        self.chain = chain
        self.core = lax.axis_index("section")
        self.dp = lax.axis_index("dp")
        self.head = lax.axis_index("head")
        self.z = self.dp // 2
        self.y = self.dp % 2
        self.mate_z = self.z + 1 - 2 * (self.z % 2)
        self.above = (self.core, self.dp + 2, self.head)
        self.below = (self.core, self.dp - 2, self.head)
        self.across = (self.core, self.z * 2 + 1 - self.y, self.head)
        self.mate = (self.core, self.mate_z * 2 + self.y, self.head)
        self.other = (1 - self.core, self.dp, self.head)
        self.beside = (self.core, self.dp, 1 - self.head)

        self.beyond = (1 - self.core, self.dp, 1 - self.head)
        self.count = 2 * chain

    def peer(self, k):
        return lax.rem(self.dp + k, self.count)

    def source(self, k):
        return lax.rem(self.dp + self.count - k, self.count)

    def flip(self, b):
        bit = lax.rem(self.dp // (1 << b), 2)
        return self.dp + (1 << b) * (1 - 2 * bit)

    def in_dp(self, dp):
        return (self.core, dp, self.head)

    def greet(self):
        barrier = pltpu.get_barrier_semaphore()
        others = [self.other, self.beside, self.beyond]
        others += [self.in_dp(self.peer(k)) for k in range(1, self.count)]
        for device in others:
            pl.semaphore_signal(barrier, inc=1, device_id=device, device_id_type=MESH)
        pl.semaphore_wait(barrier, len(others))


def remote(src, dst, ssem, rsem, device):
    return pltpu.make_async_remote_copy(
        src_ref=src, dst_ref=dst, send_sem=ssem, recv_sem=rsem, device_id=device, device_id_type=MESH
    )


class Numbered:
    def __init__(self, ref):
        self.ref = ref
        self.count = 0

    def next(self):
        self.count += 1
        assert self.count <= self.ref.shape[0]
        return self.ref.at[self.count - 1]


class Links:
    def __init__(self, at, ssem, rsem):
        self.at, self.sends, self.recvs = at, Numbered(ssem), Numbered(rsem)
        self.waiting = []

    def copy(self, src, dst, device):
        copy = remote(src, dst, self.sends.next(), self.recvs.next(), device)
        copy.start()
        self.waiting.append(copy.wait_send)
        return copy

    def to_all(self, src_of, dst):
        copies = []
        for k in range(1, self.at.count):
            peer = self.at.peer(k)
            copies.append(self.copy(src_of(peer), dst, self.at.in_dp(peer)))
        return copies

    def around(self, ref):
        mine_ = ref.at[self.at.core, self.at.head]
        return [
            self.copy(mine_, mine_, device)
            for device in (self.at.other, self.at.beside, self.at.beyond)
        ]


COPY_BY_MATE = (1, 3, 5)
SUM_BY_MATE = (1, 2, 3, 4)


class Gather:
    def __init__(self, at, pack, w, ssem, rsem, lsem):
        self.at, self.pack, self.w = at, pack, w
        self.ssem, self.rsem, self.lsem = ssem, rsem, lsem
        self.pieces = w.shape[0]

    def local(self, t):
        core = self.at.core
        return pltpu.make_async_copy(
            self.pack.at[core, t], self.w.at[3 * core + t, core, self.at.dp], self.lsem.at[t]
        )

    def share(self, t):
        core = self.at.core
        return remote(
            self.pack.at[1 - core, t],
            self.w.at[3 * core + t, 1 - core, self.at.dp],
            self.ssem.at[t, 5 * self.at.chain + 1],
            self.rsem.at[t, 5 * self.at.chain + 1],
            self.at.other,
        )

    def shared(self, t):
        core = self.at.core
        block = self.w.at[3 * (1 - core) + t, core, self.at.dp]
        return remote(
            self.pack.at[1 - core, t],
            block,
            self.ssem.at[t, 5 * self.at.chain + 1],
            self.rsem.at[t, 5 * self.at.chain + 1],
            self.at.other,
        )

    def split(self):
        for t in range(3):
            self.local(t).start()
            self.share(t).start()

    def block(self, p, zz, yy):
        return self.w.at[p, self.at.core, zz * 2 + yy]

    def copy(self, src, dst, p, kind, device):
        return remote(src, dst, self.ssem.at[p, kind], self.rsem.at[p, kind], device)

    def up(self, p, k):
        b = self.block(p, self.at.z - (k - 1), self.at.y)
        return self.copy(b, b, p, k - 1, self.at.above)

    def up_in(self, p, k):
        b = self.block(p, self.at.z - k, self.at.y)
        return self.copy(b, b, p, k - 1, self.at.below)

    def down(self, p, k):
        b = self.block(p, self.at.z + (k - 1), self.at.y)
        return self.copy(b, b, p, self.at.chain + k - 1, self.at.below)

    def down_in(self, p, k):
        b = self.block(p, self.at.z + k, self.at.y)
        return self.copy(b, b, p, self.at.chain + k - 1, self.at.above)

    def cross(self, p, zz):
        b = self.block(p, zz, self.at.y)
        return self.copy(b, b, p, 2 * self.at.chain + zz, self.at.across)

    def cross_in(self, p, zz):
        b = self.block(p, zz, 1 - self.at.y)
        return self.copy(b, b, p, 2 * self.at.chain + zz, self.at.across)

    def mate_out(self, p):
        b = self.block(p, self.at.z, 1 - self.at.y)
        return self.copy(b, b, p, 3 * self.at.chain, self.at.mate)

    def mate_in(self, p):
        b = self.block(p, self.at.mate_z, 1 - self.at.y)
        return self.copy(b, b, p, 3 * self.at.chain, self.at.mate)

    def over(self, p, zz, yy):
        b = self.block(p, zz, yy)
        own = jnp.where(yy == self.at.y, 0, 1)
        return self.copy(b, b, p, 3 * self.at.chain + 1 + 2 * zz + own, self.at.other)

    def over_in(self, p, zz, own):
        yy = self.at.y if own == 0 else 1 - self.at.y
        b = self.w.at[p, 1 - self.at.core, zz * 2 + yy]
        return self.copy(b, b, p, 3 * self.at.chain + 1 + 2 * zz + own, self.at.other)

    def other_in(self, p):
        for zz in range(self.at.chain):
            for own in range(2):
                self.over_in(p, zz, own).wait_recv()

    def start(self, p):
        s, t = divmod(p, 3)

        @pl.when(self.at.core == s)
        def _():
            self.local(t).wait()

        @pl.when(self.at.core != s)
        def _():
            self.shared(t).wait_recv()

        self.cross(p, self.at.z).start()

        @pl.when(self.at.z < self.at.chain - 1)
        def _():
            self.up(p, 1).start()

        @pl.when(self.at.z > 0)
        def _():
            self.down(p, 1).start()

        self.over(p, self.at.z, self.at.y).start()

    def step(self, p, k):
        z, chain = self.at.z, self.at.chain
        odd = p in COPY_BY_MATE

        @pl.when(z >= k)
        def _():
            self.up_in(p, k).wait_recv()

            @pl.when(z < chain - 1)
            def _():
                self.up(p, k + 1).start()

            if k == 1 and odd:

                @pl.when(z % 2 == 0)
                def _():
                    self.cross(p, z - k).start()

            else:
                self.cross(p, z - k).start()
            self.over(p, z - k, self.at.y).start()

        @pl.when(z + k < chain)
        def _():
            self.down_in(p, k).wait_recv()

            @pl.when(z > 0)
            def _():
                self.down(p, k + 1).start()

            if k == 1 and odd:

                @pl.when(z % 2 == 1)
                def _():
                    self.cross(p, z + k).start()

            else:
                self.cross(p, z + k).start()
            self.over(p, z + k, self.at.y).start()

        if k == 1 and odd:
            self.cross_in(p, z).wait_recv()
            self.mate_out(p).start()
            self.over(p, z, 1 - self.at.y).start()

    def finish(self, p):
        z = self.at.z
        for j in range(self.at.chain):
            if p in COPY_BY_MATE:

                @pl.when((j != z) & (j != self.at.mate_z))
                def _():
                    self.cross_in(p, j).wait_recv()
                    self.over(p, j, 1 - self.at.y).start()

            else:
                self.cross_in(p, j).wait_recv()
                self.over(p, j, 1 - self.at.y).start()
        if p in COPY_BY_MATE:
            self.mate_in(p).wait_recv()
            self.over(p, self.at.mate_z, 1 - self.at.y).start()

    def drain(self, p):
        z, chain = self.at.z, self.at.chain
        for j in range(chain):
            if p in COPY_BY_MATE:

                @pl.when(j != self.at.mate_z)
                def _():
                    self.cross(p, j).wait_send()

            else:
                self.cross(p, j).wait_send()
        if p in COPY_BY_MATE:
            self.mate_out(p).wait_send()
        for k in range(1, chain):

            @pl.when((z < chain - 1) & (z >= k - 1))
            def _():
                self.up(p, k).wait_send()

            @pl.when((z > 0) & (z + k - 1 < chain))
            def _():
                self.down(p, k).wait_send()

        for j in range(chain):
            for yy in range(2):
                self.over(p, j, yy).wait_send()
        if p < 3:
            self.share(p).wait_send()


TILE = 32


def silu(v):
    return v / (1.0 + jnp.exp(-v))


def thirds(v):
    a = v.astype(BF)
    rest = v - a.astype(F32)
    b = rest.astype(BF)
    return a, b, (rest - b.astype(F32)).astype(BF)


def by_rows(rows, body, carry, tile=TILE):
    def step(i, c):
        return body(pl.ds(pl.multiple_of(i * tile, tile), tile), c)

    return lax.fori_loop(0, rows // tile, step, carry)


def column_sum(value):
    rows, width = value.shape
    return jnp.sum(value.reshape(rows // 8, 8, width), axis=0)


def layer_norm(v):
    cen = v - jnp.mean(v, axis=-1, keepdims=True)
    inv = lax.rsqrt(jnp.mean(cen * cen, axis=-1, keepdims=True) + EPSILON)
    return cen * inv, inv


def layer_norm_back(w, hat, inv):
    return inv * (
        w - jnp.mean(w, axis=-1, keepdims=True) - hat * jnp.mean(w * hat, axis=-1, keepdims=True)
    )


def spread_masks(kept, place, pos, drop, seg=None):
    length = kept.shape[1]
    u = lax.broadcasted_iota(jnp.int32, (length, length), 0)
    v = lax.broadcasted_iota(jnp.int32, (length, length), 1)
    uf, vf = u.astype(F32), v.astype(F32)
    column = jnp.sum(jnp.where(u == v, kept, 0.0), axis=1, keepdims=True)
    source = jnp.sum(jnp.where(v <= u, kept, 0.0), axis=1, keepdims=True) - 1.0
    source_row = jnp.sum(jnp.where(u <= v, column, 0.0), axis=0, keepdims=True) - 1.0
    count = jnp.sum(kept, axis=1, keepdims=True)
    place[...] = (jnp.where(source == vf, 1.0, 0.0) * column).astype(BF)
    pad = jnp.where(uf >= count, 1.0, 0.0)
    first = jnp.where(v == 0, pad, 0.0)
    pos[...] = (jnp.where(source_row == uf, 1.0, 0.0) * kept + first).astype(BF)
    drop[...] = jnp.broadcast_to(1.0 - column, drop.shape)
    if seg is not None:
        seg[...] = jnp.where(pad == jnp.where(vf >= count, 1.0, 0.0), 0.0, NEGATIVE)


def diagonal(length, mirrored=False):
    u = lax.broadcasted_iota(jnp.int32, (length, length), 0)
    v = lax.broadcasted_iota(jnp.int32, (length, length), 1)
    return jnp.where(u + v == length - 1 if mirrored else u == v, 1.0, 0.0).astype(BF)


def head_mask(i, head_dim):
    lane = lax.broadcasted_iota(jnp.int32, (1, HEAD_LANES), 1)
    return ((lane >= i * head_dim) & (lane < (i + 1) * head_dim)).astype(F32)


def forward_kernel(cfg, *refs):
    fused, chain, heads, head_dim = cfg
    refs = list(refs)
    pack = refs.pop(0)
    i_tok, cond, i_wada, b_ada, kept, b_qv, b_out, b_down, b_up, rel, mtok = refs[:11]
    refs = refs[11:]
    w = refs.pop(0) if fused else pack
    (
        s_hat1, s_inv, s_n1, s_qkv, s_p, s_o, s_branch, s_hat2, s_n2, s_hid, s_slope, s_y,
        s_full, s_xm, o_mod, o_cl, o_small, s_e,
    ) = refs[:18]
    refs = refs[18:]
    (
        wa, wu, wd, res, hat, inv, n, r, qkv, prob, o, branch, hid, slope, y_keep,
        xs, xr, toep, small, cl, part, got, pair, mod, tok, wada, pos, seg, place, drop,
        eye, small_own, wide, bada,
        gs, gr, gl, ssem, rsem, lsem, ms, mr,
    ) = refs
    at = Place(chain)
    rows, width = res.shape
    lw = heads * head_dim
    shard = width // at.count
    half_heads = heads // 2
    scale = 1.0 / math.sqrt(head_dim)
    sends, recvs, locals_ = Numbered(ssem), Numbered(rsem), Numbered(lsem)
    at.greet()
    gather = Gather(at, pack, w, gs, gr, gl) if fused else None
    links = Links(at, ms, mr)
    waiting = {}

    def keep(name, src, dst):
        copy = pltpu.make_async_copy(src, dst, locals_.next())
        copy.start()
        waiting.setdefault(name, []).append(copy.wait)

    def give(name, src, dst):
        copy = remote(src, dst, sends.next(), recvs.next(), at.other)
        copy.start()
        waiting.setdefault(name, []).append(copy.wait_send)
        waiting.setdefault("end", []).append(copy.wait_recv)

    def settle(name):
        for wait in waiting.pop(name, []):
            wait()

    def pump(*what):
        if not fused:
            return
        for name, p, *k in what:
            if p < gather.pieces:
                getattr(gather, name)(p, *k)

    def load(p, slot):
        if fused:
            gather.other_in(p)
        keep("load%d" % p, w.at[p], slot)

    def send_cond():
        cl[pl.ds(at.dp, 1)] = cond[pl.ds(at.dp, 1)]
        return links.to_all(lambda peer: cond.at[peer], cl.at[at.dp])

    def modulation_terms(copies):
        for copy in copies:
            copy.wait_recv()
        part[...] = jnp.zeros_like(part)
        parts = thirds(silu(flat(cl[...])[:, :shard]))
        for k in range(6):
            cols = wada[:, k * ADA_LANES : (k + 1) * ADA_LANES]
            value = nn(parts[0], cols) + (nn(parts[1], cols) + nn(parts[2], cols))
            value = value.reshape(at.count, 8, ADA_LANES)
            for m in range(2):
                part[:, m * 8 + k, :] = value[:, m, :]
        got[pl.ds(at.dp, 1)] = part[pl.ds(at.dp, 1)]
        return links.to_all(lambda peer: part.at[peer], got.at[at.dp])

    def modulation_sum(copies):
        for copy in copies:
            copy.wait_recv()
        value = got[0]
        for j in range(1, at.count):
            value = value + got[j]
        pair[at.core, at.head] = value + jnp.concatenate([bada[...], bada[...]], axis=0)
        return links.around(pair)

    def modulation(copies):
        for copy in copies:
            copy.wait_recv()
        lane = lax.broadcasted_iota(jnp.int32, (8, ADA_LANES), 1)
        blank = jnp.zeros((8, width - ADA_LANES), F32)
        mine_ = pl.ds(pl.multiple_of(at.core * 8, 8), 8)
        for s in range(2):
            a, b = [
                jnp.concatenate([jnp.where(lane < lw, pair[s, h, mine_, :], 0.0), blank], axis=1)
                for h in range(2)
            ]
            mod[s] = a + pltpu.roll(b, lw, 1)
        keep("mod", mod, o_mod)
        keep("cl", cl, o_cl)

    def share_small():
        wide[...] = jnp.zeros_like(wide)
        wide[0:2, :lw] = b_qv[0].astype(F32)
        small_own[...] = jnp.zeros_like(small_own)
        value = wide[...]
        for half in range(2):
            for k in range(2):
                row = half * 4 + 2 * k
                small_own[row : row + 1, :HEAD_LANES] = value[k : k + 1, :HEAD_LANES]
            value = pltpu.roll(value, ADA_LANES - lw // 2, 1)
        small_own[8:9, :] = b_out[...].astype(F32)
        small_own[9:10, :] = b_down[...].astype(F32)
        small_own[10:11, :] = b_up[:, :width].astype(F32)
        small_own[11:12, :] = b_up[:, width:].astype(F32)
        small_own[16 : 16 + heads, : 2 * rows - 1] = rel[0].astype(F32)
        bada[...] = jnp.zeros_like(bada)
        bada[0:6, :lw] = b_ada[0].astype(F32)
        small[pl.ds(at.core, 1)] = small_own[...][None]
        return links.copy(small_own, small.at[at.core], at.other)

    def bqv_row(s, half, kind):
        return small[s, half * 4 + kind : half * 4 + kind + 1, :HEAD_LANES]

    def bup_row(s, half, cols):
        return small[s, 10 + half : 11 + half, cols]

    def send_across(i):
        copy = remote(xs.at[i], xr.at[i], sends.next(), recvs.next(), at.beside)
        copy.start()
        waiting.setdefault("end", []).append(copy.wait_send)
        return copy

    def total(i, ds):
        return xs[i, ds, :].astype(F32) + xr[i, ds, :].astype(F32)

    def norm_one(s):
        settle("hat1")
        settle("n1")
        settle("inv")

        def body(ds, c):
            v, iv = layer_norm(res[ds, :])
            hat[0, ds, :] = v.astype(BF)
            inv[0, ds, :] = jnp.broadcast_to(iv, (TILE, 128))
            n[0, ds, :] = (v * (1.0 + mod[s, 1:2, :]) + mod[s, 0:1, :]).astype(BF)
            return c

        by_rows(rows, body, 0)
        keep("hat1", hat.at[0], s_hat1.at[s])
        keep("n1", n.at[0], s_n1.at[s, 0])
        give("n1", n.at[0], s_n1.at[s, 1])

    def project(s):
        settle("qkv")
        for half in range(2):
            for j in range(3):
                cols = slice(j * 384, (j + 1) * 384)
                r[:, cols] = nn(n[0], flat(wa[half, :, :, cols]))

            def body(ds, c):
                v = r[ds, :]
                for kind, shift in ((0, 864), (1, 576), (2, 288)):
                    piece = pltpu.roll(v, shift, 1)[:, :HEAD_LANES]
                    qkv[kind, half, ds, :] = (piece + bqv_row(s, half, kind)).astype(BF)
                return c

            by_rows(rows, body, 0)
        keep("qkv", qkv, s_qkv.at[s])

    def attend(s, half):
        if half == 0:
            settle("p")
            settle("o")
        o[half] = jnp.zeros_like(o[half])

        def one(i, c):
            index = half * half_heads + i
            mask = head_mask(i, head_dim).astype(BF)
            line = small[s, pl.ds(16 + index, 1), : 2 * rows]
            skew = pltpu.roll(
                jnp.broadcast_to(line, (rows, 2 * rows)), rows + 1, 1, stride=1, stride_axis=0
            )
            toep[...] = skew[:, :rows].astype(BF)
            if s == 0:
                left = nt(pos[...], toep[...]).astype(BF)
                bias = nt(left, pos[...]) + seg[...]
            else:
                bias = nt(eye[...], toep[...])
            z = nt(qkv[0, half] * mask, qkv[1, half]) * scale + bias
            e = jnp.exp(z - jnp.max(z, axis=-1, keepdims=True))
            p = (e / jnp.sum(e, axis=-1, keepdims=True)).astype(BF)
            prob[index] = p
            o[half] = o[half] + nn(p, qkv[2, half]).astype(BF) * mask
            return c

        lax.fori_loop(0, half_heads, one, 0)
        if half == 1:
            keep("p", prob, s_p.at[s])
            keep("o", o.at[at.core], s_o.at[s, 0])
            give("o", o.at[1 - at.core], s_o.at[s, 1])

    def project_out(i):
        xs[i] = (
            nt(o[0], flat(wa[0, :, :, :HEAD_LANES])) + nt(o[1], flat(wa[1, :, :, :HEAD_LANES]))
        ).astype(BF)
        return send_across(i)

    def norm_two(s, i, copy):
        copy.wait_recv()
        settle("branch")
        settle("hat2")
        settle("n2")

        def body(ds, c):
            b = total(i, ds) + small[s, 8:9, :]
            branch[ds, :] = b.astype(BF)
            xm = res[ds, :] + mod[s, 2:3, :] * b
            res[ds, :] = xm
            v, iv = layer_norm(xm)
            hat[1, ds, :] = v.astype(BF)
            inv[1, ds, :] = jnp.broadcast_to(iv, (TILE, 128))
            n[1, ds, :] = (v * (1.0 + mod[s, 4:5, :]) + mod[s, 3:4, :]).astype(BF)
            return c

        by_rows(rows, body, 0)
        keep("branch", branch, s_branch.at[s])
        keep("inv", inv, s_inv.at[s])
        keep("hat2", hat.at[1], s_hat2.at[s])
        if s == 1:
            keep("out", res, s_xm)
        keep("n2", n.at[1], s_n2.at[s, 0])
        give("n2", n.at[1], s_n2.at[s, 1])

    def hidden(s, half):
        if half == 0:
            settle("hid")
            settle("slope")
        for j in range(3):
            cols = slice(j * 384, (j + 1) * 384)
            r[:, cols] = nn(n[1], flat(wu[half, :, :, cols])) + bup_row(s, half, cols)

        def body(ds, c):
            value, sl = gelu_both(r[ds, :])
            hid[half, ds, :] = value.astype(BF)
            slope[half, ds, :] = sl.astype(BF)
            return c

        by_rows(rows, body, 0)
        if half == 1:
            keep("slope", slope, s_slope.at[s])
            keep("hid", hid.at[at.core], s_hid.at[s, 0])
            give("hid", hid.at[1 - at.core], s_hid.at[s, 1])
            if s == 1:
                keep("hid", hid, s_full)

    def project_down(i):
        xs[i] = (nt(hid[0], flat(wd[0])) + nt(hid[1], flat(wd[1]))).astype(BF)
        return send_across(i)

    def end_block(s, i, copy):
        copy.wait_recv()
        settle("y")
        settle("out")

        def body(ds, c):
            v = total(i, ds) + small[s, 9:10, :]
            y_keep[ds, :] = v.astype(BF)
            res[ds, :] = res[ds, :] + mod[s, 5:6, :] * v
            return c

        by_rows(rows, body, 0)
        keep("y", y_keep, s_y)
        keep("out", res, s_e)

    def spread():
        r[...] = nn(place[...], res[...].astype(BF))
        settle("out")

        def body(ds, c):
            res[ds, :] = r[ds, :] + drop[ds, 0:1] * mtok[...].astype(F32)
            return c

        by_rows(rows, body, 0)

    copies = send_cond()
    small_copy = share_small()
    if fused:
        gather.split()
        gather.start(0)
        gather.start(1)
    keep("tok", i_tok.at[at.core], tok)
    keep("wada", i_wada, wada)
    spread_masks(kept[at.core].astype(F32), place, pos, drop, seg)
    eye[...] = diagonal(rows)
    settle("tok")

    def start_residual(ds, c):
        res[ds, :] = tok[ds, :].astype(F32)
        return c

    by_rows(rows, start_residual, 0)
    pump(("step", 0, 1))
    settle("wada")
    copies = modulation_terms(copies)
    pump(("step", 0, 2), ("start", 2), ("step", 0, 3))
    copies = modulation_sum(copies)
    small_copy.wait_recv()
    keep("small", small, o_small)
    pump(("step", 1, 1))
    modulation(copies)
    norm_one(0)
    pump(("step", 1, 2), ("start", 3), ("finish", 0), ("step", 1, 3))
    load(0, wa)
    settle("load0")
    project(0)
    pump(("step", 2, 1))
    attend(0, 0)
    pump(("step", 2, 2), ("start", 4), ("finish", 1))
    attend(0, 1)
    copy = project_out(0)
    pump(("step", 2, 3))
    load(1, wu)
    pump(("step", 3, 1))
    norm_two(0, 0, copy)
    settle("load1")
    pump(("step", 3, 2), ("start", 5), ("finish", 2))
    hidden(0, 0)
    hidden(0, 1)
    pump(("step", 3, 3))
    load(2, wd)
    settle("load2")
    copy = project_down(1)
    pump(("step", 4, 1), ("step", 4, 2), ("finish", 3))
    end_block(0, 1, copy)
    spread()
    norm_one(1)
    pump(("step", 4, 3))
    load(3, wa)
    settle("load3")
    project(1)
    pump(("step", 5, 1))
    attend(1, 0)
    pump(("step", 5, 2), ("finish", 4))
    attend(1, 1)
    copy = project_out(2)
    load(4, wu)
    pump(("step", 5, 3), ("finish", 5))
    norm_two(1, 2, copy)
    settle("load4")
    hidden(1, 0)
    hidden(1, 1)
    if fused:
        gather.other_in(5)
        for p in range(gather.pieces):
            gather.drain(p)
    for wait in links.waiting:
        wait()
    for name in list(waiting):
        settle(name)


def forward_call(cfg, own, small, dp_count):
    fused, chain, heads, head_dim = cfg
    _, rows, width = small[0].shape
    pieces = 6
    shard = own.shape[-2]
    groups = width // shard
    cond_lanes = small[1].shape[2]
    bf, f = lambda *s: jax.ShapeDtypeStruct(s, BF), lambda *s: jax.ShapeDtypeStruct(s, F32)
    out_shape = [
        bf(2, rows, width),
        f(2, 2, rows, 128),
        bf(2, 2, rows, width),
        bf(2, 3, 2, rows, HEAD_LANES),
        bf(2, heads, rows, rows),
        bf(2, 2, rows, HEAD_LANES),
        bf(2, rows, width),
        bf(2, rows, width),
        bf(2, 2, rows, width),
        bf(2, 2, rows, width),
        bf(2, 2, rows, width),
        bf(rows, width),
        bf(2, rows, width),
        f(rows, width),
        f(2, 8, width),
        f(dp_count, 8, cond_lanes),
        f(2, 24, width),
        f(rows, width),
    ]
    if fused:
        out_shape = [bf(pieces, 2, groups, shard, width)] + out_shape
    kinds = 5 * chain + 2
    many = 2 * (dp_count - 1) + 8
    slot = pltpu.VMEM((2, groups, shard, width), BF)
    scratch = [
        slot,
        slot,
        slot,
        pltpu.VMEM((rows, width), F32),
        pltpu.VMEM((2, rows, width), BF),
        pltpu.VMEM((2, rows, 128), F32),
        pltpu.VMEM((2, rows, width), BF),
        pltpu.VMEM((rows, width), F32),
        pltpu.VMEM((3, 2, rows, HEAD_LANES), BF),
        pltpu.VMEM((heads, rows, rows), BF),
        pltpu.VMEM((2, rows, HEAD_LANES), BF),
        pltpu.VMEM((rows, width), BF),
        pltpu.VMEM((2, rows, width), BF),
        pltpu.VMEM((2, rows, width), BF),
        pltpu.VMEM((rows, width), BF),
        pltpu.VMEM((4, rows, width), BF),
        pltpu.VMEM((4, rows, width), BF),
        pltpu.VMEM((rows, rows), BF),
        pltpu.VMEM((2, 24, width), F32),
        pltpu.VMEM((dp_count, 8, cond_lanes), F32),
        pltpu.VMEM((dp_count, 16, ADA_LANES), F32),
        pltpu.VMEM((dp_count, 16, ADA_LANES), F32),
        pltpu.VMEM((2, 2, 16, ADA_LANES), F32),
        pltpu.VMEM((2, 8, width), F32),
        pltpu.VMEM((rows, width), BF),
        pltpu.VMEM(small[2].shape, BF),
        pltpu.VMEM((rows, rows), BF),
        pltpu.VMEM((rows, rows), F32),
        pltpu.VMEM((rows, rows), BF),
        pltpu.VMEM((rows, 128), F32),
        pltpu.VMEM((rows, rows), BF),
        pltpu.VMEM((24, width), F32),
        pltpu.VMEM((8, ADA_LANES), F32),
        pltpu.VMEM((8, ADA_LANES), F32),
        pltpu.SemaphoreType.DMA((pieces, kinds)),
        pltpu.SemaphoreType.DMA((pieces, kinds)),
        pltpu.SemaphoreType.DMA((3,)),
        pltpu.SemaphoreType.DMA((16,)),
        pltpu.SemaphoreType.DMA((16,)),
        pltpu.SemaphoreType.DMA((48,)),
        pltpu.SemaphoreType.DMA((many,)),
        pltpu.SemaphoreType.DMA((many,)),
    ]

    def body(*refs):
        forward_kernel(cfg, *refs)

    vm = pl.BlockSpec(memory_space=pltpu.VMEM)
    hbm = pl.BlockSpec(memory_space=pl.ANY)
    result = pl.pallas_call(
        body,
        out_shape=out_shape,
        in_specs=[hbm] + [hbm, vm, hbm] + [vm] * 8,
        out_specs=[hbm] * len(out_shape),
        scratch_shapes=scratch,
        compiler_params=pltpu.CompilerParams(
            collective_id=0, has_side_effects=True, vmem_limit_bytes=VMEM_BYTES
        ),
        name="forward_blocks",
    )(own, *small)
    return result if fused else [own] + list(result)


class Scatter:
    def __init__(self, at, order, g, yr, zr, mr, red, out, ssem, rsem, osem, isem, lsem, credit):
        self.at, self.order = at, order
        self.g, self.yr, self.zr, self.mr, self.red, self.out = g, yr, zr, mr, red, out
        self.ssem, self.rsem, self.osem, self.isem, self.lsem = ssem, rsem, osem, isem, lsem
        self.credit = credit
        chain = at.chain
        need = lambda z, t: chain if t == z else (chain - t + z if t > z else chain - z + t)
        self.table = [sorted(range(chain), key=lambda t: (need(z, t), t)) for z in range(chain)]

    def slots(self, r):
        return r % self.g.shape[0], r % self.yr.shape[0]

    def target(self, i):
        return sum(jnp.where(self.at.z == z, self.table[z][i], 0) for z in range(self.at.chain))

    def own(self, r, t):
        return self.g.at[self.slots(r)[0], t * 2 + self.at.y]

    def theirs(self, r, t):
        return self.g.at[self.slots(r)[0], t * 2 + 1 - self.at.y]

    def copy(self, src, dst, r, kind, device):
        return remote(src, dst, self.ssem.at[r, kind], self.rsem.at[r, kind], device)

    def cross(self, r, t):
        return self.copy(
            self.theirs(r, t), self.yr.at[self.slots(r)[1], t], r, t, self.at.across
        )

    def up(self, r, t):
        return self.copy(
            self.own(r, t), self.zr.at[self.slots(r)[1], t], r, self.at.chain + t, self.at.above
        )

    def down(self, r, t, last=None):
        z = self.at.z - 1 if last is None else last
        place = jnp.where(t == z, self.at.chain, t)
        return self.copy(
            self.own(r, t), self.zr.at[self.slots(r)[1], place], r, 2 * self.at.chain + t, self.at.below
        )

    def to_mate(self, r):
        return self.copy(
            self.theirs(r, self.at.mate_z), self.mr.at[self.slots(r)[1]], r, 3 * self.at.chain, self.at.mate
        )

    def add(self, block, got):
        block[...] = (block[...].astype(F32) + got[...].astype(F32)).astype(BF)

    def begin(self, r):
        at, chain = self.at, self.at.chain
        if r >= self.yr.shape[0]:
            pl.semaphore_wait(self.credit.at[0], 1)

            @pl.when(at.z < chain - 1)
            def _():
                pl.semaphore_wait(self.credit.at[1], 1)

            @pl.when(at.z > 0)
            def _():
                pl.semaphore_wait(self.credit.at[2], 1)

        if r in SUM_BY_MATE:
            self.to_mate(r).start()
        for i in range(chain - 1):
            t = self.target(i)
            if r in SUM_BY_MATE:

                @pl.when(t != at.mate_z)
                def _():
                    self.cross(r, t).start()

            else:
                self.cross(r, t).start()
        if r not in SUM_BY_MATE:
            self.cross(r, at.z).start()

    def mated(self, r):
        if r in SUM_BY_MATE:
            self.to_mate(r).wait_recv()
            self.add(self.theirs(r, self.at.z), self.mr.at[self.slots(r)[1]])
            self.cross(r, self.at.z).start()

    def arrive(self, r, i):
        t = self.target(i)

        def take():
            self.cross(r, t).wait_recv()
            self.add(self.own(r, t), self.yr.at[self.slots(r)[1], t])

        if r in SUM_BY_MATE:
            pl.when(t != self.at.mate_z)(take)
        else:
            take()

    def step(self, r, k):
        z, chain = self.at.z, self.at.chain

        @pl.when((z <= k - 1) & (z < chain - 1))
        def _():
            t = chain - k + z
            if k > 1:

                @pl.when(z > 0)
                def _():
                    self.up(r, t).wait_recv()
                    self.add(self.own(r, t), self.zr.at[self.slots(r)[1], t])

            self.up(r, t).start()

        @pl.when((chain - 1 - z <= k - 1) & (z > 0))
        def _():
            t = k - chain + z
            if k > 1:

                @pl.when(z < chain - 1)
                def _():
                    self.down(r, t, last=z).wait_recv()
                    self.add(self.own(r, t), self.zr.at[self.slots(r)[1], t])

            self.down(r, t).start()

    def finish(self, r):
        at, chain = self.at, self.at.chain
        z = at.z
        slot = self.slots(r)[1]
        held = self.red.shape[0]
        if r >= held:
            self.hand_over_done(r - held)
        red = self.red.at[r % held]
        red[...] = self.own(r, z)[...].astype(F32)

        @pl.when(z > 0)
        def _():
            self.up(r, z).wait_recv()
            red[...] = red[...] + self.zr[slot, z].astype(F32)

        @pl.when(z < chain - 1)
        def _():
            self.down(r, z, last=z).wait_recv()
            red[...] = red[...] + self.zr[slot, chain].astype(F32)

        if r + self.yr.shape[0] < len(self.order):
            pl.semaphore_signal(self.credit.at[0], inc=1, device_id=at.across, device_id_type=MESH)

            @pl.when(z > 0)
            def _():
                pl.semaphore_signal(self.credit.at[1], inc=1, device_id=at.below, device_id_type=MESH)

            @pl.when(z < chain - 1)
            def _():
                pl.semaphore_signal(self.credit.at[2], inc=1, device_id=at.above, device_id_type=MESH)

        s, t = self.order[r]

        @pl.when(at.core == s)
        def _():
            self.keep(r).start()

        @pl.when(at.core != s)
        def _():
            self.hand_over(r).start()

    def keep(self, r):
        return pltpu.make_async_copy(
            self.red.at[r % self.red.shape[0]], self.out.at[self.order[r][1], self.at.core], self.lsem.at[r]
        )

    def hand_over(self, r):
        return remote(
            self.red.at[r % self.red.shape[0]],
            self.out.at[self.order[r][1], self.at.core],
            self.osem.at[r],
            self.isem.at[r],
            self.at.other,
        )

    def hand_over_done(self, r):
        s, t = self.order[r]

        @pl.when(self.at.core == s)
        def _():
            self.keep(r).wait()

        @pl.when(self.at.core != s)
        def _():
            self.hand_over(r).wait_send()

    def drain(self, r):
        z, chain = self.at.z, self.at.chain
        if r in SUM_BY_MATE:
            self.to_mate(r).wait_send()
        for t in range(chain):
            if r in SUM_BY_MATE:

                @pl.when(t != self.at.mate_z)
                def _():
                    self.cross(r, t).wait_send()

            else:
                self.cross(r, t).wait_send()

            @pl.when(t > z)
            def _():
                self.up(r, t).wait_send()

            @pl.when(t < z)
            def _():
                self.down(r, t).wait_send()

    def end(self):
        for r in range(len(self.order)):
            if r + self.red.shape[0] >= len(self.order):
                self.hand_over_done(r)
            s, t = self.order[r]

            @pl.when(self.at.core == s)
            def _():
                remote(
                    self.red.at[0],
                    self.out.at[t, 1 - self.at.core],
                    self.osem.at[r],
                    self.isem.at[r],
                    self.at.other,
                ).wait_recv()


ORDER = ((1, 2), (1, 1), (1, 0), (0, 2), (0, 1), (0, 0))


def backward_kernel(cfg, *refs):
    fused, chain, heads, head_dim = cfg
    refs = list(refs)
    w = refs.pop(0)
    (
        i_hat1, i_inv, i_n1, i_qkv, i_p, i_o, i_branch, i_hat2, i_n2, i_hid, i_slope, i_y, i_full, i_xm,
        i_e,
    ) = refs[:15]
    refs = refs[15:]
    i_dout, mod, i_small, i_cl, i_wada, kept = refs[:6]
    refs = refs[6:]
    red_out, o_dx, o_out, o_sums, o_dm, o_dc = refs[:6]
    refs = refs[6:]
    (
        wslot, hat1, inv, qkv, prob, o, branch, hat2, n2, hid, slope,
        d, r, dy, dpre, dattn, dqkv, do, xs, xr, g, yr, zr, mr, red,
        stats, got, sums, msg, dc, dg, small, cl, wada, flips, pos, place, drop, eye, dout, gs, gr, go, gi, gl, credit, ssem, rsem, lsem, ms, mrs,
    ) = refs
    at = Place(chain)
    rows, width = d.shape
    lw = heads * head_dim
    shard = width // at.count
    half_heads = heads // 2
    scale = 1.0 / math.sqrt(head_dim)
    sends, recvs, locals_ = Numbered(ssem), Numbered(rsem), Numbered(lsem)
    at.greet()
    links = Links(at, ms, mrs)
    stats[...] = jnp.zeros_like(stats)
    dc[...] = jnp.zeros_like(dc)
    scatter = (
        Scatter(at, ORDER, g, yr, zr, mr, red, red_out, gs, gr, go, gi, gl, credit) if fused else None
    )
    slots = g.shape[0]
    waiting = {}

    def fetch(name, src, dst):
        copy = pltpu.make_async_copy(src, dst, locals_.next())
        copy.start()
        waiting.setdefault(name, []).append(copy.wait)

    def settle(name):
        for wait in waiting.pop(name, []):
            wait()

    def give(name, src, dst):
        copy = remote(src, dst, sends.next(), recvs.next(), at.other)
        copy.start()
        waiting.setdefault(name + " in", []).append(copy.wait_recv)
        waiting.setdefault(name + " out", []).append(copy.wait_send)

    def pump(*what):
        if not fused:
            return
        for name, r_, *k in what:
            if 0 <= r_ < len(ORDER):
                getattr(scatter, name)(r_, *k)

    def pump_rest(r_, start):
        for i in range(start, chain):
            pump(("arrive", r_, i))
            if i < chain - 1:
                pump(("step", r_, i + 1))
        pump(("finish", r_))

    def send_across(i):
        if i > 1:
            settle("x out %d" % (i - 2))
        copy = remote(xs.at[i % 2], xr.at[i % 2], sends.next(), recvs.next(), at.beside)
        copy.start()
        waiting.setdefault("x in %d" % i, []).append(copy.wait_recv)
        waiting.setdefault("x out %d" % i, []).append(copy.wait_send)

    def total(i, ds):
        return xs[i % 2, ds, :].astype(F32) + xr[i % 2, ds, :].astype(F32)

    def stat(s, row, value):
        stats[s, row : row + 1, :] = jnp.sum(value, axis=0, keepdims=True)

    zero8 = lambda: jnp.zeros((8, width), F32)
    spans = [slice(k * HEAD_LANES, (k + 1) * HEAD_LANES) for k in range(3)]
    spot = lambda half: jnp.where(half == at.core, 0, 2)

    def load(name, s):
        src, dst = {
            "slope": (i_slope, slope),
            "hid": (i_hid, hid),
            "n1": (i_n1, hid),
            "n2": (i_n2, n2),
            "hat2": (i_hat2, hat2),
            "inv": (i_inv, inv),
            "branch": (i_branch, branch),
            "p": (i_p, prob),
            "qkv": (i_qkv, qkv),
            "o": (i_o, o),
            "hat1": (i_hat1, hat1),
        }[name]
        fetch(name, src.at[s], dst)

    def weight(p, slot):
        fetch("w%d" % slot, w.at[p], wslot.at[slot])

    def product(r_, parts):
        slot = r_ % slots
        if r_ >= slots:
            if fused:
                scatter.drain(r_ - slots)
            else:
                settle("g%d" % (r_ - slots))
        for j in range(width // 384):
            cols = slice(j * 384, (j + 1) * 384)
            value = 0.0
            for lhs, rhs in parts(j):
                value = value + tn(lhs, rhs)
            g[slot, :, :, cols] = value.astype(BF).reshape(g.shape[1], g.shape[2], 384)
        if not fused:
            s, t = ORDER[r_]
            fetch("g%d" % r_, g.at[slot], red_out.at[s * 3 + t])

    def cols_of(ref, j):
        return flat(ref[0:2, :, j * 384 : (j + 1) * 384])

    down_slot, up_slot, att_slot = (1, 0), (0, 1), (1, 0)

    def base(s):
        return 0 if s == 1 else 3

    def exchange(s):
        return 0 if s == 1 else 2

    def back_gate(s):
        settle("dy out")
        if s == 0:
            settle("y")

        def one(ds, c):
            a, b = c
            dv = d[ds, :]
            v = (dv * mod[s, 5:6, :]).astype(BF)
            dy[0, ds, :] = v
            if s == 0:
                a = a + column_sum(dv * xs[2, ds, :].astype(F32))
            return (a, b + column_sum(v.astype(F32)))

        a, b = by_rows(rows, one, (zero8(), zero8()))
        if s == 0:
            stat(s, 5, a)
        stat(s, 8, b)
        give("dy", dy.at[0], dy.at[1])

    def back_hidden(s):
        slot = down_slot[s]
        settle("w%d" % slot)
        settle("slope")
        settle("dpre out")
        for half in range(2):
            for j in range(3):
                cols = slice(j * 384, (j + 1) * 384)
                v = (nn(dy[0], flat(wslot[slot, half, :, :, cols])) * slope[half, :, cols].astype(F32)).astype(BF)
                dpre[spot(half), :, cols] = v
                stats[s, 10 + half : 11 + half, cols] = jnp.sum(v.astype(F32), axis=0, keepdims=True)
        give("dpre", dpre.at[2], dpre.at[1])

    def down_product(s):
        settle("dy in")
        settle("hid")
        product(base(s), lambda j: [(flat(dy[...]), cols_of(hid, j))])
        load("n1", s)

    def back_up(s):
        slot = up_slot[s]
        xi = exchange(s)
        settle("w%d" % slot)
        if xi > 1:
            settle("x out %d" % (xi - 2))
        xs[xi % 2] = (
            nt(dpre[spot(0)], flat(wslot[slot, 0])) + nt(dpre[spot(1)], flat(wslot[slot, 1]))
        ).astype(BF)
        send_across(xi)

    def up_product(s):
        settle("dpre in")
        settle("n2")
        product(base(s) + 1, lambda j: [(flat(n2[...]), cols_of(dpre, j))])

    def back_norm_two(s):
        xi = exchange(s)
        settle("x in %d" % xi)
        settle("hat2")
        settle("inv")
        settle("branch")
        settle("dattn out")

        def two(ds, c):
            c0, c1, c2, c3 = c
            dn = total(xi, ds)
            hv = hat2[ds, :].astype(F32)
            dxm = d[ds, :] + layer_norm_back(dn * (1.0 + mod[s, 4:5, :]), hv, inv[1, ds, 0:1])
            d[ds, :] = dxm
            da = (dxm * mod[s, 2:3, :]).astype(BF)
            dattn[0, ds, :] = da
            return (
                c0 + column_sum(dn),
                c1 + column_sum(dn * hv),
                c2 + column_sum(dxm * branch[ds, :].astype(F32)),
                c3 + column_sum(da.astype(F32)),
            )

        c0, c1, c2, c3 = by_rows(rows, two, (zero8(),) * 4)
        stat(s, 3, c0)
        stat(s, 4, c1)
        stat(s, 2, c2)
        stat(s, 9, c3)
        give("dattn", dattn.at[0], dattn.at[1])

    def back_heads(s, half):
        slot = att_slot[s]
        if half == 0:
            settle("w%d" % slot)
            settle("p")
            settle("qkv")
            settle("dqkv out")
        if True:
            do[half] = nn(dattn[0], flat(wslot[slot, half, :, :, :HEAD_LANES])).astype(BF)
            r[...] = jnp.zeros_like(r)

            def head(i, c):
                index = half * half_heads + i
                mask = head_mask(i, head_dim)
                low_mask = mask.astype(BF)
                p = prob[index]
                dom = do[half] * low_mask
                r[:, spans[2]] = r[:, spans[2]] + tn(p, dom)
                ds = nt(dom, qkv[2, half])
                pf = p.astype(F32)
                dz = (pf * (ds - jnp.sum(pf * ds, axis=-1, keepdims=True))).astype(BF)
                r[:, spans[0]] = r[:, spans[0]] + nn(dz, qkv[1, half]) * mask
                r[:, spans[1]] = r[:, spans[1]] + tn(dz, qkv[0, half]) * mask
                square = nn(dz, flips[s])
                high = square.astype(BF)
                if s == 0:
                    low = (square - high.astype(F32)).astype(BF)
                    square = tn(high, pos[...]) + tn(low, pos[...])
                else:
                    square = tn(high, eye[...])
                wide = jnp.concatenate([square, jnp.zeros_like(square)], axis=1)
                skew = pltpu.roll(wide, 0, 1, stride=1, stride_axis=0)
                stats[s, pl.ds(16 + index, 1), : 2 * rows] = jnp.sum(skew, axis=0, keepdims=True)
                return c

            lax.fori_loop(0, half_heads, head, 0)
            where = spot(half)

            def gather_rows(ds, c):
                blank = jnp.zeros((TILE, HEAD_LANES), F32)
                v = 0.0
                for kind, shift, factor in ((0, 288, scale), (1, 576, scale), (2, 864, 1.0)):
                    part = jnp.concatenate([r[ds, spans[kind]] * factor, blank, blank], axis=1)
                    v = v + pltpu.roll(part, shift, 1)
                v = v.astype(BF)
                dqkv[where, ds, :] = v
                return c + column_sum(v.astype(F32))

            stat(s, 12 + half, by_rows(rows, gather_rows, zero8()))
        if half == 1:
            give("dqkv", dqkv.at[2], dqkv.at[1])

    def back_qkv(s):
        slot = att_slot[s]
        xi = exchange(s) + 1
        if xi > 1:
            settle("x out %d" % (xi - 2))
        xs[xi % 2] = (
            nt(dqkv[spot(0)], flat(wslot[slot, 0])) + nt(dqkv[spot(1)], flat(wslot[slot, 1]))
        ).astype(BF)
        send_across(xi)

    def att_product(s):
        settle("dqkv in")
        settle("dattn in")
        settle("n1")
        settle("o")
        product(
            base(s) + 2,
            lambda j: [(flat(hid[...]), cols_of(dqkv, j))]
            + ([(flat(dattn[...]), flat(o[...]))] if j == 0 else []),
        )

    def back_norm_one(s):
        xs_free = exchange(s) + 1
        settle("x in %d" % xs_free)
        settle("hat1")

        def three(ds, c):
            c0, c1, c2 = c
            dn = total(xs_free, ds)
            hv = hat1[ds, :].astype(F32)
            dx = d[ds, :] + layer_norm_back(dn * (1.0 + mod[s, 1:2, :]), hv, inv[0, ds, 0:1])
            d[ds, :] = dx
            return (c0 + column_sum(dn), c1 + column_sum(dn * hv), c2 + column_sum(dx * drop[ds, 0:1]))

        c0, c1, c2 = by_rows(rows, three, (zero8(),) * 3)
        stat(s, 0, c0)
        stat(s, 1, c1)
        stat(s, 14, c2)
        to_section("dx", s, d, o_dx)

    def to_section(name, s, src, out):
        here = pltpu.make_async_copy(src, out.at[at.core], locals_.next())
        ss, rs = sends.next(), recvs.next()

        @pl.when(at.core == s)
        def _():
            here.start()

        @pl.when(at.core != s)
        def _():
            remote(src, out.at[at.core], ss, rs, at.other).start()

        def sent():
            @pl.when(at.core == s)
            def _():
                here.wait()

            @pl.when(at.core != s)
            def _():
                remote(src, out.at[at.core], ss, rs, at.other).wait_send()

        def arrived():
            @pl.when(at.core == s)
            def _():
                remote(src, out.at[1 - at.core], ss, rs, at.other).wait_recv()

        waiting.setdefault(name, []).append(sent)
        waiting.setdefault("end", []).append(arrived)

    def project_down():
        settle("w0")
        settle("full")
        xs[2] = (nt(dqkv[0], flat(wslot[0, 0])) + nt(dqkv[1], flat(wslot[0, 1]))).astype(BF)
        copy = remote(xs.at[2], xr.at[2], sends.next(), recvs.next(), at.beside)
        copy.start()
        waiting.setdefault("y in", []).append(copy.wait_recv)
        waiting.setdefault("y out", []).append(copy.wait_send)

    def end_forward():
        settle("y in")
        settle("y out")
        settle("xm")
        settle("small")

        def body(ds, c):
            v = xs[2, ds, :].astype(F32) + xr[2, ds, :].astype(F32) + small[1, 9:10, :]
            r[ds, :] = r[ds, :] + mod[1, 5:6, :] * v
            return c + column_sum(dout[ds, :].astype(F32) * v)

        stat(1, 5, by_rows(rows, body, zero8()))
        to_section("result", 1, r, o_out)

    def sums_begin():
        stats[0, 14:15, :] = stats[1, 14:15, :]
        return links.copy(stats.at[1 - at.core], got, at.other)

    def sums_share(copy):
        copy.wait_recv()
        msg[at.dp, :, :width] = (stats[at.core, 8:24, :] + got[8:24, :]).astype(BF)
        row = lax.broadcasted_iota(jnp.int32, (8, ADA_LANES), 0)
        lane = lax.broadcasted_iota(jnp.int32, (8, ADA_LANES), 1)

        def cut(value):
            value = jnp.where(
                at.head == 0, value[:, :ADA_LANES], pltpu.roll(value, width - lw, 1)[:, :ADA_LANES]
            )
            return jnp.where((row < 6) & (lane < lw), value, 0.0)

        own, other = cut(stats[at.core, 0:8, :]), cut(got[0:8, :])
        both_ = [jnp.where(at.core == 0, own, other), jnp.where(at.core == 0, other, own)]
        msg[at.dp, :, width:] = jnp.concatenate(both_, axis=0).astype(BF)
        return links.to_all(lambda peer: msg.at[at.dp], msg.at[at.dp])

    def cond_terms(copies):
        for copy in copies:
            copy.wait_recv()
        settle("wada")
        settle("cl")
        fetch("dm", msg.at[:, :, pl.ds(width, ADA_LANES)], o_dm)
        value = msg[0, :, :width].astype(F32)
        for j in range(1, at.count):
            value = value + msg[j, :, :width].astype(F32)
        sums[...] = value
        fetch("sums", sums, o_sums)
        lhs = flat(msg[:, :, width:])
        row = lax.rem(lax.broadcasted_iota(jnp.int32, (lhs.shape[0], 1), 0), 8)
        total_ = jnp.zeros((lhs.shape[0], shard), F32)
        for k in range(6):
            cols = wada[:, k * ADA_LANES : (k + 1) * ADA_LANES]
            total_ = total_ + jnp.where(row == k, nt(lhs, cols), 0.0)
        total_ = total_.reshape(at.count, 16, shard)
        for m in range(2):
            dc[at.core, at.head, m, :, :shard] = jnp.sum(total_[:, m * 8 : (m + 1) * 8, :], axis=1)
        return links.around(dc)

    def cond_share(copies):
        for copy in copies:
            copy.wait_recv()
        for m in range(2):
            value = (dc[0, 0, m] + dc[0, 1, m]) + (dc[1, 0, m] + dc[1, 1, m])
            v = cl[:, m, :]
            sig = 1.0 / (1.0 + jnp.exp(-v))
            dg[at.dp, m] = value * (sig * (1.0 + v * (1.0 - sig)))
        return links.to_all(lambda peer: dg.at[at.dp], dg.at[at.dp])

    def cond_end(copies):
        for copy in copies:
            copy.wait_recv()
        fetch("dg", dg, o_dc)

    fetch("dout", i_dout.at[at.core], dout)
    weight(5, 0)
    load("slope", 1)
    load("hid", 1)
    weight(4, 1)
    for name in ("n2", "hat2", "inv", "branch", "p", "qkv", "o", "hat1"):
        load(name, 1)
    for name, src, dst in (
        ("y", i_y, xs.at[2]),
        ("small", i_small, small),
        ("cl", i_cl, cl),
        ("wada", i_wada, wada),
    ):
        fetch(name, src, dst)

    to_section("e", 0, i_e, o_out)
    settle("dout")

    def start_rows(ds, c):
        d[ds, :] = dout[ds, :].astype(F32)
        return c

    by_rows(rows, start_rows, 0)

    def to_encoder():
        r[...] = tn(place[...], d[...].astype(BF))
        settle("dx")

        def move(ds, c):
            d[ds, :] = r[ds, :]
            return c

        by_rows(rows, move, 0)

    back_gate(1)
    back_hidden(1)
    weight(3, 0)
    load("slope", 0)
    down_product(1)
    pump(("begin", 0))
    back_up(1)
    weight(2, 1)
    up_product(1)
    load("n2", 0)
    pump(("begin", 1))
    pump(("arrive", 0, 0), ("step", 0, 1), ("arrive", 0, 1), ("step", 0, 2))
    spread_masks(kept[at.core].astype(F32), place, pos, drop)
    eye[...] = diagonal(rows)
    flips[1] = diagonal(rows, True)
    flips[0] = nn(pos[...], flips[1]).astype(BF)
    back_norm_two(1)
    load("hat2", 0)
    load("branch", 0)
    back_heads(1, 0)
    pump(("arrive", 0, 2), ("step", 0, 3))
    back_heads(1, 1)
    load("p", 0)
    load("qkv", 0)
    back_qkv(1)
    weight(1, 0)
    pump(("arrive", 0, 3))
    att_product(1)
    load("hid", 0)
    load("o", 0)
    pump(("begin", 2))
    pump(("mated", 1), ("arrive", 1, 0), ("step", 1, 1), ("finish", 0))
    back_norm_one(1)
    load("hat1", 0)
    load("inv", 0)
    to_encoder()
    back_gate(0)
    pump(("arrive", 1, 1), ("step", 1, 2))
    back_hidden(0)
    weight(0, 1)
    down_product(0)
    pump(("begin", 3))
    pump(("arrive", 1, 2), ("step", 1, 3))
    back_up(0)
    weight(5, 0)
    pump(("arrive", 1, 3), ("mated", 2), ("arrive", 2, 0), ("step", 2, 1), ("finish", 1))
    up_product(0)
    pump(("begin", 4))
    pump(("arrive", 2, 1), ("step", 2, 2))
    back_norm_two(0)
    back_heads(0, 0)
    pump(("arrive", 2, 2), ("step", 2, 3))
    back_heads(0, 1)
    back_qkv(0)
    fetch("xm", i_xm, r)
    pump(("arrive", 2, 3), ("mated", 3), ("arrive", 3, 0), ("step", 3, 1), ("finish", 2))
    att_product(0)
    fetch("full", i_full, dqkv.at[0:2])
    pump(("begin", 5))
    pump(("arrive", 3, 1), ("step", 3, 2))
    project_down()
    back_norm_one(0)
    pump(("arrive", 3, 2), ("step", 3, 3))
    end_forward()
    copy = sums_begin()
    pump(("arrive", 3, 3), ("mated", 4), ("arrive", 4, 0), ("step", 4, 1), ("finish", 3))
    copies = sums_share(copy)
    pump(("arrive", 4, 1), ("step", 4, 2), ("arrive", 4, 2), ("step", 4, 3), ("arrive", 4, 3))
    copies = cond_terms(copies)
    pump(("arrive", 5, 0), ("step", 5, 1), ("finish", 4))
    copies = cond_share(copies)
    pump(("arrive", 5, 1), ("step", 5, 2), ("arrive", 5, 2), ("step", 5, 3), ("arrive", 5, 3))
    cond_end(copies)
    pump(("finish", 5))
    if fused:
        for r_ in range(len(ORDER) - slots, len(ORDER)):
            scatter.drain(r_)
        scatter.end()
    for wait in links.waiting:
        wait()
    for name in list(waiting):
        settle(name)


def backward_call(cfg, w, saved, small):
    fused, chain, heads, head_dim = cfg
    _, rows, width = small[0].shape
    pieces, _, groups, shard, _ = w.shape
    count, _, cond_lanes = small[3].shape
    many = 2 * (count - 1) + 6
    bf, f = lambda *s: pltpu.VMEM(s, BF), lambda *s: pltpu.VMEM(s, F32)
    dma = lambda *s: pltpu.SemaphoreType.DMA(s)
    out_shape = [
        jax.ShapeDtypeStruct((3, 2, shard, width), F32)
        if fused
        else jax.ShapeDtypeStruct((pieces, groups, shard, width), BF),
        jax.ShapeDtypeStruct((2, rows, width), F32),
        jax.ShapeDtypeStruct((2, rows, width), F32),
        jax.ShapeDtypeStruct((16, width), F32),
        jax.ShapeDtypeStruct((count, 16, ADA_LANES), BF),
        jax.ShapeDtypeStruct((count, 2, count, cond_lanes), F32),
    ]
    some = 3 if fused else 1
    links = chain if fused else 1
    block = shard if fused else 16
    scratch = [
        bf(2, 2, groups, shard, width),
        bf(rows, width),
        f(2, rows, 128),
        bf(3, 2, rows, HEAD_LANES),
        bf(heads, rows, rows),
        bf(2, rows, HEAD_LANES),
        bf(rows, width),
        bf(rows, width),
        bf(2, rows, width),
        bf(2, rows, width),
        bf(2, rows, width),
        f(rows, width),
        f(rows, width),
        bf(2, rows, width),
        bf(3, rows, width),
        bf(2, rows, width),
        bf(3, rows, width),
        bf(2, rows, HEAD_LANES),
        bf(3, rows, width),
        bf(3, rows, width),
        bf(4, groups, shard, width),
        bf(some, links, block, width),
        bf(some, links + 1, block, width),
        bf(some, block, width),
        f(2, block, width),
        f(2, 24, width),
        f(24, width),
        f(16, width),
        bf(count, 16, width + ADA_LANES),
        f(2, 2, 2, count, cond_lanes),
        f(count, 2, count, cond_lanes),
        f(2, 24, width),
        f(count, 8, cond_lanes),
        bf(*small[4].shape),
        bf(2, rows, rows),
        bf(rows, rows),
        bf(rows, rows),
        f(rows, 128),
        bf(rows, rows),
        bf(rows, width),
        dma(6, 3 * links + 1),
        dma(6, 3 * links + 1),
        dma(6),
        dma(6),
        dma(6),
        pltpu.SemaphoreType.REGULAR((3,)),
        dma(20),
        dma(20),
        dma(56),
        dma(many),
        dma(many),
    ]

    def body(*refs):
        backward_kernel(cfg, *refs)

    vm = pl.BlockSpec(memory_space=pltpu.VMEM)
    hbm = pl.BlockSpec(memory_space=pl.ANY)
    return pl.pallas_call(
        body,
        out_shape=out_shape,
        in_specs=[hbm] * (1 + len(saved)) + [hbm, vm, hbm, hbm, hbm, vm],
        out_specs=[hbm] * len(out_shape),
        scratch_shapes=scratch,
        compiler_params=pltpu.CompilerParams(
            collective_id=1, has_side_effects=True, vmem_limit_bytes=VMEM_BYTES
        ),
        name="backward_blocks",
    )(w, *saved, *small)


def per_device(
    tokens,
    kept_mask,
    timesteps,
    labels,
    w_qkv,
    b_qv,
    w_out,
    b_out,
    w_up,
    b_up,
    w_down,
    b_down,
    w_ada,
    b_ada,
    rel_table,
    mask_token,
    class_table,
    out_grad,
):
    micro, rows, width = tokens.shape
    length = kept_mask.shape[2]
    classes = class_table.shape[0]
    heads = rel_table.shape[1]
    lw = w_qkv.shape[3]
    head_dim = lw // heads
    hw = lw // 2
    ff = w_up.shape[2]
    fw = ff // 2
    dp_count = lax.axis_size("dp")
    c = lax.axis_index("section")
    dp = lax.axis_index("dp")
    h = lax.axis_index("head")

    qkv = jnp.transpose(w_qkv[0], (1, 0, 2))
    out_t = w_out[0].T
    down_t = w_down[0].T
    halves = []
    for half in range(2):
        at = slice(half * hw, (half + 1) * hw)
        fat = slice(half * fw, (half + 1) * fw)
        a = jnp.concatenate([out_t[:, at], qkv[0][:, at], qkv[1][:, at], qkv[2][:, at]], axis=1)
        halves.append(jnp.stack([a, w_up[0][:, fat], down_t[:, fat]]))
    pack = jnp.stack(halves)
    fr = width // dp_count

    label_pick = (labels == jnp.arange(classes)[None, :]).astype(BF)
    cond = nn(label_pick, class_table) + time_features(timesteps[:, 0], width)
    blocks = jnp.transpose(cond.reshape(micro, dp_count, fr), (1, 0, 2))
    tags = jnp.broadcast_to(labels.astype(F32)[None], (dp_count, micro, 1))
    cond_lanes = -(-(fr + 1) // 128) * 128
    blocks = jnp.concatenate([blocks, tags], axis=2)
    blocks = jnp.pad(blocks, ((0, 0), (0, 8 - micro), (0, cond_lanes - fr - 1)))
    ada = jnp.pad(w_ada[0], ((0, 0), (0, 0), (0, ADA_LANES - lw))).reshape(fr, 6 * ADA_LANES)

    fused = dp_count == 8 and fr % 16 == 0
    cfg = (fused, dp_count // 2, heads, head_dim)
    if fused:
        source_w = pack
    else:
        other_w = swap(mine(1 - c, halves), "section")
        own_w = mine(c, halves)
        own_w = jnp.concatenate([pick(c, own_w, other_w), pick(c, other_w, own_w)])
        half_w_ = lax.all_gather(own_w, "dp", axis=1, tiled=True)
        other_w = swap(half_w_, "section")
        source_w = jnp.stack([pick(c, half_w_, other_w), pick(c, other_w, half_w_)], axis=1)
        source_w = source_w.reshape(6, 2, 8, width // 8, pack.shape[3])
    small_in = (
        tokens,
        blocks,
        ada,
        b_ada,
        kept_mask,
        b_qv,
        b_out,
        b_down,
        b_up,
        rel_table,
        mask_token[None, :],
    )
    full, *saved, mod, cond_all, small_all, enc = forward_call(cfg, source_w, small_in, dp_count)
    saved.append(enc)
    small_back = (out_grad, mod, small_all, cond_all, ada, kept_mask)
    red, dx, outs, sums, dm, dc = backward_call(cfg, full, saved, small_back)

    if fused:
        g0, g1 = red[:, 0], red[:, 1]
    else:
        red = lax.psum_scatter(
            red.reshape(6, width, pack.shape[3]), "dp", scatter_dimension=1, tiled=True
        ).astype(F32)
        red = red.reshape(2, 3, fr, pack.shape[3])
        g_own = mine(c, red)
        g_got = swap(mine(1 - c, red), "section")
        g0, g1 = pick(c, g_own, g_got), pick(c, g_got, g_own)
    g_qkv = jnp.stack(
        [
            jnp.concatenate([g0[0][:, i * hw : (i + 1) * hw], g1[0][:, i * hw : (i + 1) * hw]], axis=1)
            for i in (1, 2, 3)
        ],
        axis=1,
    )
    g_out = jnp.concatenate([g0[0][:, :hw], g1[0][:, :hw]], axis=1).T
    g_up = jnp.concatenate([g0[1], g1[1]], axis=1)
    g_down = jnp.concatenate([g0[2], g1[2]], axis=1).T

    half_w = width // 2

    def half(v):
        return lax.dynamic_slice_in_dim(v, h * half_w, half_w, v.ndim - 1)

    g_b_qv = jnp.stack(
        [
            jnp.concatenate([sums[4, at * hw : (at + 1) * hw], sums[5, at * hw : (at + 1) * hw]])
            for at in (1, 3)
        ]
    )
    g_b_up = sums[2:4, :fw].reshape(-1)
    g_rel = sums[8 : 8 + heads, : 2 * length - 1]

    dm = dm.astype(F32).reshape(dp_count, micro, 8, ADA_LANES)[:, :, :6, :lw]
    cond_part = jax.nn.silu(cond_all[:, :micro, :fr])
    g_ada = jnp.einsum("jmf,jmke->fke", cond_part, dm, precision=PRECISE)
    g_b_ada = jnp.sum(dm, axis=(0, 1))
    labels_all = cond_all[:, :micro, fr].astype(jnp.int32).T.reshape(-1)
    dcond = jnp.transpose(dc[..., :fr], (1, 2, 0, 3)).reshape(micro * dp_count, width)
    pick_all = (labels_all[:, None] == jnp.arange(classes)[None, :]).astype(F32)
    g_class = jnp.einsum("ic,id->cd", pick_all, half(dcond), precision=PRECISE)

    return (
        outs[None],
        dx[None],
        g_qkv[None],
        g_b_qv[None],
        g_out[None],
        half(sums[1])[None],
        g_up[None],
        g_b_up[None],
        g_down[None],
        half(sums[0])[None],
        g_ada[None],
        g_b_ada[None],
        g_rel[None],
        half(sums[6]),
        g_class,
    )


def solution(mesh):
    placed = (
        P(None, "dp", None),
        P(None, "dp", None),
        P(None, "dp"),
        P(None, "dp"),
        P("section", "dp", None, "head"),
        P("section", None, "head"),
        P("section", "head", "dp"),
        P("section", None),
        P("section", "dp", "head"),
        P("section", "head"),
        P("section", "head", "dp"),
        P("section", None),
        P("section", "dp", None, "head"),
        P("section", None, "head"),
        P("section", "head", None),
        P(),
        P(),
        P(None, "dp", None),
    )
    return jax.shard_map(
        per_device,
        mesh=mesh,
        in_specs=placed,
        out_specs=(
            P("section", None, "dp", None),
            P("section", None, "dp", None),
            P("section", "dp", None, "head"),
            P("section", None, "head"),
            P("section", "head", "dp"),
            P("section", "head"),
            P("section", "dp", "head"),
            P("section", "head"),
            P("section", "head", "dp"),
            P("section", "head"),
            P("section", "dp", None, "head"),
            P("section", None, "head"),
            P("section", "head", None),
            P("head"),
            P(None, "head"),
        ),
        check_vma=False,
    )
```

```python
import math

import jax
import jax.numpy as jnp
from jax import lax
from jax.experimental import pallas as pl
from jax.experimental.pallas import tpu as pltpu
from jax.sharding import PartitionSpec as P

PRECISE = lax.Precision.HIGHEST
EPSILON = 1e-06
NEGATIVE = -1e30
MESH = pl.DeviceIdType.MESH
BF = jnp.bfloat16
VMEM_BYTES = 62 * 1024 * 1024
F32 = jnp.float32


def time_features(step_ids, model_width):
    half_width = model_width // 2
    frequency = jnp.exp(-math.log(10000.0) * jnp.arange(half_width).astype(F32) / half_width)
    angles = step_ids.astype(F32)[..., None] * frequency
    return jnp.concatenate([jnp.cos(angles), jnp.sin(angles)], axis=-1)


def swap(value, axis):
    return lax.ppermute(value, axis, [(0, 1), (1, 0)])


def pick(index, first, second):
    return jnp.where(index == 0, first, second)


def mine(c, pair):
    return pick(c, pair[0], pair[1])


def both(value):
    c = lax.axis_index("section")
    got = swap(value, "section")
    return pick(c, value, got), pick(c, got, value)


HEAD_LANES = 384
ADA_LANES = 640


def nn(a, b):
    return lax.dot_general(a, b, (((1,), (0,)), ((), ())), preferred_element_type=F32)


def nt(a, b):
    return lax.dot_general(a, b, (((1,), (1,)), ((), ())), preferred_element_type=F32)


def tn(a, b):
    return lax.dot_general(a, b, (((0,), (0,)), ((), ())), preferred_element_type=F32)


def flat(value):
    return value.reshape(value.shape[0] * value.shape[1], value.shape[2])


GELU_SCALE = math.sqrt(2.0 / math.pi)


def gelu_both(v):
    t = jnp.tanh(GELU_SCALE * (v + 0.044715 * v * v * v))
    slope = 0.5 * (1.0 + t) + (0.5 * GELU_SCALE) * v * (1.0 - t * t) * (1.0 + 0.134145 * v * v)
    return 0.5 * v * (1.0 + t), slope


class Place:
    def __init__(self, chain):
        self.chain = chain
        self.core = lax.axis_index("section")
        self.dp = lax.axis_index("dp")
        self.head = lax.axis_index("head")
        self.z = self.dp // 2
        self.y = self.dp % 2
        self.mate_z = self.z + 1 - 2 * (self.z % 2)
        self.above = (self.core, self.dp + 2, self.head)
        self.below = (self.core, self.dp - 2, self.head)
        self.across = (self.core, self.z * 2 + 1 - self.y, self.head)
        self.mate = (self.core, self.mate_z * 2 + self.y, self.head)
        self.other = (1 - self.core, self.dp, self.head)
        self.beside = (self.core, self.dp, 1 - self.head)

        self.beyond = (1 - self.core, self.dp, 1 - self.head)
        self.count = 2 * chain

    def peer(self, k):
        return lax.rem(self.dp + k, self.count)

    def source(self, k):
        return lax.rem(self.dp + self.count - k, self.count)

    def flip(self, b):
        bit = lax.rem(self.dp // (1 << b), 2)
        return self.dp + (1 << b) * (1 - 2 * bit)

    def in_dp(self, dp):
        return (self.core, dp, self.head)

    def greet(self):
        barrier = pltpu.get_barrier_semaphore()
        others = [self.other, self.beside, self.beyond]
        others += [self.in_dp(self.peer(k)) for k in range(1, self.count)]
        for device in others:
            pl.semaphore_signal(barrier, inc=1, device_id=device, device_id_type=MESH)
        pl.semaphore_wait(barrier, len(others))


def remote(src, dst, ssem, rsem, device):
    return pltpu.make_async_remote_copy(
        src_ref=src, dst_ref=dst, send_sem=ssem, recv_sem=rsem, device_id=device, device_id_type=MESH
    )


class Numbered:
    def __init__(self, ref):
        self.ref = ref
        self.count = 0

    def next(self):
        self.count += 1
        assert self.count <= self.ref.shape[0]
        return self.ref.at[self.count - 1]


class Links:
    def __init__(self, at, ssem, rsem):
        self.at, self.sends, self.recvs = at, Numbered(ssem), Numbered(rsem)
        self.waiting = []

    def copy(self, src, dst, device):
        copy = remote(src, dst, self.sends.next(), self.recvs.next(), device)
        copy.start()
        self.waiting.append(copy.wait_send)
        return copy

    def to_all(self, src_of, dst):
        copies = []
        for k in range(1, self.at.count):
            peer = self.at.peer(k)
            copies.append(self.copy(src_of(peer), dst, self.at.in_dp(peer)))
        return copies

    def around(self, ref):
        mine_ = ref.at[self.at.core, self.at.head]
        return [
            self.copy(mine_, mine_, device)
            for device in (self.at.other, self.at.beside, self.at.beyond)
        ]


COPY_BY_MATE = (1, 3, 5)
SUM_BY_MATE = (1, 2, 3, 4)


class Gather:
    def __init__(self, at, halves, w, ssem, rsem, lsem):
        self.at, self.halves, self.w = at, halves, w
        self.ssem, self.rsem, self.lsem = ssem, rsem, lsem
        self.pieces = w.shape[0]

    def local(self, t):
        core = self.at.core
        return pltpu.make_async_copy(
            self.halves[t](core), self.w.at[3 * core + t, core, self.at.dp], self.lsem.at[t]
        )

    def share(self, t):
        core = self.at.core
        return remote(
            self.halves[t](1 - core),
            self.w.at[3 * core + t, 1 - core, self.at.dp],
            self.ssem.at[t, 5 * self.at.chain + 1],
            self.rsem.at[t, 5 * self.at.chain + 1],
            self.at.other,
        )

    def shared(self, t):
        core = self.at.core
        block = self.w.at[3 * (1 - core) + t, core, self.at.dp]
        return remote(
            self.halves[t](1 - core),
            block,
            self.ssem.at[t, 5 * self.at.chain + 1],
            self.rsem.at[t, 5 * self.at.chain + 1],
            self.at.other,
        )

    def split(self, t):
        self.local(t).start()
        self.share(t).start()

    def block(self, p, zz, yy):
        return self.w.at[p, self.at.core, zz * 2 + yy]

    def copy(self, src, dst, p, kind, device):
        return remote(src, dst, self.ssem.at[p, kind], self.rsem.at[p, kind], device)

    def up(self, p, k):
        b = self.block(p, self.at.z - (k - 1), self.at.y)
        return self.copy(b, b, p, k - 1, self.at.above)

    def up_in(self, p, k):
        b = self.block(p, self.at.z - k, self.at.y)
        return self.copy(b, b, p, k - 1, self.at.below)

    def down(self, p, k):
        b = self.block(p, self.at.z + (k - 1), self.at.y)
        return self.copy(b, b, p, self.at.chain + k - 1, self.at.below)

    def down_in(self, p, k):
        b = self.block(p, self.at.z + k, self.at.y)
        return self.copy(b, b, p, self.at.chain + k - 1, self.at.above)

    def cross(self, p, zz):
        b = self.block(p, zz, self.at.y)
        return self.copy(b, b, p, 2 * self.at.chain + zz, self.at.across)

    def cross_in(self, p, zz):
        b = self.block(p, zz, 1 - self.at.y)
        return self.copy(b, b, p, 2 * self.at.chain + zz, self.at.across)

    def mate_out(self, p):
        b = self.block(p, self.at.z, 1 - self.at.y)
        return self.copy(b, b, p, 3 * self.at.chain, self.at.mate)

    def mate_in(self, p):
        b = self.block(p, self.at.mate_z, 1 - self.at.y)
        return self.copy(b, b, p, 3 * self.at.chain, self.at.mate)

    def over(self, p, zz, yy):
        b = self.block(p, zz, yy)
        own = jnp.where(yy == self.at.y, 0, 1)
        return self.copy(b, b, p, 3 * self.at.chain + 1 + 2 * zz + own, self.at.other)

    def over_in(self, p, zz, own):
        yy = self.at.y if own == 0 else 1 - self.at.y
        b = self.w.at[p, 1 - self.at.core, zz * 2 + yy]
        return self.copy(b, b, p, 3 * self.at.chain + 1 + 2 * zz + own, self.at.other)

    def other_in(self, p):
        for zz in range(self.at.chain):
            for own in range(2):
                self.over_in(p, zz, own).wait_recv()

    def start(self, p):
        s, t = divmod(p, 3)

        @pl.when(self.at.core == s)
        def _():
            self.local(t).wait()

        @pl.when(self.at.core != s)
        def _():
            self.shared(t).wait_recv()

        self.cross(p, self.at.z).start()

        @pl.when(self.at.z < self.at.chain - 1)
        def _():
            self.up(p, 1).start()

        @pl.when(self.at.z > 0)
        def _():
            self.down(p, 1).start()

        self.over(p, self.at.z, self.at.y).start()

    def step(self, p, k):
        z, chain = self.at.z, self.at.chain
        odd = p in COPY_BY_MATE

        @pl.when(z >= k)
        def _():
            self.up_in(p, k).wait_recv()

            @pl.when(z < chain - 1)
            def _():
                self.up(p, k + 1).start()

            if k == 1 and odd:

                @pl.when(z % 2 == 0)
                def _():
                    self.cross(p, z - k).start()

            else:
                self.cross(p, z - k).start()
            self.over(p, z - k, self.at.y).start()

        @pl.when(z + k < chain)
        def _():
            self.down_in(p, k).wait_recv()

            @pl.when(z > 0)
            def _():
                self.down(p, k + 1).start()

            if k == 1 and odd:

                @pl.when(z % 2 == 1)
                def _():
                    self.cross(p, z + k).start()

            else:
                self.cross(p, z + k).start()
            self.over(p, z + k, self.at.y).start()

        if k == 1 and odd:
            self.cross_in(p, z).wait_recv()
            self.mate_out(p).start()
            self.over(p, z, 1 - self.at.y).start()

    def finish(self, p):
        z = self.at.z
        for j in range(self.at.chain):
            if p in COPY_BY_MATE:

                @pl.when((j != z) & (j != self.at.mate_z))
                def _():
                    self.cross_in(p, j).wait_recv()
                    self.over(p, j, 1 - self.at.y).start()

            else:
                self.cross_in(p, j).wait_recv()
                self.over(p, j, 1 - self.at.y).start()
        if p in COPY_BY_MATE:
            self.mate_in(p).wait_recv()
            self.over(p, self.at.mate_z, 1 - self.at.y).start()

    def drain(self, p):
        z, chain = self.at.z, self.at.chain
        for j in range(chain):
            if p in COPY_BY_MATE:

                @pl.when(j != self.at.mate_z)
                def _():
                    self.cross(p, j).wait_send()

            else:
                self.cross(p, j).wait_send()
        if p in COPY_BY_MATE:
            self.mate_out(p).wait_send()
        for k in range(1, chain):

            @pl.when((z < chain - 1) & (z >= k - 1))
            def _():
                self.up(p, k).wait_send()

            @pl.when((z > 0) & (z + k - 1 < chain))
            def _():
                self.down(p, k).wait_send()

        for j in range(chain):
            for yy in range(2):
                self.over(p, j, yy).wait_send()
        if p < 3:
            self.share(p).wait_send()


TILE = 32


def silu(v):
    return v / (1.0 + jnp.exp(-v))


def thirds(v):
    a = v.astype(BF)
    rest = v - a.astype(F32)
    b = rest.astype(BF)
    return a, b, (rest - b.astype(F32)).astype(BF)


def by_rows(rows, body, carry, tile=TILE):
    def step(i, c):
        return body(pl.ds(pl.multiple_of(i * tile, tile), tile), c)

    return lax.fori_loop(0, rows // tile, step, carry)


def column_sum(value):
    rows, width = value.shape
    return jnp.sum(value.reshape(rows // 8, 8, width), axis=0)


def layer_norm(v):
    cen = v - jnp.mean(v, axis=-1, keepdims=True)
    inv = lax.rsqrt(jnp.mean(cen * cen, axis=-1, keepdims=True) + EPSILON)
    return cen * inv, inv


def layer_norm_back(w, hat, inv):
    return inv * (
        w - jnp.mean(w, axis=-1, keepdims=True) - hat * jnp.mean(w * hat, axis=-1, keepdims=True)
    )


def spread_masks(kept, place, pos, drop, seg=None):
    length = kept.shape[1]
    u = lax.broadcasted_iota(jnp.int32, (length, length), 0)
    v = lax.broadcasted_iota(jnp.int32, (length, length), 1)
    uf, vf = u.astype(F32), v.astype(F32)
    column = jnp.sum(jnp.where(u == v, kept, 0.0), axis=1, keepdims=True)
    source = jnp.sum(jnp.where(v <= u, kept, 0.0), axis=1, keepdims=True) - 1.0
    source_row = jnp.sum(jnp.where(u <= v, column, 0.0), axis=0, keepdims=True) - 1.0
    count = jnp.sum(kept, axis=1, keepdims=True)
    place[...] = (jnp.where(source == vf, 1.0, 0.0) * column).astype(BF)
    pad = jnp.where(uf >= count, 1.0, 0.0)
    first = jnp.where(v == 0, pad, 0.0)
    pos[...] = (jnp.where(source_row == uf, 1.0, 0.0) * kept + first).astype(BF)
    drop[...] = jnp.broadcast_to(1.0 - column, drop.shape)
    if seg is not None:
        seg[...] = jnp.where(pad == jnp.where(vf >= count, 1.0, 0.0), 0.0, NEGATIVE)


def pack_sums(top, low):
    wide = 1024
    moved = jnp.concatenate(
        [low[:, : wide // 2], top[:, wide:], jnp.zeros_like(top[:, : wide // 2 - (top.shape[1] - wide)])],
        axis=1,
    )
    return jnp.concatenate([top[:, :wide], moved], axis=0)


def unpack_sums(packed):
    wide = 1024
    top = jnp.concatenate([packed[:8], packed[8:, wide // 2 : wide // 2 + 128]], axis=1)
    return top, packed[8:, : wide // 2]


def diagonal(length, mirrored=False):
    u = lax.broadcasted_iota(jnp.int32, (length, length), 0)
    v = lax.broadcasted_iota(jnp.int32, (length, length), 1)
    return jnp.where(u + v == length - 1 if mirrored else u == v, 1.0, 0.0).astype(BF)


def head_mask(i, head_dim):
    lane = lax.broadcasted_iota(jnp.int32, (1, HEAD_LANES), 1)
    return ((lane >= i * head_dim) & (lane < (i + 1) * head_dim)).astype(F32)


def forward_kernel(cfg, *refs):
    fused, chain, heads, head_dim = cfg
    refs = list(refs)
    if fused:
        i_att, i_up, i_down = refs[:3]
        refs = refs[3:]
    else:
        w = refs.pop(0)
    i_tok, cond, i_wada, b_ada, kept, b_qv, b_out, b_down, b_up, rel, mtok = refs[:11]
    refs = refs[11:]
    if fused:
        w = refs.pop(0)
    (
        s_hat1, s_inv, s_n1, s_qkv, s_p, s_o, s_branch, s_hat2, s_n2, s_hid, s_slope, s_y,
        s_full, s_xm, o_mod, o_cl, o_small, s_e,
    ) = refs[:18]
    refs = refs[18:]
    (
        wa, wu, wd, res, hat, inv, n, r, qkv, prob, o, branch, hid, slope, y_keep,
        xs, xr, toep, small, cl, part, got, pair, mod, tok, wada, pos, seg, place, drop,
        eye, small_own, wide, bada,
        gs, gr, gl, ssem, rsem, lsem, ms, mr,
    ) = refs
    at = Place(chain)
    rows, width = res.shape
    lw = heads * head_dim
    shard = width // at.count
    half_heads = heads // 2
    scale = 1.0 / math.sqrt(head_dim)
    sends, recvs, locals_ = Numbered(ssem), Numbered(rsem), Numbered(lsem)
    at.greet()
    gather = None
    if fused:
        side = lambda i: pl.ds(pl.multiple_of(i * width, 128), width)
        halves = (
            lambda i: i_att.at[i],
            lambda i: i_up.at[0, :, side(i)],
            lambda i: i_down.at[:, side(i)],
        )
        gather = Gather(at, halves, w, gs, gr, gl)
    links = Links(at, ms, mr)
    waiting = {}

    def keep(name, src, dst):
        copy = pltpu.make_async_copy(src, dst, locals_.next())
        copy.start()
        waiting.setdefault(name, []).append(copy.wait)

    def give(name, src, dst):
        copy = remote(src, dst, sends.next(), recvs.next(), at.other)
        copy.start()
        waiting.setdefault(name, []).append(copy.wait_send)
        waiting.setdefault("end", []).append(copy.wait_recv)

    def settle(name):
        for wait in waiting.pop(name, []):
            wait()

    def pump(*what):
        if not fused:
            return
        for name, p, *k in what:
            if p < gather.pieces:
                getattr(gather, name)(p, *k)

    def load(p, slot):
        if fused:
            gather.other_in(p)
        keep("load%d" % p, w.at[p], slot)

    def send_cond():
        cl[pl.ds(at.dp, 1)] = cond[pl.ds(at.dp, 1)]
        return links.to_all(lambda peer: cond.at[peer], cl.at[at.dp])

    def modulation_terms(copies):
        for copy in copies:
            copy.wait_recv()
        part[...] = jnp.zeros_like(part)
        parts = thirds(silu(flat(cl[...])[:, :shard]))
        for k in range(6):
            cols = wada[k]
            value = nn(parts[0], cols) + (nn(parts[1], cols) + nn(parts[2], cols))
            value = value.reshape(at.count, 8, lw)
            for m in range(2):
                part[:, m * 8 + k, :lw] = value[:, m, :]
        got[pl.ds(at.dp, 1)] = part[pl.ds(at.dp, 1)]
        return links.to_all(lambda peer: part.at[peer], got.at[at.dp])

    def modulation_sum(copies):
        for copy in copies:
            copy.wait_recv()
        value = got[0]
        for j in range(1, at.count):
            value = value + got[j]
        pair[at.core, at.head] = value + jnp.concatenate([bada[...], bada[...]], axis=0)
        return links.around(pair)

    def modulation(copies):
        for copy in copies:
            copy.wait_recv()
        lane = lax.broadcasted_iota(jnp.int32, (8, ADA_LANES), 1)
        blank = jnp.zeros((8, width - ADA_LANES), F32)
        mine_ = pl.ds(pl.multiple_of(at.core * 8, 8), 8)
        for s in range(2):
            a, b = [
                jnp.concatenate([jnp.where(lane < lw, pair[s, h, mine_, :], 0.0), blank], axis=1)
                for h in range(2)
            ]
            mod[s] = a + pltpu.roll(b, lw, 1)
        keep("mod", mod, o_mod)
        keep("cl", cl, o_cl)

    def share_small():
        wide[...] = jnp.zeros_like(wide)
        wide[0:2, :lw] = b_qv[0].astype(F32)
        small_own[...] = jnp.zeros_like(small_own)
        value = wide[...]
        for half in range(2):
            for k in range(2):
                row = half * 4 + 2 * k
                small_own[row : row + 1, :HEAD_LANES] = value[k : k + 1, :HEAD_LANES]
            value = pltpu.roll(value, ADA_LANES - lw // 2, 1)
        small_own[8:9, :] = b_out[...].astype(F32)
        small_own[9:10, :] = b_down[...].astype(F32)
        small_own[10:11, :] = b_up[:, :width].astype(F32)
        small_own[11:12, :] = b_up[:, width:].astype(F32)
        small_own[16 : 16 + heads, : 2 * rows - 1] = rel[0].astype(F32)
        bada[...] = jnp.zeros_like(bada)
        bada[0:6, :lw] = b_ada[0].astype(F32)
        small[pl.ds(at.core, 1)] = small_own[...][None]
        return links.copy(small_own, small.at[at.core], at.other)

    def bqv_row(s, half, kind):
        return small[s, half * 4 + kind : half * 4 + kind + 1, :HEAD_LANES]

    def bup_row(s, half, cols):
        return small[s, 10 + half : 11 + half, cols]

    def send_across(i):
        copy = remote(xs.at[i], xr.at[i], sends.next(), recvs.next(), at.beside)
        copy.start()
        waiting.setdefault("end", []).append(copy.wait_send)
        return copy

    def total(i, ds):
        return xs[i, ds, :].astype(F32) + xr[i, ds, :].astype(F32)

    def norm_one(s):
        settle("hat1")
        settle("n1")
        settle("inv")

        def body(ds, c):
            v, iv = layer_norm(res[ds, :])
            hat[0, ds, :] = v.astype(BF)
            inv[0, ds, :] = jnp.broadcast_to(iv, (TILE, 128))
            n[0, ds, :] = (v * (1.0 + mod[s, 1:2, :]) + mod[s, 0:1, :]).astype(BF)
            return c

        by_rows(rows, body, 0)
        keep("hat1", hat.at[0], s_hat1.at[s])
        keep("n1", n.at[0], s_n1.at[s, 0])
        give("n1", n.at[0], s_n1.at[s, 1])

    def project(s):
        settle("qkv")
        for half in range(2):
            for j in range(3):
                cols = slice(j * 384, (j + 1) * 384)
                r[:, cols] = nn(n[0], flat(wa[half, :, :, cols]))

            def body(ds, c):
                v = r[ds, :]
                for kind, shift in ((0, 864), (1, 576), (2, 288)):
                    piece = pltpu.roll(v, shift, 1)[:, :HEAD_LANES]
                    qkv[kind, half, ds, :] = (piece + bqv_row(s, half, kind)).astype(BF)
                return c

            by_rows(rows, body, 0)
        keep("qkv", qkv, s_qkv.at[s])

    def attend(s, half):
        if half == 0:
            settle("p")
            settle("o")
        o[half] = jnp.zeros_like(o[half])

        def one(i, c):
            index = half * half_heads + i
            mask = head_mask(i, head_dim).astype(BF)
            line = small[s, pl.ds(16 + index, 1), : 2 * rows]
            skew = pltpu.roll(
                jnp.broadcast_to(line, (rows, 2 * rows)), rows + 1, 1, stride=1, stride_axis=0
            )
            toep[...] = skew[:, :rows].astype(BF)
            if s == 0:
                left = nt(pos[...], toep[...]).astype(BF)
                bias = nt(left, pos[...]) + seg[...]
            else:
                bias = nt(eye[...], toep[...])
            z = nt(qkv[0, half] * mask, qkv[1, half]) * scale + bias
            e = jnp.exp(z - jnp.max(z, axis=-1, keepdims=True))
            p = (e / jnp.sum(e, axis=-1, keepdims=True)).astype(BF)
            prob[index] = p
            o[half] = o[half] + nn(p, qkv[2, half]).astype(BF) * mask
            return c

        lax.fori_loop(0, half_heads, one, 0)
        if half == 1:
            keep("p", prob, s_p.at[s])
            keep("o", o.at[at.core], s_o.at[s, 0])
            give("o", o.at[1 - at.core], s_o.at[s, 1])

    def project_out(i):
        xs[i] = (
            nt(o[0], flat(wa[0, :, :, :HEAD_LANES])) + nt(o[1], flat(wa[1, :, :, :HEAD_LANES]))
        ).astype(BF)
        return send_across(i)

    def norm_two(s, i, copy):
        copy.wait_recv()
        settle("branch")
        settle("hat2")
        settle("n2")

        def body(ds, c):
            b = total(i, ds) + small[s, 8:9, :]
            branch[ds, :] = b.astype(BF)
            xm = res[ds, :] + mod[s, 2:3, :] * b
            res[ds, :] = xm
            v, iv = layer_norm(xm)
            hat[1, ds, :] = v.astype(BF)
            inv[1, ds, :] = jnp.broadcast_to(iv, (TILE, 128))
            n[1, ds, :] = (v * (1.0 + mod[s, 4:5, :]) + mod[s, 3:4, :]).astype(BF)
            return c

        by_rows(rows, body, 0)
        keep("branch", branch, s_branch.at[s])
        keep("inv", inv, s_inv.at[s])
        keep("hat2", hat.at[1], s_hat2.at[s])
        if s == 1:
            keep("out", res, s_xm)
        keep("n2", n.at[1], s_n2.at[s, 0])
        give("n2", n.at[1], s_n2.at[s, 1])

    def hidden(s, half):
        if half == 0:
            settle("hid")
            settle("slope")
        for j in range(3):
            cols = slice(j * 384, (j + 1) * 384)
            r[:, cols] = nn(n[1], flat(wu[half, :, :, cols])) + bup_row(s, half, cols)

        def body(ds, c):
            value, sl = gelu_both(r[ds, :])
            hid[half, ds, :] = value.astype(BF)
            slope[half, ds, :] = sl.astype(BF)
            return c

        by_rows(rows, body, 0)
        if half == 1:
            keep("slope", slope, s_slope.at[s])
            keep("hid", hid.at[at.core], s_hid.at[s, 0])
            give("hid", hid.at[1 - at.core], s_hid.at[s, 1])
            if s == 1:
                keep("hid", hid, s_full)

    def project_down(i):
        xs[i] = (nt(hid[0], flat(wd[0])) + nt(hid[1], flat(wd[1]))).astype(BF)
        return send_across(i)

    def end_block(s, i, copy):
        copy.wait_recv()
        settle("y")
        settle("out")

        def body(ds, c):
            v = total(i, ds) + small[s, 9:10, :]
            y_keep[ds, :] = v.astype(BF)
            res[ds, :] = res[ds, :] + mod[s, 5:6, :] * v
            return c

        by_rows(rows, body, 0)
        keep("y", y_keep, s_y)
        keep("out", res, s_e)

    def spread():
        r[...] = nn(place[...], res[...].astype(BF))
        settle("out")

        def body(ds, c):
            res[ds, :] = r[ds, :] + drop[ds, 0:1] * mtok[...].astype(F32)
            return c

        by_rows(rows, body, 0)

    copies = send_cond()
    small_copy = share_small()
    if fused:
        for t in range(3):
            gather.split(t)
        gather.start(0)
        gather.start(1)
    keep("tok", i_tok.at[at.core], tok)
    keep("wada", i_wada, wada)
    spread_masks(kept[at.core].astype(F32), place, pos, drop, seg)
    eye[...] = diagonal(rows)
    settle("tok")

    def start_residual(ds, c):
        res[ds, :] = tok[ds, :].astype(F32)
        return c

    by_rows(rows, start_residual, 0)
    pump(("step", 0, 1))
    settle("wada")
    copies = modulation_terms(copies)
    pump(("step", 0, 2), ("start", 2), ("step", 0, 3))
    copies = modulation_sum(copies)
    small_copy.wait_recv()
    keep("small", small, o_small)
    pump(("step", 1, 1))
    modulation(copies)
    norm_one(0)
    pump(("step", 1, 2), ("start", 3), ("finish", 0), ("step", 1, 3))
    load(0, wa)
    settle("load0")
    project(0)
    pump(("step", 2, 1))
    attend(0, 0)
    pump(("step", 2, 2), ("start", 4), ("finish", 1))
    attend(0, 1)
    copy = project_out(0)
    pump(("step", 2, 3))
    load(1, wu)
    pump(("step", 3, 1))
    norm_two(0, 0, copy)
    settle("load1")
    pump(("step", 3, 2), ("start", 5), ("finish", 2))
    hidden(0, 0)
    hidden(0, 1)
    pump(("step", 3, 3))
    load(2, wd)
    settle("load2")
    copy = project_down(1)
    pump(("step", 4, 1), ("step", 4, 2), ("finish", 3))
    end_block(0, 1, copy)
    spread()
    norm_one(1)
    pump(("step", 4, 3))
    load(3, wa)
    settle("load3")
    project(1)
    pump(("step", 5, 1))
    attend(1, 0)
    pump(("step", 5, 2), ("finish", 4))
    attend(1, 1)
    copy = project_out(2)
    load(4, wu)
    pump(("step", 5, 3), ("finish", 5))
    norm_two(1, 2, copy)
    settle("load4")
    hidden(1, 0)
    hidden(1, 1)
    if fused:
        gather.other_in(5)
        for p in range(gather.pieces):
            gather.drain(p)
    for wait in links.waiting:
        wait()
    for name in list(waiting):
        settle(name)


def forward_call(cfg, weights, small, dp_count):
    fused, chain, heads, head_dim = cfg
    _, rows, width = small[0].shape
    pieces = 6
    shard = weights[0].shape[-2]
    groups = width // shard
    cond_lanes = small[1].shape[2]
    bf, f = lambda *s: jax.ShapeDtypeStruct(s, BF), lambda *s: jax.ShapeDtypeStruct(s, F32)
    out_shape = [
        bf(2, rows, width),
        f(2, 2, rows, 128),
        bf(2, 2, rows, width),
        bf(2, 3, 2, rows, HEAD_LANES),
        bf(2, heads, rows, rows),
        bf(2, 2, rows, HEAD_LANES),
        bf(2, rows, width),
        bf(2, rows, width),
        bf(2, 2, rows, width),
        bf(2, 2, rows, width),
        bf(2, 2, rows, width),
        bf(rows, width),
        bf(2, rows, width),
        f(rows, width),
        f(2, 8, width),
        f(dp_count, 8, cond_lanes),
        f(2, 24, width),
        f(rows, width),
    ]
    if fused:
        out_shape = [bf(pieces, 2, groups, shard, width)] + out_shape
    kinds = 5 * chain + 2
    many = 2 * (dp_count - 1) + 8
    slot = pltpu.VMEM((2, groups, shard, width), BF)
    scratch = [
        slot,
        slot,
        slot,
        pltpu.VMEM((rows, width), F32),
        pltpu.VMEM((2, rows, width), BF),
        pltpu.VMEM((2, rows, 128), F32),
        pltpu.VMEM((2, rows, width), BF),
        pltpu.VMEM((rows, width), F32),
        pltpu.VMEM((3, 2, rows, HEAD_LANES), BF),
        pltpu.VMEM((heads, rows, rows), BF),
        pltpu.VMEM((2, rows, HEAD_LANES), BF),
        pltpu.VMEM((rows, width), BF),
        pltpu.VMEM((2, rows, width), BF),
        pltpu.VMEM((2, rows, width), BF),
        pltpu.VMEM((rows, width), BF),
        pltpu.VMEM((4, rows, width), BF),
        pltpu.VMEM((4, rows, width), BF),
        pltpu.VMEM((rows, rows), BF),
        pltpu.VMEM((2, 24, width), F32),
        pltpu.VMEM((dp_count, 8, cond_lanes), F32),
        pltpu.VMEM((dp_count, 16, ADA_LANES), F32),
        pltpu.VMEM((dp_count, 16, ADA_LANES), F32),
        pltpu.VMEM((2, 2, 16, ADA_LANES), F32),
        pltpu.VMEM((2, 8, width), F32),
        pltpu.VMEM((rows, width), BF),
        pltpu.VMEM(small[2].shape, BF),
        pltpu.VMEM((rows, rows), BF),
        pltpu.VMEM((rows, rows), F32),
        pltpu.VMEM((rows, rows), BF),
        pltpu.VMEM((rows, 128), F32),
        pltpu.VMEM((rows, rows), BF),
        pltpu.VMEM((24, width), F32),
        pltpu.VMEM((8, ADA_LANES), F32),
        pltpu.VMEM((8, ADA_LANES), F32),
        pltpu.SemaphoreType.DMA((pieces, kinds)),
        pltpu.SemaphoreType.DMA((pieces, kinds)),
        pltpu.SemaphoreType.DMA((3,)),
        pltpu.SemaphoreType.DMA((16,)),
        pltpu.SemaphoreType.DMA((16,)),
        pltpu.SemaphoreType.DMA((48,)),
        pltpu.SemaphoreType.DMA((many,)),
        pltpu.SemaphoreType.DMA((many,)),
    ]

    def body(*refs):
        forward_kernel(cfg, *refs)

    vm = pl.BlockSpec(memory_space=pltpu.VMEM)
    hbm = pl.BlockSpec(memory_space=pl.ANY)
    result = pl.pallas_call(
        body,
        out_shape=out_shape,
        in_specs=[hbm] * len(weights) + [hbm, vm, hbm] + [vm] * 8,
        out_specs=[hbm] * len(out_shape),
        scratch_shapes=scratch,
        compiler_params=pltpu.CompilerParams(
            collective_id=0, has_side_effects=True, vmem_limit_bytes=VMEM_BYTES
        ),
        name="forward_blocks",
    )(*weights, *small)
    return result if fused else [weights[0]] + list(result)


class Scatter:
    def __init__(self, at, order, g, yr, zr, mr, red, out, ssem, rsem, osem, isem, lsem, credit):
        self.at, self.order = at, order
        self.g, self.yr, self.zr, self.mr, self.red, self.out = g, yr, zr, mr, red, out
        self.ssem, self.rsem, self.osem, self.isem, self.lsem = ssem, rsem, osem, isem, lsem
        self.credit = credit
        chain = at.chain
        need = lambda z, t: chain if t == z else (chain - t + z if t > z else chain - z + t)
        self.table = [sorted(range(chain), key=lambda t: (need(z, t), t)) for z in range(chain)]

    def slots(self, r):
        return r % self.g.shape[0], r % self.yr.shape[0]

    def target(self, i):
        return sum(jnp.where(self.at.z == z, self.table[z][i], 0) for z in range(self.at.chain))

    def own(self, r, t):
        return self.g.at[self.slots(r)[0], t * 2 + self.at.y]

    def theirs(self, r, t):
        return self.g.at[self.slots(r)[0], t * 2 + 1 - self.at.y]

    def copy(self, src, dst, r, kind, device):
        return remote(src, dst, self.ssem.at[r, kind], self.rsem.at[r, kind], device)

    def cross(self, r, t):
        return self.copy(
            self.theirs(r, t), self.yr.at[self.slots(r)[1], t], r, t, self.at.across
        )

    def up(self, r, t):
        return self.copy(
            self.own(r, t), self.zr.at[self.slots(r)[1], t], r, self.at.chain + t, self.at.above
        )

    def down(self, r, t, last=None):
        z = self.at.z - 1 if last is None else last
        place = jnp.where(t == z, self.at.chain, t)
        return self.copy(
            self.own(r, t), self.zr.at[self.slots(r)[1], place], r, 2 * self.at.chain + t, self.at.below
        )

    def to_mate(self, r):
        return self.copy(
            self.theirs(r, self.at.mate_z), self.mr.at[self.slots(r)[1]], r, 3 * self.at.chain, self.at.mate
        )

    def add(self, block, got):
        block[...] = (block[...].astype(F32) + got[...].astype(F32)).astype(BF)

    def begin(self, r):
        at, chain = self.at, self.at.chain
        if r >= self.yr.shape[0]:
            pl.semaphore_wait(self.credit.at[0], 1)

            @pl.when(at.z < chain - 1)
            def _():
                pl.semaphore_wait(self.credit.at[1], 1)

            @pl.when(at.z > 0)
            def _():
                pl.semaphore_wait(self.credit.at[2], 1)

        if r in SUM_BY_MATE:
            self.to_mate(r).start()
        for i in range(chain - 1):
            t = self.target(i)
            if r in SUM_BY_MATE:

                @pl.when(t != at.mate_z)
                def _():
                    self.cross(r, t).start()

            else:
                self.cross(r, t).start()
        if r not in SUM_BY_MATE:
            self.cross(r, at.z).start()

    def mated(self, r):
        if r in SUM_BY_MATE:
            self.to_mate(r).wait_recv()
            self.add(self.theirs(r, self.at.z), self.mr.at[self.slots(r)[1]])
            self.cross(r, self.at.z).start()

    def arrive(self, r, i):
        t = self.target(i)

        def take():
            self.cross(r, t).wait_recv()
            self.add(self.own(r, t), self.yr.at[self.slots(r)[1], t])

        if r in SUM_BY_MATE:
            pl.when(t != self.at.mate_z)(take)
        else:
            take()

    def step(self, r, k):
        z, chain = self.at.z, self.at.chain

        @pl.when((z <= k - 1) & (z < chain - 1))
        def _():
            t = chain - k + z
            if k > 1:

                @pl.when(z > 0)
                def _():
                    self.up(r, t).wait_recv()
                    self.add(self.own(r, t), self.zr.at[self.slots(r)[1], t])

            self.up(r, t).start()

        @pl.when((chain - 1 - z <= k - 1) & (z > 0))
        def _():
            t = k - chain + z
            if k > 1:

                @pl.when(z < chain - 1)
                def _():
                    self.down(r, t, last=z).wait_recv()
                    self.add(self.own(r, t), self.zr.at[self.slots(r)[1], t])

            self.down(r, t).start()

    def finish(self, r):
        at, chain = self.at, self.at.chain
        z = at.z
        slot = self.slots(r)[1]
        held = self.red.shape[0]
        if r >= held:
            self.hand_over_done(r - held)
        red = self.red.at[r % held]
        red[...] = self.own(r, z)[...].astype(F32)

        @pl.when(z > 0)
        def _():
            self.up(r, z).wait_recv()
            red[...] = red[...] + self.zr[slot, z].astype(F32)

        @pl.when(z < chain - 1)
        def _():
            self.down(r, z, last=z).wait_recv()
            red[...] = red[...] + self.zr[slot, chain].astype(F32)

        if r + self.yr.shape[0] < len(self.order):
            pl.semaphore_signal(self.credit.at[0], inc=1, device_id=at.across, device_id_type=MESH)

            @pl.when(z > 0)
            def _():
                pl.semaphore_signal(self.credit.at[1], inc=1, device_id=at.below, device_id_type=MESH)

            @pl.when(z < chain - 1)
            def _():
                pl.semaphore_signal(self.credit.at[2], inc=1, device_id=at.above, device_id_type=MESH)

        s, t = self.order[r]

        @pl.when(at.core == s)
        def _():
            self.keep(r).start()

        @pl.when(at.core != s)
        def _():
            self.hand_over(r).start()

    def keep(self, r):
        return pltpu.make_async_copy(
            self.red.at[r % self.red.shape[0]], self.out.at[self.order[r][1], self.at.core], self.lsem.at[r]
        )

    def hand_over(self, r):
        return remote(
            self.red.at[r % self.red.shape[0]],
            self.out.at[self.order[r][1], self.at.core],
            self.osem.at[r],
            self.isem.at[r],
            self.at.other,
        )

    def hand_over_done(self, r):
        s, t = self.order[r]

        @pl.when(self.at.core == s)
        def _():
            self.keep(r).wait()

        @pl.when(self.at.core != s)
        def _():
            self.hand_over(r).wait_send()

    def drain(self, r):
        z, chain = self.at.z, self.at.chain
        if r in SUM_BY_MATE:
            self.to_mate(r).wait_send()
        for t in range(chain):
            if r in SUM_BY_MATE:

                @pl.when(t != self.at.mate_z)
                def _():
                    self.cross(r, t).wait_send()

            else:
                self.cross(r, t).wait_send()

            @pl.when(t > z)
            def _():
                self.up(r, t).wait_send()

            @pl.when(t < z)
            def _():
                self.down(r, t).wait_send()

    def end(self):
        for r in range(len(self.order)):
            if r + self.red.shape[0] >= len(self.order):
                self.hand_over_done(r)
            s, t = self.order[r]

            @pl.when(self.at.core == s)
            def _():
                remote(
                    self.red.at[0],
                    self.out.at[t, 1 - self.at.core],
                    self.osem.at[r],
                    self.isem.at[r],
                    self.at.other,
                ).wait_recv()


ORDER = ((1, 2), (1, 1), (1, 0), (0, 2), (0, 1), (0, 0))


def backward_kernel(cfg, *refs):
    fused, chain, heads, head_dim = cfg
    refs = list(refs)
    w = refs.pop(0)
    (
        i_hat1, i_inv, i_n1, i_qkv, i_p, i_o, i_branch, i_hat2, i_n2, i_hid, i_slope, i_y, i_full, i_xm,
        i_e,
    ) = refs[:15]
    refs = refs[15:]
    i_dout, mod, i_small, i_cl, i_wada, kept = refs[:6]
    refs = refs[6:]
    red_out, o_dx, o_out, o_dm, o_two = refs[:5]
    refs = refs[5:]
    (
        wslot, hat1, inv, qkv, prob, o, branch, hat2, n2, hid, slope,
        d, r, dy, dpre, dattn, dqkv, do, xs, xr, g, yr, zr, mr, red,
        stats, got, out_one, in_one, dc, in_two, small, cl, wada, flips, pos, place, drop, eye, dout, gs, gr, go, gi, gl, credit, ssem, rsem, lsem, ms, mrs,
    ) = refs
    at = Place(chain)
    rows, width = d.shape
    lw = heads * head_dim
    shard = width // at.count
    half_heads = heads // 2
    scale = 1.0 / math.sqrt(head_dim)
    sends, recvs, locals_ = Numbered(ssem), Numbered(rsem), Numbered(lsem)
    at.greet()
    links = Links(at, ms, mrs)
    stats[...] = jnp.zeros_like(stats)
    dc[...] = jnp.zeros_like(dc)
    scatter = (
        Scatter(at, ORDER, g, yr, zr, mr, red, red_out, gs, gr, go, gi, gl, credit) if fused else None
    )
    slots = g.shape[0]
    waiting = {}

    def fetch(name, src, dst):
        copy = pltpu.make_async_copy(src, dst, locals_.next())
        copy.start()
        waiting.setdefault(name, []).append(copy.wait)

    def settle(name):
        for wait in waiting.pop(name, []):
            wait()

    def give(name, src, dst):
        copy = remote(src, dst, sends.next(), recvs.next(), at.other)
        copy.start()
        waiting.setdefault(name + " in", []).append(copy.wait_recv)
        waiting.setdefault(name + " out", []).append(copy.wait_send)

    def pump(*what):
        if not fused:
            return
        for name, r_, *k in what:
            if 0 <= r_ < len(ORDER):
                getattr(scatter, name)(r_, *k)

    def pump_rest(r_, start):
        for i in range(start, chain):
            pump(("arrive", r_, i))
            if i < chain - 1:
                pump(("step", r_, i + 1))
        pump(("finish", r_))

    def send_across(i):
        if i > 1:
            settle("x out %d" % (i - 2))
        copy = remote(xs.at[i % 2], xr.at[i % 2], sends.next(), recvs.next(), at.beside)
        copy.start()
        waiting.setdefault("x in %d" % i, []).append(copy.wait_recv)
        waiting.setdefault("x out %d" % i, []).append(copy.wait_send)

    def total(i, ds):
        return xs[i % 2, ds, :].astype(F32) + xr[i % 2, ds, :].astype(F32)

    def stat(s, row, value):
        stats[s, row : row + 1, :] = jnp.sum(value, axis=0, keepdims=True)

    zero8 = lambda: jnp.zeros((8, width), F32)
    spans = [slice(k * HEAD_LANES, (k + 1) * HEAD_LANES) for k in range(3)]
    spot = lambda half: jnp.where(half == at.core, 0, 2)

    def load(name, s):
        src, dst = {
            "slope": (i_slope, slope),
            "hid": (i_hid, hid),
            "n1": (i_n1, hid),
            "n2": (i_n2, n2),
            "hat2": (i_hat2, hat2),
            "inv": (i_inv, inv),
            "branch": (i_branch, branch),
            "p": (i_p, prob),
            "qkv": (i_qkv, qkv),
            "o": (i_o, o),
            "hat1": (i_hat1, hat1),
        }[name]
        fetch(name, src.at[s], dst)

    def weight(p, slot):
        fetch("w%d" % slot, w.at[p], wslot.at[slot])

    def product(r_, parts):
        slot = r_ % slots
        if r_ >= slots:
            if fused:
                scatter.drain(r_ - slots)
            else:
                settle("g%d" % (r_ - slots))
        for j in range(width // 384):
            cols = slice(j * 384, (j + 1) * 384)
            value = 0.0
            for lhs, rhs in parts(j):
                value = value + tn(lhs, rhs)
            g[slot, :, :, cols] = value.astype(BF).reshape(g.shape[1], g.shape[2], 384)
        if not fused:
            s, t = ORDER[r_]
            fetch("g%d" % r_, g.at[slot], red_out.at[s * 3 + t])

    def cols_of(ref, j):
        return flat(ref[0:2, :, j * 384 : (j + 1) * 384])

    down_slot, up_slot, att_slot = (1, 0), (0, 1), (1, 0)

    def base(s):
        return 0 if s == 1 else 3

    def exchange(s):
        return 0 if s == 1 else 2

    def back_gate(s):
        settle("dy out")
        if s == 0:
            settle("y")

        def one(ds, c):
            a, b = c
            dv = d[ds, :]
            v = (dv * mod[s, 5:6, :]).astype(BF)
            dy[0, ds, :] = v
            if s == 0:
                a = a + column_sum(dv * xs[2, ds, :].astype(F32))
            return (a, b + column_sum(v.astype(F32)))

        a, b = by_rows(rows, one, (zero8(), zero8()))
        if s == 0:
            stat(s, 5, a)
        stat(s, 8, b)
        give("dy", dy.at[0], dy.at[1])

    def back_hidden(s):
        slot = down_slot[s]
        settle("w%d" % slot)
        settle("slope")
        settle("dpre out")
        for half in range(2):
            for j in range(3):
                cols = slice(j * 384, (j + 1) * 384)
                v = (nn(dy[0], flat(wslot[slot, half, :, :, cols])) * slope[half, :, cols].astype(F32)).astype(BF)
                dpre[spot(half), :, cols] = v
                stats[s, 10 + half : 11 + half, cols] = jnp.sum(v.astype(F32), axis=0, keepdims=True)
        give("dpre", dpre.at[2], dpre.at[1])

    def down_product(s):
        settle("dy in")
        settle("hid")
        product(base(s), lambda j: [(flat(dy[...]), cols_of(hid, j))])
        load("n1", s)

    def back_up(s):
        slot = up_slot[s]
        xi = exchange(s)
        settle("w%d" % slot)
        if xi > 1:
            settle("x out %d" % (xi - 2))
        xs[xi % 2] = (
            nt(dpre[spot(0)], flat(wslot[slot, 0])) + nt(dpre[spot(1)], flat(wslot[slot, 1]))
        ).astype(BF)
        send_across(xi)

    def up_product(s):
        settle("dpre in")
        settle("n2")
        product(base(s) + 1, lambda j: [(flat(n2[...]), cols_of(dpre, j))])

    def back_norm_two(s):
        xi = exchange(s)
        settle("x in %d" % xi)
        settle("hat2")
        settle("inv")
        settle("branch")
        settle("dattn out")

        def two(ds, c):
            c0, c1, c2, c3 = c
            dn = total(xi, ds)
            hv = hat2[ds, :].astype(F32)
            dxm = d[ds, :] + layer_norm_back(dn * (1.0 + mod[s, 4:5, :]), hv, inv[1, ds, 0:1])
            d[ds, :] = dxm
            da = (dxm * mod[s, 2:3, :]).astype(BF)
            dattn[0, ds, :] = da
            return (
                c0 + column_sum(dn),
                c1 + column_sum(dn * hv),
                c2 + column_sum(dxm * branch[ds, :].astype(F32)),
                c3 + column_sum(da.astype(F32)),
            )

        c0, c1, c2, c3 = by_rows(rows, two, (zero8(),) * 4)
        stat(s, 3, c0)
        stat(s, 4, c1)
        stat(s, 2, c2)
        stat(s, 9, c3)
        give("dattn", dattn.at[0], dattn.at[1])

    def back_heads(s, half):
        slot = att_slot[s]
        if half == 0:
            settle("w%d" % slot)
            settle("p")
            settle("qkv")
            settle("dqkv out")
        if True:
            do[half] = nn(dattn[0], flat(wslot[slot, half, :, :, :HEAD_LANES])).astype(BF)
            r[...] = jnp.zeros_like(r)

            def head(i, c):
                index = half * half_heads + i
                mask = head_mask(i, head_dim)
                low_mask = mask.astype(BF)
                p = prob[index]
                dom = do[half] * low_mask
                r[:, spans[2]] = r[:, spans[2]] + tn(p, dom)
                ds = nt(dom, qkv[2, half])
                pf = p.astype(F32)
                dz = (pf * (ds - jnp.sum(pf * ds, axis=-1, keepdims=True))).astype(BF)
                r[:, spans[0]] = r[:, spans[0]] + nn(dz, qkv[1, half]) * mask
                r[:, spans[1]] = r[:, spans[1]] + tn(dz, qkv[0, half]) * mask
                square = nn(dz, flips[s])
                high = square.astype(BF)
                if s == 0:
                    low = (square - high.astype(F32)).astype(BF)
                    square = tn(high, pos[...]) + tn(low, pos[...])
                else:
                    square = tn(high, eye[...])
                wide = jnp.concatenate([square, jnp.zeros_like(square)], axis=1)
                skew = pltpu.roll(wide, 0, 1, stride=1, stride_axis=0)
                stats[s, pl.ds(16 + index, 1), : 2 * rows] = jnp.sum(skew, axis=0, keepdims=True)
                return c

            lax.fori_loop(0, half_heads, head, 0)
            where = spot(half)

            def gather_rows(ds, c):
                blank = jnp.zeros((TILE, HEAD_LANES), F32)
                v = 0.0
                for kind, shift, factor in ((0, 288, scale), (1, 576, scale), (2, 864, 1.0)):
                    part = jnp.concatenate([r[ds, spans[kind]] * factor, blank, blank], axis=1)
                    v = v + pltpu.roll(part, shift, 1)
                v = v.astype(BF)
                dqkv[where, ds, :] = v
                return c + column_sum(v.astype(F32))

            stat(s, 12 + half, by_rows(rows, gather_rows, zero8()))
        if half == 1:
            give("dqkv", dqkv.at[2], dqkv.at[1])

    def back_qkv(s):
        slot = att_slot[s]
        xi = exchange(s) + 1
        if xi > 1:
            settle("x out %d" % (xi - 2))
        xs[xi % 2] = (
            nt(dqkv[spot(0)], flat(wslot[slot, 0])) + nt(dqkv[spot(1)], flat(wslot[slot, 1]))
        ).astype(BF)
        send_across(xi)

    def att_product(s):
        settle("dqkv in")
        settle("dattn in")
        settle("n1")
        settle("o")
        product(
            base(s) + 2,
            lambda j: [(flat(hid[...]), cols_of(dqkv, j))]
            + ([(flat(dattn[...]), flat(o[...]))] if j == 0 else []),
        )

    def back_norm_one(s):
        xs_free = exchange(s) + 1
        settle("x in %d" % xs_free)
        settle("hat1")

        def three(ds, c):
            c0, c1, c2 = c
            dn = total(xs_free, ds)
            hv = hat1[ds, :].astype(F32)
            dx = d[ds, :] + layer_norm_back(dn * (1.0 + mod[s, 1:2, :]), hv, inv[0, ds, 0:1])
            d[ds, :] = dx
            return (c0 + column_sum(dn), c1 + column_sum(dn * hv), c2 + column_sum(dx * drop[ds, 0:1]))

        c0, c1, c2 = by_rows(rows, three, (zero8(),) * 3)
        stat(s, 0, c0)
        stat(s, 1, c1)
        stat(s, 14, c2)
        to_section("dx", s, d, o_dx)

    def to_section(name, s, src, out):
        here = pltpu.make_async_copy(src, out.at[at.core], locals_.next())
        ss, rs = sends.next(), recvs.next()

        @pl.when(at.core == s)
        def _():
            here.start()

        @pl.when(at.core != s)
        def _():
            remote(src, out.at[at.core], ss, rs, at.other).start()

        def sent():
            @pl.when(at.core == s)
            def _():
                here.wait()

            @pl.when(at.core != s)
            def _():
                remote(src, out.at[at.core], ss, rs, at.other).wait_send()

        def arrived():
            @pl.when(at.core == s)
            def _():
                remote(src, out.at[1 - at.core], ss, rs, at.other).wait_recv()

        waiting.setdefault(name, []).append(sent)
        waiting.setdefault("end", []).append(arrived)

    def project_down():
        settle("w0")
        settle("full")
        xs[2] = (nt(dqkv[0], flat(wslot[0, 0])) + nt(dqkv[1], flat(wslot[0, 1]))).astype(BF)
        copy = remote(xs.at[2], xr.at[2], sends.next(), recvs.next(), at.beside)
        copy.start()
        waiting.setdefault("y in", []).append(copy.wait_recv)
        waiting.setdefault("y out", []).append(copy.wait_send)

    def end_forward():
        settle("y in")
        settle("y out")
        settle("xm")
        settle("small")

        def body(ds, c):
            v = xs[2, ds, :].astype(F32) + xr[2, ds, :].astype(F32) + small[1, 9:10, :]
            r[ds, :] = r[ds, :] + mod[1, 5:6, :] * v
            return c + column_sum(dout[ds, :].astype(F32) * v)

        stat(1, 5, by_rows(rows, body, zero8()))
        to_section("result", 1, r, o_out)

    def sums_begin():
        stats[0, 14:15, :] = stats[1, 14:15, :]
        return links.copy(stats.at[1 - at.core], got, at.other)

    def sums_share(copy):
        copy.wait_recv()
        top = stats[at.core, 8:16, :] + got[8:16, :]
        low = stats[at.core, 16:24, :] + got[16:24, :]
        row = lax.broadcasted_iota(jnp.int32, (8, ADA_LANES), 0)
        lane = lax.broadcasted_iota(jnp.int32, (8, ADA_LANES), 1)

        def cut(value):
            value = jnp.where(
                at.head == 0, value[:, :ADA_LANES], pltpu.roll(value, width - lw, 1)[:, :ADA_LANES]
            )
            return jnp.where((row < 6) & (lane < lw), value, 0.0)

        own, other = cut(stats[at.core, 0:8, :]), cut(got[0:8, :])
        both_ = [jnp.where(at.core == 0, own, other), jnp.where(at.core == 0, other, own)]
        both_ = jnp.concatenate(both_, axis=0).astype(BF)
        for j in range(at.count):
            out_one[j, :, :ADA_LANES] = both_
        packed = pack_sums(top, low).astype(BF)
        for j in range(at.count):
            part = (j % 8) * 128
            out_one[j, :, ADA_LANES:] = packed[:, part : part + 128]
        in_one[pl.ds(at.dp, 1)] = out_one[pl.ds(at.dp, 1)]
        return links.to_all(lambda peer: out_one.at[peer], in_one.at[at.dp])

    def cond_terms(copies):
        for copy in copies:
            copy.wait_recv()
        settle("wada")
        settle("cl")
        fetch("dm", in_one.at[:, :, pl.ds(0, ADA_LANES)], o_dm)
        lhs = flat(in_one[:, :, :lw])
        row = lax.rem(lax.broadcasted_iota(jnp.int32, (lhs.shape[0], 1), 0), 8)
        total_ = jnp.zeros((lhs.shape[0], shard), F32)
        for k in range(6):
            total_ = total_ + jnp.where(row == k, nt(lhs, wada[k]), 0.0)
        total_ = total_.reshape(at.count, 16, shard)
        for m in range(2):
            dc[at.core, at.head, m, :, :shard] = jnp.sum(total_[:, m * 8 : (m + 1) * 8, :], axis=1)
        return links.around(dc)

    def cond_share(copies):
        for copy in copies:
            copy.wait_recv()
        cond_lanes = dc.shape[4]
        for m in range(2):
            value = (dc[0, 0, m] + dc[0, 1, m]) + (dc[1, 0, m] + dc[1, 1, m])
            v = cl[:, m, :]
            sig = 1.0 / (1.0 + jnp.exp(-v))
            parts.append(value * (sig * (1.0 + v * (1.0 - sig))))
        value = in_one[0, :, ADA_LANES:].astype(F32)
        for j in range(1, at.count):
            value = value + in_one[j, :, ADA_LANES:].astype(F32)
        grads = jnp.concatenate(parts, axis=0)
        in_two[at.dp, :, :cond_lanes] = grads.astype(BF)
        in_two[at.dp, 0:16, cond_lanes:] = value.astype(BF)
        return links.to_all(lambda peer: in_two.at[at.dp], in_two.at[at.dp])

    def cond_end(copies):
        for copy in copies:
            copy.wait_recv()
        fetch("two", in_two, o_two)

    parts = []
    fetch("dout", i_dout.at[at.core], dout)
    load("hid", 1)
    weight(5, 0)
    load("slope", 1)
    weight(4, 1)
    for name in ("n2", "hat2", "inv", "branch", "p", "qkv", "o", "hat1"):
        load(name, 1)
    for name, src, dst in (
        ("y", i_y, xs.at[2]),
        ("small", i_small, small),
        ("cl", i_cl, cl),
        ("wada", i_wada, wada),
    ):
        fetch(name, src, dst)

    to_section("e", 0, i_e, o_out)
    settle("dout")

    def start_rows(ds, c):
        d[ds, :] = dout[ds, :].astype(F32)
        return c

    by_rows(rows, start_rows, 0)

    def to_encoder():
        r[...] = tn(place[...], d[...].astype(BF))
        settle("dx")

        def move(ds, c):
            d[ds, :] = r[ds, :]
            return c

        by_rows(rows, move, 0)

    back_gate(1)
    down_product(1)
    pump(("begin", 0))
    back_hidden(1)
    weight(3, 0)
    load("slope", 0)
    back_up(1)
    weight(2, 1)
    up_product(1)
    load("n2", 0)
    pump(("begin", 1))
    pump(("arrive", 0, 0), ("step", 0, 1), ("arrive", 0, 1), ("step", 0, 2))
    spread_masks(kept[at.core].astype(F32), place, pos, drop)
    eye[...] = diagonal(rows)
    flips[1] = diagonal(rows, True)
    flips[0] = nn(pos[...], flips[1]).astype(BF)
    back_norm_two(1)
    load("hat2", 0)
    load("branch", 0)
    back_heads(1, 0)
    pump(("arrive", 0, 2), ("step", 0, 3))
    back_heads(1, 1)
    load("p", 0)
    load("qkv", 0)
    back_qkv(1)
    weight(1, 0)
    pump(("arrive", 0, 3))
    att_product(1)
    load("hid", 0)
    load("o", 0)
    pump(("begin", 2))
    pump(("mated", 1), ("arrive", 1, 0), ("step", 1, 1), ("finish", 0))
    back_norm_one(1)
    load("hat1", 0)
    load("inv", 0)
    to_encoder()
    back_gate(0)
    pump(("arrive", 1, 1), ("step", 1, 2))
    back_hidden(0)
    weight(0, 1)
    down_product(0)
    pump(("begin", 3))
    pump(("arrive", 1, 2), ("step", 1, 3))
    back_up(0)
    weight(5, 0)
    pump(("arrive", 1, 3), ("mated", 2), ("arrive", 2, 0), ("step", 2, 1), ("finish", 1))
    up_product(0)
    pump(("begin", 4))
    pump(("arrive", 2, 1), ("step", 2, 2))
    back_norm_two(0)
    back_heads(0, 0)
    pump(("arrive", 2, 2), ("step", 2, 3))
    back_heads(0, 1)
    back_qkv(0)
    fetch("xm", i_xm, r)
    pump(("arrive", 2, 3), ("mated", 3), ("arrive", 3, 0), ("step", 3, 1), ("finish", 2))
    att_product(0)
    fetch("full", i_full, dqkv.at[0:2])
    pump(("begin", 5))
    pump(("arrive", 3, 1), ("step", 3, 2))
    project_down()
    back_norm_one(0)
    pump(("arrive", 3, 2), ("step", 3, 3))
    end_forward()
    copy = sums_begin()
    pump(("arrive", 3, 3), ("mated", 4), ("arrive", 4, 0), ("step", 4, 1), ("finish", 3))
    copies = sums_share(copy)
    pump(("arrive", 4, 1), ("step", 4, 2), ("arrive", 4, 2), ("step", 4, 3), ("arrive", 4, 3))
    copies = cond_terms(copies)
    pump(("arrive", 5, 0), ("step", 5, 1), ("finish", 4))
    copies = cond_share(copies)
    pump(("arrive", 5, 1), ("step", 5, 2), ("arrive", 5, 2), ("step", 5, 3), ("arrive", 5, 3))
    cond_end(copies)
    pump(("finish", 5))
    if fused:
        for r_ in range(len(ORDER) - slots, len(ORDER)):
            scatter.drain(r_)
        scatter.end()
    for wait in links.waiting:
        wait()
    for name in list(waiting):
        settle(name)


def backward_call(cfg, w, saved, small):
    fused, chain, heads, head_dim = cfg
    _, rows, width = small[0].shape
    pieces, _, groups, shard, _ = w.shape
    count, _, cond_lanes = small[3].shape
    many = 2 * (count - 1) + 6
    each = 128
    bf, f = lambda *s: pltpu.VMEM(s, BF), lambda *s: pltpu.VMEM(s, F32)
    dma = lambda *s: pltpu.SemaphoreType.DMA(s)
    out_shape = [
        jax.ShapeDtypeStruct((3, 2, shard, width), F32)
        if fused
        else jax.ShapeDtypeStruct((pieces, groups, shard, width), BF),
        jax.ShapeDtypeStruct((2, rows, width), F32),
        jax.ShapeDtypeStruct((2, rows, width), F32),
        jax.ShapeDtypeStruct((count, 16, ADA_LANES), BF),
        jax.ShapeDtypeStruct((count, 2 * count, cond_lanes + each), BF),
    ]
    some = 3 if fused else 1
    links = chain if fused else 1
    block = shard if fused else 16
    scratch = [
        bf(2, 2, groups, shard, width),
        bf(rows, width),
        f(2, rows, 128),
        bf(3, 2, rows, HEAD_LANES),
        bf(heads, rows, rows),
        bf(2, rows, HEAD_LANES),
        bf(rows, width),
        bf(rows, width),
        bf(2, rows, width),
        bf(2, rows, width),
        bf(2, rows, width),
        f(rows, width),
        f(rows, width),
        bf(2, rows, width),
        bf(3, rows, width),
        bf(2, rows, width),
        bf(3, rows, width),
        bf(2, rows, HEAD_LANES),
        bf(3, rows, width),
        bf(3, rows, width),
        bf(4, groups, shard, width),
        bf(some, links, block, width),
        bf(some, links + 1, block, width),
        bf(some, block, width),
        f(2, block, width),
        f(2, 24, width),
        f(24, width),
        bf(count, 16, ADA_LANES + each),
        bf(count, 16, ADA_LANES + each),
        f(2, 2, 2, count, cond_lanes),
        bf(count, 2 * count, cond_lanes + each),
        f(2, 24, width),
        f(count, 8, cond_lanes),
        bf(*small[4].shape),
        bf(2, rows, rows),
        bf(rows, rows),
        bf(rows, rows),
        f(rows, 128),
        bf(rows, rows),
        bf(rows, width),
        dma(6, 3 * links + 1),
        dma(6, 3 * links + 1),
        dma(6),
        dma(6),
        dma(6),
        pltpu.SemaphoreType.REGULAR((3,)),
        dma(20),
        dma(20),
        dma(56),
        dma(many),
        dma(many),
    ]

    def body(*refs):
        backward_kernel(cfg, *refs)

    vm = pl.BlockSpec(memory_space=pltpu.VMEM)
    hbm = pl.BlockSpec(memory_space=pl.ANY)
    return pl.pallas_call(
        body,
        out_shape=out_shape,
        in_specs=[hbm] * (1 + len(saved)) + [hbm, vm, hbm, hbm, hbm, vm],
        out_specs=[hbm] * len(out_shape),
        scratch_shapes=scratch,
        compiler_params=pltpu.CompilerParams(
            collective_id=1, has_side_effects=True, vmem_limit_bytes=VMEM_BYTES
        ),
        name="backward_blocks",
    )(w, *saved, *small)


def unpack_two(two, count, cond_lanes):
    top, rel = unpack_sums(
        jnp.concatenate([two[j, 0:16, cond_lanes:] for j in range(8)], axis=1).astype(F32)
    )
    blocks = [
        [two[j, m * count : (m + 1) * count, :cond_lanes].astype(F32) for m in range(2)]
        for j in range(count)
    ]
    return top, rel, blocks


def finish_kernel(cfg, red, two, dm, cl, *refs):
    _, _, heads, head_dim = cfg
    g_qkv, g_out, g_up, g_down, g_ada, g_class, b_qv, b_out, b_up, b_down, b_ada, rel, mask = refs[:13]
    att, rest, t_qkv, t_out, t_ada, t_class, sems = refs[13:]
    head = lax.axis_index("head")
    _, _, shard, width = red.shape
    lw = heads * head_dim
    hw = lw // 2
    count, _, cond_lanes = cl.shape
    slots = Numbered(sems)
    waits = []

    def move(src, dst):
        copy = pltpu.make_async_copy(src, dst, slots.next())
        copy.start()
        waits.append(copy.wait)
        return copy

    first = pltpu.make_async_copy(red.at[0], att, slots.next())
    first.start()
    second = pltpu.make_async_copy(red.at[pl.ds(1, 2)], rest, slots.next())
    second.start()

    def half(value):
        moved = pltpu.roll(value, width - lw, 1)
        return jnp.where(head == 0, value[:, :ADA_LANES], moved[:, :ADA_LANES])

    rows, table, blocks = unpack_two(two[...], count, cond_lanes)
    picks, grads, parts = [], [], []
    for m in range(2):
        block = cl[:, m, :]
        place = lax.broadcasted_iota(jnp.int32, block.shape, 1)
        label = jnp.sum(jnp.where(place == shard, block, 0.0), axis=1, keepdims=True)
        span = lax.broadcasted_iota(jnp.int32, (count, t_class.shape[1]), 1).astype(F32)
        picks.append(jnp.where(span == label, 1.0, 0.0))
        total = jnp.zeros((count, width), F32)
        for j in range(count):
            part = jnp.where(place < shard, blocks[j][m], 0.0)
            blank = jnp.zeros((count, width - part.shape[1]), F32)
            part = jnp.concatenate([part, blank], axis=1)
            total = total + (pltpu.roll(part, j * shard, 1) if j else part)
        grads.append(half(total))
        parts.append(silu(block))
    pick_all = jnp.concatenate(picks, axis=0).astype(BF)
    a, b, c = thirds(jnp.concatenate(grads, axis=0))
    t_class[...] = (tn(a, pick_all) + (tn(b, pick_all) + tn(c, pick_all)))[:lw, :]
    move(t_class, g_class)
    second.wait()
    for side in range(2):
        move(rest.at[0, side], g_up.at[0, :, pl.ds(side * width, width)])
        move(rest.at[1, side], g_down.at[:, pl.ds(side * width, width)])
    a, b, c = thirds(jnp.concatenate(parts, axis=0))
    for k in range(6):
        pair = jnp.concatenate([dm[:, k, :], dm[:, 8 + k, :]], axis=0).astype(BF)
        t_ada[k] = (tn(a, pair) + (tn(b, pair) + tn(c, pair)))[:shard, :lw]
    move(t_ada, g_ada)
    first.wait()
    wide = lax.broadcasted_iota(jnp.int32, (shard, width), 1)
    for k in range(4):
        value = 0.0
        for side in range(2):
            moved = pltpu.roll(att[side], (side - k) * hw % width, 1) if side != k else att[side]
            value = value + jnp.where((wide >= side * hw) & (wide < (side + 1) * hw), moved, 0.0)
        if k == 0:
            t_out[...] = value[:, :lw]
        else:
            t_qkv[k - 1] = value[:, :lw]
    move(t_out, g_out)
    move(t_qkv, g_qkv)
    for side in range(2):
        b_up[:, side * width : (side + 1) * width] = rows[2 + side : 3 + side, :]
    lane = lax.broadcasted_iota(jnp.int32, (8, width), 1)
    for k, at in enumerate((1, 3)):
        own = jnp.where(lane < hw, pltpu.roll(rows, width - at * hw, 1), 0.0)
        b_qv[0, k : k + 1, :] = (own[4:5] + pltpu.roll(own, hw, 1)[5:6])[:, :lw]
    cut = half(rows)
    b_down[...] = cut[0:1, :lw]
    b_out[...] = cut[1:2, :lw]
    mask[...] = cut[6:7, :lw]
    rel[0] = table[:, : rel.shape[2]]
    value = dm[0].astype(F32)
    for j in range(1, count):
        value = value + dm[j].astype(F32)
    b_ada[:, 0, :] = (value[0:8] + value[8:16])[0:6, :lw]
    for wait in waits:
        wait()


def finish_call(cfg, classes, length, red, two, dm, cl):
    _, _, heads, head_dim = cfg
    lw = heads * head_dim
    shard, width = red.shape[2:]
    f = lambda *s: jax.ShapeDtypeStruct(s, F32)

    def body(*refs):
        finish_kernel(cfg, *refs)

    vm = pl.BlockSpec(memory_space=pltpu.VMEM)
    hbm = pl.BlockSpec(memory_space=pl.ANY)
    large = [
        f(3, shard, lw),
        f(shard, lw),
        f(1, shard, 2 * width),
        f(shard, 2 * width),
        f(6, shard, lw),
        f(lw, classes),
    ]
    small = [
        f(1, 2, lw),
        f(1, lw),
        f(1, 2 * width),
        f(1, lw),
        f(6, 1, lw),
        f(1, heads, 2 * length - 1),
        f(1, lw),
    ]
    return pl.pallas_call(
        body,
        out_shape=large + small,
        in_specs=[hbm, vm, vm, vm],
        out_specs=[hbm] * len(large) + [vm] * len(small),
        scratch_shapes=[
            pltpu.VMEM((2, shard, width), F32),
            pltpu.VMEM((2, 2, shard, width), F32),
            pltpu.VMEM((3, shard, lw), F32),
            pltpu.VMEM((shard, lw), F32),
            pltpu.VMEM((6, shard, lw), F32),
            pltpu.VMEM((lw, classes), F32),
            pltpu.SemaphoreType.DMA((10,)),
        ],
        compiler_params=pltpu.CompilerParams(vmem_limit_bytes=VMEM_BYTES),
        name="last_layouts",
    )(red, two, dm, cl)


def per_device(
    tokens,
    kept_mask,
    timesteps,
    labels,
    w_qkv,
    b_qv,
    w_out,
    b_out,
    w_up,
    b_up,
    w_down,
    b_down,
    w_ada,
    b_ada,
    rel_table,
    mask_token,
    class_table,
    out_grad,
):
    micro, rows, width = tokens.shape
    length = kept_mask.shape[2]
    classes = class_table.shape[0]
    heads = rel_table.shape[1]
    lw = w_qkv.shape[3]
    head_dim = lw // heads
    hw = lw // 2
    ff = w_up.shape[2]
    fw = ff // 2
    dp_count = lax.axis_size("dp")
    c = lax.axis_index("section")
    dp = lax.axis_index("dp")
    h = lax.axis_index("head")

    qkv = jnp.transpose(w_qkv[0], (1, 0, 2))
    out_t = w_out[0].T
    down_t = w_down[0].T
    fr = width // dp_count

    label_pick = (labels == jnp.arange(classes)[None, :]).astype(BF)
    cond = nn(label_pick, class_table) + time_features(timesteps[:, 0], width)
    blocks = jnp.transpose(cond.reshape(micro, dp_count, fr), (1, 0, 2))
    tags = jnp.broadcast_to(labels.astype(F32)[None], (dp_count, micro, 1))
    cond_lanes = -(-(fr + 1) // 128) * 128
    blocks = jnp.concatenate([blocks, tags], axis=2)
    blocks = jnp.pad(blocks, ((0, 0), (0, 8 - micro), (0, cond_lanes - fr - 1)))
    ada = jnp.transpose(w_ada[0], (1, 0, 2))

    fused = dp_count == 8 and fr % 16 == 0
    cfg = (fused, dp_count // 2, heads, head_dim)
    att = []
    for half in range(2):
        at = slice(half * hw, (half + 1) * hw)
        att.append(jnp.concatenate([out_t[:, at], qkv[0][:, at], qkv[1][:, at], qkv[2][:, at]], axis=1))
    if fused:
        source_w = (jnp.stack(att), w_up, down_t)
    else:
        halves = []
        for half in range(2):
            fat = slice(half * fw, (half + 1) * fw)
            halves.append(jnp.stack([att[half], w_up[0][:, fat], down_t[:, fat]]))
        other_w = swap(mine(1 - c, halves), "section")
        own_w = mine(c, halves)
        own_w = jnp.concatenate([pick(c, own_w, other_w), pick(c, other_w, own_w)])
        half_w_ = lax.all_gather(own_w, "dp", axis=1, tiled=True)
        other_w = swap(half_w_, "section")
        source_w = jnp.stack([pick(c, half_w_, other_w), pick(c, other_w, half_w_)], axis=1)
        source_w = (source_w.reshape(6, 2, 8, width // 8, 4 * hw),)
    small_in = (
        tokens,
        blocks,
        ada,
        b_ada,
        kept_mask,
        b_qv,
        b_out,
        b_down,
        b_up,
        rel_table,
        mask_token[None, :],
    )
    full, *saved, mod, cond_all, small_all, enc = forward_call(cfg, source_w, small_in, dp_count)
    saved.append(enc)
    small_back = (out_grad, mod, small_all, cond_all, ada, kept_mask)
    red, dx, outs, dm, two = backward_call(cfg, full, saved, small_back)

    if fused:
        last = finish_call(cfg, classes, length, red, two, dm, cond_all)
        g_qkv, g_out, g_up, g_down, g_ada, g_class = last[:6]
        g_b_qv, g_b_out, g_b_up, g_b_down, g_b_ada, g_rel, g_mask = last[6:]
        return (
            outs[None],
            dx[None],
            jnp.transpose(g_qkv, (1, 0, 2))[None],
            g_b_qv,
            g_out.T[None],
            g_b_out,
            g_up,
            g_b_up,
            g_down.T[None],
            g_b_down,
            jnp.transpose(g_ada, (1, 0, 2))[None],
            jnp.transpose(g_b_ada, (1, 0, 2)),
            g_rel,
            g_mask[0],
            g_class.T,
        )
    red = lax.psum_scatter(
        red.reshape(6, width, 4 * hw), "dp", scatter_dimension=1, tiled=True
    ).astype(F32)
    red = red.reshape(2, 3, fr, 4 * hw)
    g_own = mine(c, red)
    g_got = swap(mine(1 - c, red), "section")
    g0, g1 = pick(c, g_own, g_got), pick(c, g_got, g_own)
    g_qkv = jnp.stack(
        [
            jnp.concatenate([g0[0][:, i * hw : (i + 1) * hw], g1[0][:, i * hw : (i + 1) * hw]], axis=1)
            for i in (1, 2, 3)
        ],
        axis=1,
    )
    g_out = jnp.concatenate([g0[0][:, :hw], g1[0][:, :hw]], axis=1).T
    g_up = jnp.concatenate([g0[1], g1[1]], axis=1)
    g_down = jnp.concatenate([g0[2], g1[2]], axis=1).T

    cond_lanes = cond_all.shape[2]
    sums, rel_rows, dc = unpack_two(two, dp_count, cond_lanes)
    dc = jnp.stack([jnp.stack(pair) for pair in dc])
    half_w = width // 2

    def half(v):
        return lax.dynamic_slice_in_dim(v, h * half_w, half_w, v.ndim - 1)

    g_b_qv = jnp.stack(
        [
            jnp.concatenate([sums[4, at * hw : (at + 1) * hw], sums[5, at * hw : (at + 1) * hw]])
            for at in (1, 3)
        ]
    )
    g_b_up = sums[2:4, :fw].reshape(-1)
    g_rel = rel_rows[:, : 2 * length - 1]

    dm = dm.astype(F32).reshape(dp_count, micro, 8, ADA_LANES)[:, :, :6, :lw]
    cond_part = jax.nn.silu(cond_all[:, :micro, :fr])
    g_ada = jnp.einsum("jmf,jmke->fke", cond_part, dm, precision=PRECISE)
    g_b_ada = jnp.sum(dm, axis=(0, 1))
    labels_all = cond_all[:, :micro, fr].astype(jnp.int32).T.reshape(-1)
    dcond = jnp.transpose(dc[..., :fr], (1, 2, 0, 3)).reshape(micro * dp_count, width)
    pick_all = (labels_all[:, None] == jnp.arange(classes)[None, :]).astype(F32)
    g_class = jnp.einsum("ic,id->cd", pick_all, half(dcond), precision=PRECISE)

    return (
        outs[None],
        dx[None],
        g_qkv[None],
        g_b_qv[None],
        g_out[None],
        half(sums[1])[None],
        g_up[None],
        g_b_up[None],
        g_down[None],
        half(sums[0])[None],
        g_ada[None],
        g_b_ada[None],
        g_rel[None],
        half(sums[6]),
        g_class,
    )


def solution(mesh):
    placed = (
        P(None, "dp", None),
        P(None, "dp", None),
        P(None, "dp"),
        P(None, "dp"),
        P("section", "dp", None, "head"),
        P("section", None, "head"),
        P("section", "head", "dp"),
        P("section", None),
        P("section", "dp", "head"),
        P("section", "head"),
        P("section", "head", "dp"),
        P("section", None),
        P("section", "dp", None, "head"),
        P("section", None, "head"),
        P("section", "head", None),
        P(),
        P(),
        P(None, "dp", None),
    )
    return jax.shard_map(
        per_device,
        mesh=mesh,
        in_specs=placed,
        out_specs=(
            P("section", None, "dp", None),
            P("section", None, "dp", None),
            P("section", "dp", None, "head"),
            P("section", None, "head"),
            P("section", "head", "dp"),
            P("section", "head"),
            P("section", "dp", "head"),
            P("section", "head"),
            P("section", "head", "dp"),
            P("section", "head"),
            P("section", "dp", None, "head"),
            P("section", None, "head"),
            P("section", "head", None),
            P("head"),
            P(None, "head"),
        ),
        check_vma=False,
    )
```

```python
import math

import jax
import jax.numpy as jnp
from jax import lax
from jax.experimental import pallas as pl
from jax.experimental.pallas import tpu as pltpu
from jax.sharding import PartitionSpec as P

PRECISE = lax.Precision.HIGHEST
EPSILON = 1e-06
NEGATIVE = -1e30
MESH = pl.DeviceIdType.MESH
BF = jnp.bfloat16
VMEM_BYTES = 62 * 1024 * 1024
F32 = jnp.float32


def time_features(step_ids, model_width):
    half_width = model_width // 2
    frequency = jnp.exp(-math.log(10000.0) * jnp.arange(half_width).astype(F32) / half_width)
    angles = step_ids.astype(F32)[..., None] * frequency
    return jnp.concatenate([jnp.cos(angles), jnp.sin(angles)], axis=-1)


def swap(value, axis):
    return lax.ppermute(value, axis, [(0, 1), (1, 0)])


def pick(index, first, second):
    return jnp.where(index == 0, first, second)


def mine(c, pair):
    return pick(c, pair[0], pair[1])


def both(value):
    c = lax.axis_index("section")
    got = swap(value, "section")
    return pick(c, value, got), pick(c, got, value)


HEAD_LANES = 384
ADA_LANES = 640


def nn(a, b):
    return lax.dot_general(a, b, (((1,), (0,)), ((), ())), preferred_element_type=F32)


def nt(a, b):
    return lax.dot_general(a, b, (((1,), (1,)), ((), ())), preferred_element_type=F32)


def tn(a, b):
    return lax.dot_general(a, b, (((0,), (0,)), ((), ())), preferred_element_type=F32)


def flat(value):
    return value.reshape(value.shape[0] * value.shape[1], value.shape[2])


GELU_SCALE = math.sqrt(2.0 / math.pi)


def gelu_both(v):
    t = jnp.tanh(GELU_SCALE * (v + 0.044715 * v * v * v))
    slope = 0.5 * (1.0 + t) + (0.5 * GELU_SCALE) * v * (1.0 - t * t) * (1.0 + 0.134145 * v * v)
    return 0.5 * v * (1.0 + t), slope


class Place:
    def __init__(self, chain):
        self.chain = chain
        self.core = lax.axis_index("section")
        self.dp = lax.axis_index("dp")
        self.head = lax.axis_index("head")
        self.z = self.dp // 2
        self.y = self.dp % 2
        self.mate_z = self.z + 1 - 2 * (self.z % 2)
        self.above = (self.core, self.dp + 2, self.head)
        self.below = (self.core, self.dp - 2, self.head)
        self.across = (self.core, self.z * 2 + 1 - self.y, self.head)
        self.mate = (self.core, self.mate_z * 2 + self.y, self.head)
        self.other = (1 - self.core, self.dp, self.head)
        self.beside = (self.core, self.dp, 1 - self.head)

        self.beyond = (1 - self.core, self.dp, 1 - self.head)
        self.count = 2 * chain

    def peer(self, k):
        return lax.rem(self.dp + k, self.count)

    def source(self, k):
        return lax.rem(self.dp + self.count - k, self.count)

    def flip(self, b):
        bit = lax.rem(self.dp // (1 << b), 2)
        return self.dp + (1 << b) * (1 - 2 * bit)

    def in_dp(self, dp):
        return (self.core, dp, self.head)

    def greet(self):
        barrier = pltpu.get_barrier_semaphore()
        others = [self.other, self.beside, self.beyond]
        others += [self.in_dp(self.peer(k)) for k in range(1, self.count)]
        for device in others:
            pl.semaphore_signal(barrier, inc=1, device_id=device, device_id_type=MESH)
        pl.semaphore_wait(barrier, len(others))


def remote(src, dst, ssem, rsem, device):
    return pltpu.make_async_remote_copy(
        src_ref=src, dst_ref=dst, send_sem=ssem, recv_sem=rsem, device_id=device, device_id_type=MESH
    )


class Numbered:
    def __init__(self, ref):
        self.ref = ref
        self.count = 0

    def next(self):
        self.count += 1
        assert self.count <= self.ref.shape[0]
        return self.ref.at[self.count - 1]


class Links:
    def __init__(self, at, ssem, rsem):
        self.at, self.sends, self.recvs = at, Numbered(ssem), Numbered(rsem)
        self.waiting = []

    def copy(self, src, dst, device):
        copy = remote(src, dst, self.sends.next(), self.recvs.next(), device)
        copy.start()
        self.waiting.append(copy.wait_send)
        return copy

    def to_all(self, src_of, dst):
        copies = []
        for k in range(1, self.at.count):
            peer = self.at.peer(k)
            copies.append(self.copy(src_of(peer), dst, self.at.in_dp(peer)))
        return copies

    def around(self, ref):
        mine_ = ref.at[self.at.core, self.at.head]
        return [
            self.copy(mine_, mine_, device)
            for device in (self.at.other, self.at.beside, self.at.beyond)
        ]


COPY_BY_MATE = (1, 3, 5)
SUM_BY_MATE = (1, 2, 3, 4)


class Gather:
    def __init__(self, at, halves, w, ssem, rsem, lsem):
        self.at, self.halves, self.w = at, halves, w
        self.ssem, self.rsem, self.lsem = ssem, rsem, lsem
        self.pieces = w.shape[0]

    def local(self, t):
        core = self.at.core
        return pltpu.make_async_copy(
            self.halves[t](core), self.w.at[3 * core + t, core, self.at.dp], self.lsem.at[t]
        )

    def share(self, t):
        core = self.at.core
        return remote(
            self.halves[t](1 - core),
            self.w.at[3 * core + t, 1 - core, self.at.dp],
            self.ssem.at[t, 5 * self.at.chain + 1],
            self.rsem.at[t, 5 * self.at.chain + 1],
            self.at.other,
        )

    def shared(self, t):
        core = self.at.core
        block = self.w.at[3 * (1 - core) + t, core, self.at.dp]
        return remote(
            self.halves[t](1 - core),
            block,
            self.ssem.at[t, 5 * self.at.chain + 1],
            self.rsem.at[t, 5 * self.at.chain + 1],
            self.at.other,
        )

    def split(self, t):
        self.local(t).start()
        self.share(t).start()

    def block(self, p, zz, yy):
        return self.w.at[p, self.at.core, zz * 2 + yy]

    def copy(self, src, dst, p, kind, device):
        return remote(src, dst, self.ssem.at[p, kind], self.rsem.at[p, kind], device)

    def up(self, p, k):
        b = self.block(p, self.at.z - (k - 1), self.at.y)
        return self.copy(b, b, p, k - 1, self.at.above)

    def up_in(self, p, k):
        b = self.block(p, self.at.z - k, self.at.y)
        return self.copy(b, b, p, k - 1, self.at.below)

    def down(self, p, k):
        b = self.block(p, self.at.z + (k - 1), self.at.y)
        return self.copy(b, b, p, self.at.chain + k - 1, self.at.below)

    def down_in(self, p, k):
        b = self.block(p, self.at.z + k, self.at.y)
        return self.copy(b, b, p, self.at.chain + k - 1, self.at.above)

    def cross(self, p, zz):
        b = self.block(p, zz, self.at.y)
        return self.copy(b, b, p, 2 * self.at.chain + zz, self.at.across)

    def cross_in(self, p, zz):
        b = self.block(p, zz, 1 - self.at.y)
        return self.copy(b, b, p, 2 * self.at.chain + zz, self.at.across)

    def mate_out(self, p):
        b = self.block(p, self.at.z, 1 - self.at.y)
        return self.copy(b, b, p, 3 * self.at.chain, self.at.mate)

    def mate_in(self, p):
        b = self.block(p, self.at.mate_z, 1 - self.at.y)
        return self.copy(b, b, p, 3 * self.at.chain, self.at.mate)

    def over(self, p, zz, yy):
        b = self.block(p, zz, yy)
        own = jnp.where(yy == self.at.y, 0, 1)
        return self.copy(b, b, p, 3 * self.at.chain + 1 + 2 * zz + own, self.at.other)

    def over_in(self, p, zz, own):
        yy = self.at.y if own == 0 else 1 - self.at.y
        b = self.w.at[p, 1 - self.at.core, zz * 2 + yy]
        return self.copy(b, b, p, 3 * self.at.chain + 1 + 2 * zz + own, self.at.other)

    def other_in(self, p):
        for zz in range(self.at.chain):
            for own in range(2):
                self.over_in(p, zz, own).wait_recv()

    def start(self, p):
        s, t = divmod(p, 3)

        @pl.when(self.at.core == s)
        def _():
            self.local(t).wait()

        @pl.when(self.at.core != s)
        def _():
            self.shared(t).wait_recv()

        self.cross(p, self.at.z).start()

        @pl.when(self.at.z < self.at.chain - 1)
        def _():
            self.up(p, 1).start()

        @pl.when(self.at.z > 0)
        def _():
            self.down(p, 1).start()

        self.over(p, self.at.z, self.at.y).start()

    def step(self, p, k):
        z, chain = self.at.z, self.at.chain
        odd = p in COPY_BY_MATE

        @pl.when(z >= k)
        def _():
            self.up_in(p, k).wait_recv()

            @pl.when(z < chain - 1)
            def _():
                self.up(p, k + 1).start()

            if k == 1 and odd:

                @pl.when(z % 2 == 0)
                def _():
                    self.cross(p, z - k).start()

            else:
                self.cross(p, z - k).start()
            self.over(p, z - k, self.at.y).start()

        @pl.when(z + k < chain)
        def _():
            self.down_in(p, k).wait_recv()

            @pl.when(z > 0)
            def _():
                self.down(p, k + 1).start()

            if k == 1 and odd:

                @pl.when(z % 2 == 1)
                def _():
                    self.cross(p, z + k).start()

            else:
                self.cross(p, z + k).start()
            self.over(p, z + k, self.at.y).start()

        if k == 1 and odd:
            self.cross_in(p, z).wait_recv()
            self.mate_out(p).start()
            self.over(p, z, 1 - self.at.y).start()

    def finish(self, p):
        z = self.at.z
        for j in range(self.at.chain):
            if p in COPY_BY_MATE:

                @pl.when((j != z) & (j != self.at.mate_z))
                def _():
                    self.cross_in(p, j).wait_recv()
                    self.over(p, j, 1 - self.at.y).start()

            else:
                self.cross_in(p, j).wait_recv()
                self.over(p, j, 1 - self.at.y).start()
        if p in COPY_BY_MATE:
            self.mate_in(p).wait_recv()
            self.over(p, self.at.mate_z, 1 - self.at.y).start()

    def drain(self, p):
        z, chain = self.at.z, self.at.chain
        for j in range(chain):
            if p in COPY_BY_MATE:

                @pl.when(j != self.at.mate_z)
                def _():
                    self.cross(p, j).wait_send()

            else:
                self.cross(p, j).wait_send()
        if p in COPY_BY_MATE:
            self.mate_out(p).wait_send()
        for k in range(1, chain):

            @pl.when((z < chain - 1) & (z >= k - 1))
            def _():
                self.up(p, k).wait_send()

            @pl.when((z > 0) & (z + k - 1 < chain))
            def _():
                self.down(p, k).wait_send()

        for j in range(chain):
            for yy in range(2):
                self.over(p, j, yy).wait_send()
        if p < 3:
            self.share(p).wait_send()


TILE = 32


def silu(v):
    return v / (1.0 + jnp.exp(-v))


def thirds(v):
    a = v.astype(BF)
    rest = v - a.astype(F32)
    b = rest.astype(BF)
    return a, b, (rest - b.astype(F32)).astype(BF)


def by_rows(rows, body, carry, tile=TILE):
    def step(i, c):
        return body(pl.ds(pl.multiple_of(i * tile, tile), tile), c)

    return lax.fori_loop(0, rows // tile, step, carry)


def column_sum(value):
    rows, width = value.shape
    return jnp.sum(value.reshape(rows // 8, 8, width), axis=0)


def layer_norm(v):
    cen = v - jnp.mean(v, axis=-1, keepdims=True)
    inv = lax.rsqrt(jnp.mean(cen * cen, axis=-1, keepdims=True) + EPSILON)
    return cen * inv, inv


def layer_norm_back(w, hat, inv):
    return inv * (
        w - jnp.mean(w, axis=-1, keepdims=True) - hat * jnp.mean(w * hat, axis=-1, keepdims=True)
    )


def spread_masks(kept, place, pos, drop, seg=None):
    length = kept.shape[1]
    u = lax.broadcasted_iota(jnp.int32, (length, length), 0)
    v = lax.broadcasted_iota(jnp.int32, (length, length), 1)
    uf, vf = u.astype(F32), v.astype(F32)
    column = jnp.sum(jnp.where(u == v, kept, 0.0), axis=1, keepdims=True)
    source = jnp.sum(jnp.where(v <= u, kept, 0.0), axis=1, keepdims=True) - 1.0
    source_row = jnp.sum(jnp.where(u <= v, column, 0.0), axis=0, keepdims=True) - 1.0
    count = jnp.sum(kept, axis=1, keepdims=True)
    place[...] = (jnp.where(source == vf, 1.0, 0.0) * column).astype(BF)
    pad = jnp.where(uf >= count, 1.0, 0.0)
    first = jnp.where(v == 0, pad, 0.0)
    pos[...] = (jnp.where(source_row == uf, 1.0, 0.0) * kept + first).astype(BF)
    drop[...] = jnp.broadcast_to(1.0 - column, drop.shape)
    if seg is not None:
        seg[...] = jnp.where(pad == jnp.where(vf >= count, 1.0, 0.0), 0.0, NEGATIVE)


def join_blocks(blocks, shard, width):
    count, lanes = blocks[0].shape
    lane = lax.broadcasted_iota(jnp.int32, (count, lanes), 1)
    blank = jnp.zeros((count, width - lanes), F32)
    total = jnp.zeros((count, width), F32)
    for j, block in enumerate(blocks):
        part = jnp.concatenate([jnp.where(lane < shard, block, 0.0), blank], axis=1)
        total = total + (pltpu.roll(part, j * shard, 1) if j else part)
    return total


def pack_sums(top, low):
    wide = 1024
    moved = jnp.concatenate(
        [low[:, : wide // 2], top[:, wide:], jnp.zeros_like(top[:, : wide // 2 - (top.shape[1] - wide)])],
        axis=1,
    )
    return jnp.concatenate([top[:, :wide], moved], axis=0)


def unpack_sums(packed):
    wide = 1024
    top = jnp.concatenate([packed[:8], packed[8:, wide // 2 : wide // 2 + 128]], axis=1)
    return top, packed[8:, : wide // 2]


def diagonal(length, mirrored=False):
    u = lax.broadcasted_iota(jnp.int32, (length, length), 0)
    v = lax.broadcasted_iota(jnp.int32, (length, length), 1)
    return jnp.where(u + v == length - 1 if mirrored else u == v, 1.0, 0.0).astype(BF)


def head_mask(i, head_dim):
    lane = lax.broadcasted_iota(jnp.int32, (1, HEAD_LANES), 1)
    return ((lane >= i * head_dim) & (lane < (i + 1) * head_dim)).astype(F32)


def forward_kernel(cfg, *refs):
    fused, chain, heads, head_dim = cfg
    refs = list(refs)
    if fused:
        i_att, i_up, i_down = refs[:3]
        refs = refs[3:]
    else:
        w = refs.pop(0)
    i_tok, cond, i_wada, b_ada, kept, b_qv, b_out, b_down, b_up, rel = refs[:10]
    refs = refs[10:]
    if fused:
        w = refs.pop(0)
    (
        s_hat1, s_inv, s_n1, s_qkv, s_p, s_o, s_branch, s_hat2, s_n2, s_hid, s_slope, s_y,
        s_full, s_xm, o_mod, o_cl, o_small, s_e,
    ) = refs[:18]
    refs = refs[18:]
    (
        wa, wu, wd, res, hat, inv, n, r, qkv, prob, o, branch, hid, slope, y_keep,
        xs, xr, toep, small, cl, part, got, pair, mod, tok, wada, pos, seg, place, drop,
        eye, small_own, wide, bada, mtok,
        gs, gr, gl, ssem, rsem, lsem, ms, mr,
    ) = refs
    at = Place(chain)
    rows, width = res.shape
    lw = heads * head_dim
    shard = width // at.count
    half_heads = heads // 2
    scale = 1.0 / math.sqrt(head_dim)
    sends, recvs, locals_ = Numbered(ssem), Numbered(rsem), Numbered(lsem)
    at.greet()
    gather = None
    if fused:
        side = lambda i: pl.ds(pl.multiple_of(i * width, 128), width)
        halves = (
            lambda i: i_att.at[i],
            lambda i: i_up.at[0, :, side(i)],
            lambda i: i_down.at[:, side(i)],
        )
        gather = Gather(at, halves, w, gs, gr, gl)
    links = Links(at, ms, mr)
    waiting = {}

    def keep(name, src, dst):
        copy = pltpu.make_async_copy(src, dst, locals_.next())
        copy.start()
        waiting.setdefault(name, []).append(copy.wait)

    def give(name, src, dst):
        copy = remote(src, dst, sends.next(), recvs.next(), at.other)
        copy.start()
        waiting.setdefault(name, []).append(copy.wait_send)
        waiting.setdefault("end", []).append(copy.wait_recv)

    def settle(name):
        for wait in waiting.pop(name, []):
            wait()

    def pump(*what):
        if not fused:
            return
        for name, p, *k in what:
            if p < gather.pieces:
                getattr(gather, name)(p, *k)

    def load(p, slot):
        if fused:
            gather.other_in(p)
        keep("load%d" % p, w.at[p], slot)

    def send_cond():
        cl[pl.ds(at.dp, 1)] = cond[pl.ds(at.dp, 1)]
        return links.to_all(lambda peer: cond.at[peer], cl.at[at.dp])

    def modulation_terms(copies):
        for copy in copies:
            copy.wait_recv()
        part[...] = jnp.zeros_like(part)
        parts = thirds(silu(flat(cl[...])[:, :shard]))
        for k in range(6):
            cols = wada[k]
            value = nn(parts[0], cols) + (nn(parts[1], cols) + nn(parts[2], cols))
            value = value.reshape(at.count, 8, lw)
            for m in range(2):
                part[:, m * 8 + k, :lw] = value[:, m, :]
        got[pl.ds(at.dp, 1)] = part[pl.ds(at.dp, 1)]
        return links.to_all(lambda peer: part.at[peer], got.at[at.dp])

    def modulation_sum(copies):
        for copy in copies:
            copy.wait_recv()
        value = got[0]
        for j in range(1, at.count):
            value = value + got[j]
        pair[at.core, at.head] = value + jnp.concatenate([bada[...], bada[...]], axis=0)
        return links.around(pair)

    def modulation(copies):
        for copy in copies:
            copy.wait_recv()
        lane = lax.broadcasted_iota(jnp.int32, (8, ADA_LANES), 1)
        blank = jnp.zeros((8, width - ADA_LANES), F32)
        mine_ = pl.ds(pl.multiple_of(at.core * 8, 8), 8)
        for s in range(2):
            a, b = [
                jnp.concatenate([jnp.where(lane < lw, pair[s, h, mine_, :], 0.0), blank], axis=1)
                for h in range(2)
            ]
            mod[s] = a + pltpu.roll(b, lw, 1)
        keep("mod", mod, o_mod)
        keep("cl", cl, o_cl)

    def share_small():
        wide[...] = jnp.zeros_like(wide)
        wide[0:2, :lw] = b_qv[0].astype(F32)
        small_own[...] = jnp.zeros_like(small_own)
        value = wide[...]
        for half in range(2):
            for k in range(2):
                row = half * 4 + 2 * k
                small_own[row : row + 1, :HEAD_LANES] = value[k : k + 1, :HEAD_LANES]
            value = pltpu.roll(value, ADA_LANES - lw // 2, 1)
        small_own[8:9, :] = b_out[...].astype(F32)
        small_own[9:10, :] = b_down[...].astype(F32)
        small_own[10:11, :] = b_up[:, :width].astype(F32)
        small_own[11:12, :] = b_up[:, width:].astype(F32)
        small_own[16 : 16 + heads, : 2 * rows - 1] = rel[0].astype(F32)
        bada[...] = jnp.zeros_like(bada)
        bada[0:6, :lw] = b_ada[0].astype(F32)
        small[pl.ds(at.core, 1)] = small_own[...][None]
        return links.copy(small_own, small.at[at.core], at.other)

    def bqv_row(s, half, kind):
        return small[s, half * 4 + kind : half * 4 + kind + 1, :HEAD_LANES]

    def bup_row(s, half, cols):
        return small[s, 10 + half : 11 + half, cols]

    def send_across(i):
        copy = remote(xs.at[i], xr.at[i], sends.next(), recvs.next(), at.beside)
        copy.start()
        waiting.setdefault("end", []).append(copy.wait_send)
        return copy

    def total(i, ds):
        return xs[i, ds, :].astype(F32) + xr[i, ds, :].astype(F32)

    def norm_one(s):
        settle("hat1")
        settle("n1")
        settle("inv")

        def body(ds, c):
            v, iv = layer_norm(res[ds, :])
            hat[0, ds, :] = v.astype(BF)
            inv[0, ds, :] = jnp.broadcast_to(iv, (TILE, 128))
            n[0, ds, :] = (v * (1.0 + mod[s, 1:2, :]) + mod[s, 0:1, :]).astype(BF)
            return c

        by_rows(rows, body, 0)
        keep("hat1", hat.at[0], s_hat1.at[s])
        keep("n1", n.at[0], s_n1.at[s, 0])
        give("n1", n.at[0], s_n1.at[s, 1])

    def project(s):
        settle("qkv")
        for half in range(2):
            for j in range(3):
                cols = slice(j * 384, (j + 1) * 384)
                r[:, cols] = nn(n[0], flat(wa[half, :, :, cols]))

            def body(ds, c):
                v = r[ds, :]
                for kind, shift in ((0, 864), (1, 576), (2, 288)):
                    piece = pltpu.roll(v, shift, 1)[:, :HEAD_LANES]
                    qkv[kind, half, ds, :] = (piece + bqv_row(s, half, kind)).astype(BF)
                return c

            by_rows(rows, body, 0)
        keep("qkv", qkv, s_qkv.at[s])

    def attend(s, half):
        if half == 0:
            settle("p")
            settle("o")
        o[half] = jnp.zeros_like(o[half])

        def one(i, c):
            index = half * half_heads + i
            mask = head_mask(i, head_dim).astype(BF)
            line = small[s, pl.ds(16 + index, 1), : 2 * rows]
            skew = pltpu.roll(
                jnp.broadcast_to(line, (rows, 2 * rows)), rows + 1, 1, stride=1, stride_axis=0
            )
            toep[...] = skew[:, :rows].astype(BF)
            if s == 0:
                left = nt(pos[...], toep[...]).astype(BF)
                bias = nt(left, pos[...]) + seg[...]
            else:
                bias = nt(eye[...], toep[...])
            z = nt(qkv[0, half] * mask, qkv[1, half]) * scale + bias
            e = jnp.exp(z - jnp.max(z, axis=-1, keepdims=True))
            p = (e / jnp.sum(e, axis=-1, keepdims=True)).astype(BF)
            prob[index] = p
            o[half] = o[half] + nn(p, qkv[2, half]).astype(BF) * mask
            return c

        lax.fori_loop(0, half_heads, one, 0)
        if half == 1:
            keep("p", prob, s_p.at[s])
            keep("o", o.at[at.core], s_o.at[s, 0])
            give("o", o.at[1 - at.core], s_o.at[s, 1])

    def project_out(i):
        xs[i] = (
            nt(o[0], flat(wa[0, :, :, :HEAD_LANES])) + nt(o[1], flat(wa[1, :, :, :HEAD_LANES]))
        ).astype(BF)
        return send_across(i)

    def norm_two(s, i, copy):
        copy.wait_recv()
        settle("branch")
        settle("hat2")
        settle("n2")

        def body(ds, c):
            b = total(i, ds) + small[s, 8:9, :]
            branch[ds, :] = b.astype(BF)
            xm = res[ds, :] + mod[s, 2:3, :] * b
            res[ds, :] = xm
            v, iv = layer_norm(xm)
            hat[1, ds, :] = v.astype(BF)
            inv[1, ds, :] = jnp.broadcast_to(iv, (TILE, 128))
            n[1, ds, :] = (v * (1.0 + mod[s, 4:5, :]) + mod[s, 3:4, :]).astype(BF)
            return c

        by_rows(rows, body, 0)
        keep("branch", branch, s_branch.at[s])
        keep("inv", inv, s_inv.at[s])
        keep("hat2", hat.at[1], s_hat2.at[s])
        if s == 1:
            keep("out", res, s_xm)
        keep("n2", n.at[1], s_n2.at[s, 0])
        give("n2", n.at[1], s_n2.at[s, 1])

    def hidden(s, half):
        if half == 0:
            settle("hid")
            settle("slope")
        for j in range(3):
            cols = slice(j * 384, (j + 1) * 384)
            r[:, cols] = nn(n[1], flat(wu[half, :, :, cols])) + bup_row(s, half, cols)

        def body(ds, c):
            value, sl = gelu_both(r[ds, :])
            hid[half, ds, :] = value.astype(BF)
            slope[half, ds, :] = sl.astype(BF)
            return c

        by_rows(rows, body, 0)
        if half == 1:
            keep("slope", slope, s_slope.at[s])
            keep("hid", hid.at[at.core], s_hid.at[s, 0])
            give("hid", hid.at[1 - at.core], s_hid.at[s, 1])
            if s == 1:
                keep("hid", hid, s_full)

    def project_down(i):
        xs[i] = (nt(hid[0], flat(wd[0])) + nt(hid[1], flat(wd[1]))).astype(BF)
        return send_across(i)

    def end_block(s, i, copy):
        copy.wait_recv()
        settle("y")
        settle("out")

        def body(ds, c):
            v = total(i, ds) + small[s, 9:10, :]
            y_keep[ds, :] = v.astype(BF)
            res[ds, :] = res[ds, :] + mod[s, 5:6, :] * v
            return c

        by_rows(rows, body, 0)
        keep("y", y_keep, s_y)
        keep("out", res, s_e)

    def spread():
        r[...] = nn(place[...], res[...].astype(BF))
        settle("out")

        def body(ds, c):
            res[ds, :] = r[ds, :] + drop[ds, 0:1] * mtok[2:3, :]
            return c

        by_rows(rows, body, 0)

    copies = send_cond()
    small_copy = share_small()
    if fused:
        for t in range(3):
            gather.split(t)
        gather.start(0)
        gather.start(1)
    keep("tok", i_tok.at[at.core], tok)
    keep("wada", i_wada, wada)
    spread_masks(kept[at.core].astype(F32), place, pos, drop, seg)
    eye[...] = diagonal(rows)
    mtok[...] = join_blocks([cond[j] for j in range(at.count)], shard, width)
    settle("tok")

    def start_residual(ds, c):
        res[ds, :] = tok[ds, :].astype(F32)
        return c

    by_rows(rows, start_residual, 0)
    pump(("step", 0, 1))
    settle("wada")
    copies = modulation_terms(copies)
    pump(("step", 0, 2), ("start", 2), ("step", 0, 3))
    copies = modulation_sum(copies)
    small_copy.wait_recv()
    keep("small", small, o_small)
    pump(("step", 1, 1))
    modulation(copies)
    norm_one(0)
    pump(("step", 1, 2), ("start", 3), ("finish", 0), ("step", 1, 3))
    load(0, wa)
    settle("load0")
    project(0)
    pump(("step", 2, 1))
    attend(0, 0)
    pump(("step", 2, 2), ("start", 4), ("finish", 1))
    attend(0, 1)
    copy = project_out(0)
    pump(("step", 2, 3))
    load(1, wu)
    pump(("step", 3, 1))
    norm_two(0, 0, copy)
    settle("load1")
    pump(("step", 3, 2), ("start", 5), ("finish", 2))
    hidden(0, 0)
    hidden(0, 1)
    pump(("step", 3, 3))
    load(2, wd)
    settle("load2")
    copy = project_down(1)
    pump(("step", 4, 1), ("step", 4, 2), ("finish", 3))
    end_block(0, 1, copy)
    spread()
    norm_one(1)
    load(3, wa)
    pump(("step", 4, 3))
    settle("load3")
    project(1)
    attend(1, 0)
    pump(("step", 5, 1))
    attend(1, 1)
    copy = project_out(2)
    pump(("step", 5, 2), ("finish", 4))
    load(4, wu)
    pump(("step", 5, 3))
    norm_two(1, 2, copy)
    settle("load4")
    hidden(1, 0)
    pump(("finish", 5))
    hidden(1, 1)
    if fused:
        gather.other_in(5)
        for p in range(gather.pieces):
            gather.drain(p)
    for wait in links.waiting:
        wait()
    for name in list(waiting):
        settle(name)


def forward_call(cfg, weights, small, dp_count):
    fused, chain, heads, head_dim = cfg
    _, rows, width = small[0].shape
    pieces = 6
    shard = weights[0].shape[-2]
    groups = width // shard
    cond_lanes = small[1].shape[2]
    bf, f = lambda *s: jax.ShapeDtypeStruct(s, BF), lambda *s: jax.ShapeDtypeStruct(s, F32)
    out_shape = [
        bf(2, rows, width),
        f(2, 2, rows, 128),
        bf(2, 2, rows, width),
        bf(2, 3, 2, rows, HEAD_LANES),
        bf(2, heads, rows, rows),
        bf(2, 2, rows, HEAD_LANES),
        bf(2, rows, width),
        bf(2, rows, width),
        bf(2, 2, rows, width),
        bf(2, 2, rows, width),
        bf(2, 2, rows, width),
        bf(rows, width),
        bf(2, rows, width),
        f(rows, width),
        f(2, 8, width),
        f(dp_count, 8, cond_lanes),
        f(2, 24, width),
        f(rows, width),
    ]
    if fused:
        out_shape = [bf(pieces, 2, groups, shard, width)] + out_shape
    kinds = 5 * chain + 2
    many = 2 * (dp_count - 1) + 8
    slot = pltpu.VMEM((2, groups, shard, width), BF)
    scratch = [
        slot,
        slot,
        slot,
        pltpu.VMEM((rows, width), F32),
        pltpu.VMEM((2, rows, width), BF),
        pltpu.VMEM((2, rows, 128), F32),
        pltpu.VMEM((2, rows, width), BF),
        pltpu.VMEM((rows, width), F32),
        pltpu.VMEM((3, 2, rows, HEAD_LANES), BF),
        pltpu.VMEM((heads, rows, rows), BF),
        pltpu.VMEM((2, rows, HEAD_LANES), BF),
        pltpu.VMEM((rows, width), BF),
        pltpu.VMEM((2, rows, width), BF),
        pltpu.VMEM((2, rows, width), BF),
        pltpu.VMEM((rows, width), BF),
        pltpu.VMEM((4, rows, width), BF),
        pltpu.VMEM((4, rows, width), BF),
        pltpu.VMEM((rows, rows), BF),
        pltpu.VMEM((2, 24, width), F32),
        pltpu.VMEM((dp_count, 8, cond_lanes), F32),
        pltpu.VMEM((dp_count, 16, ADA_LANES), F32),
        pltpu.VMEM((dp_count, 16, ADA_LANES), F32),
        pltpu.VMEM((2, 2, 16, ADA_LANES), F32),
        pltpu.VMEM((2, 8, width), F32),
        pltpu.VMEM((rows, width), BF),
        pltpu.VMEM(small[2].shape, BF),
        pltpu.VMEM((rows, rows), BF),
        pltpu.VMEM((rows, rows), F32),
        pltpu.VMEM((rows, rows), BF),
        pltpu.VMEM((rows, 128), F32),
        pltpu.VMEM((rows, rows), BF),
        pltpu.VMEM((24, width), F32),
        pltpu.VMEM((8, ADA_LANES), F32),
        pltpu.VMEM((8, ADA_LANES), F32),
        pltpu.VMEM((8, width), F32),
        pltpu.SemaphoreType.DMA((pieces, kinds)),
        pltpu.SemaphoreType.DMA((pieces, kinds)),
        pltpu.SemaphoreType.DMA((3,)),
        pltpu.SemaphoreType.DMA((16,)),
        pltpu.SemaphoreType.DMA((16,)),
        pltpu.SemaphoreType.DMA((48,)),
        pltpu.SemaphoreType.DMA((many,)),
        pltpu.SemaphoreType.DMA((many,)),
    ]

    def body(*refs):
        forward_kernel(cfg, *refs)

    vm = pl.BlockSpec(memory_space=pltpu.VMEM)
    hbm = pl.BlockSpec(memory_space=pl.ANY)
    result = pl.pallas_call(
        body,
        out_shape=out_shape,
        in_specs=[hbm] * len(weights) + [hbm, vm, hbm] + [vm] * 7,
        out_specs=[hbm] * len(out_shape),
        scratch_shapes=scratch,
        compiler_params=pltpu.CompilerParams(
            collective_id=0, has_side_effects=True, vmem_limit_bytes=VMEM_BYTES
        ),
        name="forward_blocks",
    )(*weights, *small)
    return result if fused else [weights[0]] + list(result)


class Scatter:
    def __init__(self, at, order, g, yr, zr, mr, red, out, ssem, rsem, osem, isem, lsem, credit):
        self.at, self.order = at, order
        self.g, self.yr, self.zr, self.mr, self.red, self.out = g, yr, zr, mr, red, out
        self.ssem, self.rsem, self.osem, self.isem, self.lsem = ssem, rsem, osem, isem, lsem
        self.credit = credit
        chain = at.chain
        need = lambda z, t: chain if t == z else (chain - t + z if t > z else chain - z + t)
        self.table = [sorted(range(chain), key=lambda t: (need(z, t), t)) for z in range(chain)]

    def slots(self, r):
        return r % self.g.shape[0], r % self.yr.shape[0]

    def target(self, i):
        return sum(jnp.where(self.at.z == z, self.table[z][i], 0) for z in range(self.at.chain))

    def own(self, r, t):
        return self.g.at[self.slots(r)[0], t * 2 + self.at.y]

    def theirs(self, r, t):
        return self.g.at[self.slots(r)[0], t * 2 + 1 - self.at.y]

    def copy(self, src, dst, r, kind, device):
        return remote(src, dst, self.ssem.at[r, kind], self.rsem.at[r, kind], device)

    def cross(self, r, t):
        return self.copy(
            self.theirs(r, t), self.yr.at[self.slots(r)[1], t], r, t, self.at.across
        )

    def up(self, r, t):
        return self.copy(
            self.own(r, t), self.zr.at[self.slots(r)[1], t], r, self.at.chain + t, self.at.above
        )

    def down(self, r, t, last=None):
        z = self.at.z - 1 if last is None else last
        place = jnp.where(t == z, self.at.chain, t)
        return self.copy(
            self.own(r, t), self.zr.at[self.slots(r)[1], place], r, 2 * self.at.chain + t, self.at.below
        )

    def to_mate(self, r):
        return self.copy(
            self.theirs(r, self.at.mate_z), self.mr.at[self.slots(r)[1]], r, 3 * self.at.chain, self.at.mate
        )

    def add(self, block, got):
        block[...] = (block[...].astype(F32) + got[...].astype(F32)).astype(BF)

    def begin(self, r):
        at, chain = self.at, self.at.chain
        if r >= self.yr.shape[0]:
            pl.semaphore_wait(self.credit.at[0], 1)

            @pl.when(at.z < chain - 1)
            def _():
                pl.semaphore_wait(self.credit.at[1], 1)

            @pl.when(at.z > 0)
            def _():
                pl.semaphore_wait(self.credit.at[2], 1)

        if r in SUM_BY_MATE:
            self.to_mate(r).start()
        for i in range(chain - 1):
            t = self.target(i)
            if r in SUM_BY_MATE:

                @pl.when(t != at.mate_z)
                def _():
                    self.cross(r, t).start()

            else:
                self.cross(r, t).start()
        if r not in SUM_BY_MATE:
            self.cross(r, at.z).start()

    def mated(self, r):
        if r in SUM_BY_MATE:
            self.to_mate(r).wait_recv()
            self.add(self.theirs(r, self.at.z), self.mr.at[self.slots(r)[1]])
            self.cross(r, self.at.z).start()

    def arrive(self, r, i):
        t = self.target(i)

        def take():
            self.cross(r, t).wait_recv()
            self.add(self.own(r, t), self.yr.at[self.slots(r)[1], t])

        if r in SUM_BY_MATE:
            pl.when(t != self.at.mate_z)(take)
        else:
            take()

    def step(self, r, k):
        z, chain = self.at.z, self.at.chain

        @pl.when((z <= k - 1) & (z < chain - 1))
        def _():
            t = chain - k + z
            if k > 1:

                @pl.when(z > 0)
                def _():
                    self.up(r, t).wait_recv()
                    self.add(self.own(r, t), self.zr.at[self.slots(r)[1], t])

            self.up(r, t).start()

        @pl.when((chain - 1 - z <= k - 1) & (z > 0))
        def _():
            t = k - chain + z
            if k > 1:

                @pl.when(z < chain - 1)
                def _():
                    self.down(r, t, last=z).wait_recv()
                    self.add(self.own(r, t), self.zr.at[self.slots(r)[1], t])

            self.down(r, t).start()

    def finish(self, r):
        at, chain = self.at, self.at.chain
        z = at.z
        slot = self.slots(r)[1]
        held = self.red.shape[0]
        if r >= held:
            self.hand_over_done(r - held)
        red = self.red.at[r % held]
        red[...] = self.own(r, z)[...].astype(F32)

        @pl.when(z > 0)
        def _():
            self.up(r, z).wait_recv()
            red[...] = red[...] + self.zr[slot, z].astype(F32)

        @pl.when(z < chain - 1)
        def _():
            self.down(r, z, last=z).wait_recv()
            red[...] = red[...] + self.zr[slot, chain].astype(F32)

        if r + self.yr.shape[0] < len(self.order):
            pl.semaphore_signal(self.credit.at[0], inc=1, device_id=at.across, device_id_type=MESH)

            @pl.when(z > 0)
            def _():
                pl.semaphore_signal(self.credit.at[1], inc=1, device_id=at.below, device_id_type=MESH)

            @pl.when(z < chain - 1)
            def _():
                pl.semaphore_signal(self.credit.at[2], inc=1, device_id=at.above, device_id_type=MESH)

        s, t = self.order[r]

        @pl.when(at.core == s)
        def _():
            self.keep(r).start()

        @pl.when(at.core != s)
        def _():
            self.hand_over(r).start()

    def keep(self, r):
        return pltpu.make_async_copy(
            self.red.at[r % self.red.shape[0]], self.out.at[self.order[r][1], self.at.core], self.lsem.at[r]
        )

    def hand_over(self, r):
        return remote(
            self.red.at[r % self.red.shape[0]],
            self.out.at[self.order[r][1], self.at.core],
            self.osem.at[r],
            self.isem.at[r],
            self.at.other,
        )

    def hand_over_done(self, r):
        s, t = self.order[r]

        @pl.when(self.at.core == s)
        def _():
            self.keep(r).wait()

        @pl.when(self.at.core != s)
        def _():
            self.hand_over(r).wait_send()

    def drain(self, r):
        z, chain = self.at.z, self.at.chain
        if r in SUM_BY_MATE:
            self.to_mate(r).wait_send()
        for t in range(chain):
            if r in SUM_BY_MATE:

                @pl.when(t != self.at.mate_z)
                def _():
                    self.cross(r, t).wait_send()

            else:
                self.cross(r, t).wait_send()

            @pl.when(t > z)
            def _():
                self.up(r, t).wait_send()

            @pl.when(t < z)
            def _():
                self.down(r, t).wait_send()

    def end(self):
        for r in range(len(self.order)):
            if r + self.red.shape[0] >= len(self.order):
                self.hand_over_done(r)
            s, t = self.order[r]

            @pl.when(self.at.core == s)
            def _():
                remote(
                    self.red.at[0],
                    self.out.at[t, 1 - self.at.core],
                    self.osem.at[r],
                    self.isem.at[r],
                    self.at.other,
                ).wait_recv()


ORDER = ((1, 2), (1, 1), (1, 0), (0, 2), (0, 1), (0, 0))


def backward_kernel(cfg, *refs):
    fused, chain, heads, head_dim = cfg
    refs = list(refs)
    w = refs.pop(0)
    (
        i_hat1, i_inv, i_n1, i_qkv, i_p, i_o, i_branch, i_hat2, i_n2, i_hid, i_slope, i_y, i_full, i_xm,
        i_e,
    ) = refs[:15]
    refs = refs[15:]
    i_dout, mod, i_small, i_cl, i_wada, kept = refs[:6]
    refs = refs[6:]
    red_out, o_dx, o_out, o_dm, o_two = refs[:5]
    refs = refs[5:]
    (
        wslot, hat1, inv, qkv, prob, o, branch, hat2, n2, hid, slope,
        d, r, dy, dpre, dattn, dqkv, do, xs, xr, g, yr, zr, mr, red,
        stats, got, out_one, in_one, dc, in_two, small, cl, wada, flips, pos, place, drop, eye, dout, gs, gr, go, gi, gl, credit, ssem, rsem, lsem, ms, mrs,
    ) = refs
    at = Place(chain)
    rows, width = d.shape
    lw = heads * head_dim
    shard = width // at.count
    half_heads = heads // 2
    scale = 1.0 / math.sqrt(head_dim)
    sends, recvs, locals_ = Numbered(ssem), Numbered(rsem), Numbered(lsem)
    at.greet()
    links = Links(at, ms, mrs)
    stats[...] = jnp.zeros_like(stats)
    dc[...] = jnp.zeros_like(dc)
    scatter = (
        Scatter(at, ORDER, g, yr, zr, mr, red, red_out, gs, gr, go, gi, gl, credit) if fused else None
    )
    slots = g.shape[0]
    waiting = {}

    def fetch(name, src, dst):
        copy = pltpu.make_async_copy(src, dst, locals_.next())
        copy.start()
        waiting.setdefault(name, []).append(copy.wait)

    def settle(name):
        for wait in waiting.pop(name, []):
            wait()

    def give(name, src, dst):
        copy = remote(src, dst, sends.next(), recvs.next(), at.other)
        copy.start()
        waiting.setdefault(name + " in", []).append(copy.wait_recv)
        waiting.setdefault(name + " out", []).append(copy.wait_send)

    def pump(*what):
        if not fused:
            return
        for name, r_, *k in what:
            if 0 <= r_ < len(ORDER):
                getattr(scatter, name)(r_, *k)

    def pump_rest(r_, start):
        for i in range(start, chain):
            pump(("arrive", r_, i))
            if i < chain - 1:
                pump(("step", r_, i + 1))
        pump(("finish", r_))

    def send_across(i):
        if i > 1:
            settle("x out %d" % (i - 2))
        copy = remote(xs.at[i % 2], xr.at[i % 2], sends.next(), recvs.next(), at.beside)
        copy.start()
        waiting.setdefault("x in %d" % i, []).append(copy.wait_recv)
        waiting.setdefault("x out %d" % i, []).append(copy.wait_send)

    def total(i, ds):
        return xs[i % 2, ds, :].astype(F32) + xr[i % 2, ds, :].astype(F32)

    def stat(s, row, value):
        stats[s, row : row + 1, :] = jnp.sum(value, axis=0, keepdims=True)

    zero8 = lambda: jnp.zeros((8, width), F32)
    spans = [slice(k * HEAD_LANES, (k + 1) * HEAD_LANES) for k in range(3)]
    spot = lambda half: jnp.where(half == at.core, 0, 2)

    def load(name, s):
        src, dst = {
            "slope": (i_slope, slope),
            "hid": (i_hid, hid),
            "n1": (i_n1, hid),
            "n2": (i_n2, n2),
            "hat2": (i_hat2, hat2),
            "inv": (i_inv, inv),
            "branch": (i_branch, branch),
            "p": (i_p, prob),
            "qkv": (i_qkv, qkv),
            "o": (i_o, o),
            "hat1": (i_hat1, hat1),
        }[name]
        fetch(name, src.at[s], dst)

    def weight(p, slot):
        fetch("w%d" % slot, w.at[p], wslot.at[slot])

    def product(r_, parts):
        slot = r_ % slots
        if r_ >= slots:
            if fused:
                scatter.drain(r_ - slots)
            else:
                settle("g%d" % (r_ - slots))
        for j in range(width // 384):
            cols = slice(j * 384, (j + 1) * 384)
            value = 0.0
            for lhs, rhs in parts(j):
                value = value + tn(lhs, rhs)
            g[slot, :, :, cols] = value.astype(BF).reshape(g.shape[1], g.shape[2], 384)
        if not fused:
            s, t = ORDER[r_]
            fetch("g%d" % r_, g.at[slot], red_out.at[s * 3 + t])

    def cols_of(ref, j):
        return flat(ref[0:2, :, j * 384 : (j + 1) * 384])

    down_slot, up_slot, att_slot = (1, 0), (0, 1), (1, 0)

    def base(s):
        return 0 if s == 1 else 3

    def exchange(s):
        return 0 if s == 1 else 2

    def back_gate(s):
        settle("dy out")
        if s == 0:
            settle("y")

        def one(ds, c):
            a, b = c
            dv = d[ds, :]
            v = (dv * mod[s, 5:6, :]).astype(BF)
            dy[0, ds, :] = v
            if s == 0:
                a = a + column_sum(dv * xs[2, ds, :].astype(F32))
            return (a, b + column_sum(v.astype(F32)))

        a, b = by_rows(rows, one, (zero8(), zero8()))
        if s == 0:
            stat(s, 5, a)
        stat(s, 8, b)
        give("dy", dy.at[0], dy.at[1])

    def back_hidden(s):
        slot = down_slot[s]
        settle("w%d" % slot)
        settle("slope")
        settle("dpre out")
        for half in range(2):
            for j in range(3):
                cols = slice(j * 384, (j + 1) * 384)
                v = (nn(dy[0], flat(wslot[slot, half, :, :, cols])) * slope[half, :, cols].astype(F32)).astype(BF)
                dpre[spot(half), :, cols] = v
                stats[s, 10 + half : 11 + half, cols] = jnp.sum(v.astype(F32), axis=0, keepdims=True)
        give("dpre", dpre.at[2], dpre.at[1])

    def down_product(s):
        settle("dy in")
        settle("hid")
        product(base(s), lambda j: [(flat(dy[...]), cols_of(hid, j))])
        load("n1", s)

    def back_up(s):
        slot = up_slot[s]
        xi = exchange(s)
        settle("w%d" % slot)
        if xi > 1:
            settle("x out %d" % (xi - 2))
        xs[xi % 2] = (
            nt(dpre[spot(0)], flat(wslot[slot, 0])) + nt(dpre[spot(1)], flat(wslot[slot, 1]))
        ).astype(BF)
        send_across(xi)

    def up_product(s):
        settle("dpre in")
        settle("n2")
        product(base(s) + 1, lambda j: [(flat(n2[...]), cols_of(dpre, j))])

    def back_norm_two(s):
        xi = exchange(s)
        settle("x in %d" % xi)
        settle("hat2")
        settle("inv")
        settle("branch")
        settle("dattn out")

        def two(ds, c):
            c0, c1, c2, c3 = c
            dn = total(xi, ds)
            hv = hat2[ds, :].astype(F32)
            dxm = d[ds, :] + layer_norm_back(dn * (1.0 + mod[s, 4:5, :]), hv, inv[1, ds, 0:1])
            d[ds, :] = dxm
            da = (dxm * mod[s, 2:3, :]).astype(BF)
            dattn[0, ds, :] = da
            return (
                c0 + column_sum(dn),
                c1 + column_sum(dn * hv),
                c2 + column_sum(dxm * branch[ds, :].astype(F32)),
                c3 + column_sum(da.astype(F32)),
            )

        c0, c1, c2, c3 = by_rows(rows, two, (zero8(),) * 4)
        stat(s, 3, c0)
        stat(s, 4, c1)
        stat(s, 2, c2)
        stat(s, 9, c3)
        give("dattn", dattn.at[0], dattn.at[1])

    def back_heads(s, half):
        slot = att_slot[s]
        if half == 0:
            settle("w%d" % slot)
            settle("p")
            settle("qkv")
            settle("dqkv out")
        if True:
            do[half] = nn(dattn[0], flat(wslot[slot, half, :, :, :HEAD_LANES])).astype(BF)
            r[...] = jnp.zeros_like(r)

            def head(i, c):
                index = half * half_heads + i
                mask = head_mask(i, head_dim)
                low_mask = mask.astype(BF)
                p = prob[index]
                dom = do[half] * low_mask
                r[:, spans[2]] = r[:, spans[2]] + tn(p, dom)
                ds = nt(dom, qkv[2, half])
                pf = p.astype(F32)
                dz = (pf * (ds - jnp.sum(pf * ds, axis=-1, keepdims=True))).astype(BF)
                r[:, spans[0]] = r[:, spans[0]] + nn(dz, qkv[1, half]) * mask
                r[:, spans[1]] = r[:, spans[1]] + tn(dz, qkv[0, half]) * mask
                square = nn(dz, flips[s])
                high = square.astype(BF)
                if s == 0:
                    low = (square - high.astype(F32)).astype(BF)
                    square = tn(high, pos[...]) + tn(low, pos[...])
                else:
                    square = tn(high, eye[...])
                wide = jnp.concatenate([square, jnp.zeros_like(square)], axis=1)
                skew = pltpu.roll(wide, 0, 1, stride=1, stride_axis=0)
                stats[s, pl.ds(16 + index, 1), : 2 * rows] = jnp.sum(skew, axis=0, keepdims=True)
                return c

            lax.fori_loop(0, half_heads, head, 0)
            where = spot(half)

            def gather_rows(ds, c):
                blank = jnp.zeros((TILE, HEAD_LANES), F32)
                v = 0.0
                for kind, shift, factor in ((0, 288, scale), (1, 576, scale), (2, 864, 1.0)):
                    part = jnp.concatenate([r[ds, spans[kind]] * factor, blank, blank], axis=1)
                    v = v + pltpu.roll(part, shift, 1)
                v = v.astype(BF)
                dqkv[where, ds, :] = v
                return c + column_sum(v.astype(F32))

            stat(s, 12 + half, by_rows(rows, gather_rows, zero8()))
        if half == 1:
            give("dqkv", dqkv.at[2], dqkv.at[1])

    def back_qkv(s):
        slot = att_slot[s]
        xi = exchange(s) + 1
        if xi > 1:
            settle("x out %d" % (xi - 2))
        xs[xi % 2] = (
            nt(dqkv[spot(0)], flat(wslot[slot, 0])) + nt(dqkv[spot(1)], flat(wslot[slot, 1]))
        ).astype(BF)
        send_across(xi)

    def att_product(s):
        settle("dqkv in")
        settle("dattn in")
        settle("n1")
        settle("o")
        product(
            base(s) + 2,
            lambda j: [(flat(hid[...]), cols_of(dqkv, j))]
            + ([(flat(dattn[...]), flat(o[...]))] if j == 0 else []),
        )

    def back_norm_one(s):
        xs_free = exchange(s) + 1
        settle("x in %d" % xs_free)
        settle("hat1")

        def three(ds, c):
            c0, c1, c2 = c
            dn = total(xs_free, ds)
            hv = hat1[ds, :].astype(F32)
            dx = d[ds, :] + layer_norm_back(dn * (1.0 + mod[s, 1:2, :]), hv, inv[0, ds, 0:1])
            d[ds, :] = dx
            return (c0 + column_sum(dn), c1 + column_sum(dn * hv), c2 + column_sum(dx * drop[ds, 0:1]))

        c0, c1, c2 = by_rows(rows, three, (zero8(),) * 3)
        stat(s, 0, c0)
        stat(s, 1, c1)
        stat(s, 14, c2)
        to_section("dx", s, d, o_dx)

    def to_section(name, s, src, out):
        here = pltpu.make_async_copy(src, out.at[at.core], locals_.next())
        ss, rs = sends.next(), recvs.next()

        @pl.when(at.core == s)
        def _():
            here.start()

        @pl.when(at.core != s)
        def _():
            remote(src, out.at[at.core], ss, rs, at.other).start()

        def sent():
            @pl.when(at.core == s)
            def _():
                here.wait()

            @pl.when(at.core != s)
            def _():
                remote(src, out.at[at.core], ss, rs, at.other).wait_send()

        def arrived():
            @pl.when(at.core == s)
            def _():
                remote(src, out.at[1 - at.core], ss, rs, at.other).wait_recv()

        waiting.setdefault(name, []).append(sent)
        waiting.setdefault("end", []).append(arrived)

    def project_down():
        settle("w0")
        settle("full")
        xs[2] = (nt(dqkv[0], flat(wslot[0, 0])) + nt(dqkv[1], flat(wslot[0, 1]))).astype(BF)
        copy = remote(xs.at[2], xr.at[2], sends.next(), recvs.next(), at.beside)
        copy.start()
        waiting.setdefault("y in", []).append(copy.wait_recv)
        waiting.setdefault("y out", []).append(copy.wait_send)

    def end_forward():
        settle("y in")
        settle("y out")
        settle("xm")
        settle("small")

        def body(ds, c):
            v = xs[2, ds, :].astype(F32) + xr[2, ds, :].astype(F32) + small[1, 9:10, :]
            r[ds, :] = r[ds, :] + mod[1, 5:6, :] * v
            return c + column_sum(dout[ds, :].astype(F32) * v)

        stat(1, 5, by_rows(rows, body, zero8()))
        to_section("result", 1, r, o_out)

    def sums_begin():
        stats[0, 14:15, :] = stats[1, 14:15, :]
        return links.copy(stats.at[1 - at.core], got, at.other)

    def sums_share(copy):
        copy.wait_recv()
        top = stats[at.core, 8:16, :] + got[8:16, :]
        low = stats[at.core, 16:24, :] + got[16:24, :]
        row = lax.broadcasted_iota(jnp.int32, (8, ADA_LANES), 0)
        lane = lax.broadcasted_iota(jnp.int32, (8, ADA_LANES), 1)

        def cut(value):
            value = jnp.where(
                at.head == 0, value[:, :ADA_LANES], pltpu.roll(value, width - lw, 1)[:, :ADA_LANES]
            )
            return jnp.where((row < 6) & (lane < lw), value, 0.0)

        own, other = cut(stats[at.core, 0:8, :]), cut(got[0:8, :])
        both_ = [jnp.where(at.core == 0, own, other), jnp.where(at.core == 0, other, own)]
        both_ = jnp.concatenate(both_, axis=0).astype(BF)
        for j in range(at.count):
            out_one[j, :, :ADA_LANES] = both_
        packed = pack_sums(top, low).astype(BF)
        for j in range(at.count):
            part = (j % 8) * 128
            out_one[j, :, ADA_LANES:] = packed[:, part : part + 128]
        in_one[pl.ds(at.dp, 1)] = out_one[pl.ds(at.dp, 1)]
        return links.to_all(lambda peer: out_one.at[peer], in_one.at[at.dp])

    def cond_terms(copies):
        for copy in copies:
            copy.wait_recv()
        settle("wada")
        settle("cl")
        fetch("dm", in_one.at[:, :, pl.ds(0, ADA_LANES)], o_dm)
        lhs = flat(in_one[:, :, :lw])
        row = lax.rem(lax.broadcasted_iota(jnp.int32, (lhs.shape[0], 1), 0), 8)
        total_ = jnp.zeros((lhs.shape[0], shard), F32)
        for k in range(6):
            total_ = total_ + jnp.where(row == k, nt(lhs, wada[k]), 0.0)
        total_ = total_.reshape(at.count, 16, shard)
        for m in range(2):
            dc[at.core, at.head, m, :, :shard] = jnp.sum(total_[:, m * 8 : (m + 1) * 8, :], axis=1)
        return links.around(dc)

    def cond_share(copies):
        for copy in copies:
            copy.wait_recv()
        cond_lanes = dc.shape[4]
        for m in range(2):
            value = (dc[0, 0, m] + dc[0, 1, m]) + (dc[1, 0, m] + dc[1, 1, m])
            v = cl[:, m, :]
            sig = 1.0 / (1.0 + jnp.exp(-v))
            parts.append(value * (sig * (1.0 + v * (1.0 - sig))))
        value = in_one[0, :, ADA_LANES:].astype(F32)
        for j in range(1, at.count):
            value = value + in_one[j, :, ADA_LANES:].astype(F32)
        grads = jnp.concatenate(parts, axis=0)
        in_two[at.dp, :, :cond_lanes] = grads.astype(BF)
        in_two[at.dp, 0:16, cond_lanes:] = value.astype(BF)
        return links.to_all(lambda peer: in_two.at[at.dp], in_two.at[at.dp])

    def cond_end(copies):
        for copy in copies:
            copy.wait_recv()
        fetch("two", in_two, o_two)

    parts = []
    fetch("dout", i_dout.at[at.core], dout)
    load("hid", 1)
    weight(5, 0)
    load("slope", 1)
    weight(4, 1)
    for name in ("n2", "hat2", "inv", "branch", "p", "qkv", "o", "hat1"):
        load(name, 1)
    for name, src, dst in (
        ("y", i_y, xs.at[2]),
        ("small", i_small, small),
        ("cl", i_cl, cl),
        ("wada", i_wada, wada),
    ):
        fetch(name, src, dst)

    to_section("e", 0, i_e, o_out)
    settle("dout")

    def start_rows(ds, c):
        d[ds, :] = dout[ds, :].astype(F32)
        return c

    by_rows(rows, start_rows, 0)

    def to_encoder():
        r[...] = tn(place[...], d[...].astype(BF))
        settle("dx")

        def move(ds, c):
            d[ds, :] = r[ds, :]
            return c

        by_rows(rows, move, 0)

    back_gate(1)
    down_product(1)
    pump(("begin", 0))
    back_hidden(1)
    weight(3, 0)
    load("slope", 0)
    back_up(1)
    weight(2, 1)
    up_product(1)
    load("n2", 0)
    pump(("begin", 1))
    pump(("arrive", 0, 0), ("step", 0, 1), ("arrive", 0, 1), ("step", 0, 2))
    spread_masks(kept[at.core].astype(F32), place, pos, drop)
    eye[...] = diagonal(rows)
    flips[1] = diagonal(rows, True)
    flips[0] = nn(pos[...], flips[1]).astype(BF)
    back_norm_two(1)
    load("hat2", 0)
    load("branch", 0)
    back_heads(1, 0)
    pump(("arrive", 0, 2), ("step", 0, 3))
    back_heads(1, 1)
    load("p", 0)
    load("qkv", 0)
    back_qkv(1)
    weight(1, 0)
    pump(("arrive", 0, 3))
    att_product(1)
    load("hid", 0)
    load("o", 0)
    pump(("begin", 2))
    pump(("mated", 1), ("arrive", 1, 0), ("step", 1, 1), ("finish", 0))
    back_norm_one(1)
    load("hat1", 0)
    load("inv", 0)
    to_encoder()
    back_gate(0)
    pump(("arrive", 1, 1), ("step", 1, 2))
    back_hidden(0)
    weight(0, 1)
    down_product(0)
    pump(("begin", 3))
    pump(("arrive", 1, 2), ("step", 1, 3))
    back_up(0)
    weight(5, 0)
    pump(("arrive", 1, 3), ("mated", 2), ("arrive", 2, 0), ("step", 2, 1), ("finish", 1))
    up_product(0)
    pump(("begin", 4))
    pump(("arrive", 2, 1), ("step", 2, 2))
    back_norm_two(0)
    back_heads(0, 0)
    pump(("arrive", 2, 2), ("step", 2, 3))
    back_heads(0, 1)
    back_qkv(0)
    fetch("xm", i_xm, r)
    pump(("arrive", 2, 3), ("mated", 3), ("arrive", 3, 0), ("step", 3, 1), ("finish", 2))
    att_product(0)
    fetch("full", i_full, dqkv.at[0:2])
    pump(("begin", 5))
    pump(("arrive", 3, 1), ("step", 3, 2))
    project_down()
    back_norm_one(0)
    pump(("arrive", 3, 2), ("step", 3, 3))
    end_forward()
    copy = sums_begin()
    pump(("arrive", 3, 3), ("mated", 4), ("arrive", 4, 0), ("step", 4, 1), ("finish", 3))
    copies = sums_share(copy)
    pump(("arrive", 4, 1), ("step", 4, 2), ("arrive", 4, 2), ("step", 4, 3), ("arrive", 4, 3))
    copies = cond_terms(copies)
    pump(("arrive", 5, 0), ("step", 5, 1), ("finish", 4))
    copies = cond_share(copies)
    pump(("arrive", 5, 1), ("step", 5, 2), ("arrive", 5, 2), ("step", 5, 3), ("arrive", 5, 3))
    cond_end(copies)
    pump(("finish", 5))
    if fused:
        for r_ in range(len(ORDER) - slots, len(ORDER)):
            scatter.drain(r_)
        scatter.end()
    for wait in links.waiting:
        wait()
    for name in list(waiting):
        settle(name)


def backward_call(cfg, w, saved, small):
    fused, chain, heads, head_dim = cfg
    _, rows, width = small[0].shape
    pieces, _, groups, shard, _ = w.shape
    count, _, cond_lanes = small[3].shape
    many = 2 * (count - 1) + 6
    each = 128
    bf, f = lambda *s: pltpu.VMEM(s, BF), lambda *s: pltpu.VMEM(s, F32)
    dma = lambda *s: pltpu.SemaphoreType.DMA(s)
    out_shape = [
        jax.ShapeDtypeStruct((3, 2, shard, width), F32)
        if fused
        else jax.ShapeDtypeStruct((pieces, groups, shard, width), BF),
        jax.ShapeDtypeStruct((2, rows, width), F32),
        jax.ShapeDtypeStruct((2, rows, width), F32),
        jax.ShapeDtypeStruct((count, 16, ADA_LANES), BF),
        jax.ShapeDtypeStruct((count, 2 * count, cond_lanes + each), BF),
    ]
    some = 3 if fused else 1
    links = chain if fused else 1
    block = shard if fused else 16
    scratch = [
        bf(2, 2, groups, shard, width),
        bf(rows, width),
        f(2, rows, 128),
        bf(3, 2, rows, HEAD_LANES),
        bf(heads, rows, rows),
        bf(2, rows, HEAD_LANES),
        bf(rows, width),
        bf(rows, width),
        bf(2, rows, width),
        bf(2, rows, width),
        bf(2, rows, width),
        f(rows, width),
        f(rows, width),
        bf(2, rows, width),
        bf(3, rows, width),
        bf(2, rows, width),
        bf(3, rows, width),
        bf(2, rows, HEAD_LANES),
        bf(3, rows, width),
        bf(3, rows, width),
        bf(4, groups, shard, width),
        bf(some, links, block, width),
        bf(some, links + 1, block, width),
        bf(some, block, width),
        f(2, block, width),
        f(2, 24, width),
        f(24, width),
        bf(count, 16, ADA_LANES + each),
        bf(count, 16, ADA_LANES + each),
        f(2, 2, 2, count, cond_lanes),
        bf(count, 2 * count, cond_lanes + each),
        f(2, 24, width),
        f(count, 8, cond_lanes),
        bf(*small[4].shape),
        bf(2, rows, rows),
        bf(rows, rows),
        bf(rows, rows),
        f(rows, 128),
        bf(rows, rows),
        bf(rows, width),
        dma(6, 3 * links + 1),
        dma(6, 3 * links + 1),
        dma(6),
        dma(6),
        dma(6),
        pltpu.SemaphoreType.REGULAR((3,)),
        dma(20),
        dma(20),
        dma(56),
        dma(many),
        dma(many),
    ]

    def body(*refs):
        backward_kernel(cfg, *refs)

    vm = pl.BlockSpec(memory_space=pltpu.VMEM)
    hbm = pl.BlockSpec(memory_space=pl.ANY)
    return pl.pallas_call(
        body,
        out_shape=out_shape,
        in_specs=[hbm] * (1 + len(saved)) + [hbm, vm, hbm, hbm, hbm, vm],
        out_specs=[hbm] * len(out_shape),
        scratch_shapes=scratch,
        compiler_params=pltpu.CompilerParams(
            collective_id=1, has_side_effects=True, vmem_limit_bytes=VMEM_BYTES
        ),
        name="backward_blocks",
    )(w, *saved, *small)


def unpack_two(two, count, cond_lanes):
    top, rel = unpack_sums(
        jnp.concatenate([two[j, 0:16, cond_lanes:] for j in range(8)], axis=1).astype(F32)
    )
    blocks = [
        [two[j, m * count : (m + 1) * count, :cond_lanes].astype(F32) for m in range(2)]
        for j in range(count)
    ]
    return top, rel, blocks


def finish_kernel(cfg, red, outs, dx, two, dm, cl, *refs):
    _, _, heads, head_dim = cfg
    r_outs, r_dx, g_qkv, g_out, g_up, g_down, g_ada, g_class = refs[:8]
    b_qv, b_out, b_up, b_down, b_ada, rel, mask = refs[8:15]
    att, rest, t_qkv, t_out, t_ada, t_class, t_rows, sems = refs[15:]
    head = lax.axis_index("head")
    _, _, shard, width = red.shape
    lw = heads * head_dim
    hw = lw // 2
    count, _, cond_lanes = cl.shape
    slots = Numbered(sems)
    waits = []

    def move(src, dst):
        copy = pltpu.make_async_copy(src, dst, slots.next())
        copy.start()
        waits.append(copy.wait)
        return copy

    first = pltpu.make_async_copy(red.at[0], att, slots.next())
    first.start()
    second = pltpu.make_async_copy(red.at[pl.ds(1, 2)], rest, slots.next())
    second.start()
    third = []
    for i, source in enumerate((outs, dx)):
        third.append(pltpu.make_async_copy(source, t_rows.at[i], slots.next()))
        third[i].start()

    def half(value):
        moved = pltpu.roll(value, width - lw, 1)
        return jnp.where(head == 0, value[:, :ADA_LANES], moved[:, :ADA_LANES])

    rows, table, blocks = unpack_two(two[...], count, cond_lanes)
    picks, grads, parts = [], [], []
    for m in range(2):
        block = cl[:, m, :]
        place = lax.broadcasted_iota(jnp.int32, block.shape, 1)
        label = jnp.sum(jnp.where(place == shard, block, 0.0), axis=1, keepdims=True)
        span = lax.broadcasted_iota(jnp.int32, (count, t_class.shape[1]), 1).astype(F32)
        picks.append(jnp.where(span == label, 1.0, 0.0))
        grads.append(half(join_blocks([pair[m] for pair in blocks], shard, width)))
        parts.append(silu(block))
    pick_all = jnp.concatenate(picks, axis=0).astype(BF)
    a, b, c = thirds(jnp.concatenate(grads, axis=0))
    t_class[...] = (tn(a, pick_all) + (tn(b, pick_all) + tn(c, pick_all)))[:lw, :]
    move(t_class, g_class)
    second.wait()
    for side in range(2):
        move(rest.at[0, side], g_up.at[0, :, pl.ds(side * width, width)])
        move(rest.at[1, side], g_down.at[:, pl.ds(side * width, width)])
    a, b, c = thirds(jnp.concatenate(parts, axis=0))
    for k in range(6):
        pair = jnp.concatenate([dm[:, k, :], dm[:, 8 + k, :]], axis=0).astype(BF)
        t_ada[k] = (tn(a, pair) + (tn(b, pair) + tn(c, pair)))[:shard, :lw]
    move(t_ada, g_ada)
    for i, target in enumerate((r_outs, r_dx)):
        third[i].wait()
        move(t_rows.at[i], target.at[0])
    first.wait()
    wide = lax.broadcasted_iota(jnp.int32, (shard, width), 1)
    for k in range(4):
        value = 0.0
        for side in range(2):
            moved = pltpu.roll(att[side], (side - k) * hw % width, 1) if side != k else att[side]
            value = value + jnp.where((wide >= side * hw) & (wide < (side + 1) * hw), moved, 0.0)
        if k == 0:
            t_out[...] = value[:, :lw]
        else:
            t_qkv[k - 1] = value[:, :lw]
    move(t_out, g_out)
    move(t_qkv, g_qkv)
    for side in range(2):
        b_up[:, side * width : (side + 1) * width] = rows[2 + side : 3 + side, :]
    lane = lax.broadcasted_iota(jnp.int32, (8, width), 1)
    for k, at in enumerate((1, 3)):
        own = jnp.where(lane < hw, pltpu.roll(rows, width - at * hw, 1), 0.0)
        b_qv[0, k : k + 1, :] = (own[4:5] + pltpu.roll(own, hw, 1)[5:6])[:, :lw]
    cut = half(rows)
    b_down[...] = cut[0:1, :lw]
    b_out[...] = cut[1:2, :lw]
    mask[...] = cut[6:7, :lw]
    rel[0] = table[:, : rel.shape[2]]
    value = dm[0].astype(F32)
    for j in range(1, count):
        value = value + dm[j].astype(F32)
    b_ada[:, 0, :] = (value[0:8] + value[8:16])[0:6, :lw]
    for wait in waits:
        wait()


def finish_call(cfg, classes, length, red, outs, dx, two, dm, cl):
    _, _, heads, head_dim = cfg
    lw = heads * head_dim
    shard, width = red.shape[2:]
    f = lambda *s: jax.ShapeDtypeStruct(s, F32)

    def body(*refs):
        finish_kernel(cfg, *refs)

    vm = pl.BlockSpec(memory_space=pltpu.VMEM)
    hbm = pl.BlockSpec(memory_space=pl.ANY)
    large = [
        f(1, *outs.shape),
        f(1, *dx.shape),
        f(3, shard, lw),
        f(shard, lw),
        f(1, shard, 2 * width),
        f(shard, 2 * width),
        f(6, shard, lw),
        f(lw, classes),
    ]
    small = [
        f(1, 2, lw),
        f(1, lw),
        f(1, 2 * width),
        f(1, lw),
        f(6, 1, lw),
        f(1, heads, 2 * length - 1),
        f(1, lw),
    ]
    return pl.pallas_call(
        body,
        out_shape=large + small,
        in_specs=[hbm, hbm, hbm, vm, vm, vm],
        out_specs=[hbm] * len(large) + [vm] * len(small),
        scratch_shapes=[
            pltpu.VMEM((2, shard, width), F32),
            pltpu.VMEM((2, 2, shard, width), F32),
            pltpu.VMEM((3, shard, lw), F32),
            pltpu.VMEM((shard, lw), F32),
            pltpu.VMEM((6, shard, lw), F32),
            pltpu.VMEM((lw, classes), F32),
            pltpu.VMEM((2, *outs.shape), F32),
            pltpu.SemaphoreType.DMA((14,)),
        ],
        compiler_params=pltpu.CompilerParams(vmem_limit_bytes=VMEM_BYTES),
        name="last_layouts",
    )(red, outs, dx, two, dm, cl)


def per_device(
    tokens,
    kept_mask,
    timesteps,
    labels,
    w_qkv,
    b_qv,
    w_out,
    b_out,
    w_up,
    b_up,
    w_down,
    b_down,
    w_ada,
    b_ada,
    rel_table,
    mask_token,
    class_table,
    out_grad,
):
    micro, rows, width = tokens.shape
    length = kept_mask.shape[2]
    classes = class_table.shape[0]
    heads = rel_table.shape[1]
    lw = w_qkv.shape[3]
    head_dim = lw // heads
    hw = lw // 2
    ff = w_up.shape[2]
    fw = ff // 2
    dp_count = lax.axis_size("dp")
    c = lax.axis_index("section")
    dp = lax.axis_index("dp")
    h = lax.axis_index("head")

    qkv = jnp.transpose(w_qkv[0], (1, 0, 2))
    out_t = w_out[0].T
    down_t = w_down[0].T
    fr = width // dp_count

    label_pick = (labels == jnp.arange(classes)[None, :]).astype(BF)
    cond = nn(label_pick, class_table) + time_features(timesteps[:, 0], width)
    cond = jnp.concatenate([cond, mask_token[None, :].astype(F32)])
    blocks = jnp.transpose(cond.reshape(micro + 1, dp_count, fr), (1, 0, 2))
    tags = jnp.pad(labels.astype(F32), ((0, 1), (0, 0)))
    tags = jnp.broadcast_to(tags[None], (dp_count, micro + 1, 1))
    cond_lanes = -(-(fr + 1) // 128) * 128
    blocks = jnp.concatenate([blocks, tags], axis=2)
    blocks = jnp.pad(blocks, ((0, 0), (0, 7 - micro), (0, cond_lanes - fr - 1)))
    ada = jnp.transpose(w_ada[0], (1, 0, 2))

    fused = dp_count == 8 and fr % 16 == 0
    cfg = (fused, dp_count // 2, heads, head_dim)
    att = []
    for half in range(2):
        at = slice(half * hw, (half + 1) * hw)
        att.append(jnp.concatenate([out_t[:, at], qkv[0][:, at], qkv[1][:, at], qkv[2][:, at]], axis=1))
    if fused:
        source_w = (jnp.stack(att), w_up, down_t)
    else:
        halves = []
        for half in range(2):
            fat = slice(half * fw, (half + 1) * fw)
            halves.append(jnp.stack([att[half], w_up[0][:, fat], down_t[:, fat]]))
        other_w = swap(mine(1 - c, halves), "section")
        own_w = mine(c, halves)
        own_w = jnp.concatenate([pick(c, own_w, other_w), pick(c, other_w, own_w)])
        half_w_ = lax.all_gather(own_w, "dp", axis=1, tiled=True)
        other_w = swap(half_w_, "section")
        source_w = jnp.stack([pick(c, half_w_, other_w), pick(c, other_w, half_w_)], axis=1)
        source_w = (source_w.reshape(6, 2, 8, width // 8, 4 * hw),)
    small_in = (
        tokens,
        blocks,
        ada,
        b_ada,
        kept_mask,
        b_qv,
        b_out,
        b_down,
        b_up,
        rel_table,
    )
    full, *saved, mod, cond_all, small_all, enc = forward_call(cfg, source_w, small_in, dp_count)
    saved.append(enc)
    small_back = (out_grad, mod, small_all, cond_all, ada, kept_mask)
    red, dx, outs, dm, two = backward_call(cfg, full, saved, small_back)

    if fused:
        last = finish_call(cfg, classes, length, red, outs, dx, two, dm, cond_all)
        outs, dx, g_qkv, g_out, g_up, g_down, g_ada, g_class = last[:8]
        g_b_qv, g_b_out, g_b_up, g_b_down, g_b_ada, g_rel, g_mask = last[8:]
        return (
            outs,
            dx,
            jnp.transpose(g_qkv, (1, 0, 2))[None],
            g_b_qv,
            g_out.T[None],
            g_b_out,
            g_up,
            g_b_up,
            g_down.T[None],
            g_b_down,
            jnp.transpose(g_ada, (1, 0, 2))[None],
            jnp.transpose(g_b_ada, (1, 0, 2)),
            g_rel,
            g_mask[0],
            g_class.T,
        )
    red = lax.psum_scatter(
        red.reshape(6, width, 4 * hw), "dp", scatter_dimension=1, tiled=True
    ).astype(F32)
    red = red.reshape(2, 3, fr, 4 * hw)
    g_own = mine(c, red)
    g_got = swap(mine(1 - c, red), "section")
    g0, g1 = pick(c, g_own, g_got), pick(c, g_got, g_own)
    g_qkv = jnp.stack(
        [
            jnp.concatenate([g0[0][:, i * hw : (i + 1) * hw], g1[0][:, i * hw : (i + 1) * hw]], axis=1)
            for i in (1, 2, 3)
        ],
        axis=1,
    )
    g_out = jnp.concatenate([g0[0][:, :hw], g1[0][:, :hw]], axis=1).T
    g_up = jnp.concatenate([g0[1], g1[1]], axis=1)
    g_down = jnp.concatenate([g0[2], g1[2]], axis=1).T

    cond_lanes = cond_all.shape[2]
    sums, rel_rows, dc = unpack_two(two, dp_count, cond_lanes)
    dc = jnp.stack([jnp.stack(pair) for pair in dc])
    half_w = width // 2

    def half(v):
        return lax.dynamic_slice_in_dim(v, h * half_w, half_w, v.ndim - 1)

    g_b_qv = jnp.stack(
        [
            jnp.concatenate([sums[4, at * hw : (at + 1) * hw], sums[5, at * hw : (at + 1) * hw]])
            for at in (1, 3)
        ]
    )
    g_b_up = sums[2:4, :fw].reshape(-1)
    g_rel = rel_rows[:, : 2 * length - 1]

    dm = dm.astype(F32).reshape(dp_count, micro, 8, ADA_LANES)[:, :, :6, :lw]
    cond_part = jax.nn.silu(cond_all[:, :micro, :fr])
    g_ada = jnp.einsum("jmf,jmke->fke", cond_part, dm, precision=PRECISE)
    g_b_ada = jnp.sum(dm, axis=(0, 1))
    labels_all = cond_all[:, :micro, fr].astype(jnp.int32).T.reshape(-1)
    dcond = jnp.transpose(dc[..., :fr], (1, 2, 0, 3)).reshape(micro * dp_count, width)
    pick_all = (labels_all[:, None] == jnp.arange(classes)[None, :]).astype(F32)
    g_class = jnp.einsum("ic,id->cd", pick_all, half(dcond), precision=PRECISE)

    return (
        outs[None],
        dx[None],
        g_qkv[None],
        g_b_qv[None],
        g_out[None],
        half(sums[1])[None],
        g_up[None],
        g_b_up[None],
        g_down[None],
        half(sums[0])[None],
        g_ada[None],
        g_b_ada[None],
        g_rel[None],
        half(sums[6]),
        g_class,
    )


def solution(mesh):
    placed = (
        P(None, "dp", None),
        P(None, "dp", None),
        P(None, "dp"),
        P(None, "dp"),
        P("section", "dp", None, "head"),
        P("section", None, "head"),
        P("section", "head", "dp"),
        P("section", None),
        P("section", "dp", "head"),
        P("section", "head"),
        P("section", "head", "dp"),
        P("section", None),
        P("section", "dp", None, "head"),
        P("section", None, "head"),
        P("section", "head", None),
        P(),
        P(),
        P(None, "dp", None),
    )
    return jax.shard_map(
        per_device,
        mesh=mesh,
        in_specs=placed,
        out_specs=(
            P("section", None, "dp", None),
            P("section", None, "dp", None),
            P("section", "dp", None, "head"),
            P("section", None, "head"),
            P("section", "head", "dp"),
            P("section", "head"),
            P("section", "dp", "head"),
            P("section", "head"),
            P("section", "head", "dp"),
            P("section", "head"),
            P("section", "dp", None, "head"),
            P("section", None, "head"),
            P("section", "head", None),
            P("head"),
            P(None, "head"),
        ),
        check_vma=False,
    )
```

```python
import math

import jax
import jax.numpy as jnp
from jax import lax
from jax.experimental import pallas as pl
from jax.experimental.pallas import tpu as pltpu
from jax.sharding import PartitionSpec as P

PRECISE = lax.Precision.HIGHEST
EPSILON = 1e-06
NEGATIVE = -1e30
MESH = pl.DeviceIdType.MESH
BF = jnp.bfloat16
VMEM_BYTES = 62 * 1024 * 1024
F32 = jnp.float32


def time_features(step_ids, model_width):
    half_width = model_width // 2
    frequency = jnp.exp(-math.log(10000.0) * jnp.arange(half_width).astype(F32) / half_width)
    angles = step_ids.astype(F32)[..., None] * frequency
    return jnp.concatenate([jnp.cos(angles), jnp.sin(angles)], axis=-1)


def swap(value, axis):
    return lax.ppermute(value, axis, [(0, 1), (1, 0)])


def pick(index, first, second):
    return jnp.where(index == 0, first, second)


def mine(c, pair):
    return pick(c, pair[0], pair[1])


def both(value):
    c = lax.axis_index("section")
    got = swap(value, "section")
    return pick(c, value, got), pick(c, got, value)


HEAD_LANES = 384
ADA_LANES = 640


def nn(a, b):
    return lax.dot_general(a, b, (((1,), (0,)), ((), ())), preferred_element_type=F32)


def nt(a, b):
    return lax.dot_general(a, b, (((1,), (1,)), ((), ())), preferred_element_type=F32)


def tn(a, b):
    return lax.dot_general(a, b, (((0,), (0,)), ((), ())), preferred_element_type=F32)


def flat(value):
    return value.reshape(value.shape[0] * value.shape[1], value.shape[2])


GELU_SCALE = math.sqrt(2.0 / math.pi)


def gelu_both(v):
    t = jnp.tanh(GELU_SCALE * (v + 0.044715 * v * v * v))
    slope = 0.5 * (1.0 + t) + (0.5 * GELU_SCALE) * v * (1.0 - t * t) * (1.0 + 0.134145 * v * v)
    return 0.5 * v * (1.0 + t), slope


class Place:
    def __init__(self, chain):
        self.chain = chain
        self.core = lax.axis_index("section")
        self.dp = lax.axis_index("dp")
        self.head = lax.axis_index("head")
        self.z = self.dp // 2
        self.y = self.dp % 2
        self.mate_z = self.z + 1 - 2 * (self.z % 2)
        self.above = (self.core, self.dp + 2, self.head)
        self.below = (self.core, self.dp - 2, self.head)
        self.across = (self.core, self.z * 2 + 1 - self.y, self.head)
        self.mate = (self.core, self.mate_z * 2 + self.y, self.head)
        self.other = (1 - self.core, self.dp, self.head)
        self.beside = (self.core, self.dp, 1 - self.head)

        self.beyond = (1 - self.core, self.dp, 1 - self.head)
        self.count = 2 * chain

    def peer(self, k):
        return lax.rem(self.dp + k, self.count)

    def source(self, k):
        return lax.rem(self.dp + self.count - k, self.count)

    def flip(self, b):
        bit = lax.rem(self.dp // (1 << b), 2)
        return self.dp + (1 << b) * (1 - 2 * bit)

    def in_dp(self, dp):
        return (self.core, dp, self.head)

    def greet(self):
        barrier = pltpu.get_barrier_semaphore()
        others = [self.other, self.beside, self.beyond]
        others += [self.in_dp(self.peer(k)) for k in range(1, self.count)]
        for device in others:
            pl.semaphore_signal(barrier, inc=1, device_id=device, device_id_type=MESH)
        pl.semaphore_wait(barrier, len(others))


def remote(src, dst, ssem, rsem, device):
    return pltpu.make_async_remote_copy(
        src_ref=src, dst_ref=dst, send_sem=ssem, recv_sem=rsem, device_id=device, device_id_type=MESH
    )


class Numbered:
    def __init__(self, ref):
        self.ref = ref
        self.count = 0

    def next(self):
        self.count += 1
        assert self.count <= self.ref.shape[0]
        return self.ref.at[self.count - 1]


class Links:
    def __init__(self, at, ssem, rsem):
        self.at, self.sends, self.recvs = at, Numbered(ssem), Numbered(rsem)
        self.waiting = []

    def copy(self, src, dst, device):
        copy = remote(src, dst, self.sends.next(), self.recvs.next(), device)
        copy.start()
        self.waiting.append(copy.wait_send)
        return copy

    def to_all(self, src_of, dst):
        copies = []
        for k in range(1, self.at.count):
            peer = self.at.peer(k)
            copies.append(self.copy(src_of(peer), dst, self.at.in_dp(peer)))
        return copies

    def around(self, ref):
        mine_ = ref.at[self.at.core, self.at.head]
        return [
            self.copy(mine_, mine_, device)
            for device in (self.at.other, self.at.beside, self.at.beyond)
        ]


COPY_BY_MATE = (1, 3, 5)
SUM_BY_MATE = (1, 2, 3, 4)


class Gather:
    def __init__(self, at, halves, w, ssem, rsem, lsem):
        self.at, self.halves, self.w = at, halves, w
        self.ssem, self.rsem, self.lsem = ssem, rsem, lsem
        self.pieces = w.shape[0]

    def local(self, t):
        core = self.at.core
        return pltpu.make_async_copy(
            self.halves[t](core), self.w.at[3 * core + t, core, self.at.dp], self.lsem.at[t]
        )

    def share(self, t):
        core = self.at.core
        return remote(
            self.halves[t](1 - core),
            self.w.at[3 * core + t, 1 - core, self.at.dp],
            self.ssem.at[t, 5 * self.at.chain + 1],
            self.rsem.at[t, 5 * self.at.chain + 1],
            self.at.other,
        )

    def shared(self, t):
        core = self.at.core
        block = self.w.at[3 * (1 - core) + t, core, self.at.dp]
        return remote(
            self.halves[t](1 - core),
            block,
            self.ssem.at[t, 5 * self.at.chain + 1],
            self.rsem.at[t, 5 * self.at.chain + 1],
            self.at.other,
        )

    def split(self, t):
        self.local(t).start()
        self.share(t).start()

    def block(self, p, zz, yy):
        return self.w.at[p, self.at.core, zz * 2 + yy]

    def copy(self, src, dst, p, kind, device):
        return remote(src, dst, self.ssem.at[p, kind], self.rsem.at[p, kind], device)

    def up(self, p, k):
        b = self.block(p, self.at.z - (k - 1), self.at.y)
        return self.copy(b, b, p, k - 1, self.at.above)

    def up_in(self, p, k):
        b = self.block(p, self.at.z - k, self.at.y)
        return self.copy(b, b, p, k - 1, self.at.below)

    def down(self, p, k):
        b = self.block(p, self.at.z + (k - 1), self.at.y)
        return self.copy(b, b, p, self.at.chain + k - 1, self.at.below)

    def down_in(self, p, k):
        b = self.block(p, self.at.z + k, self.at.y)
        return self.copy(b, b, p, self.at.chain + k - 1, self.at.above)

    def cross(self, p, zz):
        b = self.block(p, zz, self.at.y)
        return self.copy(b, b, p, 2 * self.at.chain + zz, self.at.across)

    def cross_in(self, p, zz):
        b = self.block(p, zz, 1 - self.at.y)
        return self.copy(b, b, p, 2 * self.at.chain + zz, self.at.across)

    def mate_out(self, p):
        b = self.block(p, self.at.z, 1 - self.at.y)
        return self.copy(b, b, p, 3 * self.at.chain, self.at.mate)

    def mate_in(self, p):
        b = self.block(p, self.at.mate_z, 1 - self.at.y)
        return self.copy(b, b, p, 3 * self.at.chain, self.at.mate)

    def over(self, p, zz, yy):
        b = self.block(p, zz, yy)
        own = jnp.where(yy == self.at.y, 0, 1)
        return self.copy(b, b, p, 3 * self.at.chain + 1 + 2 * zz + own, self.at.other)

    def over_in(self, p, zz, own):
        yy = self.at.y if own == 0 else 1 - self.at.y
        b = self.w.at[p, 1 - self.at.core, zz * 2 + yy]
        return self.copy(b, b, p, 3 * self.at.chain + 1 + 2 * zz + own, self.at.other)

    def other_in(self, p):
        for zz in range(self.at.chain):
            for own in range(2):
                self.over_in(p, zz, own).wait_recv()

    def start(self, p):
        s, t = divmod(p, 3)

        @pl.when(self.at.core == s)
        def _():
            self.local(t).wait()

        @pl.when(self.at.core != s)
        def _():
            self.shared(t).wait_recv()

        self.cross(p, self.at.z).start()

        @pl.when(self.at.z < self.at.chain - 1)
        def _():
            self.up(p, 1).start()

        @pl.when(self.at.z > 0)
        def _():
            self.down(p, 1).start()

        self.over(p, self.at.z, self.at.y).start()

    def step(self, p, k):
        z, chain = self.at.z, self.at.chain
        odd = p in COPY_BY_MATE

        @pl.when(z >= k)
        def _():
            self.up_in(p, k).wait_recv()

            @pl.when(z < chain - 1)
            def _():
                self.up(p, k + 1).start()

            if k == 1 and odd:

                @pl.when(z % 2 == 0)
                def _():
                    self.cross(p, z - k).start()

            else:
                self.cross(p, z - k).start()
            self.over(p, z - k, self.at.y).start()

        @pl.when(z + k < chain)
        def _():
            self.down_in(p, k).wait_recv()

            @pl.when(z > 0)
            def _():
                self.down(p, k + 1).start()

            if k == 1 and odd:

                @pl.when(z % 2 == 1)
                def _():
                    self.cross(p, z + k).start()

            else:
                self.cross(p, z + k).start()
            self.over(p, z + k, self.at.y).start()

        if k == 1 and odd:
            self.cross_in(p, z).wait_recv()
            self.mate_out(p).start()
            self.over(p, z, 1 - self.at.y).start()

    def finish(self, p):
        z = self.at.z
        for j in range(self.at.chain):
            if p in COPY_BY_MATE:

                @pl.when((j != z) & (j != self.at.mate_z))
                def _():
                    self.cross_in(p, j).wait_recv()
                    self.over(p, j, 1 - self.at.y).start()

            else:
                self.cross_in(p, j).wait_recv()
                self.over(p, j, 1 - self.at.y).start()
        if p in COPY_BY_MATE:
            self.mate_in(p).wait_recv()
            self.over(p, self.at.mate_z, 1 - self.at.y).start()

    def drain(self, p):
        z, chain = self.at.z, self.at.chain
        for j in range(chain):
            if p in COPY_BY_MATE:

                @pl.when(j != self.at.mate_z)
                def _():
                    self.cross(p, j).wait_send()

            else:
                self.cross(p, j).wait_send()
        if p in COPY_BY_MATE:
            self.mate_out(p).wait_send()
        for k in range(1, chain):

            @pl.when((z < chain - 1) & (z >= k - 1))
            def _():
                self.up(p, k).wait_send()

            @pl.when((z > 0) & (z + k - 1 < chain))
            def _():
                self.down(p, k).wait_send()

        for j in range(chain):
            for yy in range(2):
                self.over(p, j, yy).wait_send()
        if p < 3:
            self.share(p).wait_send()


TILE = 32


def silu(v):
    return v / (1.0 + jnp.exp(-v))


def thirds(v):
    a = v.astype(BF)
    rest = v - a.astype(F32)
    b = rest.astype(BF)
    return a, b, (rest - b.astype(F32)).astype(BF)


def by_rows(rows, body, carry, tile=TILE):
    def step(i, c):
        return body(pl.ds(pl.multiple_of(i * tile, tile), tile), c)

    return lax.fori_loop(0, rows // tile, step, carry)


def column_sum(value):
    rows, width = value.shape
    return jnp.sum(value.reshape(rows // 8, 8, width), axis=0)


def layer_norm(v):
    cen = v - jnp.mean(v, axis=-1, keepdims=True)
    inv = lax.rsqrt(jnp.mean(cen * cen, axis=-1, keepdims=True) + EPSILON)
    return cen * inv, inv


def layer_norm_back(w, hat, inv):
    return inv * (
        w - jnp.mean(w, axis=-1, keepdims=True) - hat * jnp.mean(w * hat, axis=-1, keepdims=True)
    )


def spread_masks(kept, place, pos, drop, seg=None):
    length = kept.shape[1]
    u = lax.broadcasted_iota(jnp.int32, (length, length), 0)
    v = lax.broadcasted_iota(jnp.int32, (length, length), 1)
    uf, vf = u.astype(F32), v.astype(F32)
    column = jnp.sum(jnp.where(u == v, kept, 0.0), axis=1, keepdims=True)
    source = jnp.sum(jnp.where(v <= u, kept, 0.0), axis=1, keepdims=True) - 1.0
    source_row = jnp.sum(jnp.where(u <= v, column, 0.0), axis=0, keepdims=True) - 1.0
    count = jnp.sum(kept, axis=1, keepdims=True)
    place[...] = (jnp.where(source == vf, 1.0, 0.0) * column).astype(BF)
    pad = jnp.where(uf >= count, 1.0, 0.0)
    first = jnp.where(v == 0, pad, 0.0)
    pos[...] = (jnp.where(source_row == uf, 1.0, 0.0) * kept + first).astype(BF)
    drop[...] = jnp.broadcast_to(1.0 - column, drop.shape)
    if seg is not None:
        seg[...] = jnp.where(pad == jnp.where(vf >= count, 1.0, 0.0), 0.0, NEGATIVE)


def join_blocks(blocks, shard, width):
    count, lanes = blocks[0].shape
    lane = lax.broadcasted_iota(jnp.int32, (count, lanes), 1)
    blank = jnp.zeros((count, width - lanes), F32)
    total = jnp.zeros((count, width), F32)
    for j, block in enumerate(blocks):
        part = jnp.concatenate([jnp.where(lane < shard, block, 0.0), blank], axis=1)
        total = total + (pltpu.roll(part, j * shard, 1) if j else part)
    return total


def pack_sums(top, low):
    wide = 1024
    moved = jnp.concatenate(
        [low[:, : wide // 2], top[:, wide:], jnp.zeros_like(top[:, : wide // 2 - (top.shape[1] - wide)])],
        axis=1,
    )
    return jnp.concatenate([top[:, :wide], moved], axis=0)


def unpack_sums(packed):
    wide = 1024
    top = jnp.concatenate([packed[:8], packed[8:, wide // 2 : wide // 2 + 128]], axis=1)
    return top, packed[8:, : wide // 2]


def diagonal(length, mirrored=False):
    u = lax.broadcasted_iota(jnp.int32, (length, length), 0)
    v = lax.broadcasted_iota(jnp.int32, (length, length), 1)
    return jnp.where(u + v == length - 1 if mirrored else u == v, 1.0, 0.0).astype(BF)


def head_mask(i, head_dim):
    lane = lax.broadcasted_iota(jnp.int32, (1, HEAD_LANES), 1)
    return ((lane >= i * head_dim) & (lane < (i + 1) * head_dim)).astype(F32)


def forward_kernel(cfg, *refs):
    fused, chain, heads, head_dim = cfg
    refs = list(refs)
    if fused:
        i_att, i_up, i_down = refs[:3]
        refs = refs[3:]
    else:
        w = refs.pop(0)
    i_tok, cond, i_wada, b_ada, kept, b_qv, b_out, b_down, b_up, rel = refs[:10]
    refs = refs[10:]
    if fused:
        w = refs.pop(0)
    (
        s_hat1, s_inv, s_n1, s_qkv, s_p, s_o, s_branch, s_hat2, s_n2, s_hid, s_slope, s_y,
        s_full, s_xm, o_mod, o_cl, o_small, s_e,
    ) = refs[:18]
    refs = refs[18:]
    (
        wa, wu, wd, res, hat, inv, n, r, qkv, prob, o, branch, hid, slope, y_keep,
        xs, xr, toep, small, cl, part, got, pair, mod, tok, wada, pos, seg, place, drop,
        eye, small_own, wide, bada, mtok,
        gs, gr, gl, ssem, rsem, lsem, ms, mr,
    ) = refs
    at = Place(chain)
    rows, width = res.shape
    lw = heads * head_dim
    shard = width // at.count
    half_heads = heads // 2
    scale = 1.0 / math.sqrt(head_dim)
    sends, recvs, locals_ = Numbered(ssem), Numbered(rsem), Numbered(lsem)
    at.greet()
    gather = None
    if fused:
        side = lambda i: pl.ds(pl.multiple_of(i * width, 128), width)
        halves = (
            lambda i: i_att.at[i],
            lambda i: i_up.at[0, :, side(i)],
            lambda i: i_down.at[:, side(i)],
        )
        gather = Gather(at, halves, w, gs, gr, gl)
    links = Links(at, ms, mr)
    waiting = {}

    def keep(name, src, dst):
        copy = pltpu.make_async_copy(src, dst, locals_.next())
        copy.start()
        waiting.setdefault(name, []).append(copy.wait)

    def give(name, src, dst):
        copy = remote(src, dst, sends.next(), recvs.next(), at.other)
        copy.start()
        waiting.setdefault(name, []).append(copy.wait_send)
        waiting.setdefault("end", []).append(copy.wait_recv)

    def settle(name):
        for wait in waiting.pop(name, []):
            wait()

    def pump(*what):
        if not fused:
            return
        for name, p, *k in what:
            if p < gather.pieces:
                getattr(gather, name)(p, *k)

    def load(p, slot):
        if fused:
            gather.other_in(p)
        keep("load%d" % p, w.at[p], slot)

    def send_cond():
        cl[pl.ds(at.dp, 1)] = cond[pl.ds(at.dp, 1)]
        return links.to_all(lambda peer: cond.at[peer], cl.at[at.dp])

    def modulation_terms(copies):
        for copy in copies:
            copy.wait_recv()
        part[...] = jnp.zeros_like(part)
        parts = thirds(silu(flat(cl[...])[:, :shard]))
        for k in range(6):
            cols = wada[k]
            value = nn(parts[0], cols) + (nn(parts[1], cols) + nn(parts[2], cols))
            value = value.reshape(at.count, 8, lw)
            for m in range(2):
                part[:, m * 8 + k, :lw] = value[:, m, :]
        got[pl.ds(at.dp, 1)] = part[pl.ds(at.dp, 1)]
        return links.to_all(lambda peer: part.at[peer], got.at[at.dp])

    def modulation_sum(copies):
        for copy in copies:
            copy.wait_recv()
        value = got[0]
        for j in range(1, at.count):
            value = value + got[j]
        pair[at.core, at.head] = value + jnp.concatenate([bada[...], bada[...]], axis=0)
        return links.around(pair)

    def modulation(copies):
        for copy in copies:
            copy.wait_recv()
        lane = lax.broadcasted_iota(jnp.int32, (8, ADA_LANES), 1)
        blank = jnp.zeros((8, width - ADA_LANES), F32)
        mine_ = pl.ds(pl.multiple_of(at.core * 8, 8), 8)
        for s in range(2):
            a, b = [
                jnp.concatenate([jnp.where(lane < lw, pair[s, h, mine_, :], 0.0), blank], axis=1)
                for h in range(2)
            ]
            mod[s] = a + pltpu.roll(b, lw, 1)
        keep("mod", mod, o_mod)
        keep("cl", cl, o_cl)

    def share_small():
        wide[...] = jnp.zeros_like(wide)
        wide[0:2, :lw] = b_qv[0].astype(F32)
        small_own[...] = jnp.zeros_like(small_own)
        value = wide[...]
        for half in range(2):
            for k in range(2):
                row = half * 4 + 2 * k
                small_own[row : row + 1, :HEAD_LANES] = value[k : k + 1, :HEAD_LANES]
            value = pltpu.roll(value, ADA_LANES - lw // 2, 1)
        small_own[8:9, :] = b_out[...].astype(F32)
        small_own[9:10, :] = b_down[...].astype(F32)
        small_own[10:11, :] = b_up[:, :width].astype(F32)
        small_own[11:12, :] = b_up[:, width:].astype(F32)
        small_own[16 : 16 + heads, : 2 * rows - 1] = rel[0].astype(F32)
        bada[...] = jnp.zeros_like(bada)
        bada[0:6, :lw] = b_ada[0].astype(F32)
        small[pl.ds(at.core, 1)] = small_own[...][None]
        return links.copy(small_own, small.at[at.core], at.other)

    def bqv_row(s, half, kind):
        return small[s, half * 4 + kind : half * 4 + kind + 1, :HEAD_LANES]

    def bup_row(s, half, cols):
        return small[s, 10 + half : 11 + half, cols]

    def send_across(i):
        copy = remote(xs.at[i], xr.at[i], sends.next(), recvs.next(), at.beside)
        copy.start()
        waiting.setdefault("end", []).append(copy.wait_send)
        return copy

    def total(i, ds):
        return xs[i, ds, :].astype(F32) + xr[i, ds, :].astype(F32)

    def norm_one(s):
        settle("hat1")
        settle("n1")
        settle("inv")

        def body(ds, c):
            v, iv = layer_norm(res[ds, :])
            hat[0, ds, :] = v.astype(BF)
            inv[0, ds, :] = jnp.broadcast_to(iv, (TILE, 128))
            n[0, ds, :] = (v * (1.0 + mod[s, 1:2, :]) + mod[s, 0:1, :]).astype(BF)
            return c

        by_rows(rows, body, 0)
        keep("hat1", hat.at[0], s_hat1.at[s])
        keep("n1", n.at[0], s_n1.at[s, 0])
        give("n1", n.at[0], s_n1.at[s, 1])

    def project(s):
        settle("qkv")
        for half in range(2):
            for j in range(3):
                cols = slice(j * 384, (j + 1) * 384)
                r[:, cols] = nn(n[0], flat(wa[half, :, :, cols]))

            def body(ds, c):
                v = r[ds, :]
                for kind, shift in ((0, 864), (1, 576), (2, 288)):
                    piece = pltpu.roll(v, shift, 1)[:, :HEAD_LANES]
                    qkv[kind, half, ds, :] = (piece + bqv_row(s, half, kind)).astype(BF)
                return c

            by_rows(rows, body, 0)
        keep("qkv", qkv, s_qkv.at[s])

    def attend(s, half):
        if half == 0:
            settle("p")
            settle("o")
        o[half] = jnp.zeros_like(o[half])

        def one(i, c):
            index = half * half_heads + i
            mask = head_mask(i, head_dim).astype(BF)
            line = small[s, pl.ds(16 + index, 1), : 2 * rows]
            skew = pltpu.roll(
                jnp.broadcast_to(line, (rows, 2 * rows)), rows + 1, 1, stride=1, stride_axis=0
            )
            toep[...] = skew[:, :rows].astype(BF)
            if s == 0:
                left = nt(pos[...], toep[...]).astype(BF)
                bias = nt(left, pos[...]) + seg[...]
            else:
                bias = nt(eye[...], toep[...])
            z = nt(qkv[0, half] * mask, qkv[1, half]) * scale + bias
            e = jnp.exp(z - jnp.max(z, axis=-1, keepdims=True))
            p = (e / jnp.sum(e, axis=-1, keepdims=True)).astype(BF)
            prob[index] = p
            o[half] = o[half] + nn(p, qkv[2, half]).astype(BF) * mask
            return c

        lax.fori_loop(0, half_heads, one, 0)
        if half == 1:
            keep("p", prob, s_p.at[s])
            keep("o", o.at[at.core], s_o.at[s, 0])
            give("o", o.at[1 - at.core], s_o.at[s, 1])

    def project_out(i):
        xs[i] = (
            nt(o[0], flat(wa[0, :, :, :HEAD_LANES])) + nt(o[1], flat(wa[1, :, :, :HEAD_LANES]))
        ).astype(BF)
        return send_across(i)

    def norm_two(s, i, copy):
        copy.wait_recv()
        settle("branch")
        settle("hat2")
        settle("n2")

        def body(ds, c):
            b = total(i, ds) + small[s, 8:9, :]
            branch[ds, :] = b.astype(BF)
            xm = res[ds, :] + mod[s, 2:3, :] * b
            res[ds, :] = xm
            v, iv = layer_norm(xm)
            hat[1, ds, :] = v.astype(BF)
            inv[1, ds, :] = jnp.broadcast_to(iv, (TILE, 128))
            n[1, ds, :] = (v * (1.0 + mod[s, 4:5, :]) + mod[s, 3:4, :]).astype(BF)
            return c

        by_rows(rows, body, 0)
        keep("branch", branch, s_branch.at[s])
        keep("inv", inv, s_inv.at[s])
        keep("hat2", hat.at[1], s_hat2.at[s])
        if s == 1:
            keep("out", res, s_xm)
        keep("n2", n.at[1], s_n2.at[s, 0])
        give("n2", n.at[1], s_n2.at[s, 1])

    def hidden(s, half):
        if half == 0:
            settle("hid")
            settle("slope")
        for j in range(3):
            cols = slice(j * 384, (j + 1) * 384)
            r[:, cols] = nn(n[1], flat(wu[half, :, :, cols])) + bup_row(s, half, cols)

        def body(ds, c):
            value, sl = gelu_both(r[ds, :])
            hid[half, ds, :] = value.astype(BF)
            slope[half, ds, :] = sl.astype(BF)
            return c

        by_rows(rows, body, 0)
        if half == 1:
            keep("slope", slope, s_slope.at[s])
            keep("hid", hid.at[at.core], s_hid.at[s, 0])
            give("hid", hid.at[1 - at.core], s_hid.at[s, 1])
            if s == 1:
                keep("hid", hid, s_full)

    def project_down(i):
        xs[i] = (nt(hid[0], flat(wd[0])) + nt(hid[1], flat(wd[1]))).astype(BF)
        return send_across(i)

    def end_block(s, i, copy):
        copy.wait_recv()
        settle("y")
        settle("out")

        def body(ds, c):
            v = total(i, ds) + small[s, 9:10, :]
            y_keep[ds, :] = v.astype(BF)
            res[ds, :] = res[ds, :] + mod[s, 5:6, :] * v
            return c

        by_rows(rows, body, 0)
        keep("y", y_keep, s_y)
        keep("out", res, s_e)

    def spread():
        r[...] = nn(place[...], res[...].astype(BF))
        settle("out")

        def body(ds, c):
            res[ds, :] = r[ds, :] + drop[ds, 0:1] * mtok[2:3, :]
            return c

        by_rows(rows, body, 0)

    copies = send_cond()
    small_copy = share_small()
    if fused:
        for t in range(3):
            gather.split(t)
        gather.start(0)
        gather.start(1)
    keep("tok", i_tok.at[at.core], tok)
    keep("wada", i_wada, wada)
    spread_masks(kept[at.core].astype(F32), place, pos, drop, seg)
    eye[...] = diagonal(rows)
    mtok[...] = join_blocks([cond[j] for j in range(at.count)], shard, width)
    settle("tok")

    def start_residual(ds, c):
        res[ds, :] = tok[ds, :].astype(F32)
        return c

    by_rows(rows, start_residual, 0)
    pump(("step", 0, 1))
    settle("wada")
    copies = modulation_terms(copies)
    pump(("step", 0, 2), ("start", 2), ("step", 0, 3))
    copies = modulation_sum(copies)
    small_copy.wait_recv()
    keep("small", small, o_small)
    pump(("step", 1, 1))
    modulation(copies)
    norm_one(0)
    pump(("step", 1, 2), ("start", 3), ("finish", 0), ("step", 1, 3))
    load(0, wa)
    settle("load0")
    project(0)
    pump(("step", 2, 1))
    attend(0, 0)
    pump(("step", 2, 2), ("start", 4), ("finish", 1))
    attend(0, 1)
    copy = project_out(0)
    pump(("step", 2, 3))
    load(1, wu)
    pump(("step", 3, 1))
    norm_two(0, 0, copy)
    settle("load1")
    pump(("step", 3, 2), ("start", 5), ("finish", 2))
    hidden(0, 0)
    hidden(0, 1)
    pump(("step", 3, 3))
    load(2, wd)
    settle("load2")
    copy = project_down(1)
    pump(("step", 4, 1), ("step", 4, 2), ("finish", 3))
    end_block(0, 1, copy)
    spread()
    norm_one(1)
    load(3, wa)
    pump(("step", 4, 3))
    settle("load3")
    project(1)
    attend(1, 0)
    pump(("step", 5, 1))
    attend(1, 1)
    copy = project_out(2)
    pump(("step", 5, 2), ("finish", 4))
    load(4, wu)
    pump(("step", 5, 3))
    norm_two(1, 2, copy)
    settle("load4")
    hidden(1, 0)
    pump(("finish", 5))
    hidden(1, 1)
    if fused:
        gather.other_in(5)
        for p in range(gather.pieces):
            gather.drain(p)
    for wait in links.waiting:
        wait()
    for name in list(waiting):
        settle(name)


def forward_call(cfg, weights, small, dp_count):
    fused, chain, heads, head_dim = cfg
    _, rows, width = small[0].shape
    pieces = 6
    shard = weights[0].shape[-2]
    groups = width // shard
    cond_lanes = small[1].shape[2]
    bf, f = lambda *s: jax.ShapeDtypeStruct(s, BF), lambda *s: jax.ShapeDtypeStruct(s, F32)
    out_shape = [
        bf(2, rows, width),
        f(2, 2, rows, 128),
        bf(2, 2, rows, width),
        bf(2, 3, 2, rows, HEAD_LANES),
        bf(2, heads, rows, rows),
        bf(2, 2, rows, HEAD_LANES),
        bf(2, rows, width),
        bf(2, rows, width),
        bf(2, 2, rows, width),
        bf(2, 2, rows, width),
        bf(2, 2, rows, width),
        bf(rows, width),
        bf(2, rows, width),
        f(rows, width),
        f(2, 8, width),
        f(dp_count, 8, cond_lanes),
        f(2, 24, width),
        f(rows, width),
    ]
    if fused:
        out_shape = [bf(pieces, 2, groups, shard, width)] + out_shape
    kinds = 5 * chain + 2
    many = 2 * (dp_count - 1) + 8
    slot = pltpu.VMEM((2, groups, shard, width), BF)
    scratch = [
        slot,
        slot,
        slot,
        pltpu.VMEM((rows, width), F32),
        pltpu.VMEM((2, rows, width), BF),
        pltpu.VMEM((2, rows, 128), F32),
        pltpu.VMEM((2, rows, width), BF),
        pltpu.VMEM((rows, width), F32),
        pltpu.VMEM((3, 2, rows, HEAD_LANES), BF),
        pltpu.VMEM((heads, rows, rows), BF),
        pltpu.VMEM((2, rows, HEAD_LANES), BF),
        pltpu.VMEM((rows, width), BF),
        pltpu.VMEM((2, rows, width), BF),
        pltpu.VMEM((2, rows, width), BF),
        pltpu.VMEM((rows, width), BF),
        pltpu.VMEM((4, rows, width), BF),
        pltpu.VMEM((4, rows, width), BF),
        pltpu.VMEM((rows, rows), BF),
        pltpu.VMEM((2, 24, width), F32),
        pltpu.VMEM((dp_count, 8, cond_lanes), F32),
        pltpu.VMEM((dp_count, 16, ADA_LANES), F32),
        pltpu.VMEM((dp_count, 16, ADA_LANES), F32),
        pltpu.VMEM((2, 2, 16, ADA_LANES), F32),
        pltpu.VMEM((2, 8, width), F32),
        pltpu.VMEM((rows, width), BF),
        pltpu.VMEM(small[2].shape, BF),
        pltpu.VMEM((rows, rows), BF),
        pltpu.VMEM((rows, rows), F32),
        pltpu.VMEM((rows, rows), BF),
        pltpu.VMEM((rows, 128), F32),
        pltpu.VMEM((rows, rows), BF),
        pltpu.VMEM((24, width), F32),
        pltpu.VMEM((8, ADA_LANES), F32),
        pltpu.VMEM((8, ADA_LANES), F32),
        pltpu.VMEM((8, width), F32),
        pltpu.SemaphoreType.DMA((pieces, kinds)),
        pltpu.SemaphoreType.DMA((pieces, kinds)),
        pltpu.SemaphoreType.DMA((3,)),
        pltpu.SemaphoreType.DMA((16,)),
        pltpu.SemaphoreType.DMA((16,)),
        pltpu.SemaphoreType.DMA((48,)),
        pltpu.SemaphoreType.DMA((many,)),
        pltpu.SemaphoreType.DMA((many,)),
    ]

    def body(*refs):
        forward_kernel(cfg, *refs)

    vm = pl.BlockSpec(memory_space=pltpu.VMEM)
    hbm = pl.BlockSpec(memory_space=pl.ANY)
    result = pl.pallas_call(
        body,
        out_shape=out_shape,
        in_specs=[hbm] * len(weights) + [hbm, vm, hbm] + [vm] * 7,
        out_specs=[hbm] * len(out_shape),
        scratch_shapes=scratch,
        compiler_params=pltpu.CompilerParams(
            collective_id=0, has_side_effects=True, vmem_limit_bytes=VMEM_BYTES
        ),
        name="forward_blocks",
    )(*weights, *small)
    return result if fused else [weights[0]] + list(result)


class Scatter:
    def __init__(self, at, order, g, yr, zr, mr, red, out, ssem, rsem, osem, isem, lsem, credit):
        self.at, self.order = at, order
        self.g, self.yr, self.zr, self.mr, self.red, self.out = g, yr, zr, mr, red, out
        self.ssem, self.rsem, self.osem, self.isem, self.lsem = ssem, rsem, osem, isem, lsem
        self.credit = credit
        chain = at.chain
        need = lambda z, t: chain if t == z else (chain - t + z if t > z else chain - z + t)
        self.table = [sorted(range(chain), key=lambda t: (need(z, t), t)) for z in range(chain)]

    def slots(self, r):
        return r % self.g.shape[0], r % self.yr.shape[0]

    def target(self, i):
        return sum(jnp.where(self.at.z == z, self.table[z][i], 0) for z in range(self.at.chain))

    def own(self, r, t):
        return self.g.at[self.slots(r)[0], t * 2 + self.at.y]

    def theirs(self, r, t):
        return self.g.at[self.slots(r)[0], t * 2 + 1 - self.at.y]

    def copy(self, src, dst, r, kind, device):
        return remote(src, dst, self.ssem.at[r, kind], self.rsem.at[r, kind], device)

    def cross(self, r, t):
        return self.copy(
            self.theirs(r, t), self.yr.at[self.slots(r)[1], t], r, t, self.at.across
        )

    def up(self, r, t):
        return self.copy(
            self.own(r, t), self.zr.at[self.slots(r)[1], t], r, self.at.chain + t, self.at.above
        )

    def down(self, r, t, last=None):
        z = self.at.z - 1 if last is None else last
        place = jnp.where(t == z, self.at.chain, t)
        return self.copy(
            self.own(r, t), self.zr.at[self.slots(r)[1], place], r, 2 * self.at.chain + t, self.at.below
        )

    def to_mate(self, r):
        return self.copy(
            self.theirs(r, self.at.mate_z), self.mr.at[self.slots(r)[1]], r, 3 * self.at.chain, self.at.mate
        )

    def add(self, block, got):
        block[...] = (block[...].astype(F32) + got[...].astype(F32)).astype(BF)

    def begin(self, r):
        at, chain = self.at, self.at.chain
        if r >= self.yr.shape[0]:
            pl.semaphore_wait(self.credit.at[0], 1)

            @pl.when(at.z < chain - 1)
            def _():
                pl.semaphore_wait(self.credit.at[1], 1)

            @pl.when(at.z > 0)
            def _():
                pl.semaphore_wait(self.credit.at[2], 1)

        if r in SUM_BY_MATE:
            self.to_mate(r).start()
        for i in range(chain - 1):
            t = self.target(i)
            if r in SUM_BY_MATE:

                @pl.when(t != at.mate_z)
                def _():
                    self.cross(r, t).start()

            else:
                self.cross(r, t).start()
        if r not in SUM_BY_MATE:
            self.cross(r, at.z).start()

    def mated(self, r):
        if r in SUM_BY_MATE:
            self.to_mate(r).wait_recv()
            self.add(self.theirs(r, self.at.z), self.mr.at[self.slots(r)[1]])
            self.cross(r, self.at.z).start()

    def arrive(self, r, i):
        t = self.target(i)

        def take():
            self.cross(r, t).wait_recv()
            self.add(self.own(r, t), self.yr.at[self.slots(r)[1], t])

        if r in SUM_BY_MATE:
            pl.when(t != self.at.mate_z)(take)
        else:
            take()

    def step(self, r, k):
        z, chain = self.at.z, self.at.chain

        @pl.when((z <= k - 1) & (z < chain - 1))
        def _():
            t = chain - k + z
            if k > 1:

                @pl.when(z > 0)
                def _():
                    self.up(r, t).wait_recv()
                    self.add(self.own(r, t), self.zr.at[self.slots(r)[1], t])

            self.up(r, t).start()

        @pl.when((chain - 1 - z <= k - 1) & (z > 0))
        def _():
            t = k - chain + z
            if k > 1:

                @pl.when(z < chain - 1)
                def _():
                    self.down(r, t, last=z).wait_recv()
                    self.add(self.own(r, t), self.zr.at[self.slots(r)[1], t])

            self.down(r, t).start()

    def finish(self, r):
        at, chain = self.at, self.at.chain
        z = at.z
        slot = self.slots(r)[1]
        held = self.red.shape[0]
        if r >= held:
            self.hand_over_done(r - held)
        red = self.red.at[r % held]
        red[...] = self.own(r, z)[...].astype(F32)

        @pl.when(z > 0)
        def _():
            self.up(r, z).wait_recv()
            red[...] = red[...] + self.zr[slot, z].astype(F32)

        @pl.when(z < chain - 1)
        def _():
            self.down(r, z, last=z).wait_recv()
            red[...] = red[...] + self.zr[slot, chain].astype(F32)

        if r + self.yr.shape[0] < len(self.order):
            pl.semaphore_signal(self.credit.at[0], inc=1, device_id=at.across, device_id_type=MESH)

            @pl.when(z > 0)
            def _():
                pl.semaphore_signal(self.credit.at[1], inc=1, device_id=at.below, device_id_type=MESH)

            @pl.when(z < chain - 1)
            def _():
                pl.semaphore_signal(self.credit.at[2], inc=1, device_id=at.above, device_id_type=MESH)

        s, t = self.order[r]

        @pl.when(at.core == s)
        def _():
            self.keep(r).start()

        @pl.when(at.core != s)
        def _():
            self.hand_over(r).start()

    def keep(self, r):
        return pltpu.make_async_copy(
            self.red.at[r % self.red.shape[0]], self.out.at[self.order[r][1], self.at.core], self.lsem.at[r]
        )

    def hand_over(self, r):
        return remote(
            self.red.at[r % self.red.shape[0]],
            self.out.at[self.order[r][1], self.at.core],
            self.osem.at[r],
            self.isem.at[r],
            self.at.other,
        )

    def hand_over_done(self, r):
        s, t = self.order[r]

        @pl.when(self.at.core == s)
        def _():
            self.keep(r).wait()

        @pl.when(self.at.core != s)
        def _():
            self.hand_over(r).wait_send()

    def drain(self, r):
        z, chain = self.at.z, self.at.chain
        if r in SUM_BY_MATE:
            self.to_mate(r).wait_send()
        for t in range(chain):
            if r in SUM_BY_MATE:

                @pl.when(t != self.at.mate_z)
                def _():
                    self.cross(r, t).wait_send()

            else:
                self.cross(r, t).wait_send()

            @pl.when(t > z)
            def _():
                self.up(r, t).wait_send()

            @pl.when(t < z)
            def _():
                self.down(r, t).wait_send()

    def end(self):
        for r in range(len(self.order)):
            if r + self.red.shape[0] >= len(self.order):
                self.hand_over_done(r)
            s, t = self.order[r]

            @pl.when(self.at.core == s)
            def _():
                remote(
                    self.red.at[0],
                    self.out.at[t, 1 - self.at.core],
                    self.osem.at[r],
                    self.isem.at[r],
                    self.at.other,
                ).wait_recv()


ORDER = ((1, 2), (1, 1), (1, 0), (0, 2), (0, 1), (0, 0))


def backward_kernel(cfg, *refs):
    fused, chain, heads, head_dim = cfg
    refs = list(refs)
    w = refs.pop(0)
    (
        i_hat1, i_inv, i_n1, i_qkv, i_p, i_o, i_branch, i_hat2, i_n2, i_hid, i_slope, i_y, i_full, i_xm,
        i_e,
    ) = refs[:15]
    refs = refs[15:]
    i_dout, mod, i_small, i_cl, i_wada, kept = refs[:6]
    refs = refs[6:]
    red_out, o_dx, o_out, o_dm, o_two = refs[:5]
    refs = refs[5:]
    (
        wslot, hat1, inv, qkv, prob, o, branch, hat2, n2, hid, slope,
        d, r, dy, dpre, dattn, dqkv, do, xs, xr, g, yr, zr, mr, red,
        stats, got, out_one, in_one, dc, in_two, small, cl, wada, flips, pos, place, drop, eye, dout, gs, gr, go, gi, gl, credit, ssem, rsem, lsem, ms, mrs,
    ) = refs
    at = Place(chain)
    rows, width = d.shape
    lw = heads * head_dim
    shard = width // at.count
    half_heads = heads // 2
    scale = 1.0 / math.sqrt(head_dim)
    sends, recvs, locals_ = Numbered(ssem), Numbered(rsem), Numbered(lsem)
    at.greet()
    links = Links(at, ms, mrs)
    stats[...] = jnp.zeros_like(stats)
    dc[...] = jnp.zeros_like(dc)
    scatter = (
        Scatter(at, ORDER, g, yr, zr, mr, red, red_out, gs, gr, go, gi, gl, credit) if fused else None
    )
    slots = g.shape[0]
    waiting = {}

    def fetch(name, src, dst):
        copy = pltpu.make_async_copy(src, dst, locals_.next())
        copy.start()
        waiting.setdefault(name, []).append(copy.wait)

    def settle(name):
        for wait in waiting.pop(name, []):
            wait()

    def give(name, src, dst):
        copy = remote(src, dst, sends.next(), recvs.next(), at.other)
        copy.start()
        waiting.setdefault(name + " in", []).append(copy.wait_recv)
        waiting.setdefault(name + " out", []).append(copy.wait_send)

    def pump(*what):
        if not fused:
            return
        for name, r_, *k in what:
            if 0 <= r_ < len(ORDER):
                getattr(scatter, name)(r_, *k)

    def pump_rest(r_, start):
        for i in range(start, chain):
            pump(("arrive", r_, i))
            if i < chain - 1:
                pump(("step", r_, i + 1))
        pump(("finish", r_))

    def send_across(i):
        if i > 1:
            settle("x out %d" % (i - 2))
        copy = remote(xs.at[i % 2], xr.at[i % 2], sends.next(), recvs.next(), at.beside)
        copy.start()
        waiting.setdefault("x in %d" % i, []).append(copy.wait_recv)
        waiting.setdefault("x out %d" % i, []).append(copy.wait_send)

    def total(i, ds):
        return xs[i % 2, ds, :].astype(F32) + xr[i % 2, ds, :].astype(F32)

    def stat(s, row, value):
        stats[s, row : row + 1, :] = jnp.sum(value, axis=0, keepdims=True)

    zero8 = lambda: jnp.zeros((8, width), F32)
    spans = [slice(k * HEAD_LANES, (k + 1) * HEAD_LANES) for k in range(3)]
    spot = lambda half: jnp.where(half == at.core, 0, 2)

    def load(name, s):
        src, dst = {
            "slope": (i_slope, slope),
            "hid": (i_hid, hid),
            "n1": (i_n1, hid),
            "n2": (i_n2, n2),
            "hat2": (i_hat2, hat2),
            "inv": (i_inv, inv),
            "branch": (i_branch, branch),
            "p": (i_p, prob),
            "qkv": (i_qkv, qkv),
            "o": (i_o, o),
            "hat1": (i_hat1, hat1),
        }[name]
        fetch(name, src.at[s], dst)

    def weight(p, slot):
        fetch("w%d" % slot, w.at[p], wslot.at[slot])

    def product(r_, parts):
        slot = r_ % slots
        if r_ >= slots:
            if fused:
                scatter.drain(r_ - slots)
            else:
                settle("g%d" % (r_ - slots))
        for j in range(width // 384):
            cols = slice(j * 384, (j + 1) * 384)
            value = 0.0
            for lhs, rhs in parts(j):
                value = value + tn(lhs, rhs)
            g[slot, :, :, cols] = value.astype(BF).reshape(g.shape[1], g.shape[2], 384)
        if not fused:
            s, t = ORDER[r_]
            fetch("g%d" % r_, g.at[slot], red_out.at[s * 3 + t])

    def cols_of(ref, j):
        return flat(ref[0:2, :, j * 384 : (j + 1) * 384])

    down_slot, up_slot, att_slot = (1, 0), (0, 1), (1, 0)

    def base(s):
        return 0 if s == 1 else 3

    def exchange(s):
        return 0 if s == 1 else 2

    def back_gate(s):
        settle("dy out")
        if s == 0:
            settle("y")

        def one(ds, c):
            a, b = c
            dv = d[ds, :]
            v = (dv * mod[s, 5:6, :]).astype(BF)
            dy[0, ds, :] = v
            if s == 0:
                a = a + column_sum(dv * xs[2, ds, :].astype(F32))
            return (a, b + column_sum(v.astype(F32)))

        a, b = by_rows(rows, one, (zero8(), zero8()))
        if s == 0:
            stat(s, 5, a)
        stat(s, 8, b)
        give("dy", dy.at[0], dy.at[1])

    def back_hidden(s):
        slot = down_slot[s]
        settle("w%d" % slot)
        settle("slope")
        settle("dpre out")
        for half in range(2):
            for j in range(3):
                cols = slice(j * 384, (j + 1) * 384)
                v = (nn(dy[0], flat(wslot[slot, half, :, :, cols])) * slope[half, :, cols].astype(F32)).astype(BF)
                dpre[spot(half), :, cols] = v
                stats[s, 10 + half : 11 + half, cols] = jnp.sum(v.astype(F32), axis=0, keepdims=True)
        give("dpre", dpre.at[2], dpre.at[1])

    def down_product(s):
        settle("dy in")
        settle("hid")
        product(base(s), lambda j: [(flat(dy[...]), cols_of(hid, j))])
        load("n1", s)

    def back_up(s):
        slot = up_slot[s]
        xi = exchange(s)
        settle("w%d" % slot)
        if xi > 1:
            settle("x out %d" % (xi - 2))
        xs[xi % 2] = (
            nt(dpre[spot(0)], flat(wslot[slot, 0])) + nt(dpre[spot(1)], flat(wslot[slot, 1]))
        ).astype(BF)
        send_across(xi)

    def up_product(s):
        settle("dpre in")
        settle("n2")
        product(base(s) + 1, lambda j: [(flat(n2[...]), cols_of(dpre, j))])

    def back_norm_two(s):
        xi = exchange(s)
        settle("x in %d" % xi)
        settle("hat2")
        settle("inv")
        settle("branch")
        settle("dattn out")

        def two(ds, c):
            c0, c1, c2, c3 = c
            dn = total(xi, ds)
            hv = hat2[ds, :].astype(F32)
            dxm = d[ds, :] + layer_norm_back(dn * (1.0 + mod[s, 4:5, :]), hv, inv[1, ds, 0:1])
            d[ds, :] = dxm
            da = (dxm * mod[s, 2:3, :]).astype(BF)
            dattn[0, ds, :] = da
            return (
                c0 + column_sum(dn),
                c1 + column_sum(dn * hv),
                c2 + column_sum(dxm * branch[ds, :].astype(F32)),
                c3 + column_sum(da.astype(F32)),
            )

        c0, c1, c2, c3 = by_rows(rows, two, (zero8(),) * 4)
        stat(s, 3, c0)
        stat(s, 4, c1)
        stat(s, 2, c2)
        stat(s, 9, c3)
        give("dattn", dattn.at[0], dattn.at[1])

    def back_heads(s, half):
        slot = att_slot[s]
        if half == 0:
            settle("w%d" % slot)
            settle("p")
            settle("qkv")
            settle("dqkv out")
        if True:
            do[half] = nn(dattn[0], flat(wslot[slot, half, :, :, :HEAD_LANES])).astype(BF)
            r[...] = jnp.zeros_like(r)

            def head(i, c):
                index = half * half_heads + i
                mask = head_mask(i, head_dim)
                low_mask = mask.astype(BF)
                p = prob[index]
                dom = do[half] * low_mask
                r[:, spans[2]] = r[:, spans[2]] + tn(p, dom)
                ds = nt(dom, qkv[2, half])
                pf = p.astype(F32)
                dz = (pf * (ds - jnp.sum(pf * ds, axis=-1, keepdims=True))).astype(BF)
                r[:, spans[0]] = r[:, spans[0]] + nn(dz, qkv[1, half]) * mask
                r[:, spans[1]] = r[:, spans[1]] + tn(dz, qkv[0, half]) * mask
                square = nn(dz, flips[s])
                high = square.astype(BF)
                if s == 0:
                    low = (square - high.astype(F32)).astype(BF)
                    square = tn(high, pos[...]) + tn(low, pos[...])
                else:
                    square = tn(high, eye[...])
                wide = jnp.concatenate([square, jnp.zeros_like(square)], axis=1)
                skew = pltpu.roll(wide, 0, 1, stride=1, stride_axis=0)
                stats[s, pl.ds(16 + index, 1), : 2 * rows] = jnp.sum(skew, axis=0, keepdims=True)
                return c

            lax.fori_loop(0, half_heads, head, 0)
            where = spot(half)

            def gather_rows(ds, c):
                blank = jnp.zeros((TILE, HEAD_LANES), F32)
                v = 0.0
                for kind, shift, factor in ((0, 288, scale), (1, 576, scale), (2, 864, 1.0)):
                    part = jnp.concatenate([r[ds, spans[kind]] * factor, blank, blank], axis=1)
                    v = v + pltpu.roll(part, shift, 1)
                v = v.astype(BF)
                dqkv[where, ds, :] = v
                return c + column_sum(v.astype(F32))

            stat(s, 12 + half, by_rows(rows, gather_rows, zero8()))
        if half == 1:
            give("dqkv", dqkv.at[2], dqkv.at[1])

    def back_qkv(s):
        slot = att_slot[s]
        xi = exchange(s) + 1
        if xi > 1:
            settle("x out %d" % (xi - 2))
        xs[xi % 2] = (
            nt(dqkv[spot(0)], flat(wslot[slot, 0])) + nt(dqkv[spot(1)], flat(wslot[slot, 1]))
        ).astype(BF)
        send_across(xi)

    def att_product(s):
        settle("dqkv in")
        settle("dattn in")
        settle("n1")
        settle("o")
        product(
            base(s) + 2,
            lambda j: [(flat(hid[...]), cols_of(dqkv, j))]
            + ([(flat(dattn[...]), flat(o[...]))] if j == 0 else []),
        )

    def back_norm_one(s):
        xs_free = exchange(s) + 1
        settle("x in %d" % xs_free)
        settle("hat1")

        def three(ds, c):
            c0, c1, c2 = c
            dn = total(xs_free, ds)
            hv = hat1[ds, :].astype(F32)
            dx = d[ds, :] + layer_norm_back(dn * (1.0 + mod[s, 1:2, :]), hv, inv[0, ds, 0:1])
            d[ds, :] = dx
            return (c0 + column_sum(dn), c1 + column_sum(dn * hv), c2 + column_sum(dx * drop[ds, 0:1]))

        c0, c1, c2 = by_rows(rows, three, (zero8(),) * 3)
        stat(s, 0, c0)
        stat(s, 1, c1)
        stat(s, 14, c2)
        to_section("dx", s, d, o_dx)

    def to_section(name, s, src, out):
        here = pltpu.make_async_copy(src, out.at[at.core], locals_.next())
        ss, rs = sends.next(), recvs.next()

        @pl.when(at.core == s)
        def _():
            here.start()

        @pl.when(at.core != s)
        def _():
            remote(src, out.at[at.core], ss, rs, at.other).start()

        def sent():
            @pl.when(at.core == s)
            def _():
                here.wait()

            @pl.when(at.core != s)
            def _():
                remote(src, out.at[at.core], ss, rs, at.other).wait_send()

        def arrived():
            @pl.when(at.core == s)
            def _():
                remote(src, out.at[1 - at.core], ss, rs, at.other).wait_recv()

        waiting.setdefault(name, []).append(sent)
        waiting.setdefault("end", []).append(arrived)

    def project_down():
        settle("w0")
        settle("full")
        xs[2] = (nt(dqkv[0], flat(wslot[0, 0])) + nt(dqkv[1], flat(wslot[0, 1]))).astype(BF)
        copy = remote(xs.at[2], xr.at[2], sends.next(), recvs.next(), at.beside)
        copy.start()
        waiting.setdefault("y in", []).append(copy.wait_recv)
        waiting.setdefault("y out", []).append(copy.wait_send)

    def end_forward():
        settle("y in")
        settle("y out")
        settle("xm")
        settle("small")

        def body(ds, c):
            v = xs[2, ds, :].astype(F32) + xr[2, ds, :].astype(F32) + small[1, 9:10, :]
            r[ds, :] = r[ds, :] + mod[1, 5:6, :] * v
            return c + column_sum(dout[ds, :].astype(F32) * v)

        stat(1, 5, by_rows(rows, body, zero8()))
        to_section("result", 1, r, o_out)

    def sums_begin():
        stats[0, 14:15, :] = stats[1, 14:15, :]
        return links.copy(stats.at[1 - at.core], got, at.other)

    def sums_share(copy):
        copy.wait_recv()
        top = stats[at.core, 8:16, :] + got[8:16, :]
        low = stats[at.core, 16:24, :] + got[16:24, :]
        row = lax.broadcasted_iota(jnp.int32, (8, ADA_LANES), 0)
        lane = lax.broadcasted_iota(jnp.int32, (8, ADA_LANES), 1)

        def cut(value):
            value = jnp.where(
                at.head == 0, value[:, :ADA_LANES], pltpu.roll(value, width - lw, 1)[:, :ADA_LANES]
            )
            return jnp.where((row < 6) & (lane < lw), value, 0.0)

        own, other = cut(stats[at.core, 0:8, :]), cut(got[0:8, :])
        both_ = [jnp.where(at.core == 0, own, other), jnp.where(at.core == 0, other, own)]
        both_ = jnp.concatenate(both_, axis=0).astype(BF)
        for j in range(at.count):
            out_one[j, :, :ADA_LANES] = both_
        packed = pack_sums(top, low).astype(BF)
        for j in range(at.count):
            part = (j % 8) * 128
            out_one[j, :, ADA_LANES:] = packed[:, part : part + 128]
        in_one[pl.ds(at.dp, 1)] = out_one[pl.ds(at.dp, 1)]
        return links.to_all(lambda peer: out_one.at[peer], in_one.at[at.dp])

    def cond_terms(copies):
        for copy in copies:
            copy.wait_recv()
        settle("wada")
        settle("cl")
        fetch("dm", in_one.at[:, :, pl.ds(0, ADA_LANES)], o_dm)
        lhs = flat(in_one[:, :, :lw])
        row = lax.rem(lax.broadcasted_iota(jnp.int32, (lhs.shape[0], 1), 0), 8)
        total_ = jnp.zeros((lhs.shape[0], shard), F32)
        for k in range(6):
            total_ = total_ + jnp.where(row == k, nt(lhs, wada[k]), 0.0)
        total_ = total_.reshape(at.count, 16, shard)
        for m in range(2):
            dc[at.core, at.head, m, :, :shard] = jnp.sum(total_[:, m * 8 : (m + 1) * 8, :], axis=1)
        return links.around(dc)

    def cond_share(copies):
        for copy in copies:
            copy.wait_recv()
        cond_lanes = dc.shape[4]
        for m in range(2):
            value = (dc[0, 0, m] + dc[0, 1, m]) + (dc[1, 0, m] + dc[1, 1, m])
            v = cl[:, m, :]
            sig = 1.0 / (1.0 + jnp.exp(-v))
            parts.append(value * (sig * (1.0 + v * (1.0 - sig))))
        value = in_one[0, :, ADA_LANES:].astype(F32)
        for j in range(1, at.count):
            value = value + in_one[j, :, ADA_LANES:].astype(F32)
        grads = jnp.concatenate(parts, axis=0)
        in_two[at.dp, :, :cond_lanes] = grads.astype(BF)
        in_two[at.dp, 0:16, cond_lanes:] = value.astype(BF)
        return links.to_all(lambda peer: in_two.at[at.dp], in_two.at[at.dp])

    def cond_end(copies):
        for copy in copies:
            copy.wait_recv()
        fetch("two", in_two, o_two)

    parts = []
    fetch("dout", i_dout.at[at.core], dout)
    load("hid", 1)
    weight(5, 0)
    load("slope", 1)
    weight(4, 1)
    for name in ("n2", "hat2", "inv", "branch", "p", "qkv", "o", "hat1"):
        load(name, 1)
    for name, src, dst in (
        ("y", i_y, xs.at[2]),
        ("small", i_small, small),
        ("cl", i_cl, cl),
        ("wada", i_wada, wada),
    ):
        fetch(name, src, dst)

    to_section("e", 0, i_e, o_out)
    settle("dout")

    def start_rows(ds, c):
        d[ds, :] = dout[ds, :].astype(F32)
        return c

    by_rows(rows, start_rows, 0)

    def to_encoder():
        r[...] = tn(place[...], d[...].astype(BF))
        settle("dx")

        def move(ds, c):
            d[ds, :] = r[ds, :]
            return c

        by_rows(rows, move, 0)

    back_gate(1)
    down_product(1)
    pump(("begin", 0))
    back_hidden(1)
    weight(3, 0)
    load("slope", 0)
    back_up(1)
    weight(2, 1)
    up_product(1)
    load("n2", 0)
    pump(("begin", 1))
    pump(("arrive", 0, 0), ("step", 0, 1), ("arrive", 0, 1), ("step", 0, 2))
    spread_masks(kept[at.core].astype(F32), place, pos, drop)
    eye[...] = diagonal(rows)
    flips[1] = diagonal(rows, True)
    flips[0] = nn(pos[...], flips[1]).astype(BF)
    back_norm_two(1)
    load("hat2", 0)
    load("branch", 0)
    back_heads(1, 0)
    pump(("arrive", 0, 2), ("step", 0, 3))
    back_heads(1, 1)
    load("p", 0)
    load("qkv", 0)
    back_qkv(1)
    weight(1, 0)
    pump(("arrive", 0, 3))
    att_product(1)
    load("hid", 0)
    load("o", 0)
    pump(("begin", 2))
    pump(("mated", 1), ("arrive", 1, 0), ("step", 1, 1), ("finish", 0))
    back_norm_one(1)
    load("hat1", 0)
    load("inv", 0)
    to_encoder()
    back_gate(0)
    pump(("arrive", 1, 1), ("step", 1, 2))
    back_hidden(0)
    weight(0, 1)
    down_product(0)
    pump(("begin", 3))
    pump(("arrive", 1, 2), ("step", 1, 3))
    back_up(0)
    weight(5, 0)
    pump(("arrive", 1, 3), ("mated", 2), ("arrive", 2, 0), ("step", 2, 1), ("finish", 1))
    up_product(0)
    pump(("begin", 4))
    pump(("arrive", 2, 1), ("step", 2, 2))
    back_norm_two(0)
    back_heads(0, 0)
    pump(("arrive", 2, 2), ("step", 2, 3))
    back_heads(0, 1)
    back_qkv(0)
    fetch("xm", i_xm, r)
    pump(("arrive", 2, 3), ("mated", 3), ("arrive", 3, 0), ("step", 3, 1), ("finish", 2))
    att_product(0)
    fetch("full", i_full, dqkv.at[0:2])
    pump(("begin", 5))
    pump(("arrive", 3, 1), ("step", 3, 2))
    project_down()
    back_norm_one(0)
    pump(("arrive", 3, 2), ("step", 3, 3))
    end_forward()
    copy = sums_begin()
    pump(("arrive", 3, 3), ("mated", 4), ("arrive", 4, 0), ("step", 4, 1), ("finish", 3))
    copies = sums_share(copy)
    pump(("arrive", 4, 1), ("step", 4, 2), ("arrive", 4, 2), ("step", 4, 3), ("arrive", 4, 3), ("arrive", 5, 0), ("step", 5, 1))
    copies = cond_terms(copies)
    pump(("finish", 4))
    copies = cond_share(copies)
    pump(("arrive", 5, 1), ("step", 5, 2), ("arrive", 5, 2), ("step", 5, 3), ("arrive", 5, 3), ("finish", 5))
    cond_end(copies)
    if fused:
        for r_ in range(len(ORDER) - slots, len(ORDER)):
            scatter.drain(r_)
        scatter.end()
    for wait in links.waiting:
        wait()
    for name in list(waiting):
        settle(name)


def backward_call(cfg, w, saved, small):
    fused, chain, heads, head_dim = cfg
    _, rows, width = small[0].shape
    pieces, _, groups, shard, _ = w.shape
    count, _, cond_lanes = small[3].shape
    many = 2 * (count - 1) + 6
    each = 128
    bf, f = lambda *s: pltpu.VMEM(s, BF), lambda *s: pltpu.VMEM(s, F32)
    dma = lambda *s: pltpu.SemaphoreType.DMA(s)
    out_shape = [
        jax.ShapeDtypeStruct((3, 2, shard, width), F32)
        if fused
        else jax.ShapeDtypeStruct((pieces, groups, shard, width), BF),
        jax.ShapeDtypeStruct((2, rows, width), F32),
        jax.ShapeDtypeStruct((2, rows, width), F32),
        jax.ShapeDtypeStruct((count, 16, ADA_LANES), BF),
        jax.ShapeDtypeStruct((count, 2 * count, cond_lanes + each), BF),
    ]
    some = 3 if fused else 1
    links = chain if fused else 1
    block = shard if fused else 16
    scratch = [
        bf(2, 2, groups, shard, width),
        bf(rows, width),
        f(2, rows, 128),
        bf(3, 2, rows, HEAD_LANES),
        bf(heads, rows, rows),
        bf(2, rows, HEAD_LANES),
        bf(rows, width),
        bf(rows, width),
        bf(2, rows, width),
        bf(2, rows, width),
        bf(2, rows, width),
        f(rows, width),
        f(rows, width),
        bf(2, rows, width),
        bf(3, rows, width),
        bf(2, rows, width),
        bf(3, rows, width),
        bf(2, rows, HEAD_LANES),
        bf(3, rows, width),
        bf(3, rows, width),
        bf(4, groups, shard, width),
        bf(some, links, block, width),
        bf(some, links + 1, block, width),
        bf(some, block, width),
        f(2, block, width),
        f(2, 24, width),
        f(24, width),
        bf(count, 16, ADA_LANES + each),
        bf(count, 16, ADA_LANES + each),
        f(2, 2, 2, count, cond_lanes),
        bf(count, 2 * count, cond_lanes + each),
        f(2, 24, width),
        f(count, 8, cond_lanes),
        bf(*small[4].shape),
        bf(2, rows, rows),
        bf(rows, rows),
        bf(rows, rows),
        f(rows, 128),
        bf(rows, rows),
        bf(rows, width),
        dma(6, 3 * links + 1),
        dma(6, 3 * links + 1),
        dma(6),
        dma(6),
        dma(6),
        pltpu.SemaphoreType.REGULAR((3,)),
        dma(20),
        dma(20),
        dma(56),
        dma(many),
        dma(many),
    ]

    def body(*refs):
        backward_kernel(cfg, *refs)

    vm = pl.BlockSpec(memory_space=pltpu.VMEM)
    hbm = pl.BlockSpec(memory_space=pl.ANY)
    return pl.pallas_call(
        body,
        out_shape=out_shape,
        in_specs=[hbm] * (1 + len(saved)) + [hbm, vm, hbm, hbm, hbm, vm],
        out_specs=[hbm] * len(out_shape),
        scratch_shapes=scratch,
        compiler_params=pltpu.CompilerParams(
            collective_id=1, has_side_effects=True, vmem_limit_bytes=VMEM_BYTES
        ),
        name="backward_blocks",
    )(w, *saved, *small)


def unpack_two(two, count, cond_lanes):
    top, rel = unpack_sums(
        jnp.concatenate([two[j, 0:16, cond_lanes:] for j in range(8)], axis=1).astype(F32)
    )
    blocks = [
        [two[j, m * count : (m + 1) * count, :cond_lanes].astype(F32) for m in range(2)]
        for j in range(count)
    ]
    return top, rel, blocks


def finish_kernel(cfg, red, outs, dx, two, dm, cl, *refs):
    _, _, heads, head_dim = cfg
    r_outs, r_dx, g_qkv, g_out, g_up, g_down, g_ada, g_class = refs[:8]
    b_qv, b_out, b_up, b_down, b_ada, rel, mask = refs[8:15]
    att, rest, t_qkv, t_out, t_ada, t_class, t_rows, sems = refs[15:]
    head = lax.axis_index("head")
    _, _, shard, width = red.shape
    lw = heads * head_dim
    hw = lw // 2
    count, _, cond_lanes = cl.shape
    slots = Numbered(sems)
    waits = []

    def move(src, dst):
        copy = pltpu.make_async_copy(src, dst, slots.next())
        copy.start()
        waits.append(copy.wait)
        return copy

    second = pltpu.make_async_copy(red.at[pl.ds(1, 2)], rest, slots.next())
    second.start()
    third = []
    for i, source in enumerate((outs, dx)):
        third.append(pltpu.make_async_copy(source, t_rows.at[i], slots.next()))
        third[i].start()
    first = pltpu.make_async_copy(red.at[0], att, slots.next())
    first.start()

    def half(value):
        moved = pltpu.roll(value, width - lw, 1)
        return jnp.where(head == 0, value[:, :ADA_LANES], moved[:, :ADA_LANES])

    rows, table, blocks = unpack_two(two[...], count, cond_lanes)
    picks, grads, parts = [], [], []
    for m in range(2):
        block = cl[:, m, :]
        place = lax.broadcasted_iota(jnp.int32, block.shape, 1)
        label = jnp.sum(jnp.where(place == shard, block, 0.0), axis=1, keepdims=True)
        span = lax.broadcasted_iota(jnp.int32, (count, t_class.shape[1]), 1).astype(F32)
        picks.append(jnp.where(span == label, 1.0, 0.0))
        grads.append(half(join_blocks([pair[m] for pair in blocks], shard, width)))
        parts.append(silu(block))
    pick_all = jnp.concatenate(picks, axis=0).astype(BF)
    a, b, c = thirds(jnp.concatenate(grads, axis=0))
    t_class[...] = (tn(a, pick_all) + (tn(b, pick_all) + tn(c, pick_all)))[:lw, :]
    move(t_class, g_class)
    second.wait()
    for side in range(2):
        move(rest.at[0, side], g_up.at[0, :, pl.ds(side * width, width)])
        move(rest.at[1, side], g_down.at[:, pl.ds(side * width, width)])
    for i, target in enumerate((r_outs, r_dx)):
        third[i].wait()
        move(t_rows.at[i], target.at[0])
    a, b, c = thirds(jnp.concatenate(parts, axis=0))
    for k in range(6):
        pair = jnp.concatenate([dm[:, k, :], dm[:, 8 + k, :]], axis=0).astype(BF)
        t_ada[k] = (tn(a, pair) + (tn(b, pair) + tn(c, pair)))[:shard, :lw]
    move(t_ada, g_ada)
    first.wait()
    wide = lax.broadcasted_iota(jnp.int32, (shard, width), 1)
    for k in range(4):
        value = 0.0
        for side in range(2):
            moved = pltpu.roll(att[side], (side - k) * hw % width, 1) if side != k else att[side]
            value = value + jnp.where((wide >= side * hw) & (wide < (side + 1) * hw), moved, 0.0)
        if k == 0:
            t_out[...] = value[:, :lw]
        else:
            t_qkv[k - 1] = value[:, :lw]
    move(t_out, g_out)
    move(t_qkv, g_qkv)
    for side in range(2):
        b_up[:, side * width : (side + 1) * width] = rows[2 + side : 3 + side, :]
    lane = lax.broadcasted_iota(jnp.int32, (8, width), 1)
    for k, at in enumerate((1, 3)):
        own = jnp.where(lane < hw, pltpu.roll(rows, width - at * hw, 1), 0.0)
        b_qv[0, k : k + 1, :] = (own[4:5] + pltpu.roll(own, hw, 1)[5:6])[:, :lw]
    cut = half(rows)
    b_down[...] = cut[0:1, :lw]
    b_out[...] = cut[1:2, :lw]
    mask[...] = cut[6:7, :lw]
    rel[0] = table[:, : rel.shape[2]]
    value = dm[0].astype(F32)
    for j in range(1, count):
        value = value + dm[j].astype(F32)
    b_ada[:, 0, :] = (value[0:8] + value[8:16])[0:6, :lw]
    for wait in waits:
        wait()


def finish_call(cfg, classes, length, red, outs, dx, two, dm, cl):
    _, _, heads, head_dim = cfg
    lw = heads * head_dim
    shard, width = red.shape[2:]
    f = lambda *s: jax.ShapeDtypeStruct(s, F32)

    def body(*refs):
        finish_kernel(cfg, *refs)

    vm = pl.BlockSpec(memory_space=pltpu.VMEM)
    hbm = pl.BlockSpec(memory_space=pl.ANY)
    large = [
        f(1, *outs.shape),
        f(1, *dx.shape),
        f(3, shard, lw),
        f(shard, lw),
        f(1, shard, 2 * width),
        f(shard, 2 * width),
        f(6, shard, lw),
        f(lw, classes),
    ]
    small = [
        f(1, 2, lw),
        f(1, lw),
        f(1, 2 * width),
        f(1, lw),
        f(6, 1, lw),
        f(1, heads, 2 * length - 1),
        f(1, lw),
    ]
    return pl.pallas_call(
        body,
        out_shape=large + small,
        in_specs=[hbm, hbm, hbm, vm, vm, vm],
        out_specs=[hbm] * len(large) + [vm] * len(small),
        scratch_shapes=[
            pltpu.VMEM((2, shard, width), F32),
            pltpu.VMEM((2, 2, shard, width), F32),
            pltpu.VMEM((3, shard, lw), F32),
            pltpu.VMEM((shard, lw), F32),
            pltpu.VMEM((6, shard, lw), F32),
            pltpu.VMEM((lw, classes), F32),
            pltpu.VMEM((2, *outs.shape), F32),
            pltpu.SemaphoreType.DMA((14,)),
        ],
        compiler_params=pltpu.CompilerParams(vmem_limit_bytes=VMEM_BYTES),
        name="last_layouts",
    )(red, outs, dx, two, dm, cl)


def per_device(
    tokens,
    kept_mask,
    timesteps,
    labels,
    w_qkv,
    b_qv,
    w_out,
    b_out,
    w_up,
    b_up,
    w_down,
    b_down,
    w_ada,
    b_ada,
    rel_table,
    mask_token,
    class_table,
    out_grad,
):
    micro, rows, width = tokens.shape
    length = kept_mask.shape[2]
    classes = class_table.shape[0]
    heads = rel_table.shape[1]
    lw = w_qkv.shape[3]
    head_dim = lw // heads
    hw = lw // 2
    ff = w_up.shape[2]
    fw = ff // 2
    dp_count = lax.axis_size("dp")
    c = lax.axis_index("section")
    dp = lax.axis_index("dp")
    h = lax.axis_index("head")

    qkv = jnp.transpose(w_qkv[0], (1, 0, 2))
    out_t = w_out[0].T
    down_t = w_down[0].T
    fr = width // dp_count

    label_pick = (labels == jnp.arange(classes)[None, :]).astype(BF)
    cond = nn(label_pick, class_table) + time_features(timesteps[:, 0], width)
    cond = jnp.concatenate([cond, mask_token[None, :].astype(F32)])
    blocks = jnp.transpose(cond.reshape(micro + 1, dp_count, fr), (1, 0, 2))
    tags = jnp.pad(labels.astype(F32), ((0, 1), (0, 0)))
    tags = jnp.broadcast_to(tags[None], (dp_count, micro + 1, 1))
    cond_lanes = -(-(fr + 1) // 128) * 128
    blocks = jnp.concatenate([blocks, tags], axis=2)
    blocks = jnp.pad(blocks, ((0, 0), (0, 7 - micro), (0, cond_lanes - fr - 1)))
    ada = jnp.transpose(w_ada[0], (1, 0, 2))

    fused = dp_count == 8 and fr % 16 == 0
    cfg = (fused, dp_count // 2, heads, head_dim)
    att = []
    for half in range(2):
        at = slice(half * hw, (half + 1) * hw)
        att.append(jnp.concatenate([out_t[:, at], qkv[0][:, at], qkv[1][:, at], qkv[2][:, at]], axis=1))
    if fused:
        source_w = (jnp.stack(att), w_up, down_t)
    else:
        halves = []
        for half in range(2):
            fat = slice(half * fw, (half + 1) * fw)
            halves.append(jnp.stack([att[half], w_up[0][:, fat], down_t[:, fat]]))
        other_w = swap(mine(1 - c, halves), "section")
        own_w = mine(c, halves)
        own_w = jnp.concatenate([pick(c, own_w, other_w), pick(c, other_w, own_w)])
        half_w_ = lax.all_gather(own_w, "dp", axis=1, tiled=True)
        other_w = swap(half_w_, "section")
        source_w = jnp.stack([pick(c, half_w_, other_w), pick(c, other_w, half_w_)], axis=1)
        source_w = (source_w.reshape(6, 2, 8, width // 8, 4 * hw),)
    small_in = (
        tokens,
        blocks,
        ada,
        b_ada,
        kept_mask,
        b_qv,
        b_out,
        b_down,
        b_up,
        rel_table,
    )
    full, *saved, mod, cond_all, small_all, enc = forward_call(cfg, source_w, small_in, dp_count)
    saved.append(enc)
    small_back = (out_grad, mod, small_all, cond_all, ada, kept_mask)
    red, dx, outs, dm, two = backward_call(cfg, full, saved, small_back)

    if fused:
        last = finish_call(cfg, classes, length, red, outs, dx, two, dm, cond_all)
        outs, dx, g_qkv, g_out, g_up, g_down, g_ada, g_class = last[:8]
        g_b_qv, g_b_out, g_b_up, g_b_down, g_b_ada, g_rel, g_mask = last[8:]
        return (
            outs,
            dx,
            jnp.transpose(g_qkv, (1, 0, 2))[None],
            g_b_qv,
            g_out.T[None],
            g_b_out,
            g_up,
            g_b_up,
            g_down.T[None],
            g_b_down,
            jnp.transpose(g_ada, (1, 0, 2))[None],
            jnp.transpose(g_b_ada, (1, 0, 2)),
            g_rel,
            g_mask[0],
            g_class.T,
        )
    red = lax.psum_scatter(
        red.reshape(6, width, 4 * hw), "dp", scatter_dimension=1, tiled=True
    ).astype(F32)
    red = red.reshape(2, 3, fr, 4 * hw)
    g_own = mine(c, red)
    g_got = swap(mine(1 - c, red), "section")
    g0, g1 = pick(c, g_own, g_got), pick(c, g_got, g_own)
    g_qkv = jnp.stack(
        [
            jnp.concatenate([g0[0][:, i * hw : (i + 1) * hw], g1[0][:, i * hw : (i + 1) * hw]], axis=1)
            for i in (1, 2, 3)
        ],
        axis=1,
    )
    g_out = jnp.concatenate([g0[0][:, :hw], g1[0][:, :hw]], axis=1).T
    g_up = jnp.concatenate([g0[1], g1[1]], axis=1)
    g_down = jnp.concatenate([g0[2], g1[2]], axis=1).T

    cond_lanes = cond_all.shape[2]
    sums, rel_rows, dc = unpack_two(two, dp_count, cond_lanes)
    dc = jnp.stack([jnp.stack(pair) for pair in dc])
    half_w = width // 2

    def half(v):
        return lax.dynamic_slice_in_dim(v, h * half_w, half_w, v.ndim - 1)

    g_b_qv = jnp.stack(
        [
            jnp.concatenate([sums[4, at * hw : (at + 1) * hw], sums[5, at * hw : (at + 1) * hw]])
            for at in (1, 3)
        ]
    )
    g_b_up = sums[2:4, :fw].reshape(-1)
    g_rel = rel_rows[:, : 2 * length - 1]

    dm = dm.astype(F32).reshape(dp_count, micro, 8, ADA_LANES)[:, :, :6, :lw]
    cond_part = jax.nn.silu(cond_all[:, :micro, :fr])
    g_ada = jnp.einsum("jmf,jmke->fke", cond_part, dm, precision=PRECISE)
    g_b_ada = jnp.sum(dm, axis=(0, 1))
    labels_all = cond_all[:, :micro, fr].astype(jnp.int32).T.reshape(-1)
    dcond = jnp.transpose(dc[..., :fr], (1, 2, 0, 3)).reshape(micro * dp_count, width)
    pick_all = (labels_all[:, None] == jnp.arange(classes)[None, :]).astype(F32)
    g_class = jnp.einsum("ic,id->cd", pick_all, half(dcond), precision=PRECISE)

    return (
        outs[None],
        dx[None],
        g_qkv[None],
        g_b_qv[None],
        g_out[None],
        half(sums[1])[None],
        g_up[None],
        g_b_up[None],
        g_down[None],
        half(sums[0])[None],
        g_ada[None],
        g_b_ada[None],
        g_rel[None],
        half(sums[6]),
        g_class,
    )


def solution(mesh):
    placed = (
        P(None, "dp", None),
        P(None, "dp", None),
        P(None, "dp"),
        P(None, "dp"),
        P("section", "dp", None, "head"),
        P("section", None, "head"),
        P("section", "head", "dp"),
        P("section", None),
        P("section", "dp", "head"),
        P("section", "head"),
        P("section", "head", "dp"),
        P("section", None),
        P("section", "dp", None, "head"),
        P("section", None, "head"),
        P("section", "head", None),
        P(),
        P(),
        P(None, "dp", None),
    )
    return jax.shard_map(
        per_device,
        mesh=mesh,
        in_specs=placed,
        out_specs=(
            P("section", None, "dp", None),
            P("section", None, "dp", None),
            P("section", "dp", None, "head"),
            P("section", None, "head"),
            P("section", "head", "dp"),
            P("section", "head"),
            P("section", "dp", "head"),
            P("section", "head"),
            P("section", "head", "dp"),
            P("section", "head"),
            P("section", "dp", None, "head"),
            P("section", None, "head"),
            P("section", "head", None),
            P("head"),
            P(None, "head"),
        ),
        check_vma=False,
    )
```
